32 devices in a mesh: depth: 4 (over y, x), res: 8 (over z, core).
Axes of the slice: x: 2, y: 2, z: 4, core: 2. Of those that a mesh axis runs over, the one named last changes fastest.
Arguments:
- family_activity: bfloat16 [1024, 8, 768], P('depth', 'res'), may hold values from -6 to 6
- rescale_factor: float32 [768], replicated, may hold values from 0.25 to 1.75
- asking_weights: bfloat16 [768, 768], P(('depth', 'res')), may hold values from -1.203125 to 1.203125
- lookup_weights: bfloat16 [768, 768], P(('depth', 'res')), may hold values from -1.203125 to 1.203125
- payload_weights: bfloat16 [768, 768], P(('depth', 'res')), may hold values from -0.21875 to 0.21875
- exit_weights: bfloat16 [768, 768], P(('depth', 'res')), may hold values from -0.625 to 0.625
- upstream_adjoint: bfloat16 [1024, 8, 768], P('depth', 'res'), may hold values from -6 to 6
Outputs:
- final_result: bfloat16 [1024, 8, 768], P('depth', 'res')
- alignment_gradient: bfloat16 [1024, 8, 768], P('depth', 'res')
- query_gradient: float32 [768, 768], P(('depth', 'res'))
- key_gradient: float32 [768, 768], P(('depth', 'res'))
- value_gradient: float32 [768, 768], P(('depth', 'res'))
- output_gradient: float32 [768, 768], P(('depth', 'res'))
- gain_gradient: float32 [768], P(('depth', 'res'))
The draws below stay inside these ranges and needn't reach their ends.
All inputs are finite; a program needn't handle non-finite values.
Results may differ from the reference program's by a relative error of at most 0.022.
The reference program's roundings to bfloat16 on the way count: a program that leaves them out, or rounds other values in their place, can miss the bound.
Values may be sent and summed in bfloat16 or wider, within the bound.
No kernel may reach another device: no remote copies, remote signals or barrier semaphores. Data moves between devices by JAX's collectives and lax.ppermute only.
A program may use at most 128 MiB of HBM per device.

```python
import jax
import jax.numpy as jnp
from jax import lax

HEADS = 12
HEAD_DIM = 64
EMBED_SPAN = 768
HOMOLOG_TOTAL = 1024
POSITION_TOTAL = 8
N_DEPTH = 4


def draw_asking_weights(key, part):
    key = jax.random.fold_in(key, 11)
    payload_entries = jnp.clip(jax.random.normal(key, (EMBED_SPAN, EMBED_SPAN), jnp.float32), -5.0, 5.0) * (2.0 / EMBED_SPAN) ** 0.5
    return payload_entries.astype(jnp.bfloat16)


def draw_lookup_weights(key, part):
    key = jax.random.fold_in(key, 12)
    own = jnp.clip(jax.random.normal(key, (EMBED_SPAN, EMBED_SPAN), jnp.float32), -5.0, 5.0)
    payload_entries = own * (2.0 / EMBED_SPAN) ** 0.5
    return payload_entries.astype(jnp.bfloat16)


def steps_of(rng, shape, cuts, low, largest):
    def one(dim, shards_of):
        draws = jax.random.uniform(jax.random.fold_in(jax.random.fold_in(rng, 6), dim), (shards_of,), jnp.float32, low / len(cuts), largest / len(cuts))
        return jnp.repeat(jnp.exp(draws), shape[dim] // shards_of).reshape((-1,) + (1,) * (len(shape) - dim - 1))

    gain = one(*cuts[0])
    for cut in cuts[1:]:
        gain = gain * one(*cut)
    return gain


def centred(own_key, shape, deviation, limit, shards=(), kind=jnp.bfloat16):
    values = jax.random.normal(own_key, shape, jnp.float32) * deviation
    if len(shards) > 0:
        values = steps_of(own_key, shape, shards, -0.22, 0.18) * values
    return jnp.clip(values, min=-limit, max=limit).astype(kind)


def setup_inputs(seed: int = 0) -> dict:
    key_list = jax.random.split(jax.random.key(seed), 8)
    family_activity = centred(key_list[0], (HOMOLOG_TOTAL, POSITION_TOTAL, EMBED_SPAN), 1.0, 6.0, ((0, 4), (1, 8)))
    rescale_factor = jnp.clip(1.0 + 0.15 * jax.random.normal(key_list[1], (EMBED_SPAN,), jnp.float32), 0.25, 1.75)
    asking_weights = draw_asking_weights(jax.random.fold_in(key_list[7], 71), 0)
    lookup_weights = draw_lookup_weights(jax.random.fold_in(key_list[7], 71), 0)
    payload_weights = centred(key_list[4], (EMBED_SPAN, EMBED_SPAN), EMBED_SPAN ** -0.5, 0.21875, ((0, 32),))
    exit_weights = centred(key_list[5], (EMBED_SPAN, EMBED_SPAN), (EMBED_SPAN // 8) ** -0.5, 0.625, ((0, 32),))
    upstream_adjoint = centred(key_list[6], (HOMOLOG_TOTAL, POSITION_TOTAL, EMBED_SPAN), 1.0, 6.0, ((0, 4), (1, 8)))
    return dict(family_activity=family_activity, rescale_factor=rescale_factor, asking_weights=asking_weights, lookup_weights=lookup_weights, payload_weights=payload_weights, exit_weights=exit_weights, upstream_adjoint=upstream_adjoint)


def standardize_entries(family_activity, rescale_factor):
    payload_entries = family_activity.astype(jnp.float32)
    centered = payload_entries - lax.optimization_barrier(jnp.mean(payload_entries, axis=-1, keepdims=True))
    reciprocal_spread = lax.rsqrt(lax.optimization_barrier(jnp.mean(centered * centered, axis=-1, keepdims=True)) + 1e-05)
    standardized_entries = centered * reciprocal_spread
    return ((standardized_entries * rescale_factor).astype(jnp.bfloat16), standardized_entries, reciprocal_spread)

def project(rows, weight, factor):
    return (factor * jnp.dot(rows, weight, preferred_element_type=jnp.float32)).astype(jnp.bfloat16)

def to_heads(array):
    count, cols = (array.shape[0], array.shape[1])
    return jnp.transpose(array.reshape(count, cols, HEADS, HEAD_DIM), (1, 2, 0, 3)).reshape(cols * HEADS, count, HEAD_DIM)

def from_heads(array, cols):
    count = array.shape[1]
    return jnp.transpose(array.reshape(cols, HEADS, count, HEAD_DIM), (2, 0, 1, 3)).reshape(count, cols, HEADS * HEAD_DIM)

def head_pass(query, keys, payload_entries, d_att):
    scale = HEAD_DIM ** (-0.5)
    scores = jnp.dot(query, keys.T, preferred_element_type=jnp.float32)
    probs = jax.nn.softmax(scores, axis=-1)
    probs_b = probs.astype(jnp.bfloat16)
    mixed_homologs = jnp.dot(probs_b, payload_entries, preferred_element_type=jnp.float32).astype(jnp.bfloat16)
    d_probs = jnp.dot(d_att, payload_entries.T, preferred_element_type=jnp.float32)
    d_scores = probs * (d_probs - lax.optimization_barrier(jnp.sum(probs * d_probs, axis=-1, keepdims=True)))
    d_scores_b = d_scores.astype(jnp.bfloat16)
    d_query = (scale * jnp.dot(d_scores_b, keys, preferred_element_type=jnp.float32)).astype(jnp.bfloat16)
    homolog_total = query.shape[0]
    block = homolog_total // N_DEPTH
    blocks_s = d_scores_b.astype(jnp.float32).reshape(N_DEPTH, block, homolog_total)
    blocks_p = probs_b.astype(jnp.float32).reshape(N_DEPTH, block, homolog_total)
    query_blocks = query.astype(jnp.float32).reshape(N_DEPTH, block, HEAD_DIM)
    datt_blocks = d_att.astype(jnp.float32).reshape(N_DEPTH, block, HEAD_DIM)
    key_parts = jnp.einsum('jst,jsd->jtd', blocks_s, query_blocks).astype(jnp.bfloat16)
    value_parts = jnp.einsum('jst,jsd->jtd', blocks_p, datt_blocks).astype(jnp.bfloat16)
    key_parts = lax.optimization_barrier(key_parts)
    value_parts = lax.optimization_barrier(value_parts)
    d_keys = lax.optimization_barrier(jnp.sum(key_parts.astype(jnp.float32), axis=0)).astype(jnp.bfloat16)
    d_values = lax.optimization_barrier(jnp.sum(value_parts.astype(jnp.float32), axis=0)).astype(jnp.bfloat16)
    return (mixed_homologs, d_query, d_keys, d_values)

def reference(family_activity, rescale_factor, asking_weights, lookup_weights, payload_weights, exit_weights, upstream_adjoint):
    homolog_total, position_total, embed_span = family_activity.shape
    standardized_source, standardized_entries, reciprocal_spread = standardize_entries(family_activity, rescale_factor)
    query = project(standardized_source, asking_weights, HEAD_DIM ** (-0.5))
    keys = project(standardized_source, lookup_weights, 1.0)
    payload_entries = project(standardized_source, payload_weights, 1.0)
    d_att = jnp.dot(upstream_adjoint, exit_weights.T, preferred_element_type=jnp.float32).astype(jnp.bfloat16)

    def per_head(items):
        return head_pass(items[0], items[1], items[2], items[3])
    results = lax.map(per_head, (to_heads(query), to_heads(keys), to_heads(payload_entries), to_heads(d_att)))
    mixed_homologs, d_query, d_keys, d_values = [from_heads(item, position_total) for item in results]
    final_result = (family_activity.astype(jnp.float32) + jnp.dot(mixed_homologs, exit_weights, preferred_element_type=jnp.float32)).astype(jnp.bfloat16)
    rows = homolog_total * position_total
    normed_rows = standardized_source.reshape(rows, embed_span)
    query_gradient = jnp.dot(normed_rows.T, d_query.reshape(rows, embed_span), preferred_element_type=jnp.float32)
    key_gradient = jnp.dot(normed_rows.T, d_keys.reshape(rows, embed_span), preferred_element_type=jnp.float32)
    value_gradient = jnp.dot(normed_rows.T, d_values.reshape(rows, embed_span), preferred_element_type=jnp.float32)
    output_gradient = jnp.dot(mixed_homologs.reshape(rows, embed_span).T, upstream_adjoint.reshape(rows, embed_span), preferred_element_type=jnp.float32)
    d_normed = jnp.dot(d_query, asking_weights.T, preferred_element_type=jnp.float32)
    d_normed = d_normed + jnp.dot(d_keys, lookup_weights.T, preferred_element_type=jnp.float32)
    d_normed = d_normed + jnp.dot(d_values, payload_weights.T, preferred_element_type=jnp.float32)
    gain_gradient = lax.optimization_barrier(jnp.sum((d_normed * standardized_entries).reshape(rows, embed_span), axis=0))
    unit_gradient = d_normed * rescale_factor
    alignment_gradient = upstream_adjoint.astype(jnp.float32) + reciprocal_spread * (unit_gradient - lax.optimization_barrier(jnp.mean(unit_gradient, axis=-1, keepdims=True)) - standardized_entries * lax.optimization_barrier(jnp.mean(unit_gradient * standardized_entries, axis=-1, keepdims=True)))
    return (final_result, alignment_gradient.astype(jnp.bfloat16), query_gradient, key_gradient, value_gradient, output_gradient, gain_gradient)
```

```python
import jax
import jax.numpy as jnp
from jax import lax
from jax.sharding import PartitionSpec as P

HEADS = 12
HEAD_DIM = 64


def standardize_entries(family_activity, rescale_factor):
    payload_entries = family_activity.astype(jnp.float32)
    centered = payload_entries - jnp.mean(payload_entries, axis=-1, keepdims=True)
    reciprocal_spread = lax.rsqrt(jnp.mean(centered * centered, axis=-1, keepdims=True) + 1e-05)
    standardized_entries = centered * reciprocal_spread
    return (
        (standardized_entries * rescale_factor).astype(jnp.bfloat16),
        standardized_entries,
        reciprocal_spread,
    )


def project(rows, weight, factor):
    return (factor * jnp.dot(rows, weight, preferred_element_type=jnp.float32)).astype(jnp.bfloat16)


def to_heads(array):
    count, cols = (array.shape[0], array.shape[1])
    return jnp.transpose(array.reshape(count, cols, HEADS, HEAD_DIM), (1, 2, 0, 3)).reshape(
        cols * HEADS, count, HEAD_DIM
    )


def from_heads(array, cols):
    count = array.shape[1]
    return jnp.transpose(array.reshape(cols, HEADS, count, HEAD_DIM), (2, 0, 1, 3)).reshape(
        count, cols, HEADS * HEAD_DIM
    )


def head_pass(query, keys, payload_entries, d_att):
    scale = HEAD_DIM ** (-0.5)
    scores = jnp.dot(query, keys.T, preferred_element_type=jnp.float32)
    probs = jax.nn.softmax(scores, axis=-1)
    probs_b = probs.astype(jnp.bfloat16)
    mixed_homologs = jnp.dot(probs_b, payload_entries, preferred_element_type=jnp.float32).astype(
        jnp.bfloat16
    )
    d_probs = jnp.dot(d_att, payload_entries.T, preferred_element_type=jnp.float32)
    d_scores = probs * (d_probs - jnp.sum(probs * d_probs, axis=-1, keepdims=True))
    d_scores_b = d_scores.astype(jnp.bfloat16)
    d_query = (scale * jnp.dot(d_scores_b, keys, preferred_element_type=jnp.float32)).astype(
        jnp.bfloat16
    )
    key_part = jnp.einsum("st,sd->td", d_scores_b, query, preferred_element_type=jnp.float32)
    value_part = jnp.einsum("st,sd->td", probs_b, d_att, preferred_element_type=jnp.float32)
    return (mixed_homologs, d_query, key_part, value_part)


def general_body(
    family_activity,
    rescale_factor,
    asking_weights,
    lookup_weights,
    payload_weights,
    exit_weights,
    upstream_adjoint,
):
    query_weight, key_weight, value_weight, output_matrix = (
        lax.all_gather(asking_weights, ("depth", "res"), axis=0, tiled=True),
        lax.all_gather(lookup_weights, ("depth", "res"), axis=0, tiled=True),
        lax.all_gather(payload_weights, ("depth", "res"), axis=0, tiled=True),
        lax.all_gather(exit_weights, ("depth", "res"), axis=0, tiled=True),
    )
    homologs_each_shard, positions_each_shard, embed_span = family_activity.shape
    standardized_source, standardized_entries, reciprocal_spread = standardize_entries(
        family_activity, rescale_factor
    )
    query = project(standardized_source, query_weight, HEAD_DIM ** (-0.5))
    keys = project(standardized_source, key_weight, 1.0)
    payload_entries = project(standardized_source, value_weight, 1.0)
    keys_all, values_all = (
        lax.all_gather(keys, "depth", axis=0, tiled=True),
        lax.all_gather(payload_entries, "depth", axis=0, tiled=True),
    )
    d_att = jnp.dot(upstream_adjoint, output_matrix.T, preferred_element_type=jnp.float32).astype(
        jnp.bfloat16
    )

    def per_head(items):
        return head_pass(items[0], items[1], items[2], items[3])

    mixed_homologs, d_query, key_part, value_part = lax.map(
        per_head, (to_heads(query), to_heads(keys_all), to_heads(values_all), to_heads(d_att))
    )
    mixed_homologs = from_heads(mixed_homologs, positions_each_shard)
    d_query = from_heads(d_query, positions_each_shard)
    key_part = from_heads(key_part, positions_each_shard)
    value_part = from_heads(value_part, positions_each_shard)
    rows = homologs_each_shard * positions_each_shard
    normed_rows = standardized_source.reshape(rows, embed_span)
    part_query = jnp.dot(
        normed_rows.T, d_query.reshape(rows, embed_span), preferred_element_type=jnp.float32
    )
    part_out = jnp.dot(
        mixed_homologs.reshape(rows, embed_span).T,
        upstream_adjoint.reshape(rows, embed_span),
        preferred_element_type=jnp.float32,
    )
    stacked = jnp.stack([key_part, value_part], axis=2).astype(jnp.bfloat16)
    summed = (
        lax.psum_scatter(stacked, "depth", scatter_dimension=0, tiled=True)
        .astype(jnp.float32)
        .astype(jnp.bfloat16)
    )
    d_keys = summed[:, :, 0, :]
    d_values = summed[:, :, 1, :]
    final_result = (
        family_activity.astype(jnp.float32)
        + jnp.dot(mixed_homologs, output_matrix, preferred_element_type=jnp.float32)
    ).astype(jnp.bfloat16)
    part_key = jnp.dot(
        normed_rows.T, d_keys.reshape(rows, embed_span), preferred_element_type=jnp.float32
    )
    part_value = jnp.dot(
        normed_rows.T, d_values.reshape(rows, embed_span), preferred_element_type=jnp.float32
    )
    d_normed = jnp.dot(d_query, query_weight.T, preferred_element_type=jnp.float32)
    d_normed = d_normed + jnp.dot(d_keys, key_weight.T, preferred_element_type=jnp.float32)
    d_normed = d_normed + jnp.dot(d_values, value_weight.T, preferred_element_type=jnp.float32)
    part_gain = jnp.sum((d_normed * standardized_entries).reshape(rows, embed_span), axis=0)
    unit_gradient = d_normed * rescale_factor
    alignment_gradient = upstream_adjoint.astype(jnp.float32) + reciprocal_spread * (
        unit_gradient
        - jnp.mean(unit_gradient, axis=-1, keepdims=True)
        - standardized_entries
        * jnp.mean(unit_gradient * standardized_entries, axis=-1, keepdims=True)
    )
    query_gradient, key_gradient, value_gradient, output_gradient, gain_gradient = (
        lax.psum_scatter(part_query, ("depth", "res"), scatter_dimension=0, tiled=True),
        lax.psum_scatter(part_key, ("depth", "res"), scatter_dimension=0, tiled=True),
        lax.psum_scatter(part_value, ("depth", "res"), scatter_dimension=0, tiled=True),
        lax.psum_scatter(part_out, ("depth", "res"), scatter_dimension=0, tiled=True),
        lax.psum_scatter(part_gain, ("depth", "res"), scatter_dimension=0, tiled=True),
    )
    return (
        final_result,
        alignment_gradient.astype(jnp.bfloat16),
        query_gradient,
        key_gradient,
        value_gradient,
        output_gradient,
        gain_gradient,
    )


def swap(value, axis, size, bits):
    return lax.ppermute(value, axis, [(i, i ^ bits) for i in range(size)])


def pick(array, index, axis):
    return lax.dynamic_index_in_dim(array, index, axis, keepdims=False)


def attend(query, keys, values, d_att, block):
    scale = HEAD_DIM ** (-0.5)
    scores = jnp.dot(query, keys.T, preferred_element_type=jnp.float32)
    probs = jax.nn.softmax(scores, axis=-1)
    probs_b = probs.astype(jnp.bfloat16)
    mixed = jnp.dot(probs_b, values, preferred_element_type=jnp.float32).astype(jnp.bfloat16)
    d_probs = jnp.dot(d_att, values.T, preferred_element_type=jnp.float32)
    d_scores = probs * (d_probs - jnp.sum(probs * d_probs, axis=-1, keepdims=True))
    d_scores_b = d_scores.astype(jnp.bfloat16)
    d_query = (scale * jnp.dot(d_scores_b, keys, preferred_element_type=jnp.float32)).astype(
        jnp.bfloat16
    )
    d_keys = jnp.einsum("st,sd->td", d_scores_b, query, preferred_element_type=jnp.float32)
    d_values = jnp.einsum("st,sd->td", probs_b, d_att, preferred_element_type=jnp.float32)
    return mixed, d_query, d_keys.astype(jnp.bfloat16), d_values.astype(jnp.bfloat16)


def head_body(depth, res, args):
    x, gain, w_query, w_key, w_value, w_out, upstream = args
    own_d, own_r = lax.axis_index("depth"), lax.axis_index("res")
    homologs, _, width = x.shape
    span = width // depth
    shard = w_query.shape[0]
    x = x.reshape(homologs, width)
    upstream = upstream.reshape(homologs, width)

    w3 = jnp.stack([w_query, w_key, w_value], axis=0).reshape(3, shard, depth, span)
    w_rel = [pick(w3, own_d, 2)] + [
        swap(pick(w3, own_d ^ k, 2), "depth", depth, k) for k in range(1, depth)
    ]
    w_rel = jnp.stack(w_rel, axis=0)

    def gather_res(value):
        parts = [value] + [swap(value, "res", res, 2 * k) for k in range(1, res // 2)]
        parts = jnp.stack(parts, axis=0)
        other = swap(parts, "res", res, 1)
        return jnp.stack([parts, other], axis=1).reshape((res,) + value.shape)

    w_rel = gather_res(w_rel)
    wo_rel = gather_res(w_out)
    w_rel = jnp.take(jnp.take(w_rel, jnp.arange(res) ^ own_r, axis=0), jnp.arange(depth) ^ own_d, axis=1)
    w_heads = jnp.transpose(w_rel, (2, 1, 0, 3, 4)).reshape(3, width, span)
    wo_heads = jnp.take(wo_rel, jnp.arange(res) ^ own_r, axis=0).reshape(span, width)

    x_all = jnp.concatenate([x] + [swap(x, "depth", depth, k) for k in range(1, depth)], axis=0)
    g_all = jnp.concatenate(
        [upstream] + [swap(upstream, "depth", depth, k) for k in range(1, depth)], axis=0
    )

    normed, unit, inverse = standardize_entries(x_all, gain)
    query = project(normed, w_heads[0], HEAD_DIM ** (-0.5))
    keys = project(normed, w_heads[1], 1.0)
    values = project(normed, w_heads[2], 1.0)
    d_att = jnp.dot(g_all, wo_heads.T, preferred_element_type=jnp.float32).astype(jnp.bfloat16)

    total = x_all.shape[0]
    heads = span // HEAD_DIM

    def split(a):
        return jnp.transpose(a.reshape(total, heads, HEAD_DIM), (1, 0, 2))

    def join(a):
        return jnp.transpose(a, (1, 0, 2)).reshape(total, span)

    mixed, d_query, d_keys, d_values = lax.map(
        lambda items: attend(*items, homologs),
        (split(query), split(keys), split(values), split(d_att)),
    )
    mixed, d_query, d_keys, d_values = join(mixed), join(d_query), join(d_keys), join(d_values)

    def scatter_depth(blocks):
        blocks = blocks.reshape(depth, homologs, width)
        acc = blocks[0]
        for k in range(1, depth):
            acc = acc + swap(blocks[k].astype(jnp.bfloat16), "depth", depth, k).astype(jnp.float32)
        return acc

    out_part = jnp.dot(mixed, wo_heads, preferred_element_type=jnp.float32)
    final_result = (x.astype(jnp.float32) + scatter_depth(out_part)).astype(jnp.bfloat16)

    d_normed = jnp.dot(d_query, w_heads[0].T, preferred_element_type=jnp.float32)
    d_normed = d_normed + jnp.dot(d_keys, w_heads[1].T, preferred_element_type=jnp.float32)
    d_normed = d_normed + jnp.dot(d_values, w_heads[2].T, preferred_element_type=jnp.float32)
    gain_part = jnp.sum(d_normed * unit, axis=0)
    d_normed = scatter_depth(d_normed)
    own_unit, own_inverse = unit[:homologs], inverse[:homologs]
    d_unit = d_normed * gain
    alignment = upstream.astype(jnp.float32) + own_inverse * (
        d_unit
        - jnp.mean(d_unit, axis=-1, keepdims=True)
        - own_unit * jnp.mean(d_unit * own_unit, axis=-1, keepdims=True)
    )

    grads3 = [
        jnp.dot(normed.T, d, preferred_element_type=jnp.float32) for d in (d_query, d_keys, d_values)
    ]
    grads3 = jnp.stack(grads3, axis=0).reshape(3, depth, res // 2, 2, shard, span)
    grad_out = jnp.dot(mixed.T, g_all, preferred_element_type=jnp.float32)
    grad_out = grad_out.reshape(1, 1, res // 2, 2, shard, width)

    own_core, own_z = own_r % 2, own_r // 2

    def scatter_res(value):
        kept = pick(value, own_core, 3)
        sent = pick(value, 1 - own_core, 3).astype(jnp.bfloat16)
        kept = kept + swap(sent, "res", res, 1).astype(jnp.float32)
        acc = pick(kept, own_z, 2)
        low = kept.astype(jnp.bfloat16)
        for k in range(1, res // 2):
            acc = acc + swap(pick(low, own_z ^ k, 2), "res", res, 2 * k).astype(jnp.float32)
        return acc

    grad_out = scatter_res(grad_out).reshape(shard, width)
    grads3 = scatter_res(grads3)
    grads3_b = grads3.astype(jnp.bfloat16)
    rel = [pick(grads3, own_d, 1)] + [
        swap(pick(grads3_b, own_d ^ k, 1), "depth", depth, k).astype(jnp.float32)
        for k in range(1, depth)
    ]
    rel = jnp.take(jnp.stack(rel, axis=0), jnp.arange(depth) ^ own_d, axis=0)
    grads3 = jnp.transpose(rel, (1, 2, 0, 3)).reshape(3, shard, width)

    gain_gradient = lax.psum_scatter(gain_part, ("depth", "res"), scatter_dimension=0, tiled=True)
    return (
        final_result.reshape(homologs, 1, width),
        alignment.astype(jnp.bfloat16).reshape(homologs, 1, width),
        grads3[0],
        grads3[1],
        grads3[2],
        grad_out,
        gain_gradient,
    )


def body(depth, res, *args):
    powers = depth & (depth - 1) == 0 and res & (res - 1) == 0 and res > 1
    if powers and HEADS % depth == 0 and args[0].shape[1] == 1:
        return head_body(depth, res, args)
    return general_body(*args)


def solution(mesh):
    depth, res = mesh.shape["depth"], mesh.shape["res"]
    return jax.shard_map(
        lambda *args: body(depth, res, *args),
        mesh=mesh,
        in_specs=(
            P("depth", "res", None),
            P(),
            P(("depth", "res"), None),
            P(("depth", "res"), None),
            P(("depth", "res"), None),
            P(("depth", "res"), None),
            P("depth", "res", None),
        ),
        out_specs=(
            P("depth", "res", None),
            P("depth", "res", None),
            P(("depth", "res"), None),
            P(("depth", "res"), None),
            P(("depth", "res"), None),
            P(("depth", "res"), None),
            P(("depth", "res")),
        ),
        check_vma=False,
    )
```

```python
import functools

import jax
import jax.numpy as jnp
from jax import lax
from jax.experimental import pallas as pl
from jax.experimental.pallas import tpu as pltpu
from jax.sharding import PartitionSpec as P

HEADS = 12
HEAD_DIM = 64


def standardize_entries(family_activity, rescale_factor):
    payload_entries = family_activity.astype(jnp.float32)
    centered = payload_entries - jnp.mean(payload_entries, axis=-1, keepdims=True)
    reciprocal_spread = lax.rsqrt(jnp.mean(centered * centered, axis=-1, keepdims=True) + 1e-05)
    standardized_entries = centered * reciprocal_spread
    return (
        (standardized_entries * rescale_factor).astype(jnp.bfloat16),
        standardized_entries,
        reciprocal_spread,
    )


def project(rows, weight, factor):
    return (factor * jnp.dot(rows, weight, preferred_element_type=jnp.float32)).astype(jnp.bfloat16)


def to_heads(array):
    count, cols = (array.shape[0], array.shape[1])
    return jnp.transpose(array.reshape(count, cols, HEADS, HEAD_DIM), (1, 2, 0, 3)).reshape(
        cols * HEADS, count, HEAD_DIM
    )


def from_heads(array, cols):
    count = array.shape[1]
    return jnp.transpose(array.reshape(cols, HEADS, count, HEAD_DIM), (2, 0, 1, 3)).reshape(
        count, cols, HEADS * HEAD_DIM
    )


def head_pass(query, keys, payload_entries, d_att):
    scale = HEAD_DIM ** (-0.5)
    scores = jnp.dot(query, keys.T, preferred_element_type=jnp.float32)
    probs = jax.nn.softmax(scores, axis=-1)
    probs_b = probs.astype(jnp.bfloat16)
    mixed_homologs = jnp.dot(probs_b, payload_entries, preferred_element_type=jnp.float32).astype(
        jnp.bfloat16
    )
    d_probs = jnp.dot(d_att, payload_entries.T, preferred_element_type=jnp.float32)
    d_scores = probs * (d_probs - jnp.sum(probs * d_probs, axis=-1, keepdims=True))
    d_scores_b = d_scores.astype(jnp.bfloat16)
    d_query = (scale * jnp.dot(d_scores_b, keys, preferred_element_type=jnp.float32)).astype(
        jnp.bfloat16
    )
    key_part = jnp.einsum("st,sd->td", d_scores_b, query, preferred_element_type=jnp.float32)
    value_part = jnp.einsum("st,sd->td", probs_b, d_att, preferred_element_type=jnp.float32)
    return (mixed_homologs, d_query, key_part, value_part)


def general_body(
    family_activity,
    rescale_factor,
    asking_weights,
    lookup_weights,
    payload_weights,
    exit_weights,
    upstream_adjoint,
):
    query_weight, key_weight, value_weight, output_matrix = (
        lax.all_gather(asking_weights, ("depth", "res"), axis=0, tiled=True),
        lax.all_gather(lookup_weights, ("depth", "res"), axis=0, tiled=True),
        lax.all_gather(payload_weights, ("depth", "res"), axis=0, tiled=True),
        lax.all_gather(exit_weights, ("depth", "res"), axis=0, tiled=True),
    )
    homologs_each_shard, positions_each_shard, embed_span = family_activity.shape
    standardized_source, standardized_entries, reciprocal_spread = standardize_entries(
        family_activity, rescale_factor
    )
    query = project(standardized_source, query_weight, HEAD_DIM ** (-0.5))
    keys = project(standardized_source, key_weight, 1.0)
    payload_entries = project(standardized_source, value_weight, 1.0)
    keys_all, values_all = (
        lax.all_gather(keys, "depth", axis=0, tiled=True),
        lax.all_gather(payload_entries, "depth", axis=0, tiled=True),
    )
    d_att = jnp.dot(upstream_adjoint, output_matrix.T, preferred_element_type=jnp.float32).astype(
        jnp.bfloat16
    )

    def per_head(items):
        return head_pass(items[0], items[1], items[2], items[3])

    mixed_homologs, d_query, key_part, value_part = lax.map(
        per_head, (to_heads(query), to_heads(keys_all), to_heads(values_all), to_heads(d_att))
    )
    mixed_homologs = from_heads(mixed_homologs, positions_each_shard)
    d_query = from_heads(d_query, positions_each_shard)
    key_part = from_heads(key_part, positions_each_shard)
    value_part = from_heads(value_part, positions_each_shard)
    rows = homologs_each_shard * positions_each_shard
    normed_rows = standardized_source.reshape(rows, embed_span)
    part_query = jnp.dot(
        normed_rows.T, d_query.reshape(rows, embed_span), preferred_element_type=jnp.float32
    )
    part_out = jnp.dot(
        mixed_homologs.reshape(rows, embed_span).T,
        upstream_adjoint.reshape(rows, embed_span),
        preferred_element_type=jnp.float32,
    )
    stacked = jnp.stack([key_part, value_part], axis=2).astype(jnp.bfloat16)
    summed = (
        lax.psum_scatter(stacked, "depth", scatter_dimension=0, tiled=True)
        .astype(jnp.float32)
        .astype(jnp.bfloat16)
    )
    d_keys = summed[:, :, 0, :]
    d_values = summed[:, :, 1, :]
    final_result = (
        family_activity.astype(jnp.float32)
        + jnp.dot(mixed_homologs, output_matrix, preferred_element_type=jnp.float32)
    ).astype(jnp.bfloat16)
    part_key = jnp.dot(
        normed_rows.T, d_keys.reshape(rows, embed_span), preferred_element_type=jnp.float32
    )
    part_value = jnp.dot(
        normed_rows.T, d_values.reshape(rows, embed_span), preferred_element_type=jnp.float32
    )
    d_normed = jnp.dot(d_query, query_weight.T, preferred_element_type=jnp.float32)
    d_normed = d_normed + jnp.dot(d_keys, key_weight.T, preferred_element_type=jnp.float32)
    d_normed = d_normed + jnp.dot(d_values, value_weight.T, preferred_element_type=jnp.float32)
    part_gain = jnp.sum((d_normed * standardized_entries).reshape(rows, embed_span), axis=0)
    unit_gradient = d_normed * rescale_factor
    alignment_gradient = upstream_adjoint.astype(jnp.float32) + reciprocal_spread * (
        unit_gradient
        - jnp.mean(unit_gradient, axis=-1, keepdims=True)
        - standardized_entries
        * jnp.mean(unit_gradient * standardized_entries, axis=-1, keepdims=True)
    )
    query_gradient, key_gradient, value_gradient, output_gradient, gain_gradient = (
        lax.psum_scatter(part_query, ("depth", "res"), scatter_dimension=0, tiled=True),
        lax.psum_scatter(part_key, ("depth", "res"), scatter_dimension=0, tiled=True),
        lax.psum_scatter(part_value, ("depth", "res"), scatter_dimension=0, tiled=True),
        lax.psum_scatter(part_out, ("depth", "res"), scatter_dimension=0, tiled=True),
        lax.psum_scatter(part_gain, ("depth", "res"), scatter_dimension=0, tiled=True),
    )
    return (
        final_result,
        alignment_gradient.astype(jnp.bfloat16),
        query_gradient,
        key_gradient,
        value_gradient,
        output_gradient,
        gain_gradient,
    )


F32, BF16 = jnp.float32, jnp.bfloat16
SCALE = HEAD_DIM ** (-0.5)
VMEM_LIMIT = 56 * 1024 * 1024


def swap(value, axis, size, bits):
    return lax.ppermute(value, axis, [(i, i ^ bits) for i in range(size)])


def pick(array, index, axis):
    return lax.dynamic_index_in_dim(array, index, axis, keepdims=False)


def dot(a, b, contract=(1, 0)):
    return lax.dot_general(
        a, b, (((contract[0],), (contract[1],)), ((), ())), preferred_element_type=F32
    )


def unit_rows(x):
    x = x.astype(F32)
    centered = x - jnp.mean(x, axis=-1, keepdims=True)
    inverse = lax.rsqrt(jnp.mean(centered * centered, axis=-1, keepdims=True) + 1e-05)
    return centered * inverse, inverse


def forward_kernel(dims, *refs):
    depth, zs, shard, block, span = dims
    heads = span // HEAD_DIM
    pos, refs = refs[0], refs[1:]
    xs, refs = refs[:depth], refs[depth:]
    gain, w_near, w_far, normed, query, keys, values, keys_t, att_t, lse, weights, w_out = refs[:12]
    outs, values_t = refs[12 : 12 + depth], refs[12 + depth]
    own_d, own_z, own_c = pos[0], pos[1], pos[2]

    for d in range(depth):
        for z in range(zs):
            near = w_near[z ^ own_z, d ^ own_d].astype(F32)
            far = w_far[z ^ own_z, d ^ own_d].astype(F32)
            first = own_c == 0
            pair = jnp.concatenate(
                [jnp.where(first, near, far), jnp.where(first, far, near)], axis=0
            ).astype(BF16)
            row = (d * zs + z) * 2 * shard
            weights[row : row + 2 * shard, :] = pair
            w_out[z * 2 * shard : (z + 1) * 2 * shard, d * span : (d + 1) * span] = pair[
                :, 3 * span : 4 * span
            ]

    for j in range(depth):
        rows = slice(j * block, (j + 1) * block)
        unit, _ = unit_rows(xs[j][...])
        low = (unit * gain[...]).astype(BF16)
        normed[rows, :] = low
        qkv = dot(low, weights[:, : 3 * span])
        for h in range(heads):
            lanes = slice(h * HEAD_DIM, (h + 1) * HEAD_DIM)
            query[h, rows, :] = (SCALE * qkv[:, :span][:, lanes]).astype(BF16)
            keys[h, rows, :] = qkv[:, span : 2 * span][:, lanes].astype(BF16)
            values[h, rows, :] = qkv[:, 2 * span :][:, lanes].astype(BF16)
        turned = jnp.transpose(qkv[:, span:]).astype(BF16)
        keys_t[:, rows] = turned[:span]
        values_t[:, rows] = turned[span:]

    def step(j, _):
        cols = pl.ds(pl.multiple_of(j * block, block), block)
        for h in range(heads):
            scores = dot(keys[h], query[h, cols, :], (1, 1))
            top = jnp.max(scores, axis=0, keepdims=True)
            e = jnp.exp(scores - top)
            total = jnp.sum(e, axis=0, keepdims=True)
            probs = (e * (1.0 / total)).astype(BF16)
            lanes = slice(h * HEAD_DIM, (h + 1) * HEAD_DIM)
            att_t[lanes, cols] = dot(values_t[lanes, :], probs).astype(BF16)
            lse[h, :, cols] = top + jnp.log(total)
        return 0

    lax.fori_loop(0, depth, step, 0)
    for j in range(depth):
        att = jnp.transpose(att_t[:, j * block : (j + 1) * block].astype(F32)).astype(BF16)
        outs[j][...] = dot(att, w_out[...]).astype(BF16)


def backward_kernel(dims, *refs):
    depth, zs, shard, block, span = dims
    heads = span // HEAD_DIM
    xs, refs = refs[:depth], refs[depth:]
    gs, refs = refs[:depth], refs[depth:]
    weights, w_out, query, keys, values, keys_t, lse = refs[:7]
    dns, refs = refs[7 : 7 + depth], refs[7 + depth :]
    d_qkv, gain_part, d_att, d_query_t, d_keys, d_values = refs

    for j in range(depth):
        rows = slice(j * block, (j + 1) * block)
        part = dot(gs[j][...], w_out[...], (1, 1)).astype(BF16)
        for h in range(heads):
            d_att[h, rows, :] = part[:, h * HEAD_DIM : (h + 1) * HEAD_DIM]
    d_keys[...] = jnp.zeros_like(d_keys)
    d_values[...] = jnp.zeros_like(d_values)

    def step(j, _):
        cols = pl.ds(pl.multiple_of(j * block, block), block)
        for h in range(heads):
            lanes = slice(h * HEAD_DIM, (h + 1) * HEAD_DIM)
            q_block, g_block = query[h, cols, :], d_att[h, cols, :]
            probs = jnp.exp(dot(keys[h], q_block, (1, 1)) - lse[h, :, cols])
            d_probs = dot(values[h], g_block, (1, 1))
            mean = jnp.sum(probs * d_probs, axis=0, keepdims=True)
            d_scores = (probs * (d_probs - mean)).astype(BF16)
            d_values[h] += dot(probs.astype(BF16), g_block).astype(BF16).astype(F32)
            d_keys[h] += dot(d_scores, q_block).astype(BF16).astype(F32)
            d_query_t[lanes, cols] = SCALE * dot(keys_t[lanes, :], d_scores)
        return 0

    lax.fori_loop(0, depth, step, 0)
    for h in range(heads):
        at = span + h * HEAD_DIM
        d_qkv[:, at : at + HEAD_DIM] = d_keys[h].astype(BF16)
        at = 2 * span + h * HEAD_DIM
        d_qkv[:, at : at + HEAD_DIM] = d_values[h].astype(BF16)
    gain_sum = None
    for j in range(depth):
        rows = slice(j * block, (j + 1) * block)
        d_qkv[rows, :span] = jnp.transpose(d_query_t[:, rows]).astype(BF16)
        d_normed = dot(d_qkv[rows, :], weights[:, : 3 * span], (1, 1))
        dns[j][...] = d_normed.astype(BF16)
        unit, _ = unit_rows(xs[j][...])
        part = jnp.sum(d_normed * unit, axis=0, keepdims=True)
        gain_sum = part if gain_sum is None else gain_sum + part
    gain_part[...] = jnp.broadcast_to(gain_sum, gain_part.shape)


def weight_kernel(dims, *refs):
    depth, zs, shard, block, span = dims
    pos, normed, d_qkv, att_t, gain_part = refs[:5]
    gs, (near, far) = refs[5 : 5 + depth], refs[5 + depth :]
    own_d, own_z, own_c = pos[0], pos[1], pos[2]
    grads = dot(normed[...], d_qkv[...], (0, 0))
    gain_column = jnp.transpose(jnp.broadcast_to(gain_part[0:1, :], (128, gain_part.shape[1])))
    grad_out = dot(att_t[:, :block], gs[0][...])
    for j in range(1, depth):
        grad_out = grad_out + dot(att_t[:, j * block : (j + 1) * block], gs[j][...])
    first = own_c == 0
    for d in range(depth):
        for z in range(zs):
            halves = []
            for c in range(2):
                row = ((d * zs + z) * 2 + c) * shard
                row_out = (z * 2 + c) * shard
                halves.append(
                    (
                        grads[row : row + shard],
                        gain_column[row : row + shard, :64],
                        grad_out[row_out : row_out + shard, d * span : (d + 1) * span],
                    )
                )
            at = 0
            for one, two in zip(*halves):
                lanes = slice(at, at + one.shape[1])
                at += one.shape[1]
                near[z ^ own_z, d ^ own_d, :, lanes] = jnp.where(first, one, two)
                far[z ^ own_z, d ^ own_d, :, lanes] = jnp.where(first, two, one).astype(BF16)


def call(kernel, dims, outs, scratch, args, flops, scalars=0):
    smem = pl.BlockSpec(memory_space=pltpu.SMEM)
    vmem = pl.BlockSpec(memory_space=pltpu.VMEM)
    outs = [jax.ShapeDtypeStruct(shape, kind) for shape, kind in outs]
    size = sum(a.size * a.dtype.itemsize for a in list(args) + outs)
    return pl.pallas_call(
        functools.partial(kernel, dims),
        out_shape=outs,
        in_specs=[smem] * scalars + [vmem] * (len(args) - scalars),
        out_specs=[vmem] * len(outs),
        scratch_shapes=[pltpu.VMEM(shape, kind) for shape, kind in scratch],
        compiler_params=pltpu.CompilerParams(vmem_limit_bytes=VMEM_LIMIT),
        cost_estimate=pl.CostEstimate(flops=flops, bytes_accessed=size, transcendentals=0),
    )(*args)


def head_body(depth, res, args):
    x, gain, w_query, w_key, w_value, w_out, upstream = args
    own_d, own_r = lax.axis_index("depth"), lax.axis_index("res")
    homologs, _, width = x.shape
    span, zs = width // depth, res // 2
    shard = w_query.shape[0]
    total, heads = homologs * depth, span // HEAD_DIM
    dims = (depth, zs, shard, homologs, span)
    x = x.reshape(homologs, width)
    upstream = upstream.reshape(homologs, width)
    own_z, own_c = own_r // 2, own_r % 2
    pos = jnp.stack([own_d, own_z, own_c]).astype(jnp.int32)

    def cut(w):
        return [w[:, j * span : (j + 1) * span] for j in range(depth)]

    parts = zip(cut(w_query), cut(w_key), cut(w_value))
    stacked = jnp.stack([jnp.concatenate(p, axis=1) for p in parts], axis=0)
    out_cut = jnp.stack(cut(w_out), axis=0)
    mine = [pick(stacked, own_d, 0)] + [
        swap(pick(stacked, own_d ^ k, 0), "depth", depth, k) for k in range(1, depth)
    ]
    out_cut = [pick(out_cut, own_d ^ k, 0) for k in range(depth)]
    mine = jnp.stack([jnp.concatenate(p, axis=1) for p in zip(mine, out_cut)], axis=0)
    w_near = jnp.stack([mine] + [swap(mine, "res", res, 2 * k) for k in range(1, zs)], axis=0)
    w_far = swap(w_near, "res", res, 1)

    xs = [x] + [swap(x, "depth", depth, k) for k in range(1, depth)]
    gs = [upstream] + [swap(upstream, "depth", depth, k) for k in range(1, depth)]

    per_head = ((heads, total, HEAD_DIM), BF16)
    block = ((homologs, width), BF16)
    pass_flops = 2 * total * total * span
    normed, query, keys, values, keys_t, att_t, lse, weights, wo, *outs = call(
        forward_kernel,
        dims,
        [((total, width), BF16), per_head, per_head, per_head]
        + [((span, total), BF16)] * 2
        + [((heads, 1, total), F32), ((width, width), BF16), ((span, width), BF16)]
        + [block] * depth,
        [((span, total), BF16)],
        [pos] + xs + [gain.reshape(1, width), w_near, w_far],
        8 * pass_flops,
        scalars=1,
    )

    *dns, d_qkv, gain_part = call(
        backward_kernel,
        dims,
        [block] * depth + [((total, 3 * span), BF16), ((8, width), F32)],
        [per_head, ((span, total), F32)] + [((heads, total, HEAD_DIM), F32)] * 2,
        xs + gs + [weights, wo, query, keys, values, keys_t, lse],
        24 * pass_flops,
    )

    packed = (zs, depth, shard, 4 * span + 64)
    near, far = call(
        weight_kernel,
        dims,
        [(packed, F32), (packed, BF16)],
        [],
        [pos, normed, d_qkv, att_t, gain_part] + gs,
        8 * total * width * span,
        scalars=1,
    )

    def scatter_depth(blocks):
        acc = blocks[0].astype(F32)
        for k in range(1, depth):
            acc = acc + swap(blocks[k], "depth", depth, k).astype(F32)
        return acc

    final_result = (x.astype(F32) + scatter_depth(outs)).astype(BF16)

    d_normed = scatter_depth(dns)
    unit, inverse = unit_rows(x)
    d_unit = d_normed * gain
    alignment = upstream.astype(F32) + inverse * (
        d_unit
        - jnp.mean(d_unit, axis=-1, keepdims=True)
        - unit * jnp.mean(d_unit * unit, axis=-1, keepdims=True)
    )

    near = near + swap(far, "res", res, 1).astype(F32)
    acc = near[0]
    for k in range(1, zs):
        acc = acc + swap(near[k].astype(BF16), "res", res, 2 * k).astype(F32)
    grad_out = jnp.concatenate(
        [pick(acc[:, :, 3 * span + 64 :], j ^ own_d, 0) for j in range(depth)], axis=1
    )
    acc = acc[:, :, : 3 * span + 64]
    rel = [acc[0]] + [
        swap(acc[k].astype(BF16), "depth", depth, k).astype(F32) for k in range(1, depth)
    ]
    gain_gradient = sum(r[:, 3 * span] for r in rel)
    rel = jnp.stack(rel, axis=0)
    ordered = [pick(rel, j ^ own_d, 0) for j in range(depth)]
    grads = [
        jnp.concatenate([o[:, i * span : (i + 1) * span] for o in ordered], axis=1)
        for i in range(3)
    ]
    return (
        final_result.reshape(homologs, 1, width),
        alignment.astype(BF16).reshape(homologs, 1, width),
        grads[0],
        grads[1],
        grads[2],
        grad_out,
        gain_gradient,
    )


def body(depth, res, *args):
    powers = depth & (depth - 1) == 0 and res & (res - 1) == 0 and res > 1
    if powers and HEADS % depth == 0 and args[0].shape[1] == 1:
        return head_body(depth, res, args)
    return general_body(*args)


def solution(mesh):
    depth, res = mesh.shape["depth"], mesh.shape["res"]
    return jax.shard_map(
        lambda *args: body(depth, res, *args),
        mesh=mesh,
        in_specs=(
            P("depth", "res", None),
            P(),
            P(("depth", "res"), None),
            P(("depth", "res"), None),
            P(("depth", "res"), None),
            P(("depth", "res"), None),
            P("depth", "res", None),
        ),
        out_specs=(
            P("depth", "res", None),
            P("depth", "res", None),
            P(("depth", "res"), None),
            P(("depth", "res"), None),
            P(("depth", "res"), None),
            P(("depth", "res"), None),
            P(("depth", "res")),
        ),
        check_vma=False,
    )
```

```python
import functools

import jax
import jax.numpy as jnp
from jax import lax
from jax.experimental import pallas as pl
from jax.experimental.pallas import tpu as pltpu
from jax.sharding import PartitionSpec as P

HEADS = 12
HEAD_DIM = 64


def standardize_entries(family_activity, rescale_factor):
    payload_entries = family_activity.astype(jnp.float32)
    centered = payload_entries - jnp.mean(payload_entries, axis=-1, keepdims=True)
    reciprocal_spread = lax.rsqrt(jnp.mean(centered * centered, axis=-1, keepdims=True) + 1e-05)
    standardized_entries = centered * reciprocal_spread
    return (
        (standardized_entries * rescale_factor).astype(jnp.bfloat16),
        standardized_entries,
        reciprocal_spread,
    )


def project(rows, weight, factor):
    return (factor * jnp.dot(rows, weight, preferred_element_type=jnp.float32)).astype(jnp.bfloat16)


def to_heads(array):
    count, cols = (array.shape[0], array.shape[1])
    return jnp.transpose(array.reshape(count, cols, HEADS, HEAD_DIM), (1, 2, 0, 3)).reshape(
        cols * HEADS, count, HEAD_DIM
    )


def from_heads(array, cols):
    count = array.shape[1]
    return jnp.transpose(array.reshape(cols, HEADS, count, HEAD_DIM), (2, 0, 1, 3)).reshape(
        count, cols, HEADS * HEAD_DIM
    )


def head_pass(query, keys, payload_entries, d_att):
    scale = HEAD_DIM ** (-0.5)
    scores = jnp.dot(query, keys.T, preferred_element_type=jnp.float32)
    probs = jax.nn.softmax(scores, axis=-1)
    probs_b = probs.astype(jnp.bfloat16)
    mixed_homologs = jnp.dot(probs_b, payload_entries, preferred_element_type=jnp.float32).astype(
        jnp.bfloat16
    )
    d_probs = jnp.dot(d_att, payload_entries.T, preferred_element_type=jnp.float32)
    d_scores = probs * (d_probs - jnp.sum(probs * d_probs, axis=-1, keepdims=True))
    d_scores_b = d_scores.astype(jnp.bfloat16)
    d_query = (scale * jnp.dot(d_scores_b, keys, preferred_element_type=jnp.float32)).astype(
        jnp.bfloat16
    )
    key_part = jnp.einsum("st,sd->td", d_scores_b, query, preferred_element_type=jnp.float32)
    value_part = jnp.einsum("st,sd->td", probs_b, d_att, preferred_element_type=jnp.float32)
    return (mixed_homologs, d_query, key_part, value_part)


def general_body(
    family_activity,
    rescale_factor,
    asking_weights,
    lookup_weights,
    payload_weights,
    exit_weights,
    upstream_adjoint,
):
    query_weight, key_weight, value_weight, output_matrix = (
        lax.all_gather(asking_weights, ("depth", "res"), axis=0, tiled=True),
        lax.all_gather(lookup_weights, ("depth", "res"), axis=0, tiled=True),
        lax.all_gather(payload_weights, ("depth", "res"), axis=0, tiled=True),
        lax.all_gather(exit_weights, ("depth", "res"), axis=0, tiled=True),
    )
    homologs_each_shard, positions_each_shard, embed_span = family_activity.shape
    standardized_source, standardized_entries, reciprocal_spread = standardize_entries(
        family_activity, rescale_factor
    )
    query = project(standardized_source, query_weight, HEAD_DIM ** (-0.5))
    keys = project(standardized_source, key_weight, 1.0)
    payload_entries = project(standardized_source, value_weight, 1.0)
    keys_all, values_all = (
        lax.all_gather(keys, "depth", axis=0, tiled=True),
        lax.all_gather(payload_entries, "depth", axis=0, tiled=True),
    )
    d_att = jnp.dot(upstream_adjoint, output_matrix.T, preferred_element_type=jnp.float32).astype(
        jnp.bfloat16
    )

    def per_head(items):
        return head_pass(items[0], items[1], items[2], items[3])

    mixed_homologs, d_query, key_part, value_part = lax.map(
        per_head, (to_heads(query), to_heads(keys_all), to_heads(values_all), to_heads(d_att))
    )
    mixed_homologs = from_heads(mixed_homologs, positions_each_shard)
    d_query = from_heads(d_query, positions_each_shard)
    key_part = from_heads(key_part, positions_each_shard)
    value_part = from_heads(value_part, positions_each_shard)
    rows = homologs_each_shard * positions_each_shard
    normed_rows = standardized_source.reshape(rows, embed_span)
    part_query = jnp.dot(
        normed_rows.T, d_query.reshape(rows, embed_span), preferred_element_type=jnp.float32
    )
    part_out = jnp.dot(
        mixed_homologs.reshape(rows, embed_span).T,
        upstream_adjoint.reshape(rows, embed_span),
        preferred_element_type=jnp.float32,
    )
    stacked = jnp.stack([key_part, value_part], axis=2).astype(jnp.bfloat16)
    summed = (
        lax.psum_scatter(stacked, "depth", scatter_dimension=0, tiled=True)
        .astype(jnp.float32)
        .astype(jnp.bfloat16)
    )
    d_keys = summed[:, :, 0, :]
    d_values = summed[:, :, 1, :]
    final_result = (
        family_activity.astype(jnp.float32)
        + jnp.dot(mixed_homologs, output_matrix, preferred_element_type=jnp.float32)
    ).astype(jnp.bfloat16)
    part_key = jnp.dot(
        normed_rows.T, d_keys.reshape(rows, embed_span), preferred_element_type=jnp.float32
    )
    part_value = jnp.dot(
        normed_rows.T, d_values.reshape(rows, embed_span), preferred_element_type=jnp.float32
    )
    d_normed = jnp.dot(d_query, query_weight.T, preferred_element_type=jnp.float32)
    d_normed = d_normed + jnp.dot(d_keys, key_weight.T, preferred_element_type=jnp.float32)
    d_normed = d_normed + jnp.dot(d_values, value_weight.T, preferred_element_type=jnp.float32)
    part_gain = jnp.sum((d_normed * standardized_entries).reshape(rows, embed_span), axis=0)
    unit_gradient = d_normed * rescale_factor
    alignment_gradient = upstream_adjoint.astype(jnp.float32) + reciprocal_spread * (
        unit_gradient
        - jnp.mean(unit_gradient, axis=-1, keepdims=True)
        - standardized_entries
        * jnp.mean(unit_gradient * standardized_entries, axis=-1, keepdims=True)
    )
    query_gradient, key_gradient, value_gradient, output_gradient, gain_gradient = (
        lax.psum_scatter(part_query, ("depth", "res"), scatter_dimension=0, tiled=True),
        lax.psum_scatter(part_key, ("depth", "res"), scatter_dimension=0, tiled=True),
        lax.psum_scatter(part_value, ("depth", "res"), scatter_dimension=0, tiled=True),
        lax.psum_scatter(part_out, ("depth", "res"), scatter_dimension=0, tiled=True),
        lax.psum_scatter(part_gain, ("depth", "res"), scatter_dimension=0, tiled=True),
    )
    return (
        final_result,
        alignment_gradient.astype(jnp.bfloat16),
        query_gradient,
        key_gradient,
        value_gradient,
        output_gradient,
        gain_gradient,
    )


F32, BF16 = jnp.float32, jnp.bfloat16
SCALE = HEAD_DIM ** (-0.5)
VMEM_LIMIT = 56 * 1024 * 1024


def swap(value, axis, size, bits):
    return lax.ppermute(value, axis, [(i, i ^ bits) for i in range(size)])


def pick(array, index, axis):
    return lax.dynamic_index_in_dim(array, index, axis, keepdims=False)


def dot(a, b, contract=(1, 0)):
    return lax.dot_general(
        a, b, (((contract[0],), (contract[1],)), ((), ())), preferred_element_type=F32
    )


def unit_rows(x):
    x = x.astype(F32)
    centered = x - jnp.mean(x, axis=-1, keepdims=True)
    inverse = lax.rsqrt(jnp.mean(centered * centered, axis=-1, keepdims=True) + 1e-05)
    return centered * inverse, inverse


def forward_kernel(dims, *refs):
    depth, zs, shard, block, span = dims
    heads = span // HEAD_DIM
    pos, refs = refs[0], refs[1:]
    xs, refs = refs[:depth], refs[depth:]
    gain, w_near, w_far, normed, query, keys, values, keys_t, att_t, lse, weights, w_out = refs[:12]
    outs, values_t = refs[12 : 12 + depth], refs[12 + depth]
    own_z, own_c = pos[1], pos[2]

    for d in range(depth):
        for z in range(zs):
            near = w_near[z ^ own_z, d].astype(F32)
            far = w_far[z ^ own_z, d].astype(F32)
            first = own_c == 0
            pair = jnp.concatenate(
                [jnp.where(first, near, far), jnp.where(first, far, near)], axis=0
            ).astype(BF16)
            row = (d * zs + z) * 2 * shard
            weights[row : row + 2 * shard, :] = pair
            w_out[z * 2 * shard : (z + 1) * 2 * shard, d * span : (d + 1) * span] = pair[
                :, 3 * span : 4 * span
            ]

    for j in range(depth):
        rows = slice(j * block, (j + 1) * block)
        unit, _ = unit_rows(xs[j][...])
        low = (unit * gain[...]).astype(BF16)
        normed[rows, :] = low
        qkv = dot(low, weights[:, : 3 * span])
        for h in range(heads):
            lanes = slice(h * HEAD_DIM, (h + 1) * HEAD_DIM)
            query[h, rows, :] = (SCALE * qkv[:, :span][:, lanes]).astype(BF16)
            keys[h, rows, :] = qkv[:, span : 2 * span][:, lanes].astype(BF16)
            values[h, rows, :] = qkv[:, 2 * span :][:, lanes].astype(BF16)
        turned = jnp.transpose(qkv[:, span:]).astype(BF16)
        keys_t[:, rows] = turned[:span]
        values_t[:, rows] = turned[span:]

    def step(j, _):
        cols = pl.ds(pl.multiple_of(j * block, block), block)
        for h in range(heads):
            scores = dot(keys[h], query[h, cols, :], (1, 1))
            top = jnp.max(scores, axis=0, keepdims=True)
            e = jnp.exp(scores - top)
            total = jnp.sum(e, axis=0, keepdims=True)
            probs = (e * (1.0 / total)).astype(BF16)
            lanes = slice(h * HEAD_DIM, (h + 1) * HEAD_DIM)
            att_t[lanes, cols] = dot(values_t[lanes, :], probs).astype(BF16)
            lse[h, :, cols] = top + jnp.log(total)
        return 0

    lax.fori_loop(0, depth, step, 0)
    for j in range(depth):
        att = jnp.transpose(att_t[:, j * block : (j + 1) * block].astype(F32)).astype(BF16)
        outs[j][...] = dot(att, w_out[...]).astype(BF16)


def backward_kernel(dims, *refs):
    depth, zs, shard, block, span = dims
    heads = span // HEAD_DIM
    gs, refs = refs[:depth], refs[depth:]
    w_out, query, keys, values, keys_t, lse, d_qkv, d_att, d_query_t, d_keys, d_values = refs

    for j in range(depth):
        rows = slice(j * block, (j + 1) * block)
        part = dot(gs[j][...], w_out[...], (1, 1)).astype(BF16)
        for h in range(heads):
            d_att[h, rows, :] = part[:, h * HEAD_DIM : (h + 1) * HEAD_DIM]
    d_keys[...] = jnp.zeros_like(d_keys)
    d_values[...] = jnp.zeros_like(d_values)

    def step(j, _):
        cols = pl.ds(pl.multiple_of(j * block, block), block)
        for h in range(heads):
            lanes = slice(h * HEAD_DIM, (h + 1) * HEAD_DIM)
            q_block, g_block = query[h, cols, :], d_att[h, cols, :]
            probs = jnp.exp(dot(keys[h], q_block, (1, 1)) - lse[h, :, cols])
            d_probs = dot(values[h], g_block, (1, 1))
            mean = jnp.sum(probs * d_probs, axis=0, keepdims=True)
            d_scores = (probs * (d_probs - mean)).astype(BF16)
            d_values[h] += dot(probs.astype(BF16), g_block).astype(BF16).astype(F32)
            d_keys[h] += dot(d_scores, q_block).astype(BF16).astype(F32)
            d_query_t[lanes, cols] = SCALE * dot(keys_t[lanes, :], d_scores)
        return 0

    lax.fori_loop(0, depth, step, 0)
    for h in range(heads):
        at = span + h * HEAD_DIM
        d_qkv[:, at : at + HEAD_DIM] = d_keys[h].astype(BF16)
        at = 2 * span + h * HEAD_DIM
        d_qkv[:, at : at + HEAD_DIM] = d_values[h].astype(BF16)
    for j in range(depth):
        rows = slice(j * block, (j + 1) * block)
        d_qkv[rows, :span] = jnp.transpose(d_query_t[:, rows]).astype(BF16)


def input_kernel(dims, *refs):
    depth, zs, shard, block, span = dims
    weights, d_qkv, dns = refs[0], refs[1], refs[2:]
    for j in range(depth):
        rows = slice(j * block, (j + 1) * block)
        d_normed = dot(d_qkv[rows, :], weights[:, : 3 * span], (1, 1))
        dns[j][...] = d_normed.astype(BF16)


def weight_kernel(dims, *refs):
    depth, zs, shard, block, span = dims
    pos, gain, normed, d_qkv, att_t, weights = refs[:6]
    gs, (near, far) = refs[6 : 6 + depth], refs[6 + depth :]
    own_z, own_c = pos[1], pos[2]
    grads = dot(normed[...], d_qkv[...], (0, 0))
    gain_rows = jnp.transpose(jnp.broadcast_to(gain[...], (128, gain.shape[1])))[:, :64]
    both = jnp.sum(weights[:, : 3 * span].astype(F32) * grads, axis=1, keepdims=True)
    gain_column = both / gain_rows
    grad_out = dot(att_t[:, :block], gs[0][...])
    for j in range(1, depth):
        grad_out = grad_out + dot(att_t[:, j * block : (j + 1) * block], gs[j][...])
    first = own_c == 0
    for d in range(depth):
        for z in range(zs):
            halves = []
            for c in range(2):
                row = ((d * zs + z) * 2 + c) * shard
                row_out = (z * 2 + c) * shard
                halves.append(
                    (
                        grads[row : row + shard],
                        gain_column[row : row + shard],
                        grad_out[row_out : row_out + shard, d * span : (d + 1) * span],
                    )
                )
            at = 0
            for one, two in zip(*halves):
                lanes = slice(at, at + one.shape[1])
                at += one.shape[1]
                near[z ^ own_z, d, :, lanes] = jnp.where(first, one, two)
                far[z ^ own_z, d, :, lanes] = jnp.where(first, two, one).astype(BF16)


def call(kernel, dims, outs, scratch, args, flops, scalars=0):
    smem = pl.BlockSpec(memory_space=pltpu.SMEM)
    vmem = pl.BlockSpec(memory_space=pltpu.VMEM)
    outs = [jax.ShapeDtypeStruct(shape, kind) for shape, kind in outs]
    size = sum(a.size * a.dtype.itemsize for a in list(args) + outs)
    return pl.pallas_call(
        functools.partial(kernel, dims),
        out_shape=outs,
        in_specs=[smem] * scalars + [vmem] * (len(args) - scalars),
        out_specs=[vmem] * len(outs),
        scratch_shapes=[pltpu.VMEM(shape, kind) for shape, kind in scratch],
        compiler_params=pltpu.CompilerParams(vmem_limit_bytes=VMEM_LIMIT),
        cost_estimate=pl.CostEstimate(flops=flops, bytes_accessed=size, transcendentals=0),
    )(*args)


def head_body(depth, res, args):
    x, gain, w_query, w_key, w_value, w_out, upstream = args
    own_d, own_r = lax.axis_index("depth"), lax.axis_index("res")
    homologs, _, width = x.shape
    span, zs = width // depth, res // 2
    shard = w_query.shape[0]
    total, heads = homologs * depth, span // HEAD_DIM
    dims = (depth, zs, shard, homologs, span)
    x = x.reshape(homologs, width)
    upstream = upstream.reshape(homologs, width)
    own_z, own_c = own_r // 2, own_r % 2
    pos = jnp.stack([own_d, own_z, own_c]).astype(jnp.int32)

    def cut(w):
        return [w[:, j * span : (j + 1) * span] for j in range(depth)]

    parts = zip(cut(w_query), cut(w_key), cut(w_value))
    stacked = jnp.stack([jnp.concatenate(p, axis=1) for p in parts], axis=0)
    out_cut = jnp.stack(cut(w_out), axis=0)
    mine = lax.all_to_all(stacked, "depth", 0, 0, tiled=True)
    mine = jnp.concatenate([mine, out_cut], axis=2)
    w_near = jnp.stack([mine] + [swap(mine, "res", res, 2 * k) for k in range(1, zs)], axis=0)
    xs = [x] + [swap(x, "depth", depth, k) for k in range(1, depth)]
    w_near, *xs = lax.optimization_barrier([w_near] + xs)
    w_far = swap(w_near, "res", res, 1)

    gs = [upstream] + [swap(upstream, "depth", depth, k) for k in range(1, depth)]

    per_head = ((heads, total, HEAD_DIM), BF16)
    block = ((homologs, width), BF16)
    pass_flops = 2 * total * total * span
    normed, query, keys, values, keys_t, att_t, lse, weights, wo, *outs = call(
        forward_kernel,
        dims,
        [((total, width), BF16), per_head, per_head, per_head]
        + [((span, total), BF16)] * 2
        + [((heads, 1, total), F32), ((width, width), BF16), ((span, width), BF16)]
        + [block] * depth,
        [((span, total), BF16)],
        [pos] + xs + [gain.reshape(1, width), w_near, w_far],
        8 * pass_flops,
        scalars=1,
    )

    d_qkv = call(
        backward_kernel,
        dims,
        [((total, 3 * span), BF16)],
        [per_head, ((span, total), F32)] + [((heads, total, HEAD_DIM), F32)] * 2,
        gs + [wo, query, keys, values, keys_t, lse],
        24 * pass_flops,
    )[0]

    outs = [outs[0]] + [swap(outs[k], "depth", depth, k) for k in range(1, depth)]
    d_qkv, *outs = lax.optimization_barrier([d_qkv] + outs)

    packed = (zs, depth, shard, 4 * span + 64)
    near, far = call(
        weight_kernel,
        dims,
        [(packed, F32), (packed, BF16)],
        [],
        [pos, gain.reshape(1, width), normed, d_qkv, att_t, weights] + gs,
        8 * total * width * span,
        scalars=1,
    )
    far, d_qkv = lax.optimization_barrier((far, d_qkv))
    far = swap(far, "res", res, 1)
    dns = call(
        input_kernel, dims, [block] * depth, [], [weights, d_qkv], 6 * total * width * span
    )
    dns = [dns[0]] + [swap(dns[k], "depth", depth, k) for k in range(1, depth)]

    final_result = (x.astype(F32) + sum(o.astype(F32) for o in outs)).astype(BF16)

    d_normed = sum(d.astype(F32) for d in dns)
    unit, inverse = unit_rows(x)
    d_unit = d_normed * gain
    alignment = upstream.astype(F32) + inverse * (
        d_unit
        - jnp.mean(d_unit, axis=-1, keepdims=True)
        - unit * jnp.mean(d_unit * unit, axis=-1, keepdims=True)
    )

    near = near + far.astype(F32)
    acc = near[0]
    for k in range(1, zs):
        acc = acc + swap(near[k].astype(BF16), "res", res, 2 * k).astype(F32)
    grad_out = jnp.concatenate([acc[j, :, 3 * span + 64 :] for j in range(depth)], axis=1)
    acc = acc[:, :, : 3 * span + 64].astype(BF16)
    ordered = lax.all_to_all(acc, "depth", 0, 0, tiled=True).astype(F32)
    gain_gradient = jnp.sum(ordered[:, :, 3 * span], axis=0)
    grads = [
        jnp.concatenate([o[:, i * span : (i + 1) * span] for o in ordered], axis=1)
        for i in range(3)
    ]
    return (
        final_result.reshape(homologs, 1, width),
        alignment.astype(BF16).reshape(homologs, 1, width),
        grads[0],
        grads[1],
        grads[2],
        grad_out,
        gain_gradient,
    )


def body(depth, res, *args):
    powers = depth & (depth - 1) == 0 and res & (res - 1) == 0 and res > 1
    if powers and HEADS % depth == 0 and args[0].shape[1] == 1:
        return head_body(depth, res, args)
    return general_body(*args)


def solution(mesh):
    depth, res = mesh.shape["depth"], mesh.shape["res"]
    return jax.shard_map(
        lambda *args: body(depth, res, *args),
        mesh=mesh,
        in_specs=(
            P("depth", "res", None),
            P(),
            P(("depth", "res"), None),
            P(("depth", "res"), None),
            P(("depth", "res"), None),
            P(("depth", "res"), None),
            P("depth", "res", None),
        ),
        out_specs=(
            P("depth", "res", None),
            P("depth", "res", None),
            P(("depth", "res"), None),
            P(("depth", "res"), None),
            P(("depth", "res"), None),
            P(("depth", "res"), None),
            P(("depth", "res")),
        ),
        check_vma=False,
    )
```

```python
import functools

import jax
import jax.numpy as jnp
from jax import lax
from jax.experimental import pallas as pl
from jax.experimental.pallas import tpu as pltpu
from jax.sharding import Mesh, PartitionSpec as P

HEADS = 12
HEAD_DIM = 64


def standardize_entries(family_activity, rescale_factor):
    payload_entries = family_activity.astype(jnp.float32)
    centered = payload_entries - jnp.mean(payload_entries, axis=-1, keepdims=True)
    reciprocal_spread = lax.rsqrt(jnp.mean(centered * centered, axis=-1, keepdims=True) + 1e-05)
    standardized_entries = centered * reciprocal_spread
    return (
        (standardized_entries * rescale_factor).astype(jnp.bfloat16),
        standardized_entries,
        reciprocal_spread,
    )


def project(rows, weight, factor):
    return (factor * jnp.dot(rows, weight, preferred_element_type=jnp.float32)).astype(jnp.bfloat16)


def to_heads(array):
    count, cols = (array.shape[0], array.shape[1])
    return jnp.transpose(array.reshape(count, cols, HEADS, HEAD_DIM), (1, 2, 0, 3)).reshape(
        cols * HEADS, count, HEAD_DIM
    )


def from_heads(array, cols):
    count = array.shape[1]
    return jnp.transpose(array.reshape(cols, HEADS, count, HEAD_DIM), (2, 0, 1, 3)).reshape(
        count, cols, HEADS * HEAD_DIM
    )


def head_pass(query, keys, payload_entries, d_att):
    scale = HEAD_DIM ** (-0.5)
    scores = jnp.dot(query, keys.T, preferred_element_type=jnp.float32)
    probs = jax.nn.softmax(scores, axis=-1)
    probs_b = probs.astype(jnp.bfloat16)
    mixed_homologs = jnp.dot(probs_b, payload_entries, preferred_element_type=jnp.float32).astype(
        jnp.bfloat16
    )
    d_probs = jnp.dot(d_att, payload_entries.T, preferred_element_type=jnp.float32)
    d_scores = probs * (d_probs - jnp.sum(probs * d_probs, axis=-1, keepdims=True))
    d_scores_b = d_scores.astype(jnp.bfloat16)
    d_query = (scale * jnp.dot(d_scores_b, keys, preferred_element_type=jnp.float32)).astype(
        jnp.bfloat16
    )
    key_part = jnp.einsum("st,sd->td", d_scores_b, query, preferred_element_type=jnp.float32)
    value_part = jnp.einsum("st,sd->td", probs_b, d_att, preferred_element_type=jnp.float32)
    return (mixed_homologs, d_query, key_part, value_part)


def general_body(
    family_activity,
    rescale_factor,
    asking_weights,
    lookup_weights,
    payload_weights,
    exit_weights,
    upstream_adjoint,
    axes=("depth", "res"),
):
    query_weight, key_weight, value_weight, output_matrix = (
        lax.all_gather(asking_weights, axes, axis=0, tiled=True),
        lax.all_gather(lookup_weights, axes, axis=0, tiled=True),
        lax.all_gather(payload_weights, axes, axis=0, tiled=True),
        lax.all_gather(exit_weights, axes, axis=0, tiled=True),
    )
    homologs_each_shard, positions_each_shard, embed_span = family_activity.shape
    standardized_source, standardized_entries, reciprocal_spread = standardize_entries(
        family_activity, rescale_factor
    )
    query = project(standardized_source, query_weight, HEAD_DIM ** (-0.5))
    keys = project(standardized_source, key_weight, 1.0)
    payload_entries = project(standardized_source, value_weight, 1.0)
    keys_all, values_all = (
        lax.all_gather(keys, "depth", axis=0, tiled=True),
        lax.all_gather(payload_entries, "depth", axis=0, tiled=True),
    )
    d_att = jnp.dot(upstream_adjoint, output_matrix.T, preferred_element_type=jnp.float32).astype(
        jnp.bfloat16
    )

    def per_head(items):
        return head_pass(items[0], items[1], items[2], items[3])

    mixed_homologs, d_query, key_part, value_part = lax.map(
        per_head, (to_heads(query), to_heads(keys_all), to_heads(values_all), to_heads(d_att))
    )
    mixed_homologs = from_heads(mixed_homologs, positions_each_shard)
    d_query = from_heads(d_query, positions_each_shard)
    key_part = from_heads(key_part, positions_each_shard)
    value_part = from_heads(value_part, positions_each_shard)
    rows = homologs_each_shard * positions_each_shard
    normed_rows = standardized_source.reshape(rows, embed_span)
    part_query = jnp.dot(
        normed_rows.T, d_query.reshape(rows, embed_span), preferred_element_type=jnp.float32
    )
    part_out = jnp.dot(
        mixed_homologs.reshape(rows, embed_span).T,
        upstream_adjoint.reshape(rows, embed_span),
        preferred_element_type=jnp.float32,
    )
    stacked = jnp.stack([key_part, value_part], axis=2).astype(jnp.bfloat16)
    summed = (
        lax.psum_scatter(stacked, "depth", scatter_dimension=0, tiled=True)
        .astype(jnp.float32)
        .astype(jnp.bfloat16)
    )
    d_keys = summed[:, :, 0, :]
    d_values = summed[:, :, 1, :]
    final_result = (
        family_activity.astype(jnp.float32)
        + jnp.dot(mixed_homologs, output_matrix, preferred_element_type=jnp.float32)
    ).astype(jnp.bfloat16)
    part_key = jnp.dot(
        normed_rows.T, d_keys.reshape(rows, embed_span), preferred_element_type=jnp.float32
    )
    part_value = jnp.dot(
        normed_rows.T, d_values.reshape(rows, embed_span), preferred_element_type=jnp.float32
    )
    d_normed = jnp.dot(d_query, query_weight.T, preferred_element_type=jnp.float32)
    d_normed = d_normed + jnp.dot(d_keys, key_weight.T, preferred_element_type=jnp.float32)
    d_normed = d_normed + jnp.dot(d_values, value_weight.T, preferred_element_type=jnp.float32)
    part_gain = jnp.sum((d_normed * standardized_entries).reshape(rows, embed_span), axis=0)
    unit_gradient = d_normed * rescale_factor
    alignment_gradient = upstream_adjoint.astype(jnp.float32) + reciprocal_spread * (
        unit_gradient
        - jnp.mean(unit_gradient, axis=-1, keepdims=True)
        - standardized_entries
        * jnp.mean(unit_gradient * standardized_entries, axis=-1, keepdims=True)
    )
    query_gradient, key_gradient, value_gradient, output_gradient, gain_gradient = (
        lax.psum_scatter(part_query, axes, scatter_dimension=0, tiled=True),
        lax.psum_scatter(part_key, axes, scatter_dimension=0, tiled=True),
        lax.psum_scatter(part_value, axes, scatter_dimension=0, tiled=True),
        lax.psum_scatter(part_out, axes, scatter_dimension=0, tiled=True),
        lax.psum_scatter(part_gain, axes, scatter_dimension=0, tiled=True),
    )
    return (
        final_result,
        alignment_gradient.astype(jnp.bfloat16),
        query_gradient,
        key_gradient,
        value_gradient,
        output_gradient,
        gain_gradient,
    )


F32, BF16 = jnp.float32, jnp.bfloat16
SCALE = HEAD_DIM ** (-0.5)


def swap(value, axis, size, bits):
    return lax.ppermute(value, axis, [(i, i ^ bits) for i in range(size)])


def dot(a, b, contract=(1, 0)):
    return lax.dot_general(
        a, b, (((contract[0],), (contract[1],)), ((), ())), preferred_element_type=F32
    )


def unit_rows(x):
    x = x.astype(F32)
    centered = x - jnp.mean(x, axis=-1, keepdims=True)
    inverse = lax.rsqrt(jnp.mean(centered * centered, axis=-1, keepdims=True) + 1e-05)
    return centered * inverse, inverse


def head_masks(span):
    lane = lax.broadcasted_iota(jnp.int32, (8, span), 1)
    return [
        ((lane >= at) & (lane < at + HEAD_DIM)).astype(F32)[0:1].astype(BF16)
        for at in range(0, span, HEAD_DIM)
    ]


def pack_kernel(dims, w_query, w_key, w_value, out):
    depth, zs, shard, block, span = dims
    for d in range(depth):
        lanes = slice(d * span, (d + 1) * span)
        for i, w in enumerate((w_query, w_key, w_value)):
            part = w[:, lanes]
            for z in range(zs):
                out[d * zs + z, :, i * span : (i + 1) * span] = part


def forward_kernel(dims, *refs):
    depth, zs, shard, block, span = dims
    heads = span // HEAD_DIM
    core, refs = refs[0], refs[1:]
    xs, refs = refs[:depth], refs[depth:]
    gain, w_near, w_far, w_out, normed, query, keys, values, keys_t, att_t, lse, weights = refs[:12]
    outs, values_t = refs[12 : 12 + depth], refs[12 + depth]

    first = core[0] == 0
    for i in range(depth * zs):
        near, far = w_near[i].astype(F32), w_far[i].astype(F32)
        weights[i * 2 * shard : (i + 1) * 2 * shard, :] = jnp.concatenate(
            [jnp.where(first, near, far), jnp.where(first, far, near)], axis=0
        ).astype(BF16)

    for j in range(depth):
        rows = slice(j * block, (j + 1) * block)
        unit, _ = unit_rows(xs[j][...])
        low = (unit * gain[...]).astype(BF16)
        normed[rows, :] = low
        qkv = dot(low, weights[...])
        query[rows, :] = (SCALE * qkv[:, :span]).astype(BF16)
        key, value = qkv[:, span : 2 * span], qkv[:, 2 * span :]
        keys[rows, :] = key.astype(BF16)
        values[rows, :] = value.astype(BF16)
        keys_t[:, rows] = jnp.transpose(key).astype(BF16)
        values_t[:, rows] = jnp.transpose(value).astype(BF16)

    masks = head_masks(span)

    def step(j, _):
        cols = pl.ds(pl.multiple_of(j * block, block), block)
        q_block = query[cols, :]

        def score(h):
            return dot(keys[...], q_block * masks[h], (1, 1))

        scores = [score(h) for h in range(min(2, heads))]
        for h in range(heads):
            top = jnp.max(scores[h], axis=0, keepdims=True)
            e = jnp.exp(scores[h] - top)
            total = jnp.sum(e, axis=0, keepdims=True)
            probs = (e * (1.0 / total)).astype(BF16)
            if h + 2 < heads:
                scores.append(score(h + 2))
            lanes = slice(h * HEAD_DIM, (h + 1) * HEAD_DIM)
            att_t[lanes, cols] = dot(values_t[lanes, :], probs).astype(BF16)
            lse[h, :, cols] = top + jnp.log(total)
        return 0

    lax.fori_loop(0, depth, step, 0)
    for j in range(depth):
        att = jnp.transpose(att_t[:, j * block : (j + 1) * block].astype(F32)).astype(BF16)
        outs[j][...] = dot(att, w_out[...]).astype(BF16)


def out_grad_kernel(dims, *refs):
    depth, zs, shard, block, span = dims
    gs, (att_t, out) = refs[:depth], refs[depth:]
    total = dot(att_t[:, :block], gs[0][...])
    for j in range(1, depth):
        total = total + dot(att_t[:, j * block : (j + 1) * block], gs[j][...])
    out[...] = total


def backward_kernel(dims, *refs):
    depth, zs, shard, block, span = dims
    heads = span // HEAD_DIM
    gs, refs = refs[:depth], refs[depth:]
    w_out, query, keys, values, keys_t, lse, d_qkv, d_att, d_query_t, d_keys, d_values = refs

    for j in range(depth):
        rows = slice(j * block, (j + 1) * block)
        d_att[rows, :] = dot(gs[j][...], w_out[...], (1, 1)).astype(BF16)
    d_keys[...] = jnp.zeros_like(d_keys)
    d_values[...] = jnp.zeros_like(d_values)
    masks = head_masks(span)

    def step(j, _):
        cols = pl.ds(pl.multiple_of(j * block, block), block)
        q_block, g_block = query[cols, :], d_att[cols, :]
        qs = [q_block * m for m in masks]
        ds = [g_block * m for m in masks]

        def pair(h):
            return dot(keys[...], qs[h], (1, 1)), dot(values[...], ds[h], (1, 1))

        pairs = [pair(h) for h in range(min(2, heads))]
        key_part = value_part = None
        for h in range(heads):
            scores, d_probs = pairs[h]
            probs = jnp.exp(scores - lse[h, :, cols])
            mean = jnp.sum(probs * d_probs, axis=0, keepdims=True)
            d_scores = (probs * (d_probs - mean)).astype(BF16)
            if h + 2 < heads:
                pairs.append(pair(h + 2))
            values_add = dot(probs.astype(BF16), ds[h])
            keys_add = dot(d_scores, qs[h])
            value_part = values_add if h == 0 else value_part + values_add
            key_part = keys_add if h == 0 else key_part + keys_add
            lanes = slice(h * HEAD_DIM, (h + 1) * HEAD_DIM)
            d_query_t[lanes, cols] = SCALE * dot(keys_t[lanes, :], d_scores)
        d_values[...] += value_part.astype(BF16).astype(F32)
        d_keys[...] += key_part.astype(BF16).astype(F32)
        return 0

    lax.fori_loop(0, depth, step, 0)
    d_qkv[:, span : 2 * span] = d_keys[...].astype(BF16)
    d_qkv[:, 2 * span :] = d_values[...].astype(BF16)
    for j in range(depth):
        rows = slice(j * block, (j + 1) * block)
        d_qkv[rows, :span] = jnp.transpose(d_query_t[:, rows]).astype(BF16)


def weight_kernel(dims, core, gain, normed, d_qkv, weights, near, far):
    depth, zs, shard, block, span = dims
    grads = dot(normed[...], d_qkv[...], (0, 0))
    gain_rows = jnp.transpose(jnp.broadcast_to(gain[...], (128, gain.shape[1])))[:, :64]
    both = jnp.sum(weights[...].astype(F32) * grads, axis=1, keepdims=True)
    gain_column = both / gain_rows
    first = core[0] == 0
    for i in range(depth * zs):
        one = slice(2 * i * shard, (2 * i + 1) * shard)
        two = slice((2 * i + 1) * shard, (2 * i + 2) * shard)
        near[i, :, : 3 * span] = jnp.where(first, grads[one], grads[two])
        near[i, :, 3 * span :] = jnp.where(first, gain_column[one], gain_column[two])
        far[i, :, : 3 * span] = jnp.where(first, grads[two], grads[one]).astype(BF16)
        far[i, :, 3 * span :] = jnp.where(first, gain_column[two], gain_column[one]).astype(BF16)


def input_kernel(dims, weights, d_qkv, *dns):
    depth, zs, shard, block, span = dims
    for j in range(depth):
        rows = slice(j * block, (j + 1) * block)
        dns[j][...] = dot(d_qkv[rows, :], weights[...], (1, 1)).astype(BF16)


def finish_kernel(dims, parts, *outs):
    depth, zs, shard, block, span = dims
    gain_sum = None
    for d in range(depth):
        total = parts[d * zs].astype(F32)
        for z in range(1, zs):
            total = total + parts[d * zs + z].astype(F32)
        for i in range(3):
            outs[i][:, d * span : (d + 1) * span] = total[:, i * span : (i + 1) * span]
        gain = total[:, 3 * span : 3 * span + 1]
        gain_sum = gain if gain_sum is None else gain_sum + gain
    wide = jnp.concatenate([gain_sum, jnp.zeros((128 - shard, 1), F32)], axis=0)
    outs[3][...] = jnp.transpose(jnp.broadcast_to(wide, (128, 128)))[0:8, :]


def call(kernel, dims, outs, scratch, args, flops, mib, scalars=0):
    smem = pl.BlockSpec(memory_space=pltpu.SMEM)
    vmem = pl.BlockSpec(memory_space=pltpu.VMEM)
    outs = [jax.ShapeDtypeStruct(shape, kind) for shape, kind in outs]
    size = sum(a.size * a.dtype.itemsize for a in list(args) + outs)
    return pl.pallas_call(
        functools.partial(kernel, dims),
        out_shape=outs,
        in_specs=[smem] * scalars + [vmem] * (len(args) - scalars),
        out_specs=[vmem] * len(outs),
        scratch_shapes=[pltpu.VMEM(shape, kind) for shape, kind in scratch],
        compiler_params=pltpu.CompilerParams(vmem_limit_bytes=mib * 1024 * 1024),
        cost_estimate=pl.CostEstimate(flops=flops, bytes_accessed=size, transcendentals=0),
    )(*args)


def head_body(depth, res, *args):
    x, gain, w_query, w_key, w_value, w_out, upstream = args
    homologs, _, width = x.shape
    span, zs = width // depth, res // 2
    shard = w_query.shape[0]
    total, heads = homologs * depth, span // HEAD_DIM
    dims = (depth, zs, shard, homologs, span)
    x = x.reshape(homologs, width)
    upstream = upstream.reshape(homologs, width)
    gain = gain.reshape(1, width)
    core = lax.axis_index("core").astype(jnp.int32).reshape(1)

    xs = [x] + [swap(x, "depth", depth, k) for k in range(1, depth)]
    gs = [upstream] + [swap(upstream, "depth", depth, k) for k in range(1, depth)]

    blocks = depth * zs
    packed = call(
        pack_kernel,
        dims,
        [((blocks, shard, 3 * span), BF16)],
        [],
        [w_query, w_key, w_value],
        1000,
        16,
    )[0]
    w_near = lax.all_to_all(packed, ("depth", "z"), 0, 0, tiled=True)
    w_far = swap(w_near, "core", 2, 1)
    w_out = lax.all_gather(w_out, ("z", "core"), axis=0, tiled=True)

    rows = ((total, span), BF16)
    turned = ((span, total), BF16)
    block = ((homologs, width), BF16)
    pass_flops = 2 * total * total * span
    normed, query, keys, values, keys_t, att_t, lse, weights, *outs = call(
        forward_kernel,
        dims,
        [((total, width), BF16), rows, rows, rows, turned, turned]
        + [((heads, 1, total), F32), ((width, 3 * span), BF16)]
        + [block] * depth,
        [turned],
        [core] + xs + [gain, w_near, w_far, w_out],
        8 * pass_flops,
        28,
        scalars=1,
    )

    grad_out = call(
        out_grad_kernel, dims, [((span, width), F32)], [], gs + [att_t], 2 * total * width * span, 16
    )[0]
    lse, grad_out = lax.optimization_barrier((lse, grad_out))
    grad_out = lax.psum_scatter(grad_out, ("z", "core"), scatter_dimension=0, tiled=True)

    d_qkv = call(
        backward_kernel,
        dims,
        [((total, 3 * span), BF16)],
        [rows, ((span, total), F32)] + [((total, span), F32)] * 2,
        gs + [w_out, query, keys, values, keys_t, lse],
        24 * pass_flops,
        28,
    )[0]

    outs = [outs[0]] + [swap(outs[k], "depth", depth, k) for k in range(1, depth)]
    d_qkv, *outs = lax.optimization_barrier([d_qkv] + outs)
    final_result = (x.astype(F32) + sum(o.astype(F32) for o in outs)).astype(BF16)

    lanes = 3 * span + 64
    near, far = call(
        weight_kernel,
        dims,
        [((blocks, shard, lanes), F32), ((blocks, shard, lanes), BF16)],
        [],
        [core, gain, normed, d_qkv, weights],
        6 * total * width * span,
        28,
        scalars=1,
    )
    far, d_qkv = lax.optimization_barrier((far, d_qkv))
    far = swap(far, "core", 2, 1)
    dns = call(
        input_kernel, dims, [block] * depth, [], [weights, d_qkv], 6 * total * width * span, 16
    )
    near = (near + far.astype(F32)).astype(BF16)
    near, *dns = lax.optimization_barrier([near] + list(dns))
    parts = lax.all_to_all(near, ("depth", "z"), 0, 0, tiled=True)
    dns = [dns[0]] + [swap(dns[k], "depth", depth, k) for k in range(1, depth)]
    parts, *dns = lax.optimization_barrier([parts] + dns)

    grad_query, grad_key, grad_value, gain_rows = call(
        finish_kernel,
        dims,
        [((shard, width), F32)] * 3 + [((8, 128), F32)],
        [],
        [parts],
        1000,
        16,
    )

    d_normed = sum(d.astype(F32) for d in dns)
    unit, inverse = unit_rows(x)
    d_unit = d_normed * gain
    alignment = upstream.astype(F32) + inverse * (
        d_unit
        - jnp.mean(d_unit, axis=-1, keepdims=True)
        - unit * jnp.mean(d_unit * unit, axis=-1, keepdims=True)
    )
    return (
        final_result.reshape(homologs, 1, width),
        alignment.astype(BF16).reshape(homologs, 1, width),
        grad_query,
        grad_key,
        grad_value,
        grad_out,
        gain_rows[0, :shard],
    )


def solution(mesh):
    depth, res = mesh.shape["depth"], mesh.shape["res"]
    powers = depth & (depth - 1) == 0 and res & (res - 1) == 0 and res > 1
    if powers and HEADS % depth == 0:
        axes = ("depth", "z", "core")
        mesh = Mesh(mesh.devices.reshape(depth, res // 2, 2), axes)
        res_axes, run = ("z", "core"), functools.partial(head_body, depth, res)
    else:
        axes = ("depth", "res")
        res_axes, run = ("res",), general_body

    def body(*args):
        if args[0].shape[1] != 1:
            return general_body(*args, axes=axes)
        return run(*args)

    rows = P("depth", res_axes, None)
    weight = P(axes, None)
    return jax.shard_map(
        body,
        mesh=mesh,
        in_specs=(rows, P(), weight, weight, weight, weight, rows),
        out_specs=(rows, rows, weight, weight, weight, weight, P(axes)),
        check_vma=False,
    )
```

```python
import functools

import jax
import jax.numpy as jnp
from jax import lax
from jax.experimental import pallas as pl
from jax.experimental.pallas import tpu as pltpu
from jax.sharding import Mesh, PartitionSpec as P

HEADS = 12
HEAD_DIM = 64


def standardize_entries(family_activity, rescale_factor):
    payload_entries = family_activity.astype(jnp.float32)
    centered = payload_entries - jnp.mean(payload_entries, axis=-1, keepdims=True)
    reciprocal_spread = lax.rsqrt(jnp.mean(centered * centered, axis=-1, keepdims=True) + 1e-05)
    standardized_entries = centered * reciprocal_spread
    return (
        (standardized_entries * rescale_factor).astype(jnp.bfloat16),
        standardized_entries,
        reciprocal_spread,
    )


def project(rows, weight, factor):
    return (factor * jnp.dot(rows, weight, preferred_element_type=jnp.float32)).astype(jnp.bfloat16)


def to_heads(array):
    count, cols = (array.shape[0], array.shape[1])
    return jnp.transpose(array.reshape(count, cols, HEADS, HEAD_DIM), (1, 2, 0, 3)).reshape(
        cols * HEADS, count, HEAD_DIM
    )


def from_heads(array, cols):
    count = array.shape[1]
    return jnp.transpose(array.reshape(cols, HEADS, count, HEAD_DIM), (2, 0, 1, 3)).reshape(
        count, cols, HEADS * HEAD_DIM
    )


def head_pass(query, keys, payload_entries, d_att):
    scale = HEAD_DIM ** (-0.5)
    scores = jnp.dot(query, keys.T, preferred_element_type=jnp.float32)
    probs = jax.nn.softmax(scores, axis=-1)
    probs_b = probs.astype(jnp.bfloat16)
    mixed_homologs = jnp.dot(probs_b, payload_entries, preferred_element_type=jnp.float32).astype(
        jnp.bfloat16
    )
    d_probs = jnp.dot(d_att, payload_entries.T, preferred_element_type=jnp.float32)
    d_scores = probs * (d_probs - jnp.sum(probs * d_probs, axis=-1, keepdims=True))
    d_scores_b = d_scores.astype(jnp.bfloat16)
    d_query = (scale * jnp.dot(d_scores_b, keys, preferred_element_type=jnp.float32)).astype(
        jnp.bfloat16
    )
    key_part = jnp.einsum("st,sd->td", d_scores_b, query, preferred_element_type=jnp.float32)
    value_part = jnp.einsum("st,sd->td", probs_b, d_att, preferred_element_type=jnp.float32)
    return (mixed_homologs, d_query, key_part, value_part)


def general_body(
    family_activity,
    rescale_factor,
    asking_weights,
    lookup_weights,
    payload_weights,
    exit_weights,
    upstream_adjoint,
    axes=("depth", "res"),
):
    query_weight, key_weight, value_weight, output_matrix = (
        lax.all_gather(asking_weights, axes, axis=0, tiled=True),
        lax.all_gather(lookup_weights, axes, axis=0, tiled=True),
        lax.all_gather(payload_weights, axes, axis=0, tiled=True),
        lax.all_gather(exit_weights, axes, axis=0, tiled=True),
    )
    homologs_each_shard, positions_each_shard, embed_span = family_activity.shape
    standardized_source, standardized_entries, reciprocal_spread = standardize_entries(
        family_activity, rescale_factor
    )
    query = project(standardized_source, query_weight, HEAD_DIM ** (-0.5))
    keys = project(standardized_source, key_weight, 1.0)
    payload_entries = project(standardized_source, value_weight, 1.0)
    keys_all, values_all = (
        lax.all_gather(keys, "depth", axis=0, tiled=True),
        lax.all_gather(payload_entries, "depth", axis=0, tiled=True),
    )
    d_att = jnp.dot(upstream_adjoint, output_matrix.T, preferred_element_type=jnp.float32).astype(
        jnp.bfloat16
    )

    def per_head(items):
        return head_pass(items[0], items[1], items[2], items[3])

    mixed_homologs, d_query, key_part, value_part = lax.map(
        per_head, (to_heads(query), to_heads(keys_all), to_heads(values_all), to_heads(d_att))
    )
    mixed_homologs = from_heads(mixed_homologs, positions_each_shard)
    d_query = from_heads(d_query, positions_each_shard)
    key_part = from_heads(key_part, positions_each_shard)
    value_part = from_heads(value_part, positions_each_shard)
    rows = homologs_each_shard * positions_each_shard
    normed_rows = standardized_source.reshape(rows, embed_span)
    part_query = jnp.dot(
        normed_rows.T, d_query.reshape(rows, embed_span), preferred_element_type=jnp.float32
    )
    part_out = jnp.dot(
        mixed_homologs.reshape(rows, embed_span).T,
        upstream_adjoint.reshape(rows, embed_span),
        preferred_element_type=jnp.float32,
    )
    stacked = jnp.stack([key_part, value_part], axis=2).astype(jnp.bfloat16)
    summed = (
        lax.psum_scatter(stacked, "depth", scatter_dimension=0, tiled=True)
        .astype(jnp.float32)
        .astype(jnp.bfloat16)
    )
    d_keys = summed[:, :, 0, :]
    d_values = summed[:, :, 1, :]
    final_result = (
        family_activity.astype(jnp.float32)
        + jnp.dot(mixed_homologs, output_matrix, preferred_element_type=jnp.float32)
    ).astype(jnp.bfloat16)
    part_key = jnp.dot(
        normed_rows.T, d_keys.reshape(rows, embed_span), preferred_element_type=jnp.float32
    )
    part_value = jnp.dot(
        normed_rows.T, d_values.reshape(rows, embed_span), preferred_element_type=jnp.float32
    )
    d_normed = jnp.dot(d_query, query_weight.T, preferred_element_type=jnp.float32)
    d_normed = d_normed + jnp.dot(d_keys, key_weight.T, preferred_element_type=jnp.float32)
    d_normed = d_normed + jnp.dot(d_values, value_weight.T, preferred_element_type=jnp.float32)
    part_gain = jnp.sum((d_normed * standardized_entries).reshape(rows, embed_span), axis=0)
    unit_gradient = d_normed * rescale_factor
    alignment_gradient = upstream_adjoint.astype(jnp.float32) + reciprocal_spread * (
        unit_gradient
        - jnp.mean(unit_gradient, axis=-1, keepdims=True)
        - standardized_entries
        * jnp.mean(unit_gradient * standardized_entries, axis=-1, keepdims=True)
    )
    query_gradient, key_gradient, value_gradient, output_gradient, gain_gradient = (
        lax.psum_scatter(part_query, axes, scatter_dimension=0, tiled=True),
        lax.psum_scatter(part_key, axes, scatter_dimension=0, tiled=True),
        lax.psum_scatter(part_value, axes, scatter_dimension=0, tiled=True),
        lax.psum_scatter(part_out, axes, scatter_dimension=0, tiled=True),
        lax.psum_scatter(part_gain, axes, scatter_dimension=0, tiled=True),
    )
    return (
        final_result,
        alignment_gradient.astype(jnp.bfloat16),
        query_gradient,
        key_gradient,
        value_gradient,
        output_gradient,
        gain_gradient,
    )


F32, BF16 = jnp.float32, jnp.bfloat16
SCALE = HEAD_DIM ** (-0.5)


def swap(value, axis, size, bits):
    return lax.ppermute(value, axis, [(i, i ^ bits) for i in range(size)])


def dot(a, b, contract=(1, 0)):
    return lax.dot_general(
        a, b, (((contract[0],), (contract[1],)), ((), ())), preferred_element_type=F32
    )


def unit_rows(x):
    x = x.astype(F32)
    centered = x - jnp.mean(x, axis=-1, keepdims=True)
    inverse = lax.rsqrt(jnp.mean(centered * centered, axis=-1, keepdims=True) + 1e-05)
    return centered * inverse, inverse


def head_masks(span):
    lane = lax.broadcasted_iota(jnp.int32, (8, span), 1)
    return [
        ((lane >= at) & (lane < at + HEAD_DIM)).astype(F32)[0:1].astype(BF16)
        for at in range(0, span, HEAD_DIM)
    ]


def fetch(pairs, sems):
    copies = [pltpu.make_async_copy(src, dst, sems.at[i]) for i, (src, dst) in enumerate(pairs)]
    for copy in copies:
        copy.start()
    return copies


class Sender:
    def __init__(self, sems):
        self.sems, self.copies = sems, []

    def send(self, src, dst):
        copy = pltpu.make_async_copy(src, dst, self.sems.at[len(self.copies)])
        copy.start()
        self.copies.append(copy)

    def finish(self):
        for copy in self.copies:
            copy.wait()


def pack_kernel(dims, w_query, w_key, w_value, out):
    depth, zs, shard, block, span = dims
    for d in range(depth):
        lanes = slice(d * span, (d + 1) * span)
        for i, w in enumerate((w_query, w_key, w_value)):
            out[d, :, i * span : (i + 1) * span] = w[:, lanes]


def forward_kernel(dims, *refs):
    depth, zs, shard, block, span = dims
    heads, half = span // HEAD_DIM, block // 2
    pos, gain, w_near, w_far, x0, x1, x2, x3_top, x3_bottom = refs[:9]
    (normed_h, query_h, keys_h, values_h, keys_t_h, att_t_h, lse_h, weights_h, w_out_h) = refs[9:18]
    outs_h = refs[18 : 18 + depth]
    (xs, normed, query, keys, values, keys_t, values_t) = refs[18 + depth : 25 + depth]
    (att_t, lse, weights, w_out, outs, in_sems, out_sems) = refs[25 + depth :]
    copies = fetch(
        [
            (x0, xs.at[0]),
            (x1, xs.at[1]),
            (x2, xs.at[2]),
            (x3_top, xs.at[3, pl.ds(0, half)]),
            (x3_bottom, xs.at[3, pl.ds(half, half)]),
        ],
        in_sems,
    )
    sender = Sender(out_sems)

    own_z, first = pos[0], pos[1] == 0
    for d in range(depth):
        for z in range(zs):
            near = w_near[z ^ own_z, d].astype(F32)
            far = w_far[z ^ own_z, d].astype(F32)
            pair = jnp.concatenate(
                [jnp.where(first, near, far), jnp.where(first, far, near)], axis=0
            ).astype(BF16)
            row = (d * zs + z) * 2 * shard
            weights[row : row + 2 * shard, :] = pair[:, : 3 * span]
            w_out[z * 2 * shard : (z + 1) * 2 * shard, d * span : (d + 1) * span] = pair[
                :, 3 * span :
            ]
    sender.send(weights, weights_h)
    sender.send(w_out, w_out_h)

    for j in range(depth):
        rows = slice(j * block, (j + 1) * block)
        copies[j].wait()
        if j == depth - 1:
            copies[depth].wait()
        unit, _ = unit_rows(xs[j])
        low = (unit * gain[...]).astype(BF16)
        normed[rows, :] = low
        qkv = dot(low, weights[...])
        query[rows, :] = (SCALE * qkv[:, :span]).astype(BF16)
        key, value = qkv[:, span : 2 * span], qkv[:, 2 * span :]
        keys[rows, :] = key.astype(BF16)
        values[rows, :] = value.astype(BF16)
        keys_t[:, rows] = jnp.transpose(key).astype(BF16)
        values_t[:, rows] = jnp.transpose(value).astype(BF16)
    for src, dst in (
        (normed, normed_h),
        (query, query_h),
        (keys, keys_h),
        (values, values_h),
        (keys_t, keys_t_h),
    ):
        sender.send(src, dst)

    masks = head_masks(span)

    def step(j, _):
        cols = pl.ds(pl.multiple_of(j * block, block), block)
        q_block = query[cols, :]

        def score(h):
            return dot(keys[...], q_block * masks[h], (1, 1))

        scores = [score(h) for h in range(min(2, heads))]
        for h in range(heads):
            top = jnp.max(scores[h], axis=0, keepdims=True)
            e = jnp.exp(scores[h] - top)
            total = jnp.sum(e, axis=0, keepdims=True)
            probs = (e * (1.0 / total)).astype(BF16)
            if h + 2 < heads:
                scores.append(score(h + 2))
            lanes = slice(h * HEAD_DIM, (h + 1) * HEAD_DIM)
            att_t[lanes, cols] = dot(values_t[lanes, :], probs).astype(BF16)
            lse[h, :, cols] = top + jnp.log(total)
        return 0

    lax.fori_loop(0, depth, step, 0)
    sender.send(att_t, att_t_h)
    sender.send(lse, lse_h)
    for j in range(depth):
        att = jnp.transpose(att_t[:, j * block : (j + 1) * block].astype(F32)).astype(BF16)
        outs[j] = dot(att, w_out[...]).astype(BF16)
        sender.send(outs.at[j], outs_h[j])
    sender.finish()


def backward_kernel(dims, *refs):
    depth, zs, shard, block, span = dims
    heads, half = span // HEAD_DIM, block // 2
    pos, gain = refs[:2]
    gs_h, refs = refs[2 : 2 + depth], refs[2 + depth :]
    (w_out_h, query_h, keys_h, values_h, keys_t_h, lse_h, normed_h, att_t_h, weights_h) = refs[:9]
    near, far, dn0, dn1, dn2, dn3_top, dn3_bottom = refs[9:16]
    (gs, w_out, query, keys, values, keys_t, lse, normed, att_t, weights) = refs[16:26]
    (d_qkv, d_att, d_query_t, d_keys, d_values, grad_out, dns, in_sems, out_sems) = refs[26:]
    copies = fetch(
        [(w_out_h, w_out)]
        + [(gs_h[j], gs.at[j]) for j in range(depth)]
        + [
            (keys_h, keys),
            (query_h, query),
            (values_h, values),
            (lse_h, lse),
            (keys_t_h, keys_t),
            (att_t_h, att_t),
            (normed_h, normed),
            (weights_h, weights),
        ],
        in_sems,
    )

    copies[0].wait()
    for j in range(depth):
        copies[1 + j].wait()
        d_att[j * block : (j + 1) * block, :] = dot(gs[j], w_out[...], (1, 1)).astype(BF16)
    for copy in copies[1 + depth :]:
        copy.wait()
    d_keys[...] = jnp.zeros_like(d_keys)
    d_values[...] = jnp.zeros_like(d_values)
    masks = head_masks(span)

    def step(j, _):
        cols = pl.ds(pl.multiple_of(j * block, block), block)
        q_block, g_block = query[cols, :], d_att[cols, :]
        qs = [q_block * m for m in masks]
        ds = [g_block * m for m in masks]

        def pair(h):
            return dot(keys[...], qs[h], (1, 1)), dot(values[...], ds[h], (1, 1))

        pairs = [pair(h) for h in range(min(2, heads))]
        key_part = value_part = None
        for h in range(heads):
            scores, d_probs = pairs[h]
            probs = jnp.exp(scores - lse[h, :, cols])
            mean = jnp.sum(probs * d_probs, axis=0, keepdims=True)
            d_scores = (probs * (d_probs - mean)).astype(BF16)
            if h + 2 < heads:
                pairs.append(pair(h + 2))
            values_add = dot(probs.astype(BF16), ds[h])
            keys_add = dot(d_scores, qs[h])
            value_part = values_add if h == 0 else value_part + values_add
            key_part = keys_add if h == 0 else key_part + keys_add
            lanes = slice(h * HEAD_DIM, (h + 1) * HEAD_DIM)
            d_query_t[lanes, cols] = SCALE * dot(keys_t[lanes, :], d_scores)
        d_values[...] += value_part.astype(BF16).astype(F32)
        d_keys[...] += key_part.astype(BF16).astype(F32)
        return 0

    lax.fori_loop(0, depth, step, 0)
    d_qkv[:, span : 2 * span] = d_keys[...].astype(BF16)
    d_qkv[:, 2 * span :] = d_values[...].astype(BF16)
    for j in range(depth):
        rows = slice(j * block, (j + 1) * block)
        d_qkv[rows, :span] = jnp.transpose(d_query_t[:, rows]).astype(BF16)

    sender = Sender(out_sems)
    for j in range(depth):
        rows = slice(j * block, (j + 1) * block)
        dns[j] = dot(d_qkv[rows, :], weights[...], (1, 1)).astype(BF16)
        if j < depth - 1:
            sender.send(dns.at[j], (dn0, dn1, dn2)[j])
        else:
            sender.send(dns.at[j, pl.ds(0, half)], dn3_top)
            sender.send(dns.at[j, pl.ds(half, half)], dn3_bottom)

    part = dot(att_t[:, :block], gs[0])
    for j in range(1, depth):
        part = part + dot(att_t[:, j * block : (j + 1) * block], gs[j])
    grad_out[...] = part
    grads = dot(normed[...], d_qkv[...], (0, 0))
    gain_rows = jnp.transpose(jnp.broadcast_to(gain[...], (128, gain.shape[1])))[:, :64]
    both = jnp.sum(weights[...].astype(F32) * grads, axis=1, keepdims=True)
    gain_column = both / gain_rows
    own_z, first = pos[0], pos[1] == 0
    for d in range(depth):
        for z in range(zs):
            sides = []
            for c in range(2):
                row, row_out = ((d * zs + z) * 2 + c) * shard, (z * 2 + c) * shard
                sides.append(
                    (
                        grads[row : row + shard],
                        gain_column[row : row + shard],
                        grad_out[row_out : row_out + shard, d * span : (d + 1) * span],
                    )
                )
            at = 0
            for one, two in zip(*sides):
                lanes = slice(at, at + one.shape[1])
                at += one.shape[1]
                near[z ^ own_z, d, :, lanes] = jnp.where(first, one, two)
                far[z ^ own_z, d, :, lanes] = jnp.where(first, two, one).astype(BF16)
    sender.finish()


def align_kernel(dims, gain, x, upstream, *refs):
    dns, out = refs[:-1], refs[-1]
    d_normed = dns[0][...].astype(F32)
    for part in dns[1:]:
        d_normed = d_normed + part[...].astype(F32)
    unit, inverse = unit_rows(x[...])
    d_unit = d_normed * gain[...]
    out[...] = (
        upstream[...].astype(F32)
        + inverse
        * (
            d_unit
            - jnp.mean(d_unit, axis=-1, keepdims=True)
            - unit * jnp.mean(d_unit * unit, axis=-1, keepdims=True)
        )
    ).astype(BF16)


def finish_kernel(dims, parts, *outs):
    depth, zs, shard, block, span = dims
    gain_sum = None
    for d in range(depth):
        total = parts[d].astype(F32)
        for i in range(3):
            outs[i][:, d * span : (d + 1) * span] = total[:, i * span : (i + 1) * span]
        gain = total[:, 3 * span : 3 * span + 1]
        gain_sum = gain if gain_sum is None else gain_sum + gain
    wide = jnp.concatenate([gain_sum, jnp.zeros((128 - shard, 1), F32)], axis=0)
    outs[3][...] = jnp.transpose(jnp.broadcast_to(wide, (128, 128)))[0:8, :]


VMEM, ANY, SMEM = pltpu.VMEM, pl.ANY, pltpu.SMEM


def call(kernel, dims, ins, outs, scratch, sems, flops):
    args = [a for a, _ in ins]
    shapes = [jax.ShapeDtypeStruct(shape, kind) for shape, kind, _ in outs]
    size = sum(a.size * a.dtype.itemsize for a in args + shapes)
    return pl.pallas_call(
        functools.partial(kernel, dims),
        out_shape=shapes,
        in_specs=[pl.BlockSpec(memory_space=space) for _, space in ins],
        out_specs=[pl.BlockSpec(memory_space=space) for _, _, space in outs],
        scratch_shapes=[pltpu.VMEM(shape, kind) for shape, kind in scratch]
        + [pltpu.SemaphoreType.DMA((n,)) for n in sems],
        compiler_params=pltpu.CompilerParams(vmem_limit_bytes=56 * 1024 * 1024),
        cost_estimate=pl.CostEstimate(flops=flops, bytes_accessed=size, transcendentals=0),
    )(*args)


def head_body(depth, res, *args):
    x, gain, w_query, w_key, w_value, w_out, upstream = args
    homologs, _, width = x.shape
    span, zs = width // depth, res // 2
    shard = w_query.shape[0]
    total, heads, half = homologs * depth, span // HEAD_DIM, homologs // 2
    dims = (depth, zs, shard, homologs, span)
    x = x.reshape(homologs, width)
    upstream = upstream.reshape(homologs, width)
    gain = gain.reshape(1, width)
    pos = jnp.stack([lax.axis_index("z"), lax.axis_index("core")]).astype(jnp.int32)

    x1, x2 = swap(x, "depth", depth, 1), swap(x, "depth", depth, 2)

    packed = call(
        pack_kernel,
        dims,
        [(w_query, VMEM), (w_key, VMEM), (w_value, VMEM)],
        [((depth, shard, 3 * span), BF16, VMEM)],
        [],
        [],
        1000,
    )[0]
    out_cut = jnp.stack([w_out[:, j * span : (j + 1) * span] for j in range(depth)], axis=0)
    mine = lax.all_to_all(packed, "depth", 0, 0, tiled=True)
    mine = jnp.concatenate([mine, out_cut], axis=2)
    mine, x1, x2 = lax.optimization_barrier((mine, x1, x2))
    x3_top = swap(x2[:half], "depth", depth, 1)
    x3_bottom = swap(x1[half:], "depth", depth, 2)
    w_near = jnp.stack([mine] + [swap(mine, "z", zs, k) for k in range(1, zs)], axis=0)
    w_near, x3_top, x3_bottom = lax.optimization_barrier((w_near, x3_top, x3_bottom))
    w_far = swap(w_near, "core", 2, 1)
    gs = [upstream] + [swap(upstream, "depth", depth, k) for k in range(1, depth)]

    rows, turned = ((total, span), BF16), ((span, total), BF16)
    block, halved = ((homologs, width), BF16), ((half, width), BF16)
    blocks = ((depth, homologs, width), BF16)
    norm, stats = ((total, width), BF16), ((heads, 1, total), F32)
    in_weights, out_weights = ((width, 3 * span), BF16), ((span, width), BF16)
    pass_flops = 2 * total * total * span
    saved = [norm, rows, rows, rows, turned, turned, stats, in_weights, out_weights]
    normed, query, keys, values, keys_t, att_t, lse, weights, wo, *outs = call(
        forward_kernel,
        dims,
        [(pos, SMEM), (gain, VMEM), (w_near, VMEM), (w_far, VMEM)]
        + [(a, ANY) for a in (x, x1, x2, x3_top, x3_bottom)],
        [s + (ANY,) for s in saved + [block] * depth],
        [blocks, norm, rows, rows, rows, turned, turned, turned, stats]
        + [in_weights, out_weights, blocks],
        [depth + 1, len(saved) + depth],
        8 * pass_flops,
    )

    packed = (zs, depth, shard, 4 * span + 64)
    near, far, *dns = call(
        backward_kernel,
        dims,
        [(pos, SMEM), (gain, VMEM)]
        + [(a, ANY) for a in gs + [wo, query, keys, values, keys_t, lse, normed, att_t, weights]],
        [(packed, F32, VMEM), (packed, BF16, VMEM)]
        + [s + (ANY,) for s in [block] * 3 + [halved] * 2],
        [blocks, out_weights, rows, rows, rows, turned, stats, norm, turned, in_weights]
        + [((total, 3 * span), BF16), rows, ((span, total), F32)]
        + [((total, span), F32)] * 2
        + [((span, width), F32), blocks],
        [depth + 9, depth + 1],
        24 * pass_flops,
    )

    outs = [outs[0]] + [swap(outs[k], "depth", depth, k) for k in range(1, depth)]
    near, far, *rest = lax.optimization_barrier([near, far] + dns + outs)
    dns, outs = rest[: len(dns)], rest[len(dns) :]
    final_result = (x.astype(F32) + sum(o.astype(F32) for o in outs)).astype(BF16)

    far = swap(far, "core", 2, 1)
    dn0, dn1, dn2, dn3_top, dn3_bottom = dns
    top, bottom = swap(dn3_top, "depth", depth, 1), swap(dn3_bottom, "depth", depth, 2)
    near = near + far.astype(F32)
    dn2 = dn2.astype(F32) + jnp.concatenate([top, jnp.zeros_like(top)], axis=0).astype(F32)
    dn1 = dn1.astype(F32) + jnp.concatenate([jnp.zeros_like(bottom), bottom], axis=0).astype(F32)
    low = [near[k].astype(BF16) for k in range(1, zs)]
    own = near[0]
    own, dn1, dn2, *low = lax.optimization_barrier(
        [own, dn1.astype(BF16), dn2.astype(BF16)] + low
    )
    low = [swap(low[k - 1], "z", zs, k) for k in range(1, zs)]
    dn1, dn2 = swap(dn1, "depth", depth, 1), swap(dn2, "depth", depth, 2)
    acc = own + sum(p.astype(F32) for p in low)
    grad_out = jnp.concatenate([acc[j, :, 3 * span + 64 :] for j in range(depth)], axis=1)
    acc = acc[:, :, : 3 * span + 64].astype(BF16)
    parts = lax.all_to_all(acc, "depth", 0, 0, tiled=True)
    parts, dn1, dn2 = lax.optimization_barrier((parts, dn1, dn2))

    alignment = call(
        align_kernel,
        dims,
        [(a, VMEM) for a in (gain, x, upstream, dn0, dn1, dn2)],
        [block + (VMEM,)],
        [],
        [],
        1000,
    )[0]
    grad_query, grad_key, grad_value, gain_rows = call(
        finish_kernel,
        dims,
        [(parts, VMEM)],
        [((shard, width), F32, VMEM)] * 3 + [((8, 128), F32, VMEM)],
        [],
        [],
        1000,
    )
    return (
        final_result.reshape(homologs, 1, width),
        alignment.reshape(homologs, 1, width),
        grad_query,
        grad_key,
        grad_value,
        grad_out,
        gain_rows[0, :shard],
    )


def solution(mesh):
    depth, res = mesh.shape["depth"], mesh.shape["res"]
    powers = depth & (depth - 1) == 0 and res & (res - 1) == 0 and res > 1
    if powers and depth == 4 and HEADS % depth == 0:
        axes = ("depth", "z", "core")
        mesh = Mesh(mesh.devices.reshape(depth, res // 2, 2), axes)
        res_axes, run = ("z", "core"), functools.partial(head_body, depth, res)
    else:
        axes = ("depth", "res")
        res_axes, run = ("res",), general_body

    def body(*args):
        if args[0].shape[1] != 1:
            return general_body(*args, axes=axes)
        return run(*args)

    rows = P("depth", res_axes, None)
    weight = P(axes, None)
    return jax.shard_map(
        body,
        mesh=mesh,
        in_specs=(rows, P(), weight, weight, weight, weight, rows),
        out_specs=(rows, rows, weight, weight, weight, weight, P(axes)),
        check_vma=False,
    )
```

```python
import functools

import jax
import jax.numpy as jnp
from jax import lax
from jax.experimental import pallas as pl
from jax.experimental.pallas import tpu as pltpu
from jax.sharding import Mesh, PartitionSpec as P

HEADS = 12
HEAD_DIM = 64


def standardize_entries(family_activity, rescale_factor):
    payload_entries = family_activity.astype(jnp.float32)
    centered = payload_entries - jnp.mean(payload_entries, axis=-1, keepdims=True)
    reciprocal_spread = lax.rsqrt(jnp.mean(centered * centered, axis=-1, keepdims=True) + 1e-05)
    standardized_entries = centered * reciprocal_spread
    return (
        (standardized_entries * rescale_factor).astype(jnp.bfloat16),
        standardized_entries,
        reciprocal_spread,
    )


def project(rows, weight, factor):
    return (factor * jnp.dot(rows, weight, preferred_element_type=jnp.float32)).astype(jnp.bfloat16)


def to_heads(array):
    count, cols = (array.shape[0], array.shape[1])
    return jnp.transpose(array.reshape(count, cols, HEADS, HEAD_DIM), (1, 2, 0, 3)).reshape(
        cols * HEADS, count, HEAD_DIM
    )


def from_heads(array, cols):
    count = array.shape[1]
    return jnp.transpose(array.reshape(cols, HEADS, count, HEAD_DIM), (2, 0, 1, 3)).reshape(
        count, cols, HEADS * HEAD_DIM
    )


def head_pass(query, keys, payload_entries, d_att):
    scale = HEAD_DIM ** (-0.5)
    scores = jnp.dot(query, keys.T, preferred_element_type=jnp.float32)
    probs = jax.nn.softmax(scores, axis=-1)
    probs_b = probs.astype(jnp.bfloat16)
    mixed_homologs = jnp.dot(probs_b, payload_entries, preferred_element_type=jnp.float32).astype(
        jnp.bfloat16
    )
    d_probs = jnp.dot(d_att, payload_entries.T, preferred_element_type=jnp.float32)
    d_scores = probs * (d_probs - jnp.sum(probs * d_probs, axis=-1, keepdims=True))
    d_scores_b = d_scores.astype(jnp.bfloat16)
    d_query = (scale * jnp.dot(d_scores_b, keys, preferred_element_type=jnp.float32)).astype(
        jnp.bfloat16
    )
    key_part = jnp.einsum("st,sd->td", d_scores_b, query, preferred_element_type=jnp.float32)
    value_part = jnp.einsum("st,sd->td", probs_b, d_att, preferred_element_type=jnp.float32)
    return (mixed_homologs, d_query, key_part, value_part)


def general_body(
    family_activity,
    rescale_factor,
    asking_weights,
    lookup_weights,
    payload_weights,
    exit_weights,
    upstream_adjoint,
    axes=("depth", "res"),
):
    query_weight, key_weight, value_weight, output_matrix = (
        lax.all_gather(asking_weights, axes, axis=0, tiled=True),
        lax.all_gather(lookup_weights, axes, axis=0, tiled=True),
        lax.all_gather(payload_weights, axes, axis=0, tiled=True),
        lax.all_gather(exit_weights, axes, axis=0, tiled=True),
    )
    homologs_each_shard, positions_each_shard, embed_span = family_activity.shape
    standardized_source, standardized_entries, reciprocal_spread = standardize_entries(
        family_activity, rescale_factor
    )
    query = project(standardized_source, query_weight, HEAD_DIM ** (-0.5))
    keys = project(standardized_source, key_weight, 1.0)
    payload_entries = project(standardized_source, value_weight, 1.0)
    keys_all, values_all = (
        lax.all_gather(keys, "depth", axis=0, tiled=True),
        lax.all_gather(payload_entries, "depth", axis=0, tiled=True),
    )
    d_att = jnp.dot(upstream_adjoint, output_matrix.T, preferred_element_type=jnp.float32).astype(
        jnp.bfloat16
    )

    def per_head(items):
        return head_pass(items[0], items[1], items[2], items[3])

    mixed_homologs, d_query, key_part, value_part = lax.map(
        per_head, (to_heads(query), to_heads(keys_all), to_heads(values_all), to_heads(d_att))
    )
    mixed_homologs = from_heads(mixed_homologs, positions_each_shard)
    d_query = from_heads(d_query, positions_each_shard)
    key_part = from_heads(key_part, positions_each_shard)
    value_part = from_heads(value_part, positions_each_shard)
    rows = homologs_each_shard * positions_each_shard
    normed_rows = standardized_source.reshape(rows, embed_span)
    part_query = jnp.dot(
        normed_rows.T, d_query.reshape(rows, embed_span), preferred_element_type=jnp.float32
    )
    part_out = jnp.dot(
        mixed_homologs.reshape(rows, embed_span).T,
        upstream_adjoint.reshape(rows, embed_span),
        preferred_element_type=jnp.float32,
    )
    stacked = jnp.stack([key_part, value_part], axis=2).astype(jnp.bfloat16)
    summed = (
        lax.psum_scatter(stacked, "depth", scatter_dimension=0, tiled=True)
        .astype(jnp.float32)
        .astype(jnp.bfloat16)
    )
    d_keys = summed[:, :, 0, :]
    d_values = summed[:, :, 1, :]
    final_result = (
        family_activity.astype(jnp.float32)
        + jnp.dot(mixed_homologs, output_matrix, preferred_element_type=jnp.float32)
    ).astype(jnp.bfloat16)
    part_key = jnp.dot(
        normed_rows.T, d_keys.reshape(rows, embed_span), preferred_element_type=jnp.float32
    )
    part_value = jnp.dot(
        normed_rows.T, d_values.reshape(rows, embed_span), preferred_element_type=jnp.float32
    )
    d_normed = jnp.dot(d_query, query_weight.T, preferred_element_type=jnp.float32)
    d_normed = d_normed + jnp.dot(d_keys, key_weight.T, preferred_element_type=jnp.float32)
    d_normed = d_normed + jnp.dot(d_values, value_weight.T, preferred_element_type=jnp.float32)
    part_gain = jnp.sum((d_normed * standardized_entries).reshape(rows, embed_span), axis=0)
    unit_gradient = d_normed * rescale_factor
    alignment_gradient = upstream_adjoint.astype(jnp.float32) + reciprocal_spread * (
        unit_gradient
        - jnp.mean(unit_gradient, axis=-1, keepdims=True)
        - standardized_entries
        * jnp.mean(unit_gradient * standardized_entries, axis=-1, keepdims=True)
    )
    query_gradient, key_gradient, value_gradient, output_gradient, gain_gradient = (
        lax.psum_scatter(part_query, axes, scatter_dimension=0, tiled=True),
        lax.psum_scatter(part_key, axes, scatter_dimension=0, tiled=True),
        lax.psum_scatter(part_value, axes, scatter_dimension=0, tiled=True),
        lax.psum_scatter(part_out, axes, scatter_dimension=0, tiled=True),
        lax.psum_scatter(part_gain, axes, scatter_dimension=0, tiled=True),
    )
    return (
        final_result,
        alignment_gradient.astype(jnp.bfloat16),
        query_gradient,
        key_gradient,
        value_gradient,
        output_gradient,
        gain_gradient,
    )


F32, BF16 = jnp.float32, jnp.bfloat16
SCALE = HEAD_DIM ** (-0.5)


def swap(value, axis, size, bits):
    return lax.ppermute(value, axis, [(i, i ^ bits) for i in range(size)])


def dot(a, b, contract=(1, 0)):
    return lax.dot_general(
        a, b, (((contract[0],), (contract[1],)), ((), ())), preferred_element_type=F32
    )


def unit_rows(x):
    x = x.astype(F32)
    centered = x - jnp.mean(x, axis=-1, keepdims=True)
    inverse = lax.rsqrt(jnp.mean(centered * centered, axis=-1, keepdims=True) + 1e-05)
    return centered * inverse, inverse


def head_masks(span):
    lane = lax.broadcasted_iota(jnp.int32, (8, span), 1)
    return [
        ((lane >= at) & (lane < at + HEAD_DIM)).astype(F32)[0:1].astype(BF16)
        for at in range(0, span, HEAD_DIM)
    ]


def fetch(pairs, sems):
    copies = [pltpu.make_async_copy(src, dst, sems.at[i]) for i, (src, dst) in enumerate(pairs)]
    for copy in copies:
        copy.start()
    return copies


class Sender:
    def __init__(self, sems):
        self.sems, self.copies = sems, []

    def send(self, src, dst):
        copy = pltpu.make_async_copy(src, dst, self.sems.at[len(self.copies)])
        copy.start()
        self.copies.append(copy)

    def finish(self):
        for copy in self.copies:
            copy.wait()


def pack_kernel(dims, w_query, w_key, w_value, out):
    depth, zs, shard, block, span = dims
    for d in range(depth):
        lanes = slice(d * span, (d + 1) * span)
        for i, w in enumerate((w_query, w_key, w_value)):
            out[d, :, i * span : (i + 1) * span] = w[:, lanes]


def norm_kernel(dims, *refs):
    depth, zs, shard, block, span = dims
    half = block // 2
    gain, x0, x1, x2, x3_top, x3_bottom, normed_h, xs, normed, in_sems, out_sems = refs
    copies = fetch(
        [
            (x0, xs.at[0]),
            (x1, xs.at[1]),
            (x2, xs.at[2]),
            (x3_top, xs.at[3, pl.ds(0, half)]),
            (x3_bottom, xs.at[3, pl.ds(half, half)]),
        ],
        in_sems,
    )
    sender = Sender(out_sems)
    for j in range(depth):
        copies[j].wait()
        if j == depth - 1:
            copies[depth].wait()
        unit, _ = unit_rows(xs[j])
        rows = pl.ds(j * block, block)
        normed[rows, :] = (unit * gain[...]).astype(BF16)
        sender.send(normed.at[rows], normed_h.at[rows])
    sender.finish()


def forward_kernel(dims, *refs):
    depth, zs, shard, block, span = dims
    heads = span // HEAD_DIM
    pos, w_near, w_far, normed_h = refs[:4]
    query_h, keys_h, values_h, keys_t_h, att_t_h, lse_h, weights_h, w_out_h = refs[4:12]
    outs_h, refs = refs[12 : 12 + depth], refs[12 + depth :]
    normed, query, keys, values, keys_t, values_t, att_t, lse, weights, w_out, outs = refs[:11]
    in_sems, out_sems = refs[11:]
    copies = fetch(
        [
            (normed_h.at[pl.ds(j * block, block)], normed.at[pl.ds(j * block, block)])
            for j in range(depth)
        ],
        in_sems,
    )
    sender = Sender(out_sems)

    own_z, first = pos[0], pos[1] == 0
    for d in range(depth):
        for z in range(zs):
            near = w_near[z ^ own_z, d].astype(F32)
            far = w_far[z ^ own_z, d].astype(F32)
            pair = jnp.concatenate(
                [jnp.where(first, near, far), jnp.where(first, far, near)], axis=0
            ).astype(BF16)
            row = (d * zs + z) * 2 * shard
            weights[row : row + 2 * shard, :] = pair[:, : 3 * span]
            w_out[z * 2 * shard : (z + 1) * 2 * shard, d * span : (d + 1) * span] = pair[
                :, 3 * span :
            ]
    sender.send(weights, weights_h)
    sender.send(w_out, w_out_h)

    for j in range(depth):
        rows = slice(j * block, (j + 1) * block)
        copies[j].wait()
        qkv = dot(normed[rows, :], weights[...])
        query[rows, :] = (SCALE * qkv[:, :span]).astype(BF16)
        key, value = qkv[:, span : 2 * span], qkv[:, 2 * span :]
        keys[rows, :] = key.astype(BF16)
        values[rows, :] = value.astype(BF16)
        keys_t[:, rows] = jnp.transpose(key).astype(BF16)
        values_t[:, rows] = jnp.transpose(value).astype(BF16)
    for src, dst in ((query, query_h), (keys, keys_h), (values, values_h), (keys_t, keys_t_h)):
        sender.send(src, dst)

    masks = head_masks(span)

    def step(j, _):
        cols = pl.ds(pl.multiple_of(j * block, block), block)
        q_block = query[cols, :]

        def score(h):
            q_head = q_block * masks[h]
            return [
                dot(keys[c * block : (c + 1) * block, :], q_head, (1, 1)) for c in range(depth)
            ]

        ready = score(0)
        for h in range(heads):
            scores = ready
            top = scores[0]
            for c in range(1, depth):
                top = jnp.maximum(top, scores[c])
            top = jnp.max(top, axis=0, keepdims=True)
            if h + 1 < heads:
                ready = score(h + 1)
            lanes = slice(h * HEAD_DIM, (h + 1) * HEAD_DIM)
            total = att = None
            for c in range(depth):
                e = jnp.exp(scores[c] - top)
                part = jnp.sum(e, axis=0, keepdims=True)
                mixed = dot(values_t[lanes, c * block : (c + 1) * block], e.astype(BF16))
                total = part if c == 0 else total + part
                att = mixed if c == 0 else att + mixed
            att_t[lanes, cols] = att * (1.0 / total)
            lse[h, :, cols] = top + jnp.log(total)
        return 0

    lax.fori_loop(0, depth, step, 0)
    sender.send(att_t, att_t_h)
    sender.send(lse, lse_h)
    for j in range(depth):
        att = jnp.transpose(att_t[:, j * block : (j + 1) * block]).astype(BF16)
        outs[j] = dot(att, w_out[...]).astype(BF16)
        sender.send(outs.at[j], outs_h[j])
    sender.finish()


def backward_kernel(dims, *refs):
    depth, zs, shard, block, span = dims
    heads = span // HEAD_DIM
    pos, gain = refs[:2]
    gs_h, refs = refs[2 : 2 + depth], refs[2 + depth :]
    (w_out_h, query_h, keys_h, values_h, keys_t_h, lse_h, normed_h, att_t_h, weights_h) = refs[:9]
    near, far, d_qkv_h = refs[9:12]
    (gs, w_out, query, keys, values, keys_t, lse, normed, att_t, weights) = refs[12:22]
    (d_qkv, d_att, delta, d_query_t, d_keys, d_values, grad_out, in_sems, out_sems) = refs[22:]
    copies = fetch(
        [(w_out_h, w_out), (att_t_h, att_t)]
        + [(gs_h[j], gs.at[j]) for j in range(depth)]
        + [
            (keys_h, keys),
            (query_h, query),
            (values_h, values),
            (lse_h, lse),
            (keys_t_h, keys_t),
            (normed_h, normed),
            (weights_h, weights),
        ],
        in_sems,
    )

    copies[0].wait()
    copies[1].wait()
    for j in range(depth):
        rows = slice(j * block, (j + 1) * block)
        copies[2 + j].wait()
        part = dot(gs[j], w_out[...], (1, 1)).astype(BF16)
        d_att[rows, :] = part
        product = jnp.transpose(part.astype(F32)) * att_t[:, rows]
        for h in range(heads):
            delta[h, :, rows] = jnp.sum(
                product[h * HEAD_DIM : (h + 1) * HEAD_DIM], axis=0, keepdims=True
            )
    for copy in copies[2 + depth :]:
        copy.wait()
    d_keys[...] = jnp.zeros_like(d_keys)
    d_values[...] = jnp.zeros_like(d_values)
    masks = head_masks(span)

    def step(j, _):
        cols = pl.ds(pl.multiple_of(j * block, block), block)
        q_block, g_block = query[cols, :], d_att[cols, :]
        qs = [q_block * m for m in masks]
        ds = [g_block * m for m in masks]
        units = [(c, h) for c in range(depth) for h in range(heads)]

        def pair(c, h):
            rows = slice(c * block, (c + 1) * block)
            return dot(keys[rows, :], qs[h], (1, 1)), dot(values[rows, :], ds[h], (1, 1))

        ready = pair(*units[0])
        queries = [None] * heads
        for i, (c, h) in enumerate(units):
            scores, d_probs = ready
            if i + 1 < len(units):
                ready = pair(*units[i + 1])
            rows = slice(c * block, (c + 1) * block)
            lanes = slice(h * HEAD_DIM, (h + 1) * HEAD_DIM)
            probs = jnp.exp(scores - lse[h, :, cols])
            d_scores = (probs * (d_probs - delta[h, :, cols])).astype(BF16)
            values_add = dot(probs.astype(BF16), ds[h])
            keys_add = dot(d_scores, qs[h])
            query_add = dot(keys_t[lanes, rows], d_scores)
            value_part = values_add if h == 0 else value_part + values_add
            key_part = keys_add if h == 0 else key_part + keys_add
            queries[h] = query_add if c == 0 else queries[h] + query_add
            if h == heads - 1:
                d_values[rows, :] += value_part.astype(BF16).astype(F32)
                d_keys[rows, :] += key_part.astype(BF16).astype(F32)
        for h in range(heads):
            d_query_t[h * HEAD_DIM : (h + 1) * HEAD_DIM, cols] = SCALE * queries[h]
        return 0

    lax.fori_loop(0, depth, step, 0)
    d_qkv[:, span : 2 * span] = d_keys[...].astype(BF16)
    d_qkv[:, 2 * span :] = d_values[...].astype(BF16)
    for j in range(depth):
        rows = slice(j * block, (j + 1) * block)
        d_qkv[rows, :span] = jnp.transpose(d_query_t[:, rows]).astype(BF16)
    sender = Sender(out_sems)
    sender.send(d_qkv, d_qkv_h)

    part = dot(att_t[:, :block].astype(BF16), gs[0])
    for j in range(1, depth):
        part = part + dot(att_t[:, j * block : (j + 1) * block].astype(BF16), gs[j])
    grad_out[...] = part
    grads = dot(normed[...], d_qkv[...], (0, 0))
    gain_rows = jnp.transpose(jnp.broadcast_to(gain[...], (128, gain.shape[1])))[:, :64]
    both = jnp.sum(weights[...].astype(F32) * grads, axis=1, keepdims=True)
    gain_column = both / gain_rows
    own_z, first = pos[0], pos[1] == 0
    for d in range(depth):
        for z in range(zs):
            sides = []
            for c in range(2):
                row, row_out = ((d * zs + z) * 2 + c) * shard, (z * 2 + c) * shard
                sides.append(
                    (
                        grads[row : row + shard],
                        gain_column[row : row + shard],
                        grad_out[row_out : row_out + shard, d * span : (d + 1) * span],
                    )
                )
            at = 0
            for one, two in zip(*sides):
                lanes = slice(at, at + one.shape[1])
                at += one.shape[1]
                near[z ^ own_z, d, :, lanes] = jnp.where(first, one, two)
                far[z ^ own_z, d, :, lanes] = jnp.where(first, two, one).astype(BF16)
    sender.finish()


def input_kernel(dims, *refs):
    depth, zs, shard, block, span = dims
    half = block // 2
    weights_h, d_qkv_h, dn0, dn1, dn2, dn3_top, dn3_bottom = refs[:7]
    weights, d_qkv, dns, in_sems, out_sems = refs[7:]
    copies = fetch(
        [(weights_h, weights)]
        + [
            (d_qkv_h.at[pl.ds(j * block, block)], d_qkv.at[pl.ds(j * block, block)])
            for j in range(depth)
        ],
        in_sems,
    )
    sender = Sender(out_sems)
    copies[0].wait()
    for j in range(depth):
        copies[1 + j].wait()
        dns[j] = dot(d_qkv[j * block : (j + 1) * block, :], weights[...], (1, 1)).astype(BF16)
        if j < depth - 1:
            sender.send(dns.at[j], (dn0, dn1, dn2)[j])
        else:
            sender.send(dns.at[j, pl.ds(0, half)], dn3_top)
            sender.send(dns.at[j, pl.ds(half, half)], dn3_bottom)
    sender.finish()


def align_kernel(dims, gain, x, upstream, *refs):
    dns, out = refs[:-1], refs[-1]
    d_normed = dns[0][...].astype(F32)
    for part in dns[1:]:
        d_normed = d_normed + part[...].astype(F32)
    unit, inverse = unit_rows(x[...])
    d_unit = d_normed * gain[...]
    out[...] = (
        upstream[...].astype(F32)
        + inverse
        * (
            d_unit
            - jnp.mean(d_unit, axis=-1, keepdims=True)
            - unit * jnp.mean(d_unit * unit, axis=-1, keepdims=True)
        )
    ).astype(BF16)


def finish_kernel(dims, parts, *outs):
    depth, zs, shard, block, span = dims
    gain_sum = None
    for d in range(depth):
        total = parts[d].astype(F32)
        for i in range(3):
            outs[i][:, d * span : (d + 1) * span] = total[:, i * span : (i + 1) * span]
        gain = total[:, 3 * span : 3 * span + 1]
        gain_sum = gain if gain_sum is None else gain_sum + gain
    wide = jnp.concatenate([gain_sum, jnp.zeros((128 - shard, 1), F32)], axis=0)
    outs[3][...] = jnp.transpose(jnp.broadcast_to(wide, (128, 128)))[0:1, :shard]


VMEM, ANY, SMEM = pltpu.VMEM, pl.ANY, pltpu.SMEM


def call(kernel, dims, ins, outs, scratch, sems, flops, mib=56):
    args = [a for a, _ in ins]
    shapes = [jax.ShapeDtypeStruct(shape, kind) for shape, kind, _ in outs]
    size = sum(a.size * a.dtype.itemsize for a in args + shapes)
    return pl.pallas_call(
        functools.partial(kernel, dims),
        out_shape=shapes,
        in_specs=[pl.BlockSpec(memory_space=space) for _, space in ins],
        out_specs=[pl.BlockSpec(memory_space=space) for _, _, space in outs],
        scratch_shapes=[pltpu.VMEM(shape, kind) for shape, kind in scratch]
        + [pltpu.SemaphoreType.DMA((n,)) for n in sems],
        compiler_params=pltpu.CompilerParams(vmem_limit_bytes=mib * 1024 * 1024),
        cost_estimate=pl.CostEstimate(flops=flops, bytes_accessed=size, transcendentals=0),
    )(*args)


def head_body(depth, res, *args):
    x, gain, w_query, w_key, w_value, w_out, upstream = args
    homologs, _, width = x.shape
    span, zs = width // depth, res // 2
    shard = w_query.shape[0]
    total, heads, half = homologs * depth, span // HEAD_DIM, homologs // 2
    dims = (depth, zs, shard, homologs, span)
    x = x.reshape(homologs, width)
    upstream = upstream.reshape(homologs, width)
    gain = gain.reshape(1, width)
    pos = jnp.stack([lax.axis_index("z"), lax.axis_index("core")]).astype(jnp.int32)

    x1, x2 = swap(x, "depth", depth, 1), swap(x, "depth", depth, 2)

    packed = call(
        pack_kernel,
        dims,
        [(w_query, VMEM), (w_key, VMEM), (w_value, VMEM)],
        [((depth, shard, 3 * span), BF16, VMEM)],
        [],
        [],
        1000,
    )[0]
    out_cut = jnp.stack([w_out[:, j * span : (j + 1) * span] for j in range(depth)], axis=0)
    mine = lax.all_to_all(packed, "depth", 0, 0, tiled=True)
    mine = jnp.concatenate([mine, out_cut], axis=2)
    x3_top = swap(x2[:half], "depth", depth, 1)
    x3_bottom = swap(x1[half:], "depth", depth, 2)
    w_near = jnp.stack([mine] + [swap(mine, "z", zs, k) for k in range(1, zs)], axis=0)
    w_near, x3_top, x3_bottom = lax.optimization_barrier((w_near, x3_top, x3_bottom))
    w_far = swap(w_near, "core", 2, 1)
    gs = [upstream] + [swap(upstream, "depth", depth, k) for k in range(1, depth)]

    rows, turned = ((total, span), BF16), ((span, total), BF16)
    block, halved = ((homologs, width), BF16), ((half, width), BF16)
    blocks = ((depth, homologs, width), BF16)
    norm, stats = ((total, width), BF16), ((heads, 1, total), F32)
    in_weights, out_weights = ((width, 3 * span), BF16), ((span, width), BF16)
    pass_flops = 2 * total * total * span
    normed = call(
        norm_kernel,
        dims,
        [(gain, VMEM)] + [(a, ANY) for a in (x, x1, x2, x3_top, x3_bottom)],
        [norm + (ANY,)],
        [blocks, norm],
        [depth + 1, depth],
        1000,
    )[0]
    turned_f32 = ((span, total), F32)
    saved = [rows, rows, rows, turned, turned_f32, stats, in_weights, out_weights]
    query, keys, values, keys_t, att_t, lse, weights, wo, *outs = call(
        forward_kernel,
        dims,
        [(pos, SMEM), (w_near, VMEM), (w_far, VMEM), (normed, ANY)],
        [s + (ANY,) for s in saved + [block] * depth],
        [norm, rows, rows, rows, turned, turned, turned_f32, stats]
        + [in_weights, out_weights, blocks],
        [depth, len(saved) + depth],
        8 * pass_flops,
    )

    packed = (zs, depth, shard, 4 * span + 64)
    joined = ((total, 3 * span), BF16)
    near, far, d_qkv = call(
        backward_kernel,
        dims,
        [(pos, SMEM), (gain, VMEM)]
        + [(a, ANY) for a in gs + [wo, query, keys, values, keys_t, lse, normed, att_t, weights]],
        [(packed, F32, VMEM), (packed, BF16, VMEM), joined + (ANY,)],
        [blocks, out_weights, rows, rows, rows, turned, stats, norm, turned_f32, in_weights]
        + [joined, rows, stats, turned_f32]
        + [((total, span), F32)] * 2
        + [((span, width), F32)],
        [depth + 9, 1],
        24 * pass_flops,
    )

    outs = [outs[0]] + [swap(outs[k], "depth", depth, k) for k in range(1, depth)]
    near, far, d_qkv, *outs = lax.optimization_barrier([near, far, d_qkv] + outs)
    final_result = (x.astype(F32) + sum(o.astype(F32) for o in outs)).astype(BF16)

    far = swap(far, "core", 2, 1)
    dn0, dn1, dn2, dn3_top, dn3_bottom = call(
        input_kernel,
        dims,
        [(weights, ANY), (d_qkv, ANY)],
        [s + (ANY,) for s in [block] * 3 + [halved] * 2],
        [in_weights, joined, blocks],
        [depth + 1, depth + 1],
        6 * total * width * span,
    )
    near = near + far.astype(F32)
    own, low = near[0], [near[k].astype(BF16) for k in range(1, zs)]
    own, dn3_top, dn3_bottom, *low = lax.optimization_barrier([own, dn3_top, dn3_bottom] + low)
    low = [swap(low[k - 1], "z", zs, k) for k in range(1, zs)]
    top, bottom = swap(dn3_top, "depth", depth, 1), swap(dn3_bottom, "depth", depth, 2)
    dn2 = dn2.astype(F32) + jnp.concatenate([top, jnp.zeros_like(top)], axis=0).astype(F32)
    dn1 = dn1.astype(F32) + jnp.concatenate([jnp.zeros_like(bottom), bottom], axis=0).astype(F32)
    dn1 = swap(dn1.astype(BF16), "depth", depth, 1)
    dn2 = swap(dn2.astype(BF16), "depth", depth, 2)
    acc = own + sum(p.astype(F32) for p in low)
    acc, dn1, dn2 = lax.optimization_barrier((acc, dn1, dn2))
    grad_out = jnp.concatenate([acc[j, :, 3 * span + 64 :] for j in range(depth)], axis=1)
    acc = acc[:, :, : 3 * span + 64].astype(BF16)
    parts = lax.all_to_all(acc, "depth", 0, 0, tiled=True)
    alignment = call(
        align_kernel,
        dims,
        [(a, VMEM) for a in (gain, x, upstream, dn0, dn1, dn2)],
        [block + (VMEM,)],
        [],
        [],
        1000 * total * width,
    )[0]
    parts, alignment = lax.optimization_barrier((parts, alignment))
    grad_query, grad_key, grad_value, gain_rows = call(
        finish_kernel,
        dims,
        [(parts, VMEM)],
        [((shard, width), F32, VMEM)] * 3 + [((1, shard), F32, VMEM)],
        [],
        [],
        1000,
        16,
    )
    return (
        final_result.reshape(homologs, 1, width),
        alignment.reshape(homologs, 1, width),
        grad_query,
        grad_key,
        grad_value,
        grad_out,
        gain_rows.reshape(shard),
    )


def solution(mesh):
    depth, res = mesh.shape["depth"], mesh.shape["res"]
    powers = depth & (depth - 1) == 0 and res & (res - 1) == 0 and res > 1
    if powers and depth == 4 and HEADS % depth == 0:
        axes = ("depth", "z", "core")
        mesh = Mesh(mesh.devices.reshape(depth, res // 2, 2), axes)
        res_axes, run = ("z", "core"), functools.partial(head_body, depth, res)
    else:
        axes = ("depth", "res")
        res_axes, run = ("res",), general_body

    def body(*args):
        if args[0].shape[1] != 1:
            return general_body(*args, axes=axes)
        return run(*args)

    rows = P("depth", res_axes, None)
    weight = P(axes, None)
    return jax.shard_map(
        body,
        mesh=mesh,
        in_specs=(rows, P(), weight, weight, weight, weight, rows),
        out_specs=(rows, rows, weight, weight, weight, weight, P(axes)),
        check_vma=False,
    )
```

```python
import functools

import jax
import jax.numpy as jnp
from jax import lax
from jax.experimental import pallas as pl
from jax.experimental.pallas import tpu as pltpu
from jax.sharding import Mesh, PartitionSpec as P

HEADS = 12
HEAD_DIM = 64


def standardize_entries(family_activity, rescale_factor):
    payload_entries = family_activity.astype(jnp.float32)
    centered = payload_entries - jnp.mean(payload_entries, axis=-1, keepdims=True)
    reciprocal_spread = lax.rsqrt(jnp.mean(centered * centered, axis=-1, keepdims=True) + 1e-05)
    standardized_entries = centered * reciprocal_spread
    return (
        (standardized_entries * rescale_factor).astype(jnp.bfloat16),
        standardized_entries,
        reciprocal_spread,
    )


def project(rows, weight, factor):
    return (factor * jnp.dot(rows, weight, preferred_element_type=jnp.float32)).astype(jnp.bfloat16)


def to_heads(array):
    count, cols = (array.shape[0], array.shape[1])
    return jnp.transpose(array.reshape(count, cols, HEADS, HEAD_DIM), (1, 2, 0, 3)).reshape(
        cols * HEADS, count, HEAD_DIM
    )


def from_heads(array, cols):
    count = array.shape[1]
    return jnp.transpose(array.reshape(cols, HEADS, count, HEAD_DIM), (2, 0, 1, 3)).reshape(
        count, cols, HEADS * HEAD_DIM
    )


def head_pass(query, keys, payload_entries, d_att):
    scale = HEAD_DIM ** (-0.5)
    scores = jnp.dot(query, keys.T, preferred_element_type=jnp.float32)
    probs = jax.nn.softmax(scores, axis=-1)
    probs_b = probs.astype(jnp.bfloat16)
    mixed_homologs = jnp.dot(probs_b, payload_entries, preferred_element_type=jnp.float32).astype(
        jnp.bfloat16
    )
    d_probs = jnp.dot(d_att, payload_entries.T, preferred_element_type=jnp.float32)
    d_scores = probs * (d_probs - jnp.sum(probs * d_probs, axis=-1, keepdims=True))
    d_scores_b = d_scores.astype(jnp.bfloat16)
    d_query = (scale * jnp.dot(d_scores_b, keys, preferred_element_type=jnp.float32)).astype(
        jnp.bfloat16
    )
    key_part = jnp.einsum("st,sd->td", d_scores_b, query, preferred_element_type=jnp.float32)
    value_part = jnp.einsum("st,sd->td", probs_b, d_att, preferred_element_type=jnp.float32)
    return (mixed_homologs, d_query, key_part, value_part)


def general_body(
    family_activity,
    rescale_factor,
    asking_weights,
    lookup_weights,
    payload_weights,
    exit_weights,
    upstream_adjoint,
    axes=("depth", "res"),
):
    query_weight, key_weight, value_weight, output_matrix = (
        lax.all_gather(asking_weights, axes, axis=0, tiled=True),
        lax.all_gather(lookup_weights, axes, axis=0, tiled=True),
        lax.all_gather(payload_weights, axes, axis=0, tiled=True),
        lax.all_gather(exit_weights, axes, axis=0, tiled=True),
    )
    homologs_each_shard, positions_each_shard, embed_span = family_activity.shape
    standardized_source, standardized_entries, reciprocal_spread = standardize_entries(
        family_activity, rescale_factor
    )
    query = project(standardized_source, query_weight, HEAD_DIM ** (-0.5))
    keys = project(standardized_source, key_weight, 1.0)
    payload_entries = project(standardized_source, value_weight, 1.0)
    keys_all, values_all = (
        lax.all_gather(keys, "depth", axis=0, tiled=True),
        lax.all_gather(payload_entries, "depth", axis=0, tiled=True),
    )
    d_att = jnp.dot(upstream_adjoint, output_matrix.T, preferred_element_type=jnp.float32).astype(
        jnp.bfloat16
    )

    def per_head(items):
        return head_pass(items[0], items[1], items[2], items[3])

    mixed_homologs, d_query, key_part, value_part = lax.map(
        per_head, (to_heads(query), to_heads(keys_all), to_heads(values_all), to_heads(d_att))
    )
    mixed_homologs = from_heads(mixed_homologs, positions_each_shard)
    d_query = from_heads(d_query, positions_each_shard)
    key_part = from_heads(key_part, positions_each_shard)
    value_part = from_heads(value_part, positions_each_shard)
    rows = homologs_each_shard * positions_each_shard
    normed_rows = standardized_source.reshape(rows, embed_span)
    part_query = jnp.dot(
        normed_rows.T, d_query.reshape(rows, embed_span), preferred_element_type=jnp.float32
    )
    part_out = jnp.dot(
        mixed_homologs.reshape(rows, embed_span).T,
        upstream_adjoint.reshape(rows, embed_span),
        preferred_element_type=jnp.float32,
    )
    stacked = jnp.stack([key_part, value_part], axis=2).astype(jnp.bfloat16)
    summed = (
        lax.psum_scatter(stacked, "depth", scatter_dimension=0, tiled=True)
        .astype(jnp.float32)
        .astype(jnp.bfloat16)
    )
    d_keys = summed[:, :, 0, :]
    d_values = summed[:, :, 1, :]
    final_result = (
        family_activity.astype(jnp.float32)
        + jnp.dot(mixed_homologs, output_matrix, preferred_element_type=jnp.float32)
    ).astype(jnp.bfloat16)
    part_key = jnp.dot(
        normed_rows.T, d_keys.reshape(rows, embed_span), preferred_element_type=jnp.float32
    )
    part_value = jnp.dot(
        normed_rows.T, d_values.reshape(rows, embed_span), preferred_element_type=jnp.float32
    )
    d_normed = jnp.dot(d_query, query_weight.T, preferred_element_type=jnp.float32)
    d_normed = d_normed + jnp.dot(d_keys, key_weight.T, preferred_element_type=jnp.float32)
    d_normed = d_normed + jnp.dot(d_values, value_weight.T, preferred_element_type=jnp.float32)
    part_gain = jnp.sum((d_normed * standardized_entries).reshape(rows, embed_span), axis=0)
    unit_gradient = d_normed * rescale_factor
    alignment_gradient = upstream_adjoint.astype(jnp.float32) + reciprocal_spread * (
        unit_gradient
        - jnp.mean(unit_gradient, axis=-1, keepdims=True)
        - standardized_entries
        * jnp.mean(unit_gradient * standardized_entries, axis=-1, keepdims=True)
    )
    query_gradient, key_gradient, value_gradient, output_gradient, gain_gradient = (
        lax.psum_scatter(part_query, axes, scatter_dimension=0, tiled=True),
        lax.psum_scatter(part_key, axes, scatter_dimension=0, tiled=True),
        lax.psum_scatter(part_value, axes, scatter_dimension=0, tiled=True),
        lax.psum_scatter(part_out, axes, scatter_dimension=0, tiled=True),
        lax.psum_scatter(part_gain, axes, scatter_dimension=0, tiled=True),
    )
    return (
        final_result,
        alignment_gradient.astype(jnp.bfloat16),
        query_gradient,
        key_gradient,
        value_gradient,
        output_gradient,
        gain_gradient,
    )


F32, BF16 = jnp.float32, jnp.bfloat16
SCALE = HEAD_DIM ** (-0.5)


def swap(value, axis, size, bits):
    return lax.ppermute(value, axis, [(i, i ^ bits) for i in range(size)])


def dot(a, b, contract=(1, 0)):
    return lax.dot_general(
        a, b, (((contract[0],), (contract[1],)), ((), ())), preferred_element_type=F32
    )


def unit_rows(x):
    x = x.astype(F32)
    centered = x - jnp.mean(x, axis=-1, keepdims=True)
    inverse = lax.rsqrt(jnp.mean(centered * centered, axis=-1, keepdims=True) + 1e-05)
    return centered * inverse, inverse


def head_masks(span):
    lane = lax.broadcasted_iota(jnp.int32, (8, span), 1)
    return [
        ((lane >= at) & (lane < at + HEAD_DIM)).astype(F32)[0:1].astype(BF16)
        for at in range(0, span, HEAD_DIM)
    ]


def fetch(pairs, sems):
    copies = [pltpu.make_async_copy(src, dst, sems.at[i]) for i, (src, dst) in enumerate(pairs)]
    for copy in copies:
        copy.start()
    return copies


class Sender:
    def __init__(self, sems):
        self.sems, self.copies = sems, []

    def send(self, src, dst):
        copy = pltpu.make_async_copy(src, dst, self.sems.at[len(self.copies)])
        copy.start()
        self.copies.append(copy)

    def finish(self):
        for copy in self.copies:
            copy.wait()


def pack_kernel(dims, w_query, w_key, w_value, out):
    depth, zs, shard, block, span = dims
    for d in range(depth):
        lanes = slice(d * span, (d + 1) * span)
        for i, w in enumerate((w_query, w_key, w_value)):
            out[d, :, i * span : (i + 1) * span] = w[:, lanes]


def norm_kernel(dims, *refs):
    depth, zs, shard, block, span = dims
    gain, x0, x1, x2, normed_h, normed_t_h, xs, normed, normed_t, in_sems, out_sems = refs
    copies = fetch([(x0, xs.at[0]), (x1, xs.at[1]), (x2, xs.at[2])], in_sems)
    sender = Sender(out_sems)
    for j in range(3):
        copies[j].wait()
        unit, _ = unit_rows(xs[j])
        rows = pl.ds(j * block, block)
        wide = unit * gain[...]
        normed[rows, :] = wide.astype(BF16)
        sender.send(normed.at[rows], normed_h.at[rows])
        normed_t[:, rows] = jnp.transpose(wide).astype(BF16)
        sender.send(normed_t.at[:, rows], normed_t_h.at[:, rows])
    sender.finish()


def forward_kernel(dims, *refs):
    depth, zs, shard, block, span = dims
    heads, half = span // HEAD_DIM, block // 2
    pos, gain, w_near, w_far, wo_near, wo_far, normed_h, x3_top, x3_bottom = refs[:9]
    query_h, keys_h, values_h, keys_t_h, att_t_h, lse_h, wq_h, wk_h, wv_h, w_out_h = refs[9:19]
    last_t_h, outs_h, refs = refs[19], refs[20 : 20 + depth], refs[20 + depth :]
    x3, normed, query, keys, values, keys_t, values_t, att_t, lse = refs[:9]
    wq, wk, wv, w_out, last_t, outs, in_sems, out_sems = refs[9:]
    first_rows = pl.ds(0, (depth - 1) * block)
    copies = fetch(
        [
            (x3_top, x3.at[pl.ds(0, half)]),
            (x3_bottom, x3.at[pl.ds(half, half)]),
            (normed_h, normed.at[first_rows]),
        ],
        in_sems,
    )
    sender = Sender(out_sems)

    own_z, first = pos[0], pos[1] == 0

    def pair(near, far):
        near, far = near.astype(F32), far.astype(F32)
        return jnp.concatenate(
            [jnp.where(first, near, far), jnp.where(first, far, near)], axis=0
        ).astype(BF16)

    for z in range(zs):
        for d in range(depth):
            both = pair(w_near[z ^ own_z, d], w_far[z ^ own_z, d])
            rows = slice((d * zs + z) * 2 * shard, (d * zs + z + 1) * 2 * shard)
            for i, w in enumerate((wq, wk, wv)):
                w[rows, :] = both[:, i * span : (i + 1) * span]
        both = pair(wo_near[z ^ own_z], wo_far[z ^ own_z])
        w_out[z * 2 * shard : (z + 1) * 2 * shard, :] = both
    for src, dst in ((wq, wq_h), (wk, wk_h), (wv, wv_h), (w_out, w_out_h)):
        sender.send(src, dst)
    copies[0].wait()
    copies[1].wait()
    unit, _ = unit_rows(x3[...])
    wide = unit * gain[...]
    last_rows = slice((depth - 1) * block, depth * block)
    normed[last_rows, :] = wide.astype(BF16)
    last_t[...] = jnp.transpose(wide).astype(BF16)
    sender.send(last_t, last_t_h)
    copies[2].wait()

    query[...] = (SCALE * dot(normed[...], wq[...])).astype(BF16)
    key = dot(normed[...], wk[...])
    keys[...] = key.astype(BF16)
    keys_t[...] = jnp.transpose(key).astype(BF16)
    value = dot(normed[...], wv[...])
    values[...] = value.astype(BF16)
    values_t[...] = jnp.transpose(value).astype(BF16)
    for src, dst in ((query, query_h), (keys, keys_h), (values, values_h), (keys_t, keys_t_h)):
        sender.send(src, dst)

    masks = head_masks(span)

    def step(j, _):
        cols = pl.ds(pl.multiple_of(j * block, block), block)
        q_block = query[cols, :]

        def score(h):
            return dot(keys[...], q_block * masks[h], (1, 1))

        ready = [score(h) for h in range(min(2, heads))]
        for h in range(heads):
            scores = ready[h]
            top = jnp.max(scores, axis=0, keepdims=True)
            e = jnp.exp(scores - top)
            total = jnp.sum(e, axis=0, keepdims=True)
            if h + 2 < heads:
                ready.append(score(h + 2))
            lanes = slice(h * HEAD_DIM, (h + 1) * HEAD_DIM)
            att_t[lanes, cols] = dot(values_t[lanes, :], e.astype(BF16)) * (1.0 / total)
            lse[h, :, cols] = top + jnp.log(total)
        return 0

    lax.fori_loop(0, depth, step, 0)
    sender.send(att_t, att_t_h)
    sender.send(lse, lse_h)
    att = jnp.transpose(att_t[...]).astype(BF16)
    for j in range(depth):
        outs[j] = dot(att[j * block : (j + 1) * block], w_out[...]).astype(BF16)
        sender.send(outs.at[j], outs_h[j])
    sender.finish()


def backward_kernel(dims, *refs):
    depth, zs, shard, block, span = dims
    heads, half = span // HEAD_DIM, block // 2
    pos, gain = refs[:2]
    gs_h, refs = refs[2 : 2 + depth], refs[2 + depth :]
    (w_out_h, query_h, keys_h, values_h, keys_t_h, lse_h, first_t_h, last_t_h) = refs[:8]
    (att_t_h, wq_h, wk_h, wv_h, near, far, dn0, dn1, dn2, dn3_top, dn3_bottom) = refs[8:19]
    (gs, w_out, query, keys, values, keys_t, lse, normed_t, att_t, wq, wk, wv) = refs[19:31]
    (d_att, delta, d_query_t, d_keys, d_values, grad_out, dns, in_sems, out_sems) = refs[31:]
    cut = (depth - 1) * block
    copies = fetch(
        [(w_out_h, w_out)]
        + [(gs_h[j], gs.at[pl.ds(j * block, block)]) for j in range(depth)]
        + [
            (att_t_h, att_t),
            (keys_h, keys),
            (query_h, query),
            (values_h, values),
            (lse_h, lse),
            (keys_t_h, keys_t),
            (first_t_h, normed_t.at[:, pl.ds(0, cut)]),
            (last_t_h, normed_t.at[:, pl.ds(cut, block)]),
            (wq_h, wq),
            (wk_h, wk),
            (wv_h, wv),
        ],
        in_sems,
    )
    ready, later = 7 + depth, copies[7 + depth :]

    d_keys[...] = jnp.zeros_like(d_keys)
    d_values[...] = jnp.zeros_like(d_values)
    for copy in copies[: 2 + depth]:
        copy.wait()
    part = dot(gs[...], w_out[...], (1, 1)).astype(BF16)
    d_att[...] = part
    product = jnp.transpose(part.astype(F32)) * att_t[...]
    for h in range(heads):
        delta[h] = jnp.sum(product[h * HEAD_DIM : (h + 1) * HEAD_DIM], axis=0, keepdims=True)
    for copy in copies[2 + depth : ready]:
        copy.wait()
    masks = head_masks(span)

    def step(j, _):
        cols = pl.ds(pl.multiple_of(j * block, block), block)
        q_block, g_block = query[cols, :], d_att[cols, :]
        qs = [q_block * m for m in masks]
        ds = [g_block * m for m in masks]

        def pair(h):
            return dot(keys[...], qs[h], (1, 1)), dot(values[...], ds[h], (1, 1))

        pairs = [pair(h) for h in range(min(2, heads))]
        for h in range(heads):
            scores, d_probs = pairs[h]
            probs = jnp.exp(scores - lse[h, :, cols])
            d_scores = (probs * (d_probs - delta[h, :, cols])).astype(BF16)
            if h + 2 < heads:
                pairs.append(pair(h + 2))
            values_add = dot(probs.astype(BF16), ds[h])
            keys_add = dot(d_scores, qs[h])
            value_part = values_add if h == 0 else value_part + values_add
            key_part = keys_add if h == 0 else key_part + keys_add
            lanes = slice(h * HEAD_DIM, (h + 1) * HEAD_DIM)
            d_query_t[lanes, cols] = SCALE * dot(keys_t[lanes, :], d_scores)
        d_values[...] += value_part.astype(BF16).astype(F32)
        d_keys[...] += key_part.astype(BF16).astype(F32)
        return 0

    lax.fori_loop(0, depth, step, 0)
    for copy in later:
        copy.wait()
    d_query = jnp.transpose(d_query_t[...]).astype(BF16)
    d_key, d_value = d_keys[...].astype(BF16), d_values[...].astype(BF16)
    sender = Sender(out_sems)
    for j in range(depth):
        rows = slice(j * block, (j + 1) * block)
        d_normed = dot(d_query[rows], wq[...], (1, 1))
        d_normed = d_normed + dot(d_key[rows], wk[...], (1, 1))
        d_normed = d_normed + dot(d_value[rows], wv[...], (1, 1))
        dns[j] = d_normed.astype(BF16)
        if j < depth - 1:
            sender.send(dns.at[j], (dn0, dn1, dn2)[j])
        else:
            sender.send(dns.at[j, pl.ds(0, half)], dn3_top)
            sender.send(dns.at[j, pl.ds(half, half)], dn3_bottom)

    grad_out[...] = dot(att_t[...].astype(BF16), gs[...])
    grads = [dot(normed_t[...], d) for d in (d_query, d_key, d_value)]
    both = wq[...].astype(F32) * grads[0]
    both = both + wk[...].astype(F32) * grads[1] + wv[...].astype(F32) * grads[2]
    gain_rows = jnp.transpose(jnp.broadcast_to(gain[...], (128, gain.shape[1])))[:, :64]
    gain_column = jnp.sum(both, axis=1, keepdims=True) / gain_rows
    own_z, first = pos[0], pos[1] == 0
    for d in range(depth):
        for z in range(zs):
            sides = []
            for c in range(2):
                row, row_out = ((d * zs + z) * 2 + c) * shard, (z * 2 + c) * shard
                sides.append(
                    [g[row : row + shard] for g in grads]
                    + [
                        gain_column[row : row + shard],
                        grad_out[row_out : row_out + shard, d * span : (d + 1) * span],
                    ]
                )
            at = 0
            for one, two in zip(*sides):
                lanes = slice(at, at + one.shape[1])
                at += one.shape[1]
                near[z ^ own_z, d, :, lanes] = jnp.where(first, one, two)
                far[z ^ own_z, d, :, lanes] = jnp.where(first, two, one).astype(BF16)
    sender.finish()


def align_kernel(dims, gain, x, upstream, *refs):
    dns, out = refs[:-1], refs[-1]
    d_normed = dns[0][...].astype(F32)
    for part in dns[1:]:
        d_normed = d_normed + part[...].astype(F32)
    unit, inverse = unit_rows(x[...])
    d_unit = d_normed * gain[...]
    out[...] = (
        upstream[...].astype(F32)
        + inverse
        * (
            d_unit
            - jnp.mean(d_unit, axis=-1, keepdims=True)
            - unit * jnp.mean(d_unit * unit, axis=-1, keepdims=True)
        )
    ).astype(BF16)


def finish_kernel(dims, parts, *outs):
    depth, zs, shard, block, span = dims
    gain_sum = None
    for d in range(depth):
        total = parts[d].astype(F32)
        for i in range(3):
            outs[i][:, d * span : (d + 1) * span] = total[:, i * span : (i + 1) * span]
        gain = total[:, 3 * span : 3 * span + 1]
        gain_sum = gain if gain_sum is None else gain_sum + gain
    wide = jnp.concatenate([gain_sum, jnp.zeros((128 - shard, 1), F32)], axis=0)
    outs[3][...] = jnp.transpose(jnp.broadcast_to(wide, (128, 128)))[0:1, :shard]


VMEM, ANY, SMEM = pltpu.VMEM, pl.ANY, pltpu.SMEM


def call(kernel, dims, ins, outs, scratch, sems, flops, mib=56):
    args = [a for a, _ in ins]
    shapes = [jax.ShapeDtypeStruct(shape, kind) for shape, kind, _ in outs]
    size = sum(a.size * a.dtype.itemsize for a in args + shapes)
    return pl.pallas_call(
        functools.partial(kernel, dims),
        out_shape=shapes,
        in_specs=[pl.BlockSpec(memory_space=space) for _, space in ins],
        out_specs=[pl.BlockSpec(memory_space=space) for _, _, space in outs],
        scratch_shapes=[pltpu.VMEM(shape, kind) for shape, kind in scratch]
        + [pltpu.SemaphoreType.DMA((n,)) for n in sems],
        compiler_params=pltpu.CompilerParams(vmem_limit_bytes=mib * 1024 * 1024),
        cost_estimate=pl.CostEstimate(flops=flops, bytes_accessed=size, transcendentals=0),
    )(*args)


def head_body(depth, res, *args):
    x, gain, w_query, w_key, w_value, w_out, upstream = args
    homologs, _, width = x.shape
    span, zs = width // depth, res // 2
    shard = w_query.shape[0]
    total, heads, half = homologs * depth, span // HEAD_DIM, homologs // 2
    dims = (depth, zs, shard, homologs, span)
    x = x.reshape(homologs, width)
    upstream = upstream.reshape(homologs, width)
    gain = gain.reshape(1, width)
    pos = jnp.stack([lax.axis_index("z"), lax.axis_index("core")]).astype(jnp.int32)

    x1, x2 = swap(x, "depth", depth, 1), swap(x, "depth", depth, 2)

    packed = call(
        pack_kernel,
        dims,
        [(w_query, VMEM), (w_key, VMEM), (w_value, VMEM)],
        [((depth, shard, 3 * span), BF16, VMEM)],
        [],
        [],
        1000,
    )[0]
    packed, w_out = lax.optimization_barrier((packed, w_out))
    mine = lax.all_to_all(packed, "depth", 0, 0, tiled=True)
    wo_parts = [w_out] + [swap(w_out, "z", zs, k) for k in range(1, zs)]
    mine, *wo_parts = lax.optimization_barrier([mine] + wo_parts)
    x3_top = swap(x2[:half], "depth", depth, 1)
    x3_bottom = swap(x1[half:], "depth", depth, 2)
    parts = [mine] + [swap(mine, "z", zs, k) for k in range(1, zs)]
    gs = [upstream] + [swap(upstream, "depth", depth, k) for k in range(1, depth)]

    rows, turned = ((total, span), BF16), ((span, total), BF16)
    block, halved = ((homologs, width), BF16), ((half, width), BF16)
    blocks = ((depth, homologs, width), BF16)
    norm, stats = ((total, width), BF16), ((heads, 1, total), F32)
    kept = total - homologs
    in_weights, out_weights = ((width, span), BF16), ((span, width), BF16)
    pass_flops = 2 * total * total * span
    normed, first_t = call(
        norm_kernel,
        dims,
        [(gain, VMEM), (x, ANY), (x1, ANY), (x2, ANY)],
        [((kept, width), BF16, ANY), ((width, kept), BF16, ANY)],
        [((3, homologs, width), BF16), ((kept, width), BF16), ((width, kept), BF16)],
        [3, 6],
        1000,
    )
    x3_top, x3_bottom, normed, pos, *parts = lax.optimization_barrier(
        [x3_top, x3_bottom, normed, pos] + parts
    )
    w_near, wo_near = jnp.stack(parts, axis=0), jnp.stack(wo_parts, axis=0)
    w_far, wo_far = swap(w_near, "core", 2, 1), swap(wo_near, "core", 2, 1)

    turned_f32, last = ((span, total), F32), ((width, homologs), BF16)
    saved = [rows, rows, rows, turned, turned_f32, stats] + [in_weights] * 3 + [out_weights, last]
    query, keys, values, keys_t, att_t, lse, wq, wk, wv, wo, last_t, *outs = call(
        forward_kernel,
        dims,
        [(pos, SMEM)]
        + [(a, VMEM) for a in (gain, w_near, w_far, wo_near, wo_far)]
        + [(a, ANY) for a in (normed, x3_top, x3_bottom)],
        [s + (ANY,) for s in saved + [block] * depth],
        [block, norm, rows, rows, rows, turned, turned, turned_f32, stats]
        + [in_weights] * 3
        + [out_weights, last, blocks],
        [3, len(saved) + depth],
        8 * pass_flops,
    )

    packed = (zs, depth, shard, 4 * span + 64)
    near, far, *dns = call(
        backward_kernel,
        dims,
        [(pos, SMEM), (gain, VMEM)]
        + [(a, ANY) for a in gs + [wo, query, keys, values, keys_t, lse, first_t, last_t]]
        + [(a, ANY) for a in (att_t, wq, wk, wv)],
        [(packed, F32, VMEM), (packed, BF16, VMEM)]
        + [s + (ANY,) for s in [block] * 3 + [halved] * 2],
        [norm, out_weights, rows, rows, rows, turned, stats, ((width, total), BF16)]
        + [turned_f32, in_weights, in_weights, in_weights]
        + [rows, stats, turned_f32]
        + [((total, span), F32)] * 2
        + [((span, width), F32), blocks],
        [depth + 12, depth + 1],
        24 * pass_flops,
    )

    outs = [outs[0]] + [swap(outs[k], "depth", depth, k) for k in range(1, depth)]
    near, far, *rest = lax.optimization_barrier([near, far] + dns + outs)
    dns, outs = rest[: len(dns)], rest[len(dns) :]
    final_result = (x.astype(F32) + sum(o.astype(F32) for o in outs)).astype(BF16)

    far = swap(far, "core", 2, 1)
    dn0, dn1, dn2, dn3_top, dn3_bottom = dns
    top, bottom = swap(dn3_top, "depth", depth, 1), swap(dn3_bottom, "depth", depth, 2)
    near = near + far.astype(F32)
    own, low = near[0], [near[k].astype(BF16) for k in range(1, zs)]
    top, bottom, _ = lax.optimization_barrier((top, bottom, low[0]))
    low = [swap(low[k - 1], "z", zs, k) for k in range(1, zs)]
    dn2 = dn2.astype(F32) + jnp.concatenate([top, jnp.zeros_like(top)], axis=0).astype(F32)
    dn1 = dn1.astype(F32) + jnp.concatenate([jnp.zeros_like(bottom), bottom], axis=0).astype(F32)
    dn1 = swap(dn1.astype(BF16), "depth", depth, 1)
    dn2 = swap(dn2.astype(BF16), "depth", depth, 2)
    acc = own + sum(p.astype(F32) for p in low)
    grad_out = jnp.concatenate([acc[j, :, 3 * span + 64 :] for j in range(depth)], axis=1)
    acc = acc[:, :, : 3 * span + 64].astype(BF16)
    parts = lax.all_to_all(acc, "depth", 0, 0, tiled=True)
    alignment = call(
        align_kernel,
        dims,
        [(a, VMEM) for a in (gain, x, upstream, dn0, dn1, dn2)],
        [block + (VMEM,)],
        [],
        [],
        1000 * total * width,
    )[0]
    parts, alignment = lax.optimization_barrier((parts, alignment))
    grad_query, grad_key, grad_value, gain_rows = call(
        finish_kernel,
        dims,
        [(parts, VMEM)],
        [((shard, width), F32, VMEM)] * 3 + [((1, shard), F32, VMEM)],
        [],
        [],
        1000,
        16,
    )
    return (
        final_result.reshape(homologs, 1, width),
        alignment.reshape(homologs, 1, width),
        grad_query,
        grad_key,
        grad_value,
        grad_out,
        gain_rows.reshape(shard),
    )


def solution(mesh):
    depth, res = mesh.shape["depth"], mesh.shape["res"]
    powers = depth & (depth - 1) == 0 and res & (res - 1) == 0 and res > 1
    if powers and depth == 4 and HEADS % depth == 0:
        axes = ("depth", "z", "core")
        mesh = Mesh(mesh.devices.reshape(depth, res // 2, 2), axes)
        res_axes, run = ("z", "core"), functools.partial(head_body, depth, res)
    else:
        axes = ("depth", "res")
        res_axes, run = ("res",), general_body

    def body(*args):
        if args[0].shape[1] != 1:
            return general_body(*args, axes=axes)
        return run(*args)

    rows = P("depth", res_axes, None)
    weight = P(axes, None)
    return jax.shard_map(
        body,
        mesh=mesh,
        in_specs=(rows, P(), weight, weight, weight, weight, rows),
        out_specs=(rows, rows, weight, weight, weight, weight, P(axes)),
        check_vma=False,
    )
```

```python
import functools

import jax
import jax.numpy as jnp
from jax import lax
from jax.experimental import pallas as pl
from jax.experimental.pallas import tpu as pltpu
from jax.sharding import Mesh, PartitionSpec as P

HEADS = 12
HEAD_DIM = 64


def standardize_entries(family_activity, rescale_factor):
    payload_entries = family_activity.astype(jnp.float32)
    centered = payload_entries - jnp.mean(payload_entries, axis=-1, keepdims=True)
    reciprocal_spread = lax.rsqrt(jnp.mean(centered * centered, axis=-1, keepdims=True) + 1e-05)
    standardized_entries = centered * reciprocal_spread
    return (
        (standardized_entries * rescale_factor).astype(jnp.bfloat16),
        standardized_entries,
        reciprocal_spread,
    )


def project(rows, weight, factor):
    return (factor * jnp.dot(rows, weight, preferred_element_type=jnp.float32)).astype(jnp.bfloat16)


def to_heads(array):
    count, cols = (array.shape[0], array.shape[1])
    return jnp.transpose(array.reshape(count, cols, HEADS, HEAD_DIM), (1, 2, 0, 3)).reshape(
        cols * HEADS, count, HEAD_DIM
    )


def from_heads(array, cols):
    count = array.shape[1]
    return jnp.transpose(array.reshape(cols, HEADS, count, HEAD_DIM), (2, 0, 1, 3)).reshape(
        count, cols, HEADS * HEAD_DIM
    )


def head_pass(query, keys, payload_entries, d_att):
    scale = HEAD_DIM ** (-0.5)
    scores = jnp.dot(query, keys.T, preferred_element_type=jnp.float32)
    probs = jax.nn.softmax(scores, axis=-1)
    probs_b = probs.astype(jnp.bfloat16)
    mixed_homologs = jnp.dot(probs_b, payload_entries, preferred_element_type=jnp.float32).astype(
        jnp.bfloat16
    )
    d_probs = jnp.dot(d_att, payload_entries.T, preferred_element_type=jnp.float32)
    d_scores = probs * (d_probs - jnp.sum(probs * d_probs, axis=-1, keepdims=True))
    d_scores_b = d_scores.astype(jnp.bfloat16)
    d_query = (scale * jnp.dot(d_scores_b, keys, preferred_element_type=jnp.float32)).astype(
        jnp.bfloat16
    )
    key_part = jnp.einsum("st,sd->td", d_scores_b, query, preferred_element_type=jnp.float32)
    value_part = jnp.einsum("st,sd->td", probs_b, d_att, preferred_element_type=jnp.float32)
    return (mixed_homologs, d_query, key_part, value_part)


def general_body(
    family_activity,
    rescale_factor,
    asking_weights,
    lookup_weights,
    payload_weights,
    exit_weights,
    upstream_adjoint,
    axes=("depth", "res"),
):
    query_weight, key_weight, value_weight, output_matrix = (
        lax.all_gather(asking_weights, axes, axis=0, tiled=True),
        lax.all_gather(lookup_weights, axes, axis=0, tiled=True),
        lax.all_gather(payload_weights, axes, axis=0, tiled=True),
        lax.all_gather(exit_weights, axes, axis=0, tiled=True),
    )
    homologs_each_shard, positions_each_shard, embed_span = family_activity.shape
    standardized_source, standardized_entries, reciprocal_spread = standardize_entries(
        family_activity, rescale_factor
    )
    query = project(standardized_source, query_weight, HEAD_DIM ** (-0.5))
    keys = project(standardized_source, key_weight, 1.0)
    payload_entries = project(standardized_source, value_weight, 1.0)
    keys_all, values_all = (
        lax.all_gather(keys, "depth", axis=0, tiled=True),
        lax.all_gather(payload_entries, "depth", axis=0, tiled=True),
    )
    d_att = jnp.dot(upstream_adjoint, output_matrix.T, preferred_element_type=jnp.float32).astype(
        jnp.bfloat16
    )

    def per_head(items):
        return head_pass(items[0], items[1], items[2], items[3])

    mixed_homologs, d_query, key_part, value_part = lax.map(
        per_head, (to_heads(query), to_heads(keys_all), to_heads(values_all), to_heads(d_att))
    )
    mixed_homologs = from_heads(mixed_homologs, positions_each_shard)
    d_query = from_heads(d_query, positions_each_shard)
    key_part = from_heads(key_part, positions_each_shard)
    value_part = from_heads(value_part, positions_each_shard)
    rows = homologs_each_shard * positions_each_shard
    normed_rows = standardized_source.reshape(rows, embed_span)
    part_query = jnp.dot(
        normed_rows.T, d_query.reshape(rows, embed_span), preferred_element_type=jnp.float32
    )
    part_out = jnp.dot(
        mixed_homologs.reshape(rows, embed_span).T,
        upstream_adjoint.reshape(rows, embed_span),
        preferred_element_type=jnp.float32,
    )
    stacked = jnp.stack([key_part, value_part], axis=2).astype(jnp.bfloat16)
    summed = (
        lax.psum_scatter(stacked, "depth", scatter_dimension=0, tiled=True)
        .astype(jnp.float32)
        .astype(jnp.bfloat16)
    )
    d_keys = summed[:, :, 0, :]
    d_values = summed[:, :, 1, :]
    final_result = (
        family_activity.astype(jnp.float32)
        + jnp.dot(mixed_homologs, output_matrix, preferred_element_type=jnp.float32)
    ).astype(jnp.bfloat16)
    part_key = jnp.dot(
        normed_rows.T, d_keys.reshape(rows, embed_span), preferred_element_type=jnp.float32
    )
    part_value = jnp.dot(
        normed_rows.T, d_values.reshape(rows, embed_span), preferred_element_type=jnp.float32
    )
    d_normed = jnp.dot(d_query, query_weight.T, preferred_element_type=jnp.float32)
    d_normed = d_normed + jnp.dot(d_keys, key_weight.T, preferred_element_type=jnp.float32)
    d_normed = d_normed + jnp.dot(d_values, value_weight.T, preferred_element_type=jnp.float32)
    part_gain = jnp.sum((d_normed * standardized_entries).reshape(rows, embed_span), axis=0)
    unit_gradient = d_normed * rescale_factor
    alignment_gradient = upstream_adjoint.astype(jnp.float32) + reciprocal_spread * (
        unit_gradient
        - jnp.mean(unit_gradient, axis=-1, keepdims=True)
        - standardized_entries
        * jnp.mean(unit_gradient * standardized_entries, axis=-1, keepdims=True)
    )
    query_gradient, key_gradient, value_gradient, output_gradient, gain_gradient = (
        lax.psum_scatter(part_query, axes, scatter_dimension=0, tiled=True),
        lax.psum_scatter(part_key, axes, scatter_dimension=0, tiled=True),
        lax.psum_scatter(part_value, axes, scatter_dimension=0, tiled=True),
        lax.psum_scatter(part_out, axes, scatter_dimension=0, tiled=True),
        lax.psum_scatter(part_gain, axes, scatter_dimension=0, tiled=True),
    )
    return (
        final_result,
        alignment_gradient.astype(jnp.bfloat16),
        query_gradient,
        key_gradient,
        value_gradient,
        output_gradient,
        gain_gradient,
    )


F32, BF16 = jnp.float32, jnp.bfloat16
SCALE = HEAD_DIM ** (-0.5)


def swap(value, axis, size, bits):
    return lax.ppermute(value, axis, [(i, i ^ bits) for i in range(size)])


def dot(a, b, contract=(1, 0)):
    return lax.dot_general(
        a, b, (((contract[0],), (contract[1],)), ((), ())), preferred_element_type=F32
    )


def unit_rows(x):
    x = x.astype(F32)
    centered = x - jnp.mean(x, axis=-1, keepdims=True)
    inverse = lax.rsqrt(jnp.mean(centered * centered, axis=-1, keepdims=True) + 1e-05)
    return centered * inverse, inverse


def head_masks(span):
    lane = lax.broadcasted_iota(jnp.int32, (8, span), 1)
    return [
        ((lane >= at) & (lane < at + HEAD_DIM)).astype(F32)[0:1].astype(BF16)
        for at in range(0, span, HEAD_DIM)
    ]


def fetch(pairs, sems):
    copies = [pltpu.make_async_copy(src, dst, sems.at[i]) for i, (src, dst) in enumerate(pairs)]
    for copy in copies:
        copy.start()
    return copies


class Sender:
    def __init__(self, sems):
        self.sems, self.copies = sems, []

    def send(self, src, dst):
        copy = pltpu.make_async_copy(src, dst, self.sems.at[len(self.copies)])
        copy.start()
        self.copies.append(copy)

    def finish(self):
        for copy in self.copies:
            copy.wait()


def pack_kernel(dims, pos, w_query, w_key, w_value, w_out, out):
    depth, zs, shard, block, span = dims
    for d in range(depth):
        lanes = slice(d * span, (d + 1) * span)
        for i, w in enumerate((w_query, w_key, w_value, w_out)):
            out[d ^ pos[2], :, i * span : (i + 1) * span] = w[:, lanes]


def norm_kernel(dims, *refs):
    depth, zs, shard, block, span = dims
    gain, x0, x1, x2, normed_h, normed_t_h, xs, normed, normed_t, in_sems, out_sems = refs
    copies = fetch([(x0, xs.at[0]), (x1, xs.at[1]), (x2, xs.at[2])], in_sems)
    sender = Sender(out_sems)
    for j in range(3):
        copies[j].wait()
        unit, _ = unit_rows(xs[j])
        rows = pl.ds(j * block, block)
        wide = unit * gain[...]
        normed[rows, :] = wide.astype(BF16)
        sender.send(normed.at[rows], normed_h.at[rows])
        normed_t[:, rows] = jnp.transpose(wide).astype(BF16)
        sender.send(normed_t.at[:, rows], normed_t_h.at[:, rows])
    sender.finish()


def forward_kernel(dims, *refs):
    depth, zs, shard, block, span = dims
    heads, half = span // HEAD_DIM, block // 2
    pos, gain, w_near, w_far, normed_h, x3_top, x3_bottom = refs[:7]
    query_h, keys_h, values_h, keys_t_h, att_t_h, lse_h, wq_h, wk_h, wv_h, w_out_h = refs[7:17]
    last_t_h, outs_h, refs = refs[17], refs[18 : 18 + depth], refs[18 + depth :]
    x3, normed, query, keys, values, keys_t, values_t, att_t, lse = refs[:9]
    wq, wk, wv, w_out, last_t, outs, in_sems, out_sems = refs[9:]
    first_rows = pl.ds(0, (depth - 1) * block)
    copies = fetch(
        [
            (x3_top, x3.at[pl.ds(0, half)]),
            (x3_bottom, x3.at[pl.ds(half, half)]),
            (normed_h, normed.at[first_rows]),
        ],
        in_sems,
    )
    sender = Sender(out_sems)

    own_z, first, own_d = pos[0], pos[1] == 0, pos[2]
    for z in range(zs):
        for d in range(depth):
            near = w_near[z ^ own_z, d ^ own_d].astype(F32)
            far = w_far[z ^ own_z, d ^ own_d].astype(F32)
            both = jnp.concatenate(
                [jnp.where(first, near, far), jnp.where(first, far, near)], axis=0
            ).astype(BF16)
            rows = slice((d * zs + z) * 2 * shard, (d * zs + z + 1) * 2 * shard)
            for i, w in enumerate((wq, wk, wv)):
                w[rows, :] = both[:, i * span : (i + 1) * span]
            rows = slice(z * 2 * shard, (z + 1) * 2 * shard)
            w_out[rows, d * span : (d + 1) * span] = both[:, 3 * span :]
    for src, dst in ((wq, wq_h), (wk, wk_h), (wv, wv_h), (w_out, w_out_h)):
        sender.send(src, dst)
    copies[0].wait()
    copies[1].wait()
    unit, _ = unit_rows(x3[...])
    wide = unit * gain[...]
    last_rows = slice((depth - 1) * block, depth * block)
    normed[last_rows, :] = wide.astype(BF16)
    last_t[...] = jnp.transpose(wide).astype(BF16)
    sender.send(last_t, last_t_h)
    copies[2].wait()

    query[...] = (SCALE * dot(normed[...], wq[...])).astype(BF16)
    key = dot(normed[...], wk[...])
    keys[...] = key.astype(BF16)
    keys_t[...] = jnp.transpose(key).astype(BF16)
    value = dot(normed[...], wv[...])
    values[...] = value.astype(BF16)
    values_t[...] = jnp.transpose(value).astype(BF16)
    for src, dst in ((query, query_h), (keys, keys_h), (values, values_h), (keys_t, keys_t_h)):
        sender.send(src, dst)

    masks = head_masks(span)

    def step(j, _):
        cols = pl.ds(pl.multiple_of(j * block, block), block)
        q_block = query[cols, :]

        def score(h):
            return dot(keys[...], q_block * masks[h], (1, 1))

        ready = [score(h) for h in range(min(2, heads))]
        for h in range(heads):
            scores = ready[h]
            top = jnp.max(scores, axis=0, keepdims=True)
            e = jnp.exp(scores - top)
            total = jnp.sum(e, axis=0, keepdims=True)
            if h + 2 < heads:
                ready.append(score(h + 2))
            lanes = slice(h * HEAD_DIM, (h + 1) * HEAD_DIM)
            att_t[lanes, cols] = dot(values_t[lanes, :], e.astype(BF16)) * (1.0 / total)
            lse[h, :, cols] = top + jnp.log(total)
        return 0

    lax.fori_loop(0, depth, step, 0)
    sender.send(att_t, att_t_h)
    sender.send(lse, lse_h)
    att = jnp.transpose(att_t[...]).astype(BF16)
    for j in range(depth):
        outs[j] = dot(att[j * block : (j + 1) * block], w_out[...]).astype(BF16)
        sender.send(outs.at[j], outs_h[j])
    sender.finish()


def backward_kernel(dims, *refs):
    depth, zs, shard, block, span = dims
    heads, half = span // HEAD_DIM, block // 2
    pos, gain = refs[:2]
    gs_h, refs = refs[2 : 2 + depth], refs[2 + depth :]
    (w_out_h, query_h, keys_h, values_h, keys_t_h, lse_h, first_t_h, last_t_h) = refs[:8]
    (att_t_h, wq_h, wk_h, wv_h, near, far, dn0, dn1, dn2, dn3_top, dn3_bottom) = refs[8:19]
    (gs, w_out, query, keys, values, keys_t, lse, normed_t, att_t, wq, wk, wv) = refs[19:31]
    (d_att, delta, d_query_t, d_keys, d_values, grad_out, dns, in_sems, out_sems) = refs[31:]
    cut = (depth - 1) * block
    copies = fetch(
        [(w_out_h, w_out)]
        + [(gs_h[j], gs.at[pl.ds(j * block, block)]) for j in range(depth)]
        + [
            (att_t_h, att_t),
            (keys_h, keys),
            (query_h, query),
            (values_h, values),
            (lse_h, lse),
            (keys_t_h, keys_t),
            (first_t_h, normed_t.at[:, pl.ds(0, cut)]),
            (last_t_h, normed_t.at[:, pl.ds(cut, block)]),
            (wq_h, wq),
            (wk_h, wk),
            (wv_h, wv),
        ],
        in_sems,
    )
    ready, later = 7 + depth, copies[7 + depth :]

    d_keys[...] = jnp.zeros_like(d_keys)
    d_values[...] = jnp.zeros_like(d_values)
    for copy in copies[: 2 + depth]:
        copy.wait()
    part = dot(gs[...], w_out[...], (1, 1)).astype(BF16)
    d_att[...] = part
    product = jnp.transpose(part.astype(F32)) * att_t[...]
    for h in range(heads):
        delta[h] = jnp.sum(product[h * HEAD_DIM : (h + 1) * HEAD_DIM], axis=0, keepdims=True)
    for copy in copies[2 + depth : ready]:
        copy.wait()
    masks = head_masks(span)

    def step(j, _):
        cols = pl.ds(pl.multiple_of(j * block, block), block)
        q_block, g_block = query[cols, :], d_att[cols, :]
        qs = [q_block * m for m in masks]
        ds = [g_block * m for m in masks]

        def pair(h):
            return dot(keys[...], qs[h], (1, 1)), dot(values[...], ds[h], (1, 1))

        pairs = [pair(h) for h in range(min(2, heads))]
        for h in range(heads):
            scores, d_probs = pairs[h]
            probs = jnp.exp(scores - lse[h, :, cols])
            d_scores = (probs * (d_probs - delta[h, :, cols])).astype(BF16)
            if h + 2 < heads:
                pairs.append(pair(h + 2))
            values_add = dot(probs.astype(BF16), ds[h])
            keys_add = dot(d_scores, qs[h])
            value_part = values_add if h == 0 else value_part + values_add
            key_part = keys_add if h == 0 else key_part + keys_add
            lanes = slice(h * HEAD_DIM, (h + 1) * HEAD_DIM)
            d_query_t[lanes, cols] = SCALE * dot(keys_t[lanes, :], d_scores)
        d_values[...] += value_part.astype(BF16).astype(F32)
        d_keys[...] += key_part.astype(BF16).astype(F32)
        return 0

    lax.fori_loop(0, depth, step, 0)
    for copy in later:
        copy.wait()
    d_query = jnp.transpose(d_query_t[...]).astype(BF16)
    d_key, d_value = d_keys[...].astype(BF16), d_values[...].astype(BF16)
    sender = Sender(out_sems)
    for j in range(depth):
        rows = slice(j * block, (j + 1) * block)
        d_normed = dot(d_query[rows], wq[...], (1, 1))
        d_normed = d_normed + dot(d_key[rows], wk[...], (1, 1))
        d_normed = d_normed + dot(d_value[rows], wv[...], (1, 1))
        dns[j] = d_normed.astype(BF16)
        if j < depth - 1:
            sender.send(dns.at[j], (dn0, dn1, dn2)[j])
        else:
            sender.send(dns.at[j, pl.ds(0, half)], dn3_top)
            sender.send(dns.at[j, pl.ds(half, half)], dn3_bottom)

    grad_out[...] = dot(att_t[...].astype(BF16), gs[...])
    grads = [dot(normed_t[...], d) for d in (d_query, d_key, d_value)]
    both = wq[...].astype(F32) * grads[0]
    both = both + wk[...].astype(F32) * grads[1] + wv[...].astype(F32) * grads[2]
    gain_rows = jnp.transpose(jnp.broadcast_to(gain[...], (128, gain.shape[1])))[:, :64]
    gain_column = jnp.sum(both, axis=1, keepdims=True) / gain_rows
    own_z, first, own_d = pos[0], pos[1] == 0, pos[2]
    for d in range(depth):
        for z in range(zs):
            sides = []
            for c in range(2):
                row, row_out = ((d * zs + z) * 2 + c) * shard, (z * 2 + c) * shard
                sides.append(
                    [g[row : row + shard] for g in grads]
                    + [
                        gain_column[row : row + shard],
                        grad_out[row_out : row_out + shard, d * span : (d + 1) * span],
                    ]
                )
            at = 0
            for one, two in zip(*sides):
                lanes = slice(at, at + one.shape[1])
                at += one.shape[1]
                near[z ^ own_z, d ^ own_d, :, lanes] = jnp.where(first, one, two)
                far[z ^ own_z, d ^ own_d, :, lanes] = jnp.where(first, two, one).astype(BF16)
    sender.finish()


def align_kernel(dims, gain, x, upstream, *refs):
    dns, out = refs[:-1], refs[-1]
    d_normed = dns[0][...].astype(F32)
    for part in dns[1:]:
        d_normed = d_normed + part[...].astype(F32)
    unit, inverse = unit_rows(x[...])
    d_unit = d_normed * gain[...]
    out[...] = (
        upstream[...].astype(F32)
        + inverse
        * (
            d_unit
            - jnp.mean(d_unit, axis=-1, keepdims=True)
            - unit * jnp.mean(d_unit * unit, axis=-1, keepdims=True)
        )
    ).astype(BF16)


def finish_kernel(dims, pos, acc, *refs):
    depth, zs, shard, block, span = dims
    parts, outs = (None,) + refs[: depth - 1], refs[depth - 1 :]
    own_d = pos[2]
    lanes = 3 * span + 64
    gain_sum = None
    blocks = [acc[0][:, :lanes]] + [p[...].astype(F32) for p in parts[1:]]
    for d in range(depth):
        total = blocks[0]
        for k in range(1, depth):
            total = jnp.where((d ^ own_d) == k, blocks[k], total)
        for i in range(3):
            outs[i][:, d * span : (d + 1) * span] = total[:, i * span : (i + 1) * span]
        outs[3][:, d * span : (d + 1) * span] = acc[d ^ own_d][:, lanes:]
        gain = total[:, 3 * span : 3 * span + 1]
        gain_sum = gain if gain_sum is None else gain_sum + gain
    wide = jnp.concatenate([gain_sum, jnp.zeros((128 - shard, 1), F32)], axis=0)
    outs[4][...] = jnp.transpose(jnp.broadcast_to(wide, (128, 128)))[0:1, :shard]


VMEM, ANY, SMEM = pltpu.VMEM, pl.ANY, pltpu.SMEM


def call(kernel, dims, ins, outs, scratch, sems, flops, mib=56):
    args = [a for a, _ in ins]
    shapes = [jax.ShapeDtypeStruct(shape, kind) for shape, kind, _ in outs]
    size = sum(a.size * a.dtype.itemsize for a in args + shapes)
    return pl.pallas_call(
        functools.partial(kernel, dims),
        out_shape=shapes,
        in_specs=[pl.BlockSpec(memory_space=space) for _, space in ins],
        out_specs=[pl.BlockSpec(memory_space=space) for _, _, space in outs],
        scratch_shapes=[pltpu.VMEM(shape, kind) for shape, kind in scratch]
        + [pltpu.SemaphoreType.DMA((n,)) for n in sems],
        compiler_params=pltpu.CompilerParams(vmem_limit_bytes=mib * 1024 * 1024),
        cost_estimate=pl.CostEstimate(flops=flops, bytes_accessed=size, transcendentals=0),
    )(*args)


def head_body(depth, res, *args):
    x, gain, w_query, w_key, w_value, w_out, upstream = args
    homologs, _, width = x.shape
    span, zs = width // depth, res // 2
    shard = w_query.shape[0]
    total, heads, half = homologs * depth, span // HEAD_DIM, homologs // 2
    dims = (depth, zs, shard, homologs, span)
    x = x.reshape(homologs, width)
    upstream = upstream.reshape(homologs, width)
    gain = gain.reshape(1, width)
    pos = jnp.stack([lax.axis_index(a) for a in ("z", "core", "depth")]).astype(jnp.int32)

    x1, x2 = swap(x, "depth", depth, 1), swap(x, "depth", depth, 2)

    packed = call(
        pack_kernel,
        dims,
        [(pos, SMEM)] + [(w, VMEM) for w in (w_query, w_key, w_value, w_out)],
        [((depth, shard, 4 * span), BF16, VMEM)],
        [],
        [],
        1000,
    )[0]
    mine = [packed[0, :, : 3 * span]] + [
        swap(packed[k, :, : 3 * span], "depth", depth, k) for k in range(1, depth)
    ]
    mine = jnp.concatenate([jnp.stack(mine, axis=0), packed[:, :, 3 * span :]], axis=2)
    mine, x1, x2 = lax.optimization_barrier((mine, x1, x2))
    parts = [mine] + [swap(mine, "z", zs, k) for k in range(1, zs)]
    parts[1], top, bottom = lax.optimization_barrier((parts[1], x2[:half], x1[half:]))
    x3_top, x3_bottom = swap(top, "depth", depth, 1), swap(bottom, "depth", depth, 2)
    gs = [upstream] + [swap(upstream, "depth", depth, k) for k in range(1, depth)]

    rows, turned = ((total, span), BF16), ((span, total), BF16)
    block, halved = ((homologs, width), BF16), ((half, width), BF16)
    blocks = ((depth, homologs, width), BF16)
    norm, stats = ((total, width), BF16), ((heads, 1, total), F32)
    kept = total - homologs
    in_weights, out_weights = ((width, span), BF16), ((span, width), BF16)
    pass_flops = 2 * total * total * span
    normed, first_t = call(
        norm_kernel,
        dims,
        [(gain, VMEM), (x, ANY), (x1, ANY), (x2, ANY)],
        [((kept, width), BF16, ANY), ((width, kept), BF16, ANY)],
        [((3, homologs, width), BF16), ((kept, width), BF16), ((width, kept), BF16)],
        [3, 6],
        1000,
    )
    normed, *parts = lax.optimization_barrier([normed] + parts)
    w_near = jnp.stack(parts, axis=0)
    w_far = swap(w_near, "core", 2, 1)

    turned_f32, last = ((span, total), F32), ((width, homologs), BF16)
    saved = [rows, rows, rows, turned, turned_f32, stats] + [in_weights] * 3 + [out_weights, last]
    query, keys, values, keys_t, att_t, lse, wq, wk, wv, wo, last_t, *outs = call(
        forward_kernel,
        dims,
        [(pos, SMEM)]
        + [(a, VMEM) for a in (gain, w_near, w_far)]
        + [(a, ANY) for a in (normed, x3_top, x3_bottom)],
        [s + (ANY,) for s in saved + [block] * depth],
        [block, norm, rows, rows, rows, turned, turned, turned_f32, stats]
        + [in_weights] * 3
        + [out_weights, last, blocks],
        [3, len(saved) + depth],
        8 * pass_flops,
    )

    packed = (zs, depth, shard, 4 * span + 64)
    near, far, *dns = call(
        backward_kernel,
        dims,
        [(pos, SMEM), (gain, VMEM)]
        + [(a, ANY) for a in gs + [wo, query, keys, values, keys_t, lse, first_t, last_t]]
        + [(a, ANY) for a in (att_t, wq, wk, wv)],
        [(packed, F32, VMEM), (packed, BF16, VMEM)]
        + [s + (ANY,) for s in [block] * 3 + [halved] * 2],
        [norm, out_weights, rows, rows, rows, turned, stats, ((width, total), BF16)]
        + [turned_f32, in_weights, in_weights, in_weights]
        + [rows, stats, turned_f32]
        + [((total, span), F32)] * 2
        + [((span, width), F32), blocks],
        [depth + 12, depth + 1],
        24 * pass_flops,
    )

    outs = [outs[0]] + [swap(outs[k], "depth", depth, k) for k in range(1, depth)]
    near, far, *rest = lax.optimization_barrier([near, far] + dns + outs)
    dns, outs = rest[: len(dns)], rest[len(dns) :]
    final_result = (x.astype(F32) + sum(o.astype(F32) for o in outs)).astype(BF16)

    far = swap(far, "core", 2, 1)
    dn0, dn1, dn2, dn3_top, dn3_bottom = dns
    top, bottom = swap(dn3_top, "depth", depth, 1), swap(dn3_bottom, "depth", depth, 2)
    near = near + far.astype(F32)
    own, low = near[0], [near[k].astype(BF16) for k in range(1, zs)]
    low = [swap(low[k - 1], "z", zs, k) for k in range(1, zs)]
    top, bottom, low[0] = lax.optimization_barrier((top, bottom, low[0]))
    dn2 = dn2.astype(F32) + jnp.concatenate([top, jnp.zeros_like(top)], axis=0).astype(F32)
    dn1 = dn1.astype(F32) + jnp.concatenate([jnp.zeros_like(bottom), bottom], axis=0).astype(F32)
    dn1 = swap(dn1.astype(BF16), "depth", depth, 1)
    dn2 = swap(dn2.astype(BF16), "depth", depth, 2)
    acc = own + sum(p.astype(F32) for p in low)
    parts = [
        swap(acc[k, :, : 3 * span + 64].astype(BF16), "depth", depth, k) for k in range(1, depth)
    ]
    alignment = call(
        align_kernel,
        dims,
        [(a, VMEM) for a in (gain, x, upstream, dn0, dn1, dn2)],
        [block + (VMEM,)],
        [],
        [],
        1000 * total * width,
    )[0]
    alignment, *parts = lax.optimization_barrier([alignment] + parts)
    grad_query, grad_key, grad_value, grad_out, gain_rows = call(
        finish_kernel,
        dims,
        [(pos, SMEM), (acc, VMEM)] + [(p, VMEM) for p in parts],
        [((shard, width), F32, VMEM)] * 4 + [((1, shard), F32, VMEM)],
        [],
        [],
        1000,
        16,
    )
    return (
        final_result.reshape(homologs, 1, width),
        alignment.reshape(homologs, 1, width),
        grad_query,
        grad_key,
        grad_value,
        grad_out,
        gain_rows.reshape(shard),
    )


def solution(mesh):
    depth, res = mesh.shape["depth"], mesh.shape["res"]
    powers = depth & (depth - 1) == 0 and res & (res - 1) == 0 and res > 1
    if powers and depth == 4 and HEADS % depth == 0:
        axes = ("depth", "z", "core")
        mesh = Mesh(mesh.devices.reshape(depth, res // 2, 2), axes)
        res_axes, run = ("z", "core"), functools.partial(head_body, depth, res)
    else:
        axes = ("depth", "res")
        res_axes, run = ("res",), general_body

    def body(*args):
        if args[0].shape[1] != 1:
            return general_body(*args, axes=axes)
        return run(*args)

    rows = P("depth", res_axes, None)
    weight = P(axes, None)
    return jax.shard_map(
        body,
        mesh=mesh,
        in_specs=(rows, P(), weight, weight, weight, weight, rows),
        out_specs=(rows, rows, weight, weight, weight, weight, P(axes)),
        check_vma=False,
    )
```

```python
import functools

import jax
import jax.numpy as jnp
from jax import lax
from jax.experimental import pallas as pl
from jax.experimental.pallas import tpu as pltpu
from jax.sharding import Mesh, PartitionSpec as P

HEADS = 12
HEAD_DIM = 64


def standardize_entries(family_activity, rescale_factor):
    payload_entries = family_activity.astype(jnp.float32)
    centered = payload_entries - jnp.mean(payload_entries, axis=-1, keepdims=True)
    reciprocal_spread = lax.rsqrt(jnp.mean(centered * centered, axis=-1, keepdims=True) + 1e-05)
    standardized_entries = centered * reciprocal_spread
    return (
        (standardized_entries * rescale_factor).astype(jnp.bfloat16),
        standardized_entries,
        reciprocal_spread,
    )


def project(rows, weight, factor):
    return (factor * jnp.dot(rows, weight, preferred_element_type=jnp.float32)).astype(jnp.bfloat16)


def to_heads(array):
    count, cols = (array.shape[0], array.shape[1])
    return jnp.transpose(array.reshape(count, cols, HEADS, HEAD_DIM), (1, 2, 0, 3)).reshape(
        cols * HEADS, count, HEAD_DIM
    )


def from_heads(array, cols):
    count = array.shape[1]
    return jnp.transpose(array.reshape(cols, HEADS, count, HEAD_DIM), (2, 0, 1, 3)).reshape(
        count, cols, HEADS * HEAD_DIM
    )


def head_pass(query, keys, payload_entries, d_att):
    scale = HEAD_DIM ** (-0.5)
    scores = jnp.dot(query, keys.T, preferred_element_type=jnp.float32)
    probs = jax.nn.softmax(scores, axis=-1)
    probs_b = probs.astype(jnp.bfloat16)
    mixed_homologs = jnp.dot(probs_b, payload_entries, preferred_element_type=jnp.float32).astype(
        jnp.bfloat16
    )
    d_probs = jnp.dot(d_att, payload_entries.T, preferred_element_type=jnp.float32)
    d_scores = probs * (d_probs - jnp.sum(probs * d_probs, axis=-1, keepdims=True))
    d_scores_b = d_scores.astype(jnp.bfloat16)
    d_query = (scale * jnp.dot(d_scores_b, keys, preferred_element_type=jnp.float32)).astype(
        jnp.bfloat16
    )
    key_part = jnp.einsum("st,sd->td", d_scores_b, query, preferred_element_type=jnp.float32)
    value_part = jnp.einsum("st,sd->td", probs_b, d_att, preferred_element_type=jnp.float32)
    return (mixed_homologs, d_query, key_part, value_part)


def general_body(
    family_activity,
    rescale_factor,
    asking_weights,
    lookup_weights,
    payload_weights,
    exit_weights,
    upstream_adjoint,
    axes=("depth", "res"),
):
    query_weight, key_weight, value_weight, output_matrix = (
        lax.all_gather(asking_weights, axes, axis=0, tiled=True),
        lax.all_gather(lookup_weights, axes, axis=0, tiled=True),
        lax.all_gather(payload_weights, axes, axis=0, tiled=True),
        lax.all_gather(exit_weights, axes, axis=0, tiled=True),
    )
    homologs_each_shard, positions_each_shard, embed_span = family_activity.shape
    standardized_source, standardized_entries, reciprocal_spread = standardize_entries(
        family_activity, rescale_factor
    )
    query = project(standardized_source, query_weight, HEAD_DIM ** (-0.5))
    keys = project(standardized_source, key_weight, 1.0)
    payload_entries = project(standardized_source, value_weight, 1.0)
    keys_all, values_all = (
        lax.all_gather(keys, "depth", axis=0, tiled=True),
        lax.all_gather(payload_entries, "depth", axis=0, tiled=True),
    )
    d_att = jnp.dot(upstream_adjoint, output_matrix.T, preferred_element_type=jnp.float32).astype(
        jnp.bfloat16
    )

    def per_head(items):
        return head_pass(items[0], items[1], items[2], items[3])

    mixed_homologs, d_query, key_part, value_part = lax.map(
        per_head, (to_heads(query), to_heads(keys_all), to_heads(values_all), to_heads(d_att))
    )
    mixed_homologs = from_heads(mixed_homologs, positions_each_shard)
    d_query = from_heads(d_query, positions_each_shard)
    key_part = from_heads(key_part, positions_each_shard)
    value_part = from_heads(value_part, positions_each_shard)
    rows = homologs_each_shard * positions_each_shard
    normed_rows = standardized_source.reshape(rows, embed_span)
    part_query = jnp.dot(
        normed_rows.T, d_query.reshape(rows, embed_span), preferred_element_type=jnp.float32
    )
    part_out = jnp.dot(
        mixed_homologs.reshape(rows, embed_span).T,
        upstream_adjoint.reshape(rows, embed_span),
        preferred_element_type=jnp.float32,
    )
    stacked = jnp.stack([key_part, value_part], axis=2).astype(jnp.bfloat16)
    summed = (
        lax.psum_scatter(stacked, "depth", scatter_dimension=0, tiled=True)
        .astype(jnp.float32)
        .astype(jnp.bfloat16)
    )
    d_keys = summed[:, :, 0, :]
    d_values = summed[:, :, 1, :]
    final_result = (
        family_activity.astype(jnp.float32)
        + jnp.dot(mixed_homologs, output_matrix, preferred_element_type=jnp.float32)
    ).astype(jnp.bfloat16)
    part_key = jnp.dot(
        normed_rows.T, d_keys.reshape(rows, embed_span), preferred_element_type=jnp.float32
    )
    part_value = jnp.dot(
        normed_rows.T, d_values.reshape(rows, embed_span), preferred_element_type=jnp.float32
    )
    d_normed = jnp.dot(d_query, query_weight.T, preferred_element_type=jnp.float32)
    d_normed = d_normed + jnp.dot(d_keys, key_weight.T, preferred_element_type=jnp.float32)
    d_normed = d_normed + jnp.dot(d_values, value_weight.T, preferred_element_type=jnp.float32)
    part_gain = jnp.sum((d_normed * standardized_entries).reshape(rows, embed_span), axis=0)
    unit_gradient = d_normed * rescale_factor
    alignment_gradient = upstream_adjoint.astype(jnp.float32) + reciprocal_spread * (
        unit_gradient
        - jnp.mean(unit_gradient, axis=-1, keepdims=True)
        - standardized_entries
        * jnp.mean(unit_gradient * standardized_entries, axis=-1, keepdims=True)
    )
    query_gradient, key_gradient, value_gradient, output_gradient, gain_gradient = (
        lax.psum_scatter(part_query, axes, scatter_dimension=0, tiled=True),
        lax.psum_scatter(part_key, axes, scatter_dimension=0, tiled=True),
        lax.psum_scatter(part_value, axes, scatter_dimension=0, tiled=True),
        lax.psum_scatter(part_out, axes, scatter_dimension=0, tiled=True),
        lax.psum_scatter(part_gain, axes, scatter_dimension=0, tiled=True),
    )
    return (
        final_result,
        alignment_gradient.astype(jnp.bfloat16),
        query_gradient,
        key_gradient,
        value_gradient,
        output_gradient,
        gain_gradient,
    )


F32, BF16 = jnp.float32, jnp.bfloat16
SCALE = HEAD_DIM ** (-0.5)


def swap(value, axis, size, bits):
    return lax.ppermute(value, axis, [(i, i ^ bits) for i in range(size)])


def dot(a, b, contract=(1, 0)):
    return lax.dot_general(
        a, b, (((contract[0],), (contract[1],)), ((), ())), preferred_element_type=F32
    )


def unit_rows(x):
    x = x.astype(F32)
    centered = x - jnp.mean(x, axis=-1, keepdims=True)
    inverse = lax.rsqrt(jnp.mean(centered * centered, axis=-1, keepdims=True) + 1e-05)
    return centered * inverse, inverse


def head_masks(span):
    lane = lax.broadcasted_iota(jnp.int32, (8, span), 1)
    return [
        ((lane >= at) & (lane < at + HEAD_DIM)).astype(F32)[0:1].astype(BF16)
        for at in range(0, span, HEAD_DIM)
    ]


def fetch(pairs, sems):
    copies = [pltpu.make_async_copy(src, dst, sems.at[i]) for i, (src, dst) in enumerate(pairs)]
    for copy in copies:
        copy.start()
    return copies


class Sender:
    def __init__(self, sems):
        self.sems, self.copies = sems, []

    def send(self, src, dst):
        copy = pltpu.make_async_copy(src, dst, self.sems.at[len(self.copies)])
        copy.start()
        self.copies.append(copy)

    def finish(self):
        for copy in self.copies:
            copy.wait()


def pack_kernel(dims, w_query, w_key, w_value, w_out, out, out_cut):
    depth, zs, shard, block, span = dims
    for d in range(depth):
        lanes = slice(d * span, (d + 1) * span)
        for i, w in enumerate((w_query, w_key, w_value)):
            out[d, :, i * span : (i + 1) * span] = w[:, lanes]
        out_cut[d] = w_out[:, lanes]


def norm_kernel(dims, *refs):
    depth, zs, shard, block, span = dims
    gain, xs_h, refs = refs[0], refs[1 : 1 + depth], refs[1 + depth :]
    normed_h, normed_t_h, xs, normed, normed_t, in_sems, out_sems = refs
    copies = fetch([(xs_h[j], xs.at[j]) for j in range(depth)], in_sems)
    sender = Sender(out_sems)
    for j in range(depth):
        copies[j].wait()
        unit, _ = unit_rows(xs[j])
        rows = pl.ds(j * block, block)
        wide = unit * gain[...]
        normed[rows, :] = wide.astype(BF16)
        sender.send(normed.at[rows], normed_h.at[rows])
        normed_t[:, rows] = jnp.transpose(wide).astype(BF16)
        sender.send(normed_t.at[:, rows], normed_t_h.at[:, rows])
    sender.finish()


def forward_kernel(dims, *refs):
    depth, zs, shard, block, span = dims
    heads = span // HEAD_DIM
    pos, w_near, w_far, normed_h = refs[:4]
    query_h, keys_h, values_h, keys_t_h, att_t_h, lse_h, wq_h, wk_h, wv_h, w_out_h = refs[4:14]
    outs_h, refs = refs[14 : 14 + depth], refs[14 + depth :]
    normed, query, keys, values, keys_t, values_t, att_t, lse = refs[:8]
    wq, wk, wv, w_out, outs, in_sems, out_sems = refs[8:]
    copies = fetch([(normed_h, normed)], in_sems)
    sender = Sender(out_sems)

    own_z, first = pos[0], pos[1] == 0
    for z in range(zs):
        for d in range(depth):
            near, far = w_near[z ^ own_z, d].astype(F32), w_far[z ^ own_z, d].astype(F32)
            both = jnp.concatenate(
                [jnp.where(first, near, far), jnp.where(first, far, near)], axis=0
            ).astype(BF16)
            rows = slice((d * zs + z) * 2 * shard, (d * zs + z + 1) * 2 * shard)
            for i, w in enumerate((wq, wk, wv)):
                w[rows, :] = both[:, i * span : (i + 1) * span]
            rows = slice(z * 2 * shard, (z + 1) * 2 * shard)
            w_out[rows, d * span : (d + 1) * span] = both[:, 3 * span :]
    for src, dst in ((wq, wq_h), (wk, wk_h), (wv, wv_h), (w_out, w_out_h)):
        sender.send(src, dst)
    copies[0].wait()

    query[...] = (SCALE * dot(normed[...], wq[...])).astype(BF16)
    key = dot(normed[...], wk[...])
    keys[...] = key.astype(BF16)
    keys_t[...] = jnp.transpose(key).astype(BF16)
    value = dot(normed[...], wv[...])
    values[...] = value.astype(BF16)
    values_t[...] = jnp.transpose(value).astype(BF16)
    for src, dst in ((query, query_h), (keys, keys_h), (values, values_h), (keys_t, keys_t_h)):
        sender.send(src, dst)

    masks = head_masks(span)

    def step(j, _):
        cols = pl.ds(pl.multiple_of(j * block, block), block)
        q_block = query[cols, :]

        def score(h):
            return dot(keys[...], q_block * masks[h], (1, 1))

        ready = [score(h) for h in range(min(2, heads))]
        for h in range(heads):
            scores = ready[h]
            top = jnp.max(scores, axis=0, keepdims=True)
            e = jnp.exp(scores - top)
            total = jnp.sum(e, axis=0, keepdims=True)
            if h + 2 < heads:
                ready.append(score(h + 2))
            lanes = slice(h * HEAD_DIM, (h + 1) * HEAD_DIM)
            att_t[lanes, cols] = dot(values_t[lanes, :], e.astype(BF16)) * (1.0 / total)
            lse[h, :, cols] = top + jnp.log(total)
        return 0

    lax.fori_loop(0, depth, step, 0)
    sender.send(att_t, att_t_h)
    sender.send(lse, lse_h)
    att = jnp.transpose(att_t[...]).astype(BF16)
    for j in range(depth):
        outs[j] = dot(att[j * block : (j + 1) * block], w_out[...]).astype(BF16)
        sender.send(outs.at[j], outs_h[j])
    sender.finish()


def backward_kernel(dims, *refs):
    depth, zs, shard, block, span = dims
    heads = span // HEAD_DIM
    pos, gain = refs[:2]
    gs_h, refs = refs[2 : 2 + depth], refs[2 + depth :]
    (w_out_h, query_h, keys_h, values_h, keys_t_h, lse_h, normed_t_h, att_t_h) = refs[:8]
    (wq_h, wk_h, wv_h, near, far), refs = refs[8:13], refs[13:]
    dns_h, refs = refs[:depth], refs[depth:]
    (gs, w_out, query, keys, values, keys_t, lse, normed_t, att_t, wq, wk, wv) = refs[:12]
    (d_att, delta, d_query_t, d_keys, d_values, grad_out, dns, in_sems, out_sems) = refs[12:]
    copies = fetch(
        [(w_out_h, w_out)]
        + [(gs_h[j], gs.at[pl.ds(j * block, block)]) for j in range(depth)]
        + [
            (att_t_h, att_t),
            (keys_h, keys),
            (query_h, query),
            (values_h, values),
            (lse_h, lse),
            (keys_t_h, keys_t),
            (normed_t_h, normed_t),
            (wq_h, wq),
            (wk_h, wk),
            (wv_h, wv),
        ],
        in_sems,
    )
    ready, later = 7 + depth, copies[7 + depth :]

    d_keys[...] = jnp.zeros_like(d_keys)
    d_values[...] = jnp.zeros_like(d_values)
    for copy in copies[: 2 + depth]:
        copy.wait()
    part = dot(gs[...], w_out[...], (1, 1)).astype(BF16)
    d_att[...] = part
    product = jnp.transpose(part.astype(F32)) * att_t[...]
    for h in range(heads):
        delta[h] = jnp.sum(product[h * HEAD_DIM : (h + 1) * HEAD_DIM], axis=0, keepdims=True)
    for copy in copies[2 + depth : ready]:
        copy.wait()
    masks = head_masks(span)

    def step(j, _):
        cols = pl.ds(pl.multiple_of(j * block, block), block)
        q_block, g_block = query[cols, :], d_att[cols, :]
        qs = [q_block * m for m in masks]
        ds = [g_block * m for m in masks]

        def pair(h):
            return dot(keys[...], qs[h], (1, 1)), dot(values[...], ds[h], (1, 1))

        pairs = [pair(h) for h in range(min(2, heads))]
        for h in range(heads):
            scores, d_probs = pairs[h]
            probs = jnp.exp(scores - lse[h, :, cols])
            d_scores = (probs * (d_probs - delta[h, :, cols])).astype(BF16)
            if h + 2 < heads:
                pairs.append(pair(h + 2))
            values_add = dot(probs.astype(BF16), ds[h])
            keys_add = dot(d_scores, qs[h])
            value_part = values_add if h == 0 else value_part + values_add
            key_part = keys_add if h == 0 else key_part + keys_add
            lanes = slice(h * HEAD_DIM, (h + 1) * HEAD_DIM)
            d_query_t[lanes, cols] = SCALE * dot(keys_t[lanes, :], d_scores)
        d_values[...] += value_part.astype(BF16).astype(F32)
        d_keys[...] += key_part.astype(BF16).astype(F32)
        return 0

    lax.fori_loop(0, depth, step, 0)
    for copy in later:
        copy.wait()
    d_query = jnp.transpose(d_query_t[...]).astype(BF16)
    d_key, d_value = d_keys[...].astype(BF16), d_values[...].astype(BF16)
    sender = Sender(out_sems)
    for j in range(depth):
        rows = slice(j * block, (j + 1) * block)
        d_normed = dot(d_query[rows], wq[...], (1, 1))
        d_normed = d_normed + dot(d_key[rows], wk[...], (1, 1))
        d_normed = d_normed + dot(d_value[rows], wv[...], (1, 1))
        dns[j] = d_normed.astype(BF16)
        sender.send(dns.at[j], dns_h[j])

    grad_out[...] = dot(att_t[...].astype(BF16), gs[...])
    grads = [dot(normed_t[...], d) for d in (d_query, d_key, d_value)]
    both = wq[...].astype(F32) * grads[0]
    both = both + wk[...].astype(F32) * grads[1] + wv[...].astype(F32) * grads[2]
    gain_rows = jnp.transpose(jnp.broadcast_to(gain[...], (128, gain.shape[1])))[:, :64]
    gain_column = jnp.sum(both, axis=1, keepdims=True) / gain_rows
    own_z, first, own_d = pos[0], pos[1] == 0, pos[2]
    for d in range(depth):
        for z in range(zs):
            sides = []
            for c in range(2):
                row, row_out = ((d * zs + z) * 2 + c) * shard, (z * 2 + c) * shard
                sides.append(
                    [g[row : row + shard] for g in grads]
                    + [
                        gain_column[row : row + shard],
                        grad_out[row_out : row_out + shard, d * span : (d + 1) * span],
                    ]
                )
            at = 0
            for one, two in zip(*sides):
                lanes = slice(at, at + one.shape[1])
                at += one.shape[1]
                near[z ^ own_z, d ^ own_d, :, lanes] = jnp.where(first, one, two).astype(BF16)
                far[z ^ own_z, d ^ own_d, :, lanes] = jnp.where(first, two, one).astype(BF16)
    sender.finish()


def align_kernel(dims, gain, x, upstream, *refs):
    dns, out = refs[:-1], refs[-1]
    d_normed = dns[0][...].astype(F32)
    for part in dns[1:]:
        d_normed = d_normed + part[...].astype(F32)
    unit, inverse = unit_rows(x[...])
    d_unit = d_normed * gain[...]
    out[...] = (
        upstream[...].astype(F32)
        + inverse
        * (
            d_unit
            - jnp.mean(d_unit, axis=-1, keepdims=True)
            - unit * jnp.mean(d_unit * unit, axis=-1, keepdims=True)
        )
    ).astype(BF16)


def finish_kernel(dims, pos, acc, *refs):
    depth, zs, shard, block, span = dims
    parts, outs = (None,) + refs[: depth - 1], refs[depth - 1 :]
    own_d = pos[2]
    lanes = 3 * span + 64
    gain_sum = None
    blocks = [acc[0][:, :lanes]] + [p[...].astype(F32) for p in parts[1:]]
    for d in range(depth):
        total = blocks[0]
        for k in range(1, depth):
            total = jnp.where((d ^ own_d) == k, blocks[k], total)
        for i in range(3):
            outs[i][:, d * span : (d + 1) * span] = total[:, i * span : (i + 1) * span]
        outs[3][:, d * span : (d + 1) * span] = acc[d ^ own_d][:, lanes:]
        gain = total[:, 3 * span : 3 * span + 1]
        gain_sum = gain if gain_sum is None else gain_sum + gain
    wide = jnp.concatenate([gain_sum, jnp.zeros((128 - shard, 1), F32)], axis=0)
    outs[4][...] = jnp.transpose(jnp.broadcast_to(wide, (128, 128)))[0:1, :shard]


VMEM, ANY, SMEM = pltpu.VMEM, pl.ANY, pltpu.SMEM


def call(kernel, dims, ins, outs, scratch, sems, flops, mib=56):
    args = [a for a, _ in ins]
    shapes = [jax.ShapeDtypeStruct(shape, kind) for shape, kind, _ in outs]
    size = sum(a.size * a.dtype.itemsize for a in args + shapes)
    return pl.pallas_call(
        functools.partial(kernel, dims),
        out_shape=shapes,
        in_specs=[pl.BlockSpec(memory_space=space) for _, space in ins],
        out_specs=[pl.BlockSpec(memory_space=space) for _, _, space in outs],
        scratch_shapes=[pltpu.VMEM(shape, kind) for shape, kind in scratch]
        + [pltpu.SemaphoreType.DMA((n,)) for n in sems],
        compiler_params=pltpu.CompilerParams(vmem_limit_bytes=mib * 1024 * 1024),
        cost_estimate=pl.CostEstimate(flops=flops, bytes_accessed=size, transcendentals=0),
    )(*args)


def head_body(depth, res, *args):
    x, gain, w_query, w_key, w_value, w_out, upstream = args
    homologs, _, width = x.shape
    span, zs = width // depth, res // 2
    shard = w_query.shape[0]
    total, heads = homologs * depth, span // HEAD_DIM
    dims = (depth, zs, shard, homologs, span)
    x = x.reshape(homologs, width)
    upstream = upstream.reshape(homologs, width)
    gain = gain.reshape(1, width)
    pos = jnp.stack([lax.axis_index(a) for a in ("z", "core", "depth")]).astype(jnp.int32)

    xs = [x] + [swap(x, "depth", depth, k) for k in range(1, depth)]

    packed, out_cut = call(
        pack_kernel,
        dims,
        [(w, VMEM) for w in (w_query, w_key, w_value, w_out)],
        [((depth, shard, 3 * span), BF16, VMEM), ((depth, shard, span), BF16, VMEM)],
        [],
        [],
        1000,
    )
    mine = lax.all_to_all(packed, "depth", 0, 0, tiled=True)
    mine = jnp.concatenate([mine, out_cut], axis=2)
    parts = [mine] + [swap(mine, "z", zs, k) for k in range(1, zs)]
    gs = [upstream] + [swap(upstream, "depth", depth, k) for k in range(1, depth)]

    rows, turned = ((total, span), BF16), ((span, total), BF16)
    block = ((homologs, width), BF16)
    blocks = ((depth, homologs, width), BF16)
    norm, stats = ((total, width), BF16), ((heads, 1, total), F32)
    in_weights, out_weights = ((width, span), BF16), ((span, width), BF16)
    pass_flops = 2 * total * total * span
    normed, normed_t = call(
        norm_kernel,
        dims,
        [(gain, VMEM)] + [(a, ANY) for a in xs],
        [norm + (ANY,), ((width, total), BF16, ANY)],
        [blocks, norm, ((width, total), BF16)],
        [depth, 2 * depth],
        1000,
    )
    normed, pos, *parts = lax.optimization_barrier([normed, pos] + parts)
    w_near = jnp.stack(parts, axis=0)
    w_far = swap(w_near, "core", 2, 1)

    turned_f32 = ((span, total), F32)
    saved = [rows, rows, rows, turned, turned_f32, stats] + [in_weights] * 3 + [out_weights]
    query, keys, values, keys_t, att_t, lse, wq, wk, wv, wo, *outs = call(
        forward_kernel,
        dims,
        [(pos, SMEM), (w_near, VMEM), (w_far, VMEM), (normed, ANY)],
        [s + (ANY,) for s in saved + [block] * depth],
        [norm, rows, rows, rows, turned, turned, turned_f32, stats]
        + [in_weights] * 3
        + [out_weights, blocks],
        [1, len(saved) + depth],
        8 * pass_flops,
    )

    packed = (zs, depth, shard, 4 * span + 64)
    near, far, *dns = call(
        backward_kernel,
        dims,
        [(pos, SMEM), (gain, VMEM)]
        + [(a, ANY) for a in gs + [wo, query, keys, values, keys_t, lse, normed_t]]
        + [(a, ANY) for a in (att_t, wq, wk, wv)],
        [(packed, BF16, VMEM)] * 2 + [block + (ANY,)] * depth,
        [norm, out_weights, rows, rows, rows, turned, stats, ((width, total), BF16)]
        + [turned_f32, in_weights, in_weights, in_weights]
        + [rows, stats, turned_f32]
        + [((total, span), F32)] * 2
        + [((span, width), F32), blocks],
        [depth + 11, depth],
        24 * pass_flops,
    )

    outs = [outs[0]] + [swap(outs[k], "depth", depth, k) for k in range(1, depth)]
    near, far, *rest = lax.optimization_barrier([near, far] + dns + outs)
    dns, outs = rest[:depth], rest[depth:]

    far = swap(far, "core", 2, 1)
    dns = [dns[0]] + [swap(dns[k], "depth", depth, k) for k in range(1, depth)]
    near = near.astype(F32) + far.astype(F32)
    low = [swap(near[k].astype(BF16), "z", zs, k) for k in range(1, zs)]
    middle = len(low) // 2
    low[middle], *rest = lax.optimization_barrier([low[middle]] + dns + outs)
    dns, outs = rest[:depth], rest[depth:]
    final_result = (x.astype(F32) + sum(o.astype(F32) for o in outs)).astype(BF16)
    acc = near[0] + sum(p.astype(F32) for p in low)
    parts = [
        swap(acc[k, :, : 3 * span + 64].astype(BF16), "depth", depth, k) for k in range(1, depth)
    ]
    alignment = call(
        align_kernel,
        dims,
        [(a, VMEM) for a in [gain, x, upstream] + dns],
        [block + (VMEM,)],
        [],
        [],
        1000 * total * width,
        16,
    )[0]
    alignment, *parts = lax.optimization_barrier([alignment] + parts)
    grad_query, grad_key, grad_value, grad_out, gain_rows = call(
        finish_kernel,
        dims,
        [(pos, SMEM), (acc, VMEM)] + [(p, VMEM) for p in parts],
        [((shard, width), F32, VMEM)] * 4 + [((1, shard), F32, VMEM)],
        [],
        [],
        1000,
        16,
    )
    return (
        final_result.reshape(homologs, 1, width),
        alignment.reshape(homologs, 1, width),
        grad_query,
        grad_key,
        grad_value,
        grad_out,
        gain_rows.reshape(shard),
    )


def solution(mesh):
    depth, res = mesh.shape["depth"], mesh.shape["res"]
    powers = depth & (depth - 1) == 0 and res & (res - 1) == 0 and res > 1
    if powers and depth == 4 and res >= 4 and HEADS % depth == 0:
        axes = ("depth", "z", "core")
        mesh = Mesh(mesh.devices.reshape(depth, res // 2, 2), axes)
        res_axes, run = ("z", "core"), functools.partial(head_body, depth, res)
    else:
        axes = ("depth", "res")
        res_axes, run = ("res",), general_body

    def body(*args):
        if args[0].shape[1] != 1:
            return general_body(*args, axes=axes)
        return run(*args)

    rows = P("depth", res_axes, None)
    weight = P(axes, None)
    return jax.shard_map(
        body,
        mesh=mesh,
        in_specs=(rows, P(), weight, weight, weight, weight, rows),
        out_specs=(rows, rows, weight, weight, weight, weight, P(axes)),
        check_vma=False,
    )
```

```python
import functools

import jax
import jax.numpy as jnp
from jax import lax
from jax.experimental import pallas as pl
from jax.experimental.pallas import tpu as pltpu
from jax.sharding import Mesh, PartitionSpec as P

HEADS = 12
HEAD_DIM = 64


def standardize_entries(family_activity, rescale_factor):
    payload_entries = family_activity.astype(jnp.float32)
    centered = payload_entries - jnp.mean(payload_entries, axis=-1, keepdims=True)
    reciprocal_spread = lax.rsqrt(jnp.mean(centered * centered, axis=-1, keepdims=True) + 1e-05)
    standardized_entries = centered * reciprocal_spread
    return (
        (standardized_entries * rescale_factor).astype(jnp.bfloat16),
        standardized_entries,
        reciprocal_spread,
    )


def project(rows, weight, factor):
    return (factor * jnp.dot(rows, weight, preferred_element_type=jnp.float32)).astype(jnp.bfloat16)


def to_heads(array):
    count, cols = (array.shape[0], array.shape[1])
    return jnp.transpose(array.reshape(count, cols, HEADS, HEAD_DIM), (1, 2, 0, 3)).reshape(
        cols * HEADS, count, HEAD_DIM
    )


def from_heads(array, cols):
    count = array.shape[1]
    return jnp.transpose(array.reshape(cols, HEADS, count, HEAD_DIM), (2, 0, 1, 3)).reshape(
        count, cols, HEADS * HEAD_DIM
    )


def head_pass(query, keys, payload_entries, d_att):
    scale = HEAD_DIM ** (-0.5)
    scores = jnp.dot(query, keys.T, preferred_element_type=jnp.float32)
    probs = jax.nn.softmax(scores, axis=-1)
    probs_b = probs.astype(jnp.bfloat16)
    mixed_homologs = jnp.dot(probs_b, payload_entries, preferred_element_type=jnp.float32).astype(
        jnp.bfloat16
    )
    d_probs = jnp.dot(d_att, payload_entries.T, preferred_element_type=jnp.float32)
    d_scores = probs * (d_probs - jnp.sum(probs * d_probs, axis=-1, keepdims=True))
    d_scores_b = d_scores.astype(jnp.bfloat16)
    d_query = (scale * jnp.dot(d_scores_b, keys, preferred_element_type=jnp.float32)).astype(
        jnp.bfloat16
    )
    key_part = jnp.einsum("st,sd->td", d_scores_b, query, preferred_element_type=jnp.float32)
    value_part = jnp.einsum("st,sd->td", probs_b, d_att, preferred_element_type=jnp.float32)
    return (mixed_homologs, d_query, key_part, value_part)


def general_body(
    family_activity,
    rescale_factor,
    asking_weights,
    lookup_weights,
    payload_weights,
    exit_weights,
    upstream_adjoint,
    axes=("depth", "res"),
):
    query_weight, key_weight, value_weight, output_matrix = (
        lax.all_gather(asking_weights, axes, axis=0, tiled=True),
        lax.all_gather(lookup_weights, axes, axis=0, tiled=True),
        lax.all_gather(payload_weights, axes, axis=0, tiled=True),
        lax.all_gather(exit_weights, axes, axis=0, tiled=True),
    )
    homologs_each_shard, positions_each_shard, embed_span = family_activity.shape
    standardized_source, standardized_entries, reciprocal_spread = standardize_entries(
        family_activity, rescale_factor
    )
    query = project(standardized_source, query_weight, HEAD_DIM ** (-0.5))
    keys = project(standardized_source, key_weight, 1.0)
    payload_entries = project(standardized_source, value_weight, 1.0)
    keys_all, values_all = (
        lax.all_gather(keys, "depth", axis=0, tiled=True),
        lax.all_gather(payload_entries, "depth", axis=0, tiled=True),
    )
    d_att = jnp.dot(upstream_adjoint, output_matrix.T, preferred_element_type=jnp.float32).astype(
        jnp.bfloat16
    )

    def per_head(items):
        return head_pass(items[0], items[1], items[2], items[3])

    mixed_homologs, d_query, key_part, value_part = lax.map(
        per_head, (to_heads(query), to_heads(keys_all), to_heads(values_all), to_heads(d_att))
    )
    mixed_homologs = from_heads(mixed_homologs, positions_each_shard)
    d_query = from_heads(d_query, positions_each_shard)
    key_part = from_heads(key_part, positions_each_shard)
    value_part = from_heads(value_part, positions_each_shard)
    rows = homologs_each_shard * positions_each_shard
    normed_rows = standardized_source.reshape(rows, embed_span)
    part_query = jnp.dot(
        normed_rows.T, d_query.reshape(rows, embed_span), preferred_element_type=jnp.float32
    )
    part_out = jnp.dot(
        mixed_homologs.reshape(rows, embed_span).T,
        upstream_adjoint.reshape(rows, embed_span),
        preferred_element_type=jnp.float32,
    )
    stacked = jnp.stack([key_part, value_part], axis=2).astype(jnp.bfloat16)
    summed = (
        lax.psum_scatter(stacked, "depth", scatter_dimension=0, tiled=True)
        .astype(jnp.float32)
        .astype(jnp.bfloat16)
    )
    d_keys = summed[:, :, 0, :]
    d_values = summed[:, :, 1, :]
    final_result = (
        family_activity.astype(jnp.float32)
        + jnp.dot(mixed_homologs, output_matrix, preferred_element_type=jnp.float32)
    ).astype(jnp.bfloat16)
    part_key = jnp.dot(
        normed_rows.T, d_keys.reshape(rows, embed_span), preferred_element_type=jnp.float32
    )
    part_value = jnp.dot(
        normed_rows.T, d_values.reshape(rows, embed_span), preferred_element_type=jnp.float32
    )
    d_normed = jnp.dot(d_query, query_weight.T, preferred_element_type=jnp.float32)
    d_normed = d_normed + jnp.dot(d_keys, key_weight.T, preferred_element_type=jnp.float32)
    d_normed = d_normed + jnp.dot(d_values, value_weight.T, preferred_element_type=jnp.float32)
    part_gain = jnp.sum((d_normed * standardized_entries).reshape(rows, embed_span), axis=0)
    unit_gradient = d_normed * rescale_factor
    alignment_gradient = upstream_adjoint.astype(jnp.float32) + reciprocal_spread * (
        unit_gradient
        - jnp.mean(unit_gradient, axis=-1, keepdims=True)
        - standardized_entries
        * jnp.mean(unit_gradient * standardized_entries, axis=-1, keepdims=True)
    )
    query_gradient, key_gradient, value_gradient, output_gradient, gain_gradient = (
        lax.psum_scatter(part_query, axes, scatter_dimension=0, tiled=True),
        lax.psum_scatter(part_key, axes, scatter_dimension=0, tiled=True),
        lax.psum_scatter(part_value, axes, scatter_dimension=0, tiled=True),
        lax.psum_scatter(part_out, axes, scatter_dimension=0, tiled=True),
        lax.psum_scatter(part_gain, axes, scatter_dimension=0, tiled=True),
    )
    return (
        final_result,
        alignment_gradient.astype(jnp.bfloat16),
        query_gradient,
        key_gradient,
        value_gradient,
        output_gradient,
        gain_gradient,
    )


F32, BF16 = jnp.float32, jnp.bfloat16
SCALE = HEAD_DIM ** (-0.5)


def swap(value, axis, size, bits):
    return lax.ppermute(value, axis, [(i, i ^ bits) for i in range(size)])


def dot(a, b, contract=(1, 0)):
    return lax.dot_general(
        a, b, (((contract[0],), (contract[1],)), ((), ())), preferred_element_type=F32
    )


def unit_rows(x):
    x = x.astype(F32)
    centered = x - jnp.mean(x, axis=-1, keepdims=True)
    inverse = lax.rsqrt(jnp.mean(centered * centered, axis=-1, keepdims=True) + 1e-05)
    return centered * inverse, inverse


def head_masks(span):
    lane = lax.broadcasted_iota(jnp.int32, (8, span), 1)
    return [
        ((lane >= at) & (lane < at + HEAD_DIM)).astype(F32)[0:1].astype(BF16)
        for at in range(0, span, HEAD_DIM)
    ]


def fetch(pairs, sems):
    copies = [pltpu.make_async_copy(src, dst, sems.at[i]) for i, (src, dst) in enumerate(pairs)]
    for copy in copies:
        copy.start()
    return copies


class Sender:
    def __init__(self, sems):
        self.sems, self.copies = sems, []

    def send(self, src, dst):
        copy = pltpu.make_async_copy(src, dst, self.sems.at[len(self.copies)])
        copy.start()
        self.copies.append(copy)

    def finish(self):
        for copy in self.copies:
            copy.wait()


def pack_kernel(dims, w_query, w_key, w_value, w_out, out, out_cut):
    depth, zs, shard, block, span = dims
    for d in range(depth):
        lanes = slice(d * span, (d + 1) * span)
        for i, w in enumerate((w_query, w_key, w_value)):
            out[d, :, i * span : (i + 1) * span] = w[:, lanes]
        out_cut[d] = w_out[:, lanes]


def norm_kernel(dims, *refs):
    depth, zs, shard, block, span = dims
    gain, xs_h, refs = refs[0], refs[1 : 1 + depth], refs[1 + depth :]
    normed_h, normed_t_h, xs, normed, normed_t, in_sems, out_sems = refs
    copies = fetch([(xs_h[j], xs.at[j]) for j in range(depth)], in_sems)
    sender = Sender(out_sems)
    for j in range(depth):
        copies[j].wait()
        unit, _ = unit_rows(xs[j])
        rows = pl.ds(j * block, block)
        wide = unit * gain[...]
        normed[rows, :] = wide.astype(BF16)
        sender.send(normed.at[rows], normed_h.at[rows])
        normed_t[:, rows] = jnp.transpose(wide).astype(BF16)
        sender.send(normed_t.at[:, rows], normed_t_h.at[:, rows])
    sender.finish()


def forward_kernel(dims, *refs):
    depth, zs, shard, block, span = dims
    heads = span // HEAD_DIM
    pos, w_near, w_far, normed_h = refs[:4]
    query_h, keys_h, values_h, keys_t_h, att_t_h, lse_h, wq_h, wk_h, wv_h, w_out_h = refs[4:14]
    outs_h, refs = refs[14 : 14 + depth], refs[14 + depth :]
    normed, query, keys, values, keys_t, values_t, att_t, lse = refs[:8]
    wq, wk, wv, w_out, outs, in_sems, out_sems = refs[8:]
    copies = fetch([(normed_h, normed)], in_sems)
    sender = Sender(out_sems)

    own_z, first = pos[0], pos[1] == 0
    for z in range(zs):
        for d in range(depth):
            near, far = w_near[z ^ own_z, d].astype(F32), w_far[z ^ own_z, d].astype(F32)
            both = jnp.concatenate(
                [jnp.where(first, near, far), jnp.where(first, far, near)], axis=0
            ).astype(BF16)
            rows = slice((d * zs + z) * 2 * shard, (d * zs + z + 1) * 2 * shard)
            for i, w in enumerate((wq, wk, wv)):
                w[rows, :] = both[:, i * span : (i + 1) * span]
            rows = slice(z * 2 * shard, (z + 1) * 2 * shard)
            w_out[rows, d * span : (d + 1) * span] = both[:, 3 * span :]
    for src, dst in ((wq, wq_h), (wk, wk_h), (wv, wv_h), (w_out, w_out_h)):
        sender.send(src, dst)
    copies[0].wait()

    query[...] = (SCALE * dot(normed[...], wq[...])).astype(BF16)
    key = dot(normed[...], wk[...])
    keys[...] = key.astype(BF16)
    keys_t[...] = jnp.transpose(key).astype(BF16)
    value = dot(normed[...], wv[...])
    values[...] = value.astype(BF16)
    values_t[...] = jnp.transpose(value).astype(BF16)
    for src, dst in ((query, query_h), (keys, keys_h), (values, values_h), (keys_t, keys_t_h)):
        sender.send(src, dst)

    masks = head_masks(span)

    units = [(j, h) for j in range(depth) for h in range(heads)]

    def score(j, h):
        return dot(keys[...], query[j * block : (j + 1) * block, :] * masks[h], (1, 1))

    ready = [score(*unit) for unit in units[:2]]
    for i, (j, h) in enumerate(units):
        cols, lanes = slice(j * block, (j + 1) * block), slice(h * HEAD_DIM, (h + 1) * HEAD_DIM)
        scores = ready.pop(0)
        top = jnp.max(scores, axis=0, keepdims=True)
        e = jnp.exp(scores - top)
        total = jnp.sum(e, axis=0, keepdims=True)
        if i + 2 < len(units):
            ready.append(score(*units[i + 2]))
        att_t[lanes, cols] = dot(values_t[lanes, :], e.astype(BF16)) * (1.0 / total)
        lse[h, :, cols] = top + jnp.log(total)
    sender.send(att_t, att_t_h)
    sender.send(lse, lse_h)
    att = jnp.transpose(att_t[...]).astype(BF16)
    for j in range(depth):
        outs[j] = dot(att[j * block : (j + 1) * block], w_out[...]).astype(BF16)
        sender.send(outs.at[j], outs_h[j])
    sender.finish()


def backward_kernel(dims, *refs):
    depth, zs, shard, block, span = dims
    heads = span // HEAD_DIM
    pos, gain = refs[:2]
    gs_h, refs = refs[2 : 2 + depth], refs[2 + depth :]
    (w_out_h, query_h, keys_h, values_h, keys_t_h, lse_h, normed_t_h, att_t_h) = refs[:8]
    (wq_h, wk_h, wv_h, near, far), refs = refs[8:13], refs[13:]
    dns_h, refs = refs[:depth], refs[depth:]
    (gs, w_out, query, keys, values, keys_t, lse, normed_t, att_t, wq, wk, wv) = refs[:12]
    (d_att, delta, d_query_t, d_keys, d_values, grad_out, dns, in_sems, out_sems) = refs[12:]
    copies = fetch(
        [(w_out_h, w_out)]
        + [(gs_h[j], gs.at[pl.ds(j * block, block)]) for j in range(depth)]
        + [
            (att_t_h, att_t),
            (keys_h, keys),
            (query_h, query),
            (values_h, values),
            (lse_h, lse),
            (keys_t_h, keys_t),
            (normed_t_h, normed_t),
            (wq_h, wq),
            (wk_h, wk),
            (wv_h, wv),
        ],
        in_sems,
    )
    loaded, later = 7 + depth, copies[7 + depth :]

    d_keys[...] = jnp.zeros_like(d_keys)
    d_values[...] = jnp.zeros_like(d_values)
    for copy in copies[: 2 + depth]:
        copy.wait()
    part = dot(gs[...], w_out[...], (1, 1)).astype(BF16)
    d_att[...] = part
    product = jnp.transpose(part.astype(F32)) * att_t[...]
    for h in range(heads):
        delta[h] = jnp.sum(product[h * HEAD_DIM : (h + 1) * HEAD_DIM], axis=0, keepdims=True)
    for copy in copies[2 + depth : loaded]:
        copy.wait()
    masks = head_masks(span)

    units = [(j, h) for j in range(depth) for h in range(heads)]

    def pair(j, h):
        rows = slice(j * block, (j + 1) * block)
        q_head, g_head = query[rows, :] * masks[h], d_att[rows, :] * masks[h]
        scores, d_probs = dot(keys[...], q_head, (1, 1)), dot(values[...], g_head, (1, 1))
        return q_head, g_head, scores, d_probs

    ready = [pair(*unit) for unit in units[:2]]
    for i, (j, h) in enumerate(units):
        cols, lanes = slice(j * block, (j + 1) * block), slice(h * HEAD_DIM, (h + 1) * HEAD_DIM)
        q_head, g_head, scores, d_probs = ready.pop(0)
        probs = jnp.exp(scores - lse[h, :, cols])
        d_scores = (probs * (d_probs - delta[h, :, cols])).astype(BF16)
        if i + 2 < len(units):
            ready.append(pair(*units[i + 2]))
        values_add = dot(probs.astype(BF16), g_head)
        keys_add = dot(d_scores, q_head)
        value_part = values_add if h == 0 else value_part + values_add
        key_part = keys_add if h == 0 else key_part + keys_add
        d_query_t[lanes, cols] = SCALE * dot(keys_t[lanes, :], d_scores)
        if h == heads - 1:
            d_values[...] += value_part.astype(BF16).astype(F32)
            d_keys[...] += key_part.astype(BF16).astype(F32)
    for copy in later:
        copy.wait()
    d_query = jnp.transpose(d_query_t[...]).astype(BF16)
    d_key, d_value = d_keys[...].astype(BF16), d_values[...].astype(BF16)
    sender = Sender(out_sems)
    for j in range(depth):
        rows = slice(j * block, (j + 1) * block)
        d_normed = dot(d_query[rows], wq[...], (1, 1))
        d_normed = d_normed + dot(d_key[rows], wk[...], (1, 1))
        d_normed = d_normed + dot(d_value[rows], wv[...], (1, 1))
        dns[j] = d_normed.astype(BF16)
        sender.send(dns.at[j], dns_h[j])

    grad_out[...] = dot(att_t[...].astype(BF16), gs[...])
    grads = [dot(normed_t[...], d) for d in (d_query, d_key, d_value)]
    both = wq[...].astype(F32) * grads[0]
    both = both + wk[...].astype(F32) * grads[1] + wv[...].astype(F32) * grads[2]
    gain_rows = jnp.transpose(jnp.broadcast_to(gain[...], (128, gain.shape[1])))[:, :64]
    gain_column = jnp.sum(both, axis=1, keepdims=True) / gain_rows
    own_z, first, own_d = pos[0], pos[1] == 0, pos[2]
    for d in range(depth):
        for z in range(zs):
            sides = []
            for c in range(2):
                row, row_out = ((d * zs + z) * 2 + c) * shard, (z * 2 + c) * shard
                sides.append(
                    [g[row : row + shard] for g in grads]
                    + [
                        gain_column[row : row + shard],
                        grad_out[row_out : row_out + shard, d * span : (d + 1) * span],
                    ]
                )
            at = 0
            for one, two in zip(*sides):
                lanes = slice(at, at + one.shape[1])
                at += one.shape[1]
                near[z ^ own_z, d ^ own_d, :, lanes] = jnp.where(first, one, two).astype(BF16)
                far[z ^ own_z, d ^ own_d, :, lanes] = jnp.where(first, two, one).astype(BF16)
    sender.finish()


def align_kernel(dims, gain, x, upstream, *refs):
    dns, out = refs[:-1], refs[-1]
    d_normed = dns[0][...].astype(F32)
    for part in dns[1:]:
        d_normed = d_normed + part[...].astype(F32)
    unit, inverse = unit_rows(x[...])
    d_unit = d_normed * gain[...]
    out[...] = (
        upstream[...].astype(F32)
        + inverse
        * (
            d_unit
            - jnp.mean(d_unit, axis=-1, keepdims=True)
            - unit * jnp.mean(d_unit * unit, axis=-1, keepdims=True)
        )
    ).astype(BF16)


def finish_kernel(dims, pos, acc, *refs):
    depth, zs, shard, block, span = dims
    parts, outs = (None,) + refs[: depth - 1], refs[depth - 1 :]
    own_d = pos[2]
    lanes = 3 * span + 64
    gain_sum = None
    blocks = [acc[0][:, :lanes]] + [p[...].astype(F32) for p in parts[1:]]
    for d in range(depth):
        total = blocks[0]
        for k in range(1, depth):
            total = jnp.where((d ^ own_d) == k, blocks[k], total)
        for i in range(3):
            outs[i][:, d * span : (d + 1) * span] = total[:, i * span : (i + 1) * span]
        outs[3][:, d * span : (d + 1) * span] = acc[d ^ own_d][:, lanes:]
        gain = total[:, 3 * span : 3 * span + 1]
        gain_sum = gain if gain_sum is None else gain_sum + gain
    wide = jnp.concatenate([gain_sum, jnp.zeros((128 - shard, 1), F32)], axis=0)
    outs[4][...] = jnp.transpose(jnp.broadcast_to(wide, (128, 128)))[0:1, :shard]


VMEM, ANY, SMEM = pltpu.VMEM, pl.ANY, pltpu.SMEM


def call(kernel, dims, ins, outs, scratch, sems, flops, mib=56):
    args = [a for a, _ in ins]
    shapes = [jax.ShapeDtypeStruct(shape, kind) for shape, kind, _ in outs]
    size = sum(a.size * a.dtype.itemsize for a in args + shapes)
    return pl.pallas_call(
        functools.partial(kernel, dims),
        out_shape=shapes,
        in_specs=[pl.BlockSpec(memory_space=space) for _, space in ins],
        out_specs=[pl.BlockSpec(memory_space=space) for _, _, space in outs],
        scratch_shapes=[pltpu.VMEM(shape, kind) for shape, kind in scratch]
        + [pltpu.SemaphoreType.DMA((n,)) for n in sems],
        compiler_params=pltpu.CompilerParams(vmem_limit_bytes=mib * 1024 * 1024),
        cost_estimate=pl.CostEstimate(flops=flops, bytes_accessed=size, transcendentals=0),
    )(*args)


def head_body(depth, res, *args):
    x, gain, w_query, w_key, w_value, w_out, upstream = args
    homologs, _, width = x.shape
    span, zs = width // depth, res // 2
    shard = w_query.shape[0]
    total, heads = homologs * depth, span // HEAD_DIM
    dims = (depth, zs, shard, homologs, span)
    x = x.reshape(homologs, width)
    upstream = upstream.reshape(homologs, width)
    gain = gain.reshape(1, width)
    pos = jnp.stack([lax.axis_index(a) for a in ("z", "core", "depth")]).astype(jnp.int32)

    xs = [x] + [swap(x, "depth", depth, k) for k in range(1, depth - 1)]

    packed, out_cut = call(
        pack_kernel,
        dims,
        [(w, VMEM) for w in (w_query, w_key, w_value, w_out)],
        [((depth, shard, 3 * span), BF16, VMEM), ((depth, shard, span), BF16, VMEM)],
        [],
        [],
        1000,
    )
    mine = lax.all_to_all(packed, "depth", 0, 0, tiled=True)
    mine = jnp.concatenate([mine, out_cut], axis=2)
    mine, *xs = lax.optimization_barrier([mine] + xs)
    xs.append(swap(xs[0], "depth", depth, depth - 1))
    parts = [mine] + [swap(mine, "z", zs, k) for k in range(1, zs)]
    gs = [upstream] + [swap(upstream, "depth", depth, k) for k in range(1, depth)]

    rows, turned = ((total, span), BF16), ((span, total), BF16)
    block = ((homologs, width), BF16)
    blocks = ((depth, homologs, width), BF16)
    norm, stats = ((total, width), BF16), ((heads, 1, total), F32)
    in_weights, out_weights = ((width, span), BF16), ((span, width), BF16)
    pass_flops = 2 * total * total * span
    normed, normed_t = call(
        norm_kernel,
        dims,
        [(gain, VMEM)] + [(a, ANY) for a in xs],
        [norm + (ANY,), ((width, total), BF16, ANY)],
        [blocks, norm, ((width, total), BF16)],
        [depth, 2 * depth],
        1000,
    )
    normed, pos, *parts = lax.optimization_barrier([normed, pos] + parts)
    w_near = jnp.stack(parts, axis=0)
    w_far = swap(w_near, "core", 2, 1)

    turned_f32 = ((span, total), F32)
    saved = [rows, rows, rows, turned, turned_f32, stats] + [in_weights] * 3 + [out_weights]
    query, keys, values, keys_t, att_t, lse, wq, wk, wv, wo, *outs = call(
        forward_kernel,
        dims,
        [(pos, SMEM), (w_near, VMEM), (w_far, VMEM), (normed, ANY)],
        [s + (ANY,) for s in saved + [block] * depth],
        [norm, rows, rows, rows, turned, turned, turned_f32, stats]
        + [in_weights] * 3
        + [out_weights, blocks],
        [1, len(saved) + depth],
        8 * pass_flops,
    )

    packed = (zs, depth, shard, 4 * span + 64)
    near, far, *dns = call(
        backward_kernel,
        dims,
        [(pos, SMEM), (gain, VMEM)]
        + [(a, ANY) for a in gs + [wo, query, keys, values, keys_t, lse, normed_t]]
        + [(a, ANY) for a in (att_t, wq, wk, wv)],
        [(packed, BF16, VMEM)] * 2 + [block + (ANY,)] * depth,
        [norm, out_weights, rows, rows, rows, turned, stats, ((width, total), BF16)]
        + [turned_f32, in_weights, in_weights, in_weights]
        + [rows, stats, turned_f32]
        + [((total, span), F32)] * 2
        + [((span, width), F32), blocks],
        [depth + 11, depth],
        24 * pass_flops,
    )

    outs = [outs[0]] + [swap(outs[k], "depth", depth, k) for k in range(1, depth)]
    near, far, *rest = lax.optimization_barrier([near, far] + dns + outs)
    dns, outs = rest[:depth], rest[depth:]

    far = swap(far, "core", 2, 1)
    dns = [dns[0]] + [swap(dns[k], "depth", depth, k) for k in range(1, depth)]
    near = near.astype(F32) + far.astype(F32)
    low = [swap(near[k].astype(BF16), "z", zs, k) for k in range(1, zs)]
    low[1:], dns = lax.optimization_barrier((low[1:], dns))
    dns[2], outs = lax.optimization_barrier((dns[2], outs))
    final_result = (x.astype(F32) + sum(o.astype(F32) for o in outs)).astype(BF16)
    acc = near[0] + sum(p.astype(F32) for p in low)
    parts = [
        swap(acc[k, :, : 3 * span + 64].astype(BF16), "depth", depth, k) for k in range(1, depth)
    ]
    alignment = call(
        align_kernel,
        dims,
        [(a, VMEM) for a in [gain, x, upstream] + dns],
        [block + (VMEM,)],
        [],
        [],
        1000 * total * width,
        16,
    )[0]
    alignment, *parts = lax.optimization_barrier([alignment] + parts)
    grad_query, grad_key, grad_value, grad_out, gain_rows = call(
        finish_kernel,
        dims,
        [(pos, SMEM), (acc, VMEM)] + [(p, VMEM) for p in parts],
        [((shard, width), F32, VMEM)] * 4 + [((1, shard), F32, VMEM)],
        [],
        [],
        1000,
        16,
    )
    return (
        final_result.reshape(homologs, 1, width),
        alignment.reshape(homologs, 1, width),
        grad_query,
        grad_key,
        grad_value,
        grad_out,
        gain_rows.reshape(shard),
    )


def solution(mesh):
    depth, res = mesh.shape["depth"], mesh.shape["res"]
    powers = depth & (depth - 1) == 0 and res & (res - 1) == 0 and res > 1
    if powers and depth == 4 and res >= 4 and HEADS % depth == 0:
        axes = ("depth", "z", "core")
        mesh = Mesh(mesh.devices.reshape(depth, res // 2, 2), axes)
        res_axes, run = ("z", "core"), functools.partial(head_body, depth, res)
    else:
        axes = ("depth", "res")
        res_axes, run = ("res",), general_body

    def body(*args):
        if args[0].shape[1] != 1:
            return general_body(*args, axes=axes)
        return run(*args)

    rows = P("depth", res_axes, None)
    weight = P(axes, None)
    return jax.shard_map(
        body,
        mesh=mesh,
        in_specs=(rows, P(), weight, weight, weight, weight, rows),
        out_specs=(rows, rows, weight, weight, weight, weight, P(axes)),
        check_vma=False,
    )
```

```python
import functools

import jax
import jax.numpy as jnp
from jax import lax
from jax.experimental import pallas as pl
from jax.experimental.pallas import tpu as pltpu
from jax.sharding import Mesh, PartitionSpec as P

HEADS = 12
HEAD_DIM = 64


def standardize_entries(family_activity, rescale_factor):
    payload_entries = family_activity.astype(jnp.float32)
    centered = payload_entries - jnp.mean(payload_entries, axis=-1, keepdims=True)
    reciprocal_spread = lax.rsqrt(jnp.mean(centered * centered, axis=-1, keepdims=True) + 1e-05)
    standardized_entries = centered * reciprocal_spread
    return (
        (standardized_entries * rescale_factor).astype(jnp.bfloat16),
        standardized_entries,
        reciprocal_spread,
    )


def project(rows, weight, factor):
    return (factor * jnp.dot(rows, weight, preferred_element_type=jnp.float32)).astype(jnp.bfloat16)


def to_heads(array):
    count, cols = (array.shape[0], array.shape[1])
    return jnp.transpose(array.reshape(count, cols, HEADS, HEAD_DIM), (1, 2, 0, 3)).reshape(
        cols * HEADS, count, HEAD_DIM
    )


def from_heads(array, cols):
    count = array.shape[1]
    return jnp.transpose(array.reshape(cols, HEADS, count, HEAD_DIM), (2, 0, 1, 3)).reshape(
        count, cols, HEADS * HEAD_DIM
    )


def head_pass(query, keys, payload_entries, d_att):
    scale = HEAD_DIM ** (-0.5)
    scores = jnp.dot(query, keys.T, preferred_element_type=jnp.float32)
    probs = jax.nn.softmax(scores, axis=-1)
    probs_b = probs.astype(jnp.bfloat16)
    mixed_homologs = jnp.dot(probs_b, payload_entries, preferred_element_type=jnp.float32).astype(
        jnp.bfloat16
    )
    d_probs = jnp.dot(d_att, payload_entries.T, preferred_element_type=jnp.float32)
    d_scores = probs * (d_probs - jnp.sum(probs * d_probs, axis=-1, keepdims=True))
    d_scores_b = d_scores.astype(jnp.bfloat16)
    d_query = (scale * jnp.dot(d_scores_b, keys, preferred_element_type=jnp.float32)).astype(
        jnp.bfloat16
    )
    key_part = jnp.einsum("st,sd->td", d_scores_b, query, preferred_element_type=jnp.float32)
    value_part = jnp.einsum("st,sd->td", probs_b, d_att, preferred_element_type=jnp.float32)
    return (mixed_homologs, d_query, key_part, value_part)


def general_body(
    family_activity,
    rescale_factor,
    asking_weights,
    lookup_weights,
    payload_weights,
    exit_weights,
    upstream_adjoint,
    axes=("depth", "res"),
):
    query_weight, key_weight, value_weight, output_matrix = (
        lax.all_gather(asking_weights, axes, axis=0, tiled=True),
        lax.all_gather(lookup_weights, axes, axis=0, tiled=True),
        lax.all_gather(payload_weights, axes, axis=0, tiled=True),
        lax.all_gather(exit_weights, axes, axis=0, tiled=True),
    )
    homologs_each_shard, positions_each_shard, embed_span = family_activity.shape
    standardized_source, standardized_entries, reciprocal_spread = standardize_entries(
        family_activity, rescale_factor
    )
    query = project(standardized_source, query_weight, HEAD_DIM ** (-0.5))
    keys = project(standardized_source, key_weight, 1.0)
    payload_entries = project(standardized_source, value_weight, 1.0)
    keys_all, values_all = (
        lax.all_gather(keys, "depth", axis=0, tiled=True),
        lax.all_gather(payload_entries, "depth", axis=0, tiled=True),
    )
    d_att = jnp.dot(upstream_adjoint, output_matrix.T, preferred_element_type=jnp.float32).astype(
        jnp.bfloat16
    )

    def per_head(items):
        return head_pass(items[0], items[1], items[2], items[3])

    mixed_homologs, d_query, key_part, value_part = lax.map(
        per_head, (to_heads(query), to_heads(keys_all), to_heads(values_all), to_heads(d_att))
    )
    mixed_homologs = from_heads(mixed_homologs, positions_each_shard)
    d_query = from_heads(d_query, positions_each_shard)
    key_part = from_heads(key_part, positions_each_shard)
    value_part = from_heads(value_part, positions_each_shard)
    rows = homologs_each_shard * positions_each_shard
    normed_rows = standardized_source.reshape(rows, embed_span)
    part_query = jnp.dot(
        normed_rows.T, d_query.reshape(rows, embed_span), preferred_element_type=jnp.float32
    )
    part_out = jnp.dot(
        mixed_homologs.reshape(rows, embed_span).T,
        upstream_adjoint.reshape(rows, embed_span),
        preferred_element_type=jnp.float32,
    )
    stacked = jnp.stack([key_part, value_part], axis=2).astype(jnp.bfloat16)
    summed = (
        lax.psum_scatter(stacked, "depth", scatter_dimension=0, tiled=True)
        .astype(jnp.float32)
        .astype(jnp.bfloat16)
    )
    d_keys = summed[:, :, 0, :]
    d_values = summed[:, :, 1, :]
    final_result = (
        family_activity.astype(jnp.float32)
        + jnp.dot(mixed_homologs, output_matrix, preferred_element_type=jnp.float32)
    ).astype(jnp.bfloat16)
    part_key = jnp.dot(
        normed_rows.T, d_keys.reshape(rows, embed_span), preferred_element_type=jnp.float32
    )
    part_value = jnp.dot(
        normed_rows.T, d_values.reshape(rows, embed_span), preferred_element_type=jnp.float32
    )
    d_normed = jnp.dot(d_query, query_weight.T, preferred_element_type=jnp.float32)
    d_normed = d_normed + jnp.dot(d_keys, key_weight.T, preferred_element_type=jnp.float32)
    d_normed = d_normed + jnp.dot(d_values, value_weight.T, preferred_element_type=jnp.float32)
    part_gain = jnp.sum((d_normed * standardized_entries).reshape(rows, embed_span), axis=0)
    unit_gradient = d_normed * rescale_factor
    alignment_gradient = upstream_adjoint.astype(jnp.float32) + reciprocal_spread * (
        unit_gradient
        - jnp.mean(unit_gradient, axis=-1, keepdims=True)
        - standardized_entries
        * jnp.mean(unit_gradient * standardized_entries, axis=-1, keepdims=True)
    )
    query_gradient, key_gradient, value_gradient, output_gradient, gain_gradient = (
        lax.psum_scatter(part_query, axes, scatter_dimension=0, tiled=True),
        lax.psum_scatter(part_key, axes, scatter_dimension=0, tiled=True),
        lax.psum_scatter(part_value, axes, scatter_dimension=0, tiled=True),
        lax.psum_scatter(part_out, axes, scatter_dimension=0, tiled=True),
        lax.psum_scatter(part_gain, axes, scatter_dimension=0, tiled=True),
    )
    return (
        final_result,
        alignment_gradient.astype(jnp.bfloat16),
        query_gradient,
        key_gradient,
        value_gradient,
        output_gradient,
        gain_gradient,
    )


F32, BF16 = jnp.float32, jnp.bfloat16
SCALE = HEAD_DIM ** (-0.5)


def swap(value, axis, size, bits):
    return lax.ppermute(value, axis, [(i, i ^ bits) for i in range(size)])


def dot(a, b, contract=(1, 0)):
    return lax.dot_general(
        a, b, (((contract[0],), (contract[1],)), ((), ())), preferred_element_type=F32
    )


def unit_rows(x):
    x = x.astype(F32)
    centered = x - jnp.mean(x, axis=-1, keepdims=True)
    inverse = lax.rsqrt(jnp.mean(centered * centered, axis=-1, keepdims=True) + 1e-05)
    return centered * inverse, inverse


def head_masks(span):
    lane = lax.broadcasted_iota(jnp.int32, (8, span), 1)
    return [
        ((lane >= at) & (lane < at + HEAD_DIM)).astype(F32)[0:1].astype(BF16)
        for at in range(0, span, HEAD_DIM)
    ]


def fetch(pairs, sems):
    copies = [pltpu.make_async_copy(src, dst, sems.at[i]) for i, (src, dst) in enumerate(pairs)]
    for copy in copies:
        copy.start()
    return copies


class Sender:
    def __init__(self, sems):
        self.sems, self.copies = sems, []

    def send(self, src, dst):
        copy = pltpu.make_async_copy(src, dst, self.sems.at[len(self.copies)])
        copy.start()
        self.copies.append(copy)

    def finish(self):
        for copy in self.copies:
            copy.wait()


def pack_kernel(dims, pos, w_query, w_key, w_value, *outs):
    depth, zs, shard, block, span = dims
    for k in range(depth):
        for i, w in enumerate((w_query, w_key, w_value)):
            part = w[:, :span]
            for d in range(1, depth):
                part = jnp.where((d ^ pos[2]) == k, w[:, d * span : (d + 1) * span], part)
            outs[k][:, i * span : (i + 1) * span] = part


def norm_kernel(dims, *refs):
    depth, zs, shard, block, span = dims
    gain, xs_h, refs = refs[0], refs[1 : 1 + depth], refs[1 + depth :]
    normed_h, normed_t_h, xs, normed, normed_t, in_sems, out_sems = refs
    copies = fetch([(xs_h[j], xs.at[j]) for j in range(depth)], in_sems)
    sender = Sender(out_sems)
    for j in range(depth):
        copies[j].wait()
        unit, _ = unit_rows(xs[j])
        rows = pl.ds(j * block, block)
        wide = unit * gain[...]
        normed[rows, :] = wide.astype(BF16)
        sender.send(normed.at[rows], normed_h.at[rows])
        normed_t[:, rows] = jnp.transpose(wide).astype(BF16)
        sender.send(normed_t.at[:, rows], normed_t_h.at[:, rows])
    sender.finish()


def forward_kernel(dims, *refs):
    depth, zs, shard, block, span = dims
    heads = span // HEAD_DIM
    pos, w_near, w_far, wo_near, wo_far, normed_h = refs[:6]
    query_h, keys_h, values_h, keys_t_h, att_t_h, lse_h, wq_h, wk_h, wv_h, w_out_h = refs[6:16]
    outs_h, refs = refs[16 : 16 + depth], refs[16 + depth :]
    normed, query, keys, values, keys_t, values_t, att_t, lse = refs[:8]
    wq, wk, wv, w_out, outs, in_sems, out_sems = refs[8:]
    copies = fetch([(normed_h, normed)], in_sems)
    sender = Sender(out_sems)

    own_z, first, own_d = pos[0], pos[1] == 0, pos[2]

    def pair(near, far):
        near, far = near.astype(F32), far.astype(F32)
        return jnp.concatenate(
            [jnp.where(first, near, far), jnp.where(first, far, near)], axis=0
        ).astype(BF16)

    for z in range(zs):
        for d in range(depth):
            both = pair(w_near[z ^ own_z, d ^ own_d], w_far[z ^ own_z, d ^ own_d])
            rows = slice((d * zs + z) * 2 * shard, (d * zs + z + 1) * 2 * shard)
            for i, w in enumerate((wq, wk, wv)):
                w[rows, :] = both[:, i * span : (i + 1) * span]
        both = pair(wo_near[z ^ own_z], wo_far[z ^ own_z])
        w_out[z * 2 * shard : (z + 1) * 2 * shard, :] = both
    for src, dst in ((wq, wq_h), (wk, wk_h), (wv, wv_h), (w_out, w_out_h)):
        sender.send(src, dst)
    copies[0].wait()

    query[...] = (SCALE * dot(normed[...], wq[...])).astype(BF16)
    key = dot(normed[...], wk[...])
    keys[...] = key.astype(BF16)
    keys_t[...] = jnp.transpose(key).astype(BF16)
    value = dot(normed[...], wv[...])
    values[...] = value.astype(BF16)
    values_t[...] = jnp.transpose(value).astype(BF16)
    for src, dst in ((query, query_h), (keys, keys_h), (values, values_h), (keys_t, keys_t_h)):
        sender.send(src, dst)

    masks = head_masks(span)

    units = [(j, h) for j in range(depth) for h in range(heads)]

    def score(j, h):
        return dot(keys[...], query[j * block : (j + 1) * block, :] * masks[h], (1, 1))

    ready = [score(*unit) for unit in units[:2]]
    for i, (j, h) in enumerate(units):
        cols, lanes = slice(j * block, (j + 1) * block), slice(h * HEAD_DIM, (h + 1) * HEAD_DIM)
        scores = ready.pop(0)
        top = jnp.max(scores, axis=0, keepdims=True)
        e = jnp.exp(scores - top)
        total = jnp.sum(e, axis=0, keepdims=True)
        if i + 2 < len(units):
            ready.append(score(*units[i + 2]))
        att_t[lanes, cols] = dot(values_t[lanes, :], e.astype(BF16)) * (1.0 / total)
        lse[h, :, cols] = top + jnp.log(total)
    sender.send(att_t, att_t_h)
    sender.send(lse, lse_h)
    att = jnp.transpose(att_t[...]).astype(BF16)
    for j in range(depth):
        outs[j] = dot(att[j * block : (j + 1) * block], w_out[...]).astype(BF16)
        sender.send(outs.at[j], outs_h[j])
    sender.finish()


def backward_kernel(dims, *refs):
    depth, zs, shard, block, span = dims
    heads = span // HEAD_DIM
    pos, gain = refs[:2]
    gs_h, refs = refs[2 : 2 + depth], refs[2 + depth :]
    (w_out_h, query_h, keys_h, values_h, keys_t_h, lse_h, normed_t_h, att_t_h) = refs[:8]
    (wq_h, wk_h, wv_h, near, far), refs = refs[8:13], refs[13:]
    dns_h, refs = refs[: depth + 1], refs[depth + 1 :]
    (gs, w_out, query, keys, values, keys_t, lse, normed_t, att_t, wq, wk, wv) = refs[:12]
    (d_att, delta, d_query_t, d_keys, d_values, grad_out, dns, in_sems, out_sems) = refs[12:]
    copies = fetch(
        [(w_out_h, w_out)]
        + [(gs_h[j], gs.at[pl.ds(j * block, block)]) for j in range(depth)]
        + [
            (att_t_h, att_t),
            (keys_h, keys),
            (query_h, query),
            (values_h, values),
            (lse_h, lse),
            (keys_t_h, keys_t),
            (normed_t_h, normed_t),
            (wq_h, wq),
            (wk_h, wk),
            (wv_h, wv),
        ],
        in_sems,
    )
    loaded, later = 7 + depth, copies[7 + depth :]

    d_keys[...] = jnp.zeros_like(d_keys)
    d_values[...] = jnp.zeros_like(d_values)
    for copy in copies[: 2 + depth]:
        copy.wait()
    part = dot(gs[...], w_out[...], (1, 1)).astype(BF16)
    d_att[...] = part
    product = jnp.transpose(part.astype(F32)) * att_t[...]
    for h in range(heads):
        delta[h] = jnp.sum(product[h * HEAD_DIM : (h + 1) * HEAD_DIM], axis=0, keepdims=True)
    for copy in copies[2 + depth : loaded]:
        copy.wait()
    masks = head_masks(span)

    def step(j, _):
        cols = pl.ds(pl.multiple_of(j * block, block), block)
        q_block, g_block = query[cols, :], d_att[cols, :]
        qs = [q_block * m for m in masks]
        ds = [g_block * m for m in masks]

        def pair(h):
            return dot(keys[...], qs[h], (1, 1)), dot(values[...], ds[h], (1, 1))

        pairs = [pair(h) for h in range(min(2, heads))]
        for h in range(heads):
            scores, d_probs = pairs[h]
            probs = jnp.exp(scores - lse[h, :, cols])
            d_scores = (probs * (d_probs - delta[h, :, cols])).astype(BF16)
            if h + 2 < heads:
                pairs.append(pair(h + 2))
            values_add = dot(probs.astype(BF16), ds[h])
            keys_add = dot(d_scores, qs[h])
            value_part = values_add if h == 0 else value_part + values_add
            key_part = keys_add if h == 0 else key_part + keys_add
            lanes = slice(h * HEAD_DIM, (h + 1) * HEAD_DIM)
            d_query_t[lanes, cols] = SCALE * dot(keys_t[lanes, :], d_scores)
        d_values[...] += value_part.astype(BF16).astype(F32)
        d_keys[...] += key_part.astype(BF16).astype(F32)
        return 0

    lax.fori_loop(0, depth, step, 0)
    for copy in later:
        copy.wait()
    d_query = jnp.transpose(d_query_t[...]).astype(BF16)
    d_key, d_value = d_keys[...].astype(BF16), d_values[...].astype(BF16)
    sender = Sender(out_sems)
    for j in range(depth):
        rows = slice(j * block, (j + 1) * block)
        d_normed = dot(d_query[rows], wq[...], (1, 1))
        d_normed = d_normed + dot(d_key[rows], wk[...], (1, 1))
        d_normed = d_normed + dot(d_value[rows], wv[...], (1, 1))
        dns[j] = d_normed.astype(BF16)
        if j < depth - 1:
            sender.send(dns.at[j], dns_h[j])
        else:
            half = block // 2
            sender.send(dns.at[j, pl.ds(0, half)], dns_h[j])
            sender.send(dns.at[j, pl.ds(half, half)], dns_h[j + 1])

    grad_out[...] = dot(att_t[...].astype(BF16), gs[...])
    grads = [dot(normed_t[...], d) for d in (d_query, d_key, d_value)]
    both = wq[...].astype(F32) * grads[0]
    both = both + wk[...].astype(F32) * grads[1] + wv[...].astype(F32) * grads[2]
    gain_rows = jnp.transpose(jnp.broadcast_to(gain[...], (128, gain.shape[1])))[:, :64]
    gain_column = jnp.sum(both, axis=1, keepdims=True) / gain_rows
    own_z, first, own_d = pos[0], pos[1] == 0, pos[2]
    for d in range(depth):
        for z in range(zs):
            sides = []
            for c in range(2):
                row, row_out = ((d * zs + z) * 2 + c) * shard, (z * 2 + c) * shard
                sides.append(
                    [g[row : row + shard] for g in grads]
                    + [
                        gain_column[row : row + shard],
                        grad_out[row_out : row_out + shard, d * span : (d + 1) * span],
                    ]
                )
            at = 0
            for one, two in zip(*sides):
                lanes = slice(at, at + one.shape[1])
                at += one.shape[1]
                near[z ^ own_z, d ^ own_d, :, lanes] = jnp.where(first, one, two).astype(BF16)
                far[z ^ own_z, d ^ own_d, :, lanes] = jnp.where(first, two, one).astype(BF16)
    sender.finish()


def align_kernel(dims, gain, x, upstream, *refs):
    dns, out = refs[:-1], refs[-1]
    d_normed = dns[0][...].astype(F32)
    for part in dns[1:]:
        d_normed = d_normed + part[...].astype(F32)
    unit, inverse = unit_rows(x[...])
    d_unit = d_normed * gain[...]
    out[...] = (
        upstream[...].astype(F32)
        + inverse
        * (
            d_unit
            - jnp.mean(d_unit, axis=-1, keepdims=True)
            - unit * jnp.mean(d_unit * unit, axis=-1, keepdims=True)
        )
    ).astype(BF16)


def finish_kernel(dims, pos, acc, *refs):
    depth, zs, shard, block, span = dims
    parts, outs = (None,) + refs[: depth - 1], refs[depth - 1 :]
    own_d = pos[2]
    lanes = 3 * span + 64
    gain_sum = None
    blocks = [acc[0][:, :lanes]] + [p[...].astype(F32) for p in parts[1:]]
    for d in range(depth):
        total = blocks[0]
        for k in range(1, depth):
            total = jnp.where((d ^ own_d) == k, blocks[k], total)
        for i in range(3):
            outs[i][:, d * span : (d + 1) * span] = total[:, i * span : (i + 1) * span]
        outs[3][:, d * span : (d + 1) * span] = acc[d ^ own_d][:, lanes:]
        gain = total[:, 3 * span : 3 * span + 1]
        gain_sum = gain if gain_sum is None else gain_sum + gain
    wide = jnp.concatenate([gain_sum, jnp.zeros((128 - shard, 1), F32)], axis=0)
    outs[4][...] = jnp.transpose(jnp.broadcast_to(wide, (128, 128)))[0:1, :shard]


VMEM, ANY, SMEM = pltpu.VMEM, pl.ANY, pltpu.SMEM


def call(kernel, dims, ins, outs, scratch, sems, flops, mib=56):
    args = [a for a, _ in ins]
    shapes = [jax.ShapeDtypeStruct(shape, kind) for shape, kind, _ in outs]
    size = sum(a.size * a.dtype.itemsize for a in args + shapes)
    return pl.pallas_call(
        functools.partial(kernel, dims),
        out_shape=shapes,
        in_specs=[pl.BlockSpec(memory_space=space) for _, space in ins],
        out_specs=[pl.BlockSpec(memory_space=space) for _, _, space in outs],
        scratch_shapes=[pltpu.VMEM(shape, kind) for shape, kind in scratch]
        + [pltpu.SemaphoreType.DMA((n,)) for n in sems],
        compiler_params=pltpu.CompilerParams(vmem_limit_bytes=mib * 1024 * 1024),
        cost_estimate=pl.CostEstimate(flops=flops, bytes_accessed=size, transcendentals=0),
    )(*args)


def head_body(depth, res, *args):
    x, gain, w_query, w_key, w_value, w_out, upstream = args
    homologs, _, width = x.shape
    span, zs = width // depth, res // 2
    shard = w_query.shape[0]
    total, heads = homologs * depth, span // HEAD_DIM
    dims = (depth, zs, shard, homologs, span)
    x = x.reshape(homologs, width)
    upstream = upstream.reshape(homologs, width)
    gain = gain.reshape(1, width)
    pos = jnp.stack([lax.axis_index(a) for a in ("z", "core", "depth")]).astype(jnp.int32)

    xs = [x] + [swap(x, "depth", depth, k) for k in range(1, depth - 1)]

    mine = call(
        pack_kernel,
        dims,
        [(pos, SMEM), (w_query, VMEM), (w_key, VMEM), (w_value, VMEM)],
        [((shard, 3 * span), BF16, VMEM)] * depth,
        [],
        [],
        1000,
    )
    wo_parts = [w_out] + [swap(w_out, "z", zs, k) for k in range(1, zs)]
    mine, wo_parts = lax.optimization_barrier((list(mine), wo_parts))
    mine = [mine[0]] + [swap(mine[k], "depth", depth, k) for k in range(1, depth)]
    mine, xs = lax.optimization_barrier((mine, xs))
    across = swap(xs[0], "depth", depth, depth - 1)
    mine = jnp.stack(mine, axis=0)
    parts = [mine] + [swap(mine, "z", zs, k) for k in range(1, zs)]
    xs = xs + [across]
    gs = [upstream] + [swap(upstream, "depth", depth, k) for k in range(1, depth)]

    rows, turned = ((total, span), BF16), ((span, total), BF16)
    half = homologs // 2
    block, halved = ((homologs, width), BF16), ((half, width), BF16)
    blocks = ((depth, homologs, width), BF16)
    norm, stats = ((total, width), BF16), ((heads, 1, total), F32)
    in_weights, out_weights = ((width, span), BF16), ((span, width), BF16)
    pass_flops = 2 * total * total * span
    normed, normed_t = call(
        norm_kernel,
        dims,
        [(gain, VMEM)] + [(a, ANY) for a in xs],
        [norm + (ANY,), ((width, total), BF16, ANY)],
        [blocks, norm, ((width, total), BF16)],
        [depth, 2 * depth],
        1000,
    )
    normed, pos, *parts = lax.optimization_barrier([normed, pos] + parts)
    w_near, wo_near = jnp.stack(parts, axis=0), jnp.stack(wo_parts, axis=0)
    w_far, wo_far = swap(w_near, "core", 2, 1), swap(wo_near, "core", 2, 1)

    turned_f32 = ((span, total), F32)
    saved = [rows, rows, rows, turned, turned_f32, stats] + [in_weights] * 3 + [out_weights]
    query, keys, values, keys_t, att_t, lse, wq, wk, wv, wo, *outs = call(
        forward_kernel,
        dims,
        [(pos, SMEM)]
        + [(a, VMEM) for a in (w_near, w_far, wo_near, wo_far)]
        + [(normed, ANY)],
        [s + (ANY,) for s in saved + [block] * depth],
        [norm, rows, rows, rows, turned, turned, turned_f32, stats]
        + [in_weights] * 3
        + [out_weights, blocks],
        [1, len(saved) + depth],
        8 * pass_flops,
    )

    packed = (zs, depth, shard, 4 * span + 64)
    near, far, *dns = call(
        backward_kernel,
        dims,
        [(pos, SMEM), (gain, VMEM)]
        + [(a, ANY) for a in gs + [wo, query, keys, values, keys_t, lse, normed_t]]
        + [(a, ANY) for a in (att_t, wq, wk, wv)],
        [(packed, BF16, VMEM)] * 2 + [s + (ANY,) for s in [block] * 3 + [halved] * 2],
        [norm, out_weights, rows, rows, rows, turned, stats, ((width, total), BF16)]
        + [turned_f32, in_weights, in_weights, in_weights]
        + [rows, stats, turned_f32]
        + [((total, span), F32)] * 2
        + [((span, width), F32), blocks],
        [depth + 11, depth + 1],
        24 * pass_flops,
    )

    outs = [outs[0]] + [swap(outs[k], "depth", depth, k) for k in range(1, depth)]
    near, far, dns, outs = lax.optimization_barrier((near, far, dns, outs))

    far = swap(far, "core", 2, 1)
    dn0, dn1, dn2, dn3_top, dn3_bottom = dns
    top, bottom = swap(dn3_top, "depth", depth, 1), swap(dn3_bottom, "depth", depth, 2)
    sums = [near[k].astype(F32) + far[k].astype(F32) for k in range(zs)]
    low = [swap(sums[k].astype(BF16), "z", zs, k) for k in range(1, zs)]
    low[1], top, bottom = lax.optimization_barrier((low[1], top, bottom))
    dn2 = dn2.astype(F32) + jnp.concatenate([top, jnp.zeros_like(top)], axis=0).astype(F32)
    dn1 = dn1.astype(F32) + jnp.concatenate([jnp.zeros_like(bottom), bottom], axis=0).astype(F32)
    dn1 = swap(dn1.astype(BF16), "depth", depth, 1)
    dn2 = swap(dn2.astype(BF16), "depth", depth, 2)
    low[1], outs = lax.optimization_barrier((low[1], outs))
    final_result = (x.astype(F32) + sum(o.astype(F32) for o in outs)).astype(BF16)
    acc = sums[0] + sum(p.astype(F32) for p in low)
    dns = [dn0, dn1, dn2]
    parts = [
        swap(acc[k, :, : 3 * span + 64].astype(BF16), "depth", depth, k) for k in range(1, depth)
    ]
    alignment = call(
        align_kernel,
        dims,
        [(a, VMEM) for a in [gain, x, upstream] + dns],
        [block + (VMEM,)],
        [],
        [],
        1000 * total * width,
        16,
    )[0]
    alignment, *parts = lax.optimization_barrier([alignment] + parts)
    grad_query, grad_key, grad_value, grad_out, gain_rows = call(
        finish_kernel,
        dims,
        [(pos, SMEM), (acc, VMEM)] + [(p, VMEM) for p in parts],
        [((shard, width), F32, VMEM)] * 4 + [((1, shard), F32, VMEM)],
        [],
        [],
        1000,
        16,
    )
    return (
        final_result.reshape(homologs, 1, width),
        alignment.reshape(homologs, 1, width),
        grad_query,
        grad_key,
        grad_value,
        grad_out,
        gain_rows.reshape(shard),
    )


def solution(mesh):
    depth, res = mesh.shape["depth"], mesh.shape["res"]
    powers = depth & (depth - 1) == 0 and res & (res - 1) == 0 and res > 1
    if powers and depth == 4 and res >= 4 and HEADS % depth == 0:
        axes = ("depth", "z", "core")
        mesh = Mesh(mesh.devices.reshape(depth, res // 2, 2), axes)
        res_axes, run = ("z", "core"), functools.partial(head_body, depth, res)
    else:
        axes = ("depth", "res")
        res_axes, run = ("res",), general_body

    def body(*args):
        if args[0].shape[1] != 1:
            return general_body(*args, axes=axes)
        return run(*args)

    rows = P("depth", res_axes, None)
    weight = P(axes, None)
    return jax.shard_map(
        body,
        mesh=mesh,
        in_specs=(rows, P(), weight, weight, weight, weight, rows),
        out_specs=(rows, rows, weight, weight, weight, weight, P(axes)),
        check_vma=False,
    )
```

```python
import functools

import jax
import jax.numpy as jnp
from jax import lax
from jax.experimental import pallas as pl
from jax.experimental.pallas import tpu as pltpu
from jax.sharding import Mesh, PartitionSpec as P

HEADS = 12
HEAD_DIM = 64


def standardize_entries(family_activity, rescale_factor):
    payload_entries = family_activity.astype(jnp.float32)
    centered = payload_entries - jnp.mean(payload_entries, axis=-1, keepdims=True)
    reciprocal_spread = lax.rsqrt(jnp.mean(centered * centered, axis=-1, keepdims=True) + 1e-05)
    standardized_entries = centered * reciprocal_spread
    return (
        (standardized_entries * rescale_factor).astype(jnp.bfloat16),
        standardized_entries,
        reciprocal_spread,
    )


def project(rows, weight, factor):
    return (factor * jnp.dot(rows, weight, preferred_element_type=jnp.float32)).astype(jnp.bfloat16)


def to_heads(array):
    count, cols = (array.shape[0], array.shape[1])
    return jnp.transpose(array.reshape(count, cols, HEADS, HEAD_DIM), (1, 2, 0, 3)).reshape(
        cols * HEADS, count, HEAD_DIM
    )


def from_heads(array, cols):
    count = array.shape[1]
    return jnp.transpose(array.reshape(cols, HEADS, count, HEAD_DIM), (2, 0, 1, 3)).reshape(
        count, cols, HEADS * HEAD_DIM
    )


def head_pass(query, keys, payload_entries, d_att):
    scale = HEAD_DIM ** (-0.5)
    scores = jnp.dot(query, keys.T, preferred_element_type=jnp.float32)
    probs = jax.nn.softmax(scores, axis=-1)
    probs_b = probs.astype(jnp.bfloat16)
    mixed_homologs = jnp.dot(probs_b, payload_entries, preferred_element_type=jnp.float32).astype(
        jnp.bfloat16
    )
    d_probs = jnp.dot(d_att, payload_entries.T, preferred_element_type=jnp.float32)
    d_scores = probs * (d_probs - jnp.sum(probs * d_probs, axis=-1, keepdims=True))
    d_scores_b = d_scores.astype(jnp.bfloat16)
    d_query = (scale * jnp.dot(d_scores_b, keys, preferred_element_type=jnp.float32)).astype(
        jnp.bfloat16
    )
    key_part = jnp.einsum("st,sd->td", d_scores_b, query, preferred_element_type=jnp.float32)
    value_part = jnp.einsum("st,sd->td", probs_b, d_att, preferred_element_type=jnp.float32)
    return (mixed_homologs, d_query, key_part, value_part)


def general_body(
    family_activity,
    rescale_factor,
    asking_weights,
    lookup_weights,
    payload_weights,
    exit_weights,
    upstream_adjoint,
    axes=("depth", "res"),
):
    query_weight, key_weight, value_weight, output_matrix = (
        lax.all_gather(asking_weights, axes, axis=0, tiled=True),
        lax.all_gather(lookup_weights, axes, axis=0, tiled=True),
        lax.all_gather(payload_weights, axes, axis=0, tiled=True),
        lax.all_gather(exit_weights, axes, axis=0, tiled=True),
    )
    homologs_each_shard, positions_each_shard, embed_span = family_activity.shape
    standardized_source, standardized_entries, reciprocal_spread = standardize_entries(
        family_activity, rescale_factor
    )
    query = project(standardized_source, query_weight, HEAD_DIM ** (-0.5))
    keys = project(standardized_source, key_weight, 1.0)
    payload_entries = project(standardized_source, value_weight, 1.0)
    keys_all, values_all = (
        lax.all_gather(keys, "depth", axis=0, tiled=True),
        lax.all_gather(payload_entries, "depth", axis=0, tiled=True),
    )
    d_att = jnp.dot(upstream_adjoint, output_matrix.T, preferred_element_type=jnp.float32).astype(
        jnp.bfloat16
    )

    def per_head(items):
        return head_pass(items[0], items[1], items[2], items[3])

    mixed_homologs, d_query, key_part, value_part = lax.map(
        per_head, (to_heads(query), to_heads(keys_all), to_heads(values_all), to_heads(d_att))
    )
    mixed_homologs = from_heads(mixed_homologs, positions_each_shard)
    d_query = from_heads(d_query, positions_each_shard)
    key_part = from_heads(key_part, positions_each_shard)
    value_part = from_heads(value_part, positions_each_shard)
    rows = homologs_each_shard * positions_each_shard
    normed_rows = standardized_source.reshape(rows, embed_span)
    part_query = jnp.dot(
        normed_rows.T, d_query.reshape(rows, embed_span), preferred_element_type=jnp.float32
    )
    part_out = jnp.dot(
        mixed_homologs.reshape(rows, embed_span).T,
        upstream_adjoint.reshape(rows, embed_span),
        preferred_element_type=jnp.float32,
    )
    stacked = jnp.stack([key_part, value_part], axis=2).astype(jnp.bfloat16)
    summed = (
        lax.psum_scatter(stacked, "depth", scatter_dimension=0, tiled=True)
        .astype(jnp.float32)
        .astype(jnp.bfloat16)
    )
    d_keys = summed[:, :, 0, :]
    d_values = summed[:, :, 1, :]
    final_result = (
        family_activity.astype(jnp.float32)
        + jnp.dot(mixed_homologs, output_matrix, preferred_element_type=jnp.float32)
    ).astype(jnp.bfloat16)
    part_key = jnp.dot(
        normed_rows.T, d_keys.reshape(rows, embed_span), preferred_element_type=jnp.float32
    )
    part_value = jnp.dot(
        normed_rows.T, d_values.reshape(rows, embed_span), preferred_element_type=jnp.float32
    )
    d_normed = jnp.dot(d_query, query_weight.T, preferred_element_type=jnp.float32)
    d_normed = d_normed + jnp.dot(d_keys, key_weight.T, preferred_element_type=jnp.float32)
    d_normed = d_normed + jnp.dot(d_values, value_weight.T, preferred_element_type=jnp.float32)
    part_gain = jnp.sum((d_normed * standardized_entries).reshape(rows, embed_span), axis=0)
    unit_gradient = d_normed * rescale_factor
    alignment_gradient = upstream_adjoint.astype(jnp.float32) + reciprocal_spread * (
        unit_gradient
        - jnp.mean(unit_gradient, axis=-1, keepdims=True)
        - standardized_entries
        * jnp.mean(unit_gradient * standardized_entries, axis=-1, keepdims=True)
    )
    query_gradient, key_gradient, value_gradient, output_gradient, gain_gradient = (
        lax.psum_scatter(part_query, axes, scatter_dimension=0, tiled=True),
        lax.psum_scatter(part_key, axes, scatter_dimension=0, tiled=True),
        lax.psum_scatter(part_value, axes, scatter_dimension=0, tiled=True),
        lax.psum_scatter(part_out, axes, scatter_dimension=0, tiled=True),
        lax.psum_scatter(part_gain, axes, scatter_dimension=0, tiled=True),
    )
    return (
        final_result,
        alignment_gradient.astype(jnp.bfloat16),
        query_gradient,
        key_gradient,
        value_gradient,
        output_gradient,
        gain_gradient,
    )


F32, BF16 = jnp.float32, jnp.bfloat16
SCALE = HEAD_DIM ** (-0.5)


def swap(value, axis, size, bits):
    return lax.ppermute(value, axis, [(i, i ^ bits) for i in range(size)])


def dot(a, b, contract=(1, 0)):
    return lax.dot_general(
        a, b, (((contract[0],), (contract[1],)), ((), ())), preferred_element_type=F32
    )


def unit_rows(x):
    x = x.astype(F32)
    centered = x - jnp.mean(x, axis=-1, keepdims=True)
    inverse = lax.rsqrt(jnp.mean(centered * centered, axis=-1, keepdims=True) + 1e-05)
    return centered * inverse, inverse


def head_masks(span):
    lane = lax.broadcasted_iota(jnp.int32, (8, span), 1)
    return [
        ((lane >= at) & (lane < at + HEAD_DIM)).astype(F32)[0:1].astype(BF16)
        for at in range(0, span, HEAD_DIM)
    ]


def fetch(pairs, sems):
    copies = [pltpu.make_async_copy(src, dst, sems.at[i]) for i, (src, dst) in enumerate(pairs)]
    for copy in copies:
        copy.start()
    return copies


class Sender:
    def __init__(self, sems):
        self.sems, self.copies = sems, []

    def send(self, src, dst):
        copy = pltpu.make_async_copy(src, dst, self.sems.at[len(self.copies)])
        copy.start()
        self.copies.append(copy)

    def finish(self):
        for copy in self.copies:
            copy.wait()


def pack_kernel(dims, w_query, w_key, w_value, w_out, out, out_cut):
    depth, zs, shard, block, span = dims
    for d in range(depth):
        lanes = slice(d * span, (d + 1) * span)
        for i, w in enumerate((w_query, w_key, w_value)):
            out[d, :, i * span : (i + 1) * span] = w[:, lanes]
        out_cut[d] = w_out[:, lanes]


def norm_kernel(dims, *refs):
    depth, zs, shard, block, span = dims
    gain, xs_h, refs = refs[0], refs[1 : 1 + depth], refs[1 + depth :]
    normed_h, normed_t_h, xs, normed, normed_t, in_sems, out_sems = refs
    copies = fetch([(xs_h[j], xs.at[j]) for j in range(depth)], in_sems)
    sender = Sender(out_sems)
    for j in range(depth):
        copies[j].wait()
        unit, _ = unit_rows(xs[j])
        rows = pl.ds(j * block, block)
        wide = unit * gain[...]
        normed[rows, :] = wide.astype(BF16)
        sender.send(normed.at[rows], normed_h.at[rows])
        normed_t[:, rows] = jnp.transpose(wide).astype(BF16)
        sender.send(normed_t.at[:, rows], normed_t_h.at[:, rows])
    sender.finish()


def forward_kernel(dims, *refs):
    depth, zs, shard, block, span = dims
    heads = span // HEAD_DIM
    pos, w_near, w_far, normed_h = refs[:4]
    query_h, keys_h, values_h, keys_t_h, att_t_h, lse_h, wq_h, wk_h, wv_h, w_out_h = refs[4:14]
    outs_h, refs = refs[14 : 14 + depth], refs[14 + depth :]
    normed, query, keys, values, keys_t, values_t, att_t, lse = refs[:8]
    wq, wk, wv, w_out, outs, in_sems, out_sems = refs[8:]
    copies = fetch([(normed_h, normed)], in_sems)
    sender = Sender(out_sems)

    own_z, first = pos[0], pos[1] == 0
    for z in range(zs):
        for d in range(depth):
            near, far = w_near[z ^ own_z, d].astype(F32), w_far[z ^ own_z, d].astype(F32)
            both = jnp.concatenate(
                [jnp.where(first, near, far), jnp.where(first, far, near)], axis=0
            ).astype(BF16)
            rows = slice((d * zs + z) * 2 * shard, (d * zs + z + 1) * 2 * shard)
            for i, w in enumerate((wq, wk, wv)):
                w[rows, :] = both[:, i * span : (i + 1) * span]
            rows = slice(z * 2 * shard, (z + 1) * 2 * shard)
            w_out[rows, d * span : (d + 1) * span] = both[:, 3 * span :]
    for src, dst in ((wq, wq_h), (wk, wk_h), (wv, wv_h), (w_out, w_out_h)):
        sender.send(src, dst)
    copies[0].wait()

    query[...] = (SCALE * dot(normed[...], wq[...])).astype(BF16)
    key = dot(normed[...], wk[...])
    keys[...] = key.astype(BF16)
    keys_t[...] = jnp.transpose(key).astype(BF16)
    value = dot(normed[...], wv[...])
    values[...] = value.astype(BF16)
    values_t[...] = jnp.transpose(value).astype(BF16)
    for src, dst in ((query, query_h), (keys, keys_h), (values, values_h), (keys_t, keys_t_h)):
        sender.send(src, dst)

    masks = head_masks(span)

    units = [(j, h) for j in range(depth) for h in range(heads)]

    def score(j, h):
        return dot(keys[...], query[j * block : (j + 1) * block, :] * masks[h], (1, 1))

    ready = [score(*unit) for unit in units[:2]]
    for i, (j, h) in enumerate(units):
        cols, lanes = slice(j * block, (j + 1) * block), slice(h * HEAD_DIM, (h + 1) * HEAD_DIM)
        scores = ready.pop(0)
        top = jnp.max(scores, axis=0, keepdims=True)
        e = jnp.exp(scores - top)
        total = jnp.sum(e, axis=0, keepdims=True)
        if i + 2 < len(units):
            ready.append(score(*units[i + 2]))
        att_t[lanes, cols] = dot(values_t[lanes, :], e.astype(BF16)) * (1.0 / total)
        lse[h, :, cols] = top + jnp.log(total)
    sender.send(att_t, att_t_h)
    sender.send(lse, lse_h)
    att = jnp.transpose(att_t[...]).astype(BF16)
    for j in range(depth):
        outs[j] = dot(att[j * block : (j + 1) * block], w_out[...]).astype(BF16)
        sender.send(outs.at[j], outs_h[j])
    sender.finish()


def backward_kernel(dims, *refs):
    depth, zs, shard, block, span = dims
    heads = span // HEAD_DIM
    pos, refs = refs[0], refs[1:]
    gs_h, refs = refs[:depth], refs[depth:]
    (w_out_h, query_h, keys_h, values_h, keys_t_h, lse_h, normed_t_h, att_t_h) = refs[:8]
    (wq_h, wk_h, wv_h, near, far), refs = refs[8:13], refs[13:]
    dns_h, refs = refs[: depth + 1], refs[depth + 1 :]
    (gs, w_out, query, keys, values, keys_t, lse, normed_t, att_t, wq, wk, wv) = refs[:12]
    (d_att, delta, d_query_t, d_keys, d_values, grad_out, dns, in_sems, out_sems) = refs[12:]
    copies = fetch(
        [(w_out_h, w_out)]
        + [(gs_h[j], gs.at[pl.ds(j * block, block)]) for j in range(depth)]
        + [
            (att_t_h, att_t),
            (keys_h, keys),
            (query_h, query),
            (values_h, values),
            (lse_h, lse),
            (keys_t_h, keys_t),
            (normed_t_h, normed_t),
            (wq_h, wq),
            (wk_h, wk),
            (wv_h, wv),
        ],
        in_sems,
    )
    loaded, later = 7 + depth, copies[7 + depth :]

    d_keys[...] = jnp.zeros_like(d_keys)
    d_values[...] = jnp.zeros_like(d_values)
    for copy in copies[: 2 + depth]:
        copy.wait()
    part = dot(gs[...], w_out[...], (1, 1)).astype(BF16)
    d_att[...] = part
    product = jnp.transpose(part.astype(F32)) * att_t[...]
    for h in range(heads):
        delta[h] = jnp.sum(product[h * HEAD_DIM : (h + 1) * HEAD_DIM], axis=0, keepdims=True)
    for copy in copies[2 + depth : loaded]:
        copy.wait()
    masks = head_masks(span)

    def step(j, _):
        cols = pl.ds(pl.multiple_of(j * block, block), block)
        q_block, g_block = query[cols, :], d_att[cols, :]
        qs = [q_block * m for m in masks]
        ds = [g_block * m for m in masks]

        def pair(h):
            return dot(keys[...], qs[h], (1, 1)), dot(values[...], ds[h], (1, 1))

        pairs = [pair(h) for h in range(min(2, heads))]
        for h in range(heads):
            scores, d_probs = pairs[h]
            probs = jnp.exp(scores - lse[h, :, cols])
            d_scores = (probs * (d_probs - delta[h, :, cols])).astype(BF16)
            if h + 2 < heads:
                pairs.append(pair(h + 2))
            values_add = dot(probs.astype(BF16), ds[h])
            keys_add = dot(d_scores, qs[h])
            value_part = values_add if h == 0 else value_part + values_add
            key_part = keys_add if h == 0 else key_part + keys_add
            lanes = slice(h * HEAD_DIM, (h + 1) * HEAD_DIM)
            d_query_t[lanes, cols] = SCALE * dot(keys_t[lanes, :], d_scores)
        d_values[...] += value_part.astype(BF16).astype(F32)
        d_keys[...] += key_part.astype(BF16).astype(F32)
        return 0

    lax.fori_loop(0, depth, step, 0)
    for copy in later:
        copy.wait()
    d_query = jnp.transpose(d_query_t[...]).astype(BF16)
    d_key, d_value = d_keys[...].astype(BF16), d_values[...].astype(BF16)
    sender = Sender(out_sems)
    for i in range(0, depth, 2):
        rows = slice(i * block, (i + 2) * block)
        d_normed = dot(d_query[rows], wq[...], (1, 1))
        d_normed = d_normed + dot(d_key[rows], wk[...], (1, 1))
        d_normed = d_normed + dot(d_value[rows], wv[...], (1, 1))
        dns[rows, :] = d_normed.astype(BF16)
        for j in (i, i + 1):
            if j < depth - 1:
                sender.send(dns.at[pl.ds(j * block, block)], dns_h[j])
            else:
                half = block // 2
                sender.send(dns.at[pl.ds(j * block, half)], dns_h[j])
                sender.send(dns.at[pl.ds(j * block + half, half)], dns_h[j + 1])

    grad_out[...] = dot(att_t[...].astype(BF16), gs[...])
    grads = [dot(normed_t[...], d) for d in (d_query, d_key, d_value)]
    own_z, first, own_d = pos[0], pos[1] == 0, pos[2]
    for d in range(depth):
        for z in range(zs):
            sides = []
            for c in range(2):
                row, row_out = ((d * zs + z) * 2 + c) * shard, (z * 2 + c) * shard
                sides.append(
                    [g[row : row + shard] for g in grads]
                    + [grad_out[row_out : row_out + shard, d * span : (d + 1) * span]]
                )
            at = 0
            for one, two in zip(*sides):
                lanes = slice(at, at + one.shape[1])
                at += one.shape[1]
                near[z ^ own_z, d ^ own_d, :, lanes] = jnp.where(first, one, two).astype(BF16)
                far[z ^ own_z, d ^ own_d, :, lanes] = jnp.where(first, two, one).astype(BF16)
    sender.finish()


def align_kernel(dims, gain, x, upstream, *refs):
    dns, out = refs[:-1], refs[-1]
    d_normed = dns[0][...].astype(F32)
    for part in dns[1:]:
        d_normed = d_normed + part[...].astype(F32)
    unit, inverse = unit_rows(x[...])
    d_unit = d_normed * gain[...]
    out[...] = (
        upstream[...].astype(F32)
        + inverse
        * (
            d_unit
            - jnp.mean(d_unit, axis=-1, keepdims=True)
            - unit * jnp.mean(d_unit * unit, axis=-1, keepdims=True)
        )
    ).astype(BF16)


def finish_kernel(dims, *refs):
    depth, zs, shard, block, span = dims
    pos, gain, weights, acc, refs = refs[0], refs[1], refs[2:5], refs[5], refs[6:]
    parts, outs = refs[: depth - 1], refs[depth - 1 :]
    own_d = pos[2]
    blocks = [acc[0][:, : 3 * span]] + [p[...].astype(F32) for p in parts]
    for d in range(depth):
        lanes = slice(d * span, (d + 1) * span)
        total = blocks[0]
        for k in range(1, depth):
            total = jnp.where((d ^ own_d) == k, blocks[k], total)
        for i in range(3):
            outs[i][:, lanes] = total[:, i * span : (i + 1) * span]
        outs[3][:, lanes] = acc[d ^ own_d][:, 3 * span :]
    column = weights[0][...].astype(F32) * outs[0][...]
    for w, grad in zip(weights[1:], outs[1:3]):
        column = column + w[...].astype(F32) * grad[...]
    column = jnp.sum(column, axis=1, keepdims=True)
    wide = jnp.concatenate([column, jnp.zeros((128 - shard, 1), F32)], axis=0)
    row = jnp.transpose(jnp.broadcast_to(wide, (128, 128)))[0:1, :shard]
    outs[4][...] = row / gain[...]


VMEM, ANY, SMEM = pltpu.VMEM, pl.ANY, pltpu.SMEM


def call(kernel, dims, ins, outs, scratch, sems, flops, mib=56):
    args = [a for a, _ in ins]
    shapes = [jax.ShapeDtypeStruct(shape, kind) for shape, kind, _ in outs]
    size = sum(a.size * a.dtype.itemsize for a in args + shapes)
    return pl.pallas_call(
        functools.partial(kernel, dims),
        out_shape=shapes,
        in_specs=[pl.BlockSpec(memory_space=space) for _, space in ins],
        out_specs=[pl.BlockSpec(memory_space=space) for _, _, space in outs],
        scratch_shapes=[pltpu.VMEM(shape, kind) for shape, kind in scratch]
        + [pltpu.SemaphoreType.DMA((n,)) for n in sems],
        compiler_params=pltpu.CompilerParams(vmem_limit_bytes=mib * 1024 * 1024),
        cost_estimate=pl.CostEstimate(flops=flops, bytes_accessed=size, transcendentals=0),
    )(*args)


def head_body(depth, res, *args):
    x, gain, w_query, w_key, w_value, w_out, upstream = args
    homologs, _, width = x.shape
    span, zs = width // depth, res // 2
    shard = w_query.shape[0]
    total, heads = homologs * depth, span // HEAD_DIM
    dims = (depth, zs, shard, homologs, span)
    x = x.reshape(homologs, width)
    upstream = upstream.reshape(homologs, width)
    gain = gain.reshape(1, width)
    pos = jnp.stack([lax.axis_index(a) for a in ("z", "core", "depth")]).astype(jnp.int32)

    xs = [x] + [swap(x, "depth", depth, k) for k in range(1, depth - 1)]

    packed, out_cut = call(
        pack_kernel,
        dims,
        [(w, VMEM) for w in (w_query, w_key, w_value, w_out)],
        [((depth, shard, 3 * span), BF16, VMEM), ((depth, shard, span), BF16, VMEM)],
        [],
        [],
        1000,
    )
    mine = lax.all_to_all(packed, "depth", 0, 0, tiled=True)
    mine = jnp.concatenate([mine, out_cut], axis=2)
    mine, *xs = lax.optimization_barrier([mine] + xs)
    xs.append(swap(xs[0], "depth", depth, depth - 1))
    parts = [mine] + [swap(mine, "z", zs, k) for k in range(1, zs)]
    gs = [upstream] + [swap(upstream, "depth", depth, k) for k in range(1, depth)]

    rows, turned = ((total, span), BF16), ((span, total), BF16)
    half = homologs // 2
    block, halved = ((homologs, width), BF16), ((half, width), BF16)
    blocks = ((depth, homologs, width), BF16)
    norm, stats = ((total, width), BF16), ((heads, 1, total), F32)
    in_weights, out_weights = ((width, span), BF16), ((span, width), BF16)
    pass_flops = 2 * total * total * span
    normed, normed_t = call(
        norm_kernel,
        dims,
        [(gain, VMEM)] + [(a, ANY) for a in xs],
        [norm + (ANY,), ((width, total), BF16, ANY)],
        [blocks, norm, ((width, total), BF16)],
        [depth, 2 * depth],
        1000,
    )
    normed, pos, *parts = lax.optimization_barrier([normed, pos] + parts)
    w_near = jnp.stack(parts, axis=0)
    w_far = swap(w_near, "core", 2, 1)

    turned_f32 = ((span, total), F32)
    saved = [rows, rows, rows, turned, turned_f32, stats] + [in_weights] * 3 + [out_weights]
    query, keys, values, keys_t, att_t, lse, wq, wk, wv, wo, *outs = call(
        forward_kernel,
        dims,
        [(pos, SMEM), (w_near, VMEM), (w_far, VMEM), (normed, ANY)],
        [s + (ANY,) for s in saved + [block] * depth],
        [norm, rows, rows, rows, turned, turned, turned_f32, stats]
        + [in_weights] * 3
        + [out_weights, blocks],
        [1, len(saved) + depth],
        8 * pass_flops,
        44,
    )

    packed = (zs, depth, shard, 4 * span)
    near, far, *dns = call(
        backward_kernel,
        dims,
        [(pos, SMEM)]
        + [(a, ANY) for a in gs + [wo, query, keys, values, keys_t, lse, normed_t]]
        + [(a, ANY) for a in (att_t, wq, wk, wv)],
        [(packed, BF16, VMEM)] * 2 + [s + (ANY,) for s in [block] * 3 + [halved] * 2],
        [norm, out_weights, rows, rows, rows, turned, stats, ((width, total), BF16)]
        + [turned_f32, in_weights, in_weights, in_weights]
        + [rows, stats, turned_f32]
        + [((total, span), F32)] * 2
        + [((span, width), F32), norm],
        [depth + 11, depth + 1],
        24 * pass_flops,
    )

    outs = [outs[0]] + [swap(outs[k], "depth", depth, k) for k in range(1, depth)]
    near, far, dns, outs = lax.optimization_barrier((near, far, dns, outs))

    far = swap(far, "core", 2, 1)
    dn0, dn1, dn2, dn3_top, dn3_bottom = dns
    top, bottom = swap(dn3_top, "depth", depth, 1), swap(dn3_bottom, "depth", depth, 2)
    sums = [near[k].astype(F32) + far[k].astype(F32) for k in range(zs)]
    low = [swap(sums[k].astype(BF16), "z", zs, k) for k in range(1, zs)]
    low[0], top, bottom = lax.optimization_barrier((low[0], top, bottom))
    dn2 = dn2.astype(F32) + jnp.concatenate([top, jnp.zeros_like(top)], axis=0).astype(F32)
    dn1 = dn1.astype(F32) + jnp.concatenate([jnp.zeros_like(bottom), bottom], axis=0).astype(F32)
    dn1 = swap(dn1.astype(BF16), "depth", depth, 1)
    dn2 = swap(dn2.astype(BF16), "depth", depth, 2)
    low[0], outs = lax.optimization_barrier((low[0], outs))
    final_result = (x.astype(F32) + sum(o.astype(F32) for o in outs)).astype(BF16)
    acc = sums[0] + sum(p.astype(F32) for p in low)
    parts = [
        swap(acc[k, :, : 3 * span].astype(BF16), "depth", depth, k) for k in range(1, depth)
    ]
    alignment = call(
        align_kernel,
        dims,
        [(a, VMEM) for a in (gain, x, upstream, dn0, dn1, dn2)],
        [block + (VMEM,)],
        [],
        [],
        1000 * total * width,
        16,
    )[0]
    alignment, *parts = lax.optimization_barrier([alignment] + parts)
    first_row = (lax.axis_index("depth") * res + pos[0] * 2 + pos[1]) * shard
    own_gain = lax.dynamic_slice(gain, (0, first_row), (1, shard))
    grad_query, grad_key, grad_value, grad_out, gain_rows = call(
        finish_kernel,
        dims,
        [(pos, SMEM)]
        + [(a, VMEM) for a in [own_gain, w_query, w_key, w_value, acc] + parts],
        [((shard, width), F32, VMEM)] * 4 + [((1, shard), F32, VMEM)],
        [],
        [],
        1000,
        16,
    )
    return (
        final_result.reshape(homologs, 1, width),
        alignment.reshape(homologs, 1, width),
        grad_query,
        grad_key,
        grad_value,
        grad_out,
        gain_rows.reshape(shard),
    )


def solution(mesh):
    depth, res = mesh.shape["depth"], mesh.shape["res"]
    powers = depth & (depth - 1) == 0 and res & (res - 1) == 0 and res > 1
    if powers and depth == 4 and res >= 4 and HEADS % depth == 0:
        axes = ("depth", "z", "core")
        mesh = Mesh(mesh.devices.reshape(depth, res // 2, 2), axes)
        res_axes, run = ("z", "core"), functools.partial(head_body, depth, res)
    else:
        axes = ("depth", "res")
        res_axes, run = ("res",), general_body

    def body(*args):
        if args[0].shape[1] != 1:
            return general_body(*args, axes=axes)
        return run(*args)

    rows = P("depth", res_axes, None)
    weight = P(axes, None)
    return jax.shard_map(
        body,
        mesh=mesh,
        in_specs=(rows, P(), weight, weight, weight, weight, rows),
        out_specs=(rows, rows, weight, weight, weight, weight, P(axes)),
        check_vma=False,
    )
```

```python
import functools

import jax
import jax.numpy as jnp
from jax import lax
from jax.experimental import pallas as pl
from jax.experimental.pallas import tpu as pltpu
from jax.sharding import Mesh, PartitionSpec as P

HEADS = 12
HEAD_DIM = 64


def standardize_entries(family_activity, rescale_factor):
    payload_entries = family_activity.astype(jnp.float32)
    centered = payload_entries - jnp.mean(payload_entries, axis=-1, keepdims=True)
    reciprocal_spread = lax.rsqrt(jnp.mean(centered * centered, axis=-1, keepdims=True) + 1e-05)
    standardized_entries = centered * reciprocal_spread
    return (
        (standardized_entries * rescale_factor).astype(jnp.bfloat16),
        standardized_entries,
        reciprocal_spread,
    )


def project(rows, weight, factor):
    return (factor * jnp.dot(rows, weight, preferred_element_type=jnp.float32)).astype(jnp.bfloat16)


def to_heads(array):
    count, cols = (array.shape[0], array.shape[1])
    return jnp.transpose(array.reshape(count, cols, HEADS, HEAD_DIM), (1, 2, 0, 3)).reshape(
        cols * HEADS, count, HEAD_DIM
    )


def from_heads(array, cols):
    count = array.shape[1]
    return jnp.transpose(array.reshape(cols, HEADS, count, HEAD_DIM), (2, 0, 1, 3)).reshape(
        count, cols, HEADS * HEAD_DIM
    )


def head_pass(query, keys, payload_entries, d_att):
    scale = HEAD_DIM ** (-0.5)
    scores = jnp.dot(query, keys.T, preferred_element_type=jnp.float32)
    probs = jax.nn.softmax(scores, axis=-1)
    probs_b = probs.astype(jnp.bfloat16)
    mixed_homologs = jnp.dot(probs_b, payload_entries, preferred_element_type=jnp.float32).astype(
        jnp.bfloat16
    )
    d_probs = jnp.dot(d_att, payload_entries.T, preferred_element_type=jnp.float32)
    d_scores = probs * (d_probs - jnp.sum(probs * d_probs, axis=-1, keepdims=True))
    d_scores_b = d_scores.astype(jnp.bfloat16)
    d_query = (scale * jnp.dot(d_scores_b, keys, preferred_element_type=jnp.float32)).astype(
        jnp.bfloat16
    )
    key_part = jnp.einsum("st,sd->td", d_scores_b, query, preferred_element_type=jnp.float32)
    value_part = jnp.einsum("st,sd->td", probs_b, d_att, preferred_element_type=jnp.float32)
    return (mixed_homologs, d_query, key_part, value_part)


def general_body(
    family_activity,
    rescale_factor,
    asking_weights,
    lookup_weights,
    payload_weights,
    exit_weights,
    upstream_adjoint,
    axes=("depth", "res"),
):
    query_weight, key_weight, value_weight, output_matrix = (
        lax.all_gather(asking_weights, axes, axis=0, tiled=True),
        lax.all_gather(lookup_weights, axes, axis=0, tiled=True),
        lax.all_gather(payload_weights, axes, axis=0, tiled=True),
        lax.all_gather(exit_weights, axes, axis=0, tiled=True),
    )
    homologs_each_shard, positions_each_shard, embed_span = family_activity.shape
    standardized_source, standardized_entries, reciprocal_spread = standardize_entries(
        family_activity, rescale_factor
    )
    query = project(standardized_source, query_weight, HEAD_DIM ** (-0.5))
    keys = project(standardized_source, key_weight, 1.0)
    payload_entries = project(standardized_source, value_weight, 1.0)
    keys_all, values_all = (
        lax.all_gather(keys, "depth", axis=0, tiled=True),
        lax.all_gather(payload_entries, "depth", axis=0, tiled=True),
    )
    d_att = jnp.dot(upstream_adjoint, output_matrix.T, preferred_element_type=jnp.float32).astype(
        jnp.bfloat16
    )

    def per_head(items):
        return head_pass(items[0], items[1], items[2], items[3])

    mixed_homologs, d_query, key_part, value_part = lax.map(
        per_head, (to_heads(query), to_heads(keys_all), to_heads(values_all), to_heads(d_att))
    )
    mixed_homologs = from_heads(mixed_homologs, positions_each_shard)
    d_query = from_heads(d_query, positions_each_shard)
    key_part = from_heads(key_part, positions_each_shard)
    value_part = from_heads(value_part, positions_each_shard)
    rows = homologs_each_shard * positions_each_shard
    normed_rows = standardized_source.reshape(rows, embed_span)
    part_query = jnp.dot(
        normed_rows.T, d_query.reshape(rows, embed_span), preferred_element_type=jnp.float32
    )
    part_out = jnp.dot(
        mixed_homologs.reshape(rows, embed_span).T,
        upstream_adjoint.reshape(rows, embed_span),
        preferred_element_type=jnp.float32,
    )
    stacked = jnp.stack([key_part, value_part], axis=2).astype(jnp.bfloat16)
    summed = (
        lax.psum_scatter(stacked, "depth", scatter_dimension=0, tiled=True)
        .astype(jnp.float32)
        .astype(jnp.bfloat16)
    )
    d_keys = summed[:, :, 0, :]
    d_values = summed[:, :, 1, :]
    final_result = (
        family_activity.astype(jnp.float32)
        + jnp.dot(mixed_homologs, output_matrix, preferred_element_type=jnp.float32)
    ).astype(jnp.bfloat16)
    part_key = jnp.dot(
        normed_rows.T, d_keys.reshape(rows, embed_span), preferred_element_type=jnp.float32
    )
    part_value = jnp.dot(
        normed_rows.T, d_values.reshape(rows, embed_span), preferred_element_type=jnp.float32
    )
    d_normed = jnp.dot(d_query, query_weight.T, preferred_element_type=jnp.float32)
    d_normed = d_normed + jnp.dot(d_keys, key_weight.T, preferred_element_type=jnp.float32)
    d_normed = d_normed + jnp.dot(d_values, value_weight.T, preferred_element_type=jnp.float32)
    part_gain = jnp.sum((d_normed * standardized_entries).reshape(rows, embed_span), axis=0)
    unit_gradient = d_normed * rescale_factor
    alignment_gradient = upstream_adjoint.astype(jnp.float32) + reciprocal_spread * (
        unit_gradient
        - jnp.mean(unit_gradient, axis=-1, keepdims=True)
        - standardized_entries
        * jnp.mean(unit_gradient * standardized_entries, axis=-1, keepdims=True)
    )
    query_gradient, key_gradient, value_gradient, output_gradient, gain_gradient = (
        lax.psum_scatter(part_query, axes, scatter_dimension=0, tiled=True),
        lax.psum_scatter(part_key, axes, scatter_dimension=0, tiled=True),
        lax.psum_scatter(part_value, axes, scatter_dimension=0, tiled=True),
        lax.psum_scatter(part_out, axes, scatter_dimension=0, tiled=True),
        lax.psum_scatter(part_gain, axes, scatter_dimension=0, tiled=True),
    )
    return (
        final_result,
        alignment_gradient.astype(jnp.bfloat16),
        query_gradient,
        key_gradient,
        value_gradient,
        output_gradient,
        gain_gradient,
    )


F32, BF16 = jnp.float32, jnp.bfloat16
SCALE = HEAD_DIM ** (-0.5)


def swap(value, axis, size, bits):
    return lax.ppermute(value, axis, [(i, i ^ bits) for i in range(size)])


def dot(a, b, contract=(1, 0)):
    return lax.dot_general(
        a, b, (((contract[0],), (contract[1],)), ((), ())), preferred_element_type=F32
    )


def unit_rows(x):
    x = x.astype(F32)
    centered = x - jnp.mean(x, axis=-1, keepdims=True)
    inverse = lax.rsqrt(jnp.mean(centered * centered, axis=-1, keepdims=True) + 1e-05)
    return centered * inverse, inverse


def head_masks(span):
    lane = lax.broadcasted_iota(jnp.int32, (8, span), 1)
    return [
        ((lane >= at) & (lane < at + HEAD_DIM)).astype(F32)[0:1].astype(BF16)
        for at in range(0, span, HEAD_DIM)
    ]


def fetch(pairs, sems):
    copies = [pltpu.make_async_copy(src, dst, sems.at[i]) for i, (src, dst) in enumerate(pairs)]
    for copy in copies:
        copy.start()
    return copies


class Sender:
    def __init__(self, sems):
        self.sems, self.copies = sems, []

    def send(self, src, dst):
        copy = pltpu.make_async_copy(src, dst, self.sems.at[len(self.copies)])
        copy.start()
        self.copies.append(copy)

    def finish(self):
        for copy in self.copies:
            copy.wait()


def pack_kernel(dims, w_query, w_key, w_value, w_out, out, out_cut):
    depth, zs, shard, block, span = dims
    for d in range(depth):
        lanes = slice(d * span, (d + 1) * span)
        for i, w in enumerate((w_query, w_key, w_value)):
            out[d, :, i * span : (i + 1) * span] = w[:, lanes]
        out_cut[d] = w_out[:, lanes]


def norm_kernel(dims, *refs):
    depth, zs, shard, block, span = dims
    gain, xs_h, refs = refs[0], refs[1 : 1 + depth], refs[1 + depth :]
    normed_h, normed_t_h, xs, normed, normed_t, in_sems, out_sems = refs
    copies = fetch([(xs_h[j], xs.at[j]) for j in range(depth)], in_sems)
    sender = Sender(out_sems)
    for j in range(depth):
        copies[j].wait()
        unit, _ = unit_rows(xs[j])
        rows = pl.ds(j * block, block)
        wide = unit * gain[...]
        normed[rows, :] = wide.astype(BF16)
        sender.send(normed.at[rows], normed_h.at[rows])
        normed_t[:, rows] = jnp.transpose(wide).astype(BF16)
        sender.send(normed_t.at[:, rows], normed_t_h.at[:, rows])
    sender.finish()


def forward_kernel(dims, *refs):
    depth, zs, shard, block, span = dims
    heads = span // HEAD_DIM
    pos, w_near, w_far, normed_h = refs[:4]
    query_h, keys_h, values_h, keys_t_h, att_t_h, lse_h, wq_h, wk_h, wv_h, w_out_h = refs[4:14]
    outs_h, refs = refs[14 : 14 + depth], refs[14 + depth :]
    normed, query, keys, values, keys_t, values_t, att_t, lse = refs[:8]
    wq, wk, wv, w_out, outs, in_sems, out_sems = refs[8:]
    copies = fetch([(normed_h, normed)], in_sems)
    sender = Sender(out_sems)

    own_z, first = pos[0], pos[1] == 0
    for z in range(zs):
        for d in range(depth):
            near, far = w_near[z ^ own_z, d].astype(F32), w_far[z ^ own_z, d].astype(F32)
            both = jnp.concatenate(
                [jnp.where(first, near, far), jnp.where(first, far, near)], axis=0
            ).astype(BF16)
            rows = slice((d * zs + z) * 2 * shard, (d * zs + z + 1) * 2 * shard)
            for i, w in enumerate((wq, wk, wv)):
                w[rows, :] = both[:, i * span : (i + 1) * span]
            rows = slice(z * 2 * shard, (z + 1) * 2 * shard)
            w_out[rows, d * span : (d + 1) * span] = both[:, 3 * span :]
    for src, dst in ((wq, wq_h), (wk, wk_h), (wv, wv_h), (w_out, w_out_h)):
        sender.send(src, dst)
    copies[0].wait()

    query[...] = (SCALE * dot(normed[...], wq[...])).astype(BF16)
    key = dot(normed[...], wk[...])
    keys[...] = key.astype(BF16)
    keys_t[...] = jnp.transpose(key).astype(BF16)
    value = dot(normed[...], wv[...])
    values[...] = value.astype(BF16)
    values_t[...] = jnp.transpose(value).astype(BF16)
    for src, dst in ((query, query_h), (keys, keys_h), (values, values_h), (keys_t, keys_t_h)):
        sender.send(src, dst)

    masks = head_masks(span)

    units = [(j, h) for j in range(depth) for h in range(heads)]

    def score(j, h):
        return dot(keys[...], query[j * block : (j + 1) * block, :] * masks[h], (1, 1))

    ready = [score(*unit) for unit in units[:2]]
    for i, (j, h) in enumerate(units):
        cols, lanes = slice(j * block, (j + 1) * block), slice(h * HEAD_DIM, (h + 1) * HEAD_DIM)
        scores = ready.pop(0)
        top = jnp.max(scores, axis=0, keepdims=True)
        e = jnp.exp(scores - top)
        total = jnp.sum(e, axis=0, keepdims=True)
        if i + 2 < len(units):
            ready.append(score(*units[i + 2]))
        att_t[lanes, cols] = dot(values_t[lanes, :], e.astype(BF16)) * (1.0 / total)
        lse[h, :, cols] = top + jnp.log(total)
    sender.send(att_t, att_t_h)
    sender.send(lse, lse_h)
    att = jnp.transpose(att_t[...]).astype(BF16)
    for j in range(depth):
        outs[j] = dot(att[j * block : (j + 1) * block], w_out[...]).astype(BF16)
        sender.send(outs.at[j], outs_h[j])
    sender.finish()


def backward_kernel(dims, *refs):
    depth, zs, shard, block, span = dims
    heads = span // HEAD_DIM
    pos, refs = refs[0], refs[1:]
    gs_h, refs = refs[:depth], refs[depth:]
    (w_out_h, query_h, keys_h, values_h, keys_t_h, lse_h, normed_t_h, att_t_h) = refs[:8]
    (wq_h, wk_h, wv_h, near, far), refs = refs[8:13], refs[13:]
    dns_h, refs = refs[: depth + 1], refs[depth + 1 :]
    (gs, w_out, query, keys, values, keys_t, lse, normed_t, att_t, wq, wk, wv) = refs[:12]
    (d_att, delta, d_query_t, d_keys, d_values, grad_out, dns, in_sems, out_sems) = refs[12:]
    copies = fetch(
        [(w_out_h, w_out)]
        + [(gs_h[j], gs.at[pl.ds(j * block, block)]) for j in range(depth)]
        + [
            (att_t_h, att_t),
            (keys_h, keys),
            (query_h, query),
            (values_h, values),
            (lse_h, lse),
            (keys_t_h, keys_t),
            (normed_t_h, normed_t),
            (wq_h, wq),
            (wk_h, wk),
            (wv_h, wv),
        ],
        in_sems,
    )
    loaded, later = 7 + depth, copies[7 + depth :]

    d_keys[...] = jnp.zeros_like(d_keys)
    d_values[...] = jnp.zeros_like(d_values)
    for copy in copies[: 2 + depth]:
        copy.wait()
    part = dot(gs[...], w_out[...], (1, 1)).astype(BF16)
    d_att[...] = part
    product = jnp.transpose(part.astype(F32)) * att_t[...]
    for h in range(heads):
        delta[h] = jnp.sum(product[h * HEAD_DIM : (h + 1) * HEAD_DIM], axis=0, keepdims=True)
    for copy in copies[2 + depth : loaded]:
        copy.wait()
    masks = head_masks(span)

    def step(j, _):
        cols = pl.ds(pl.multiple_of(j * block, block), block)
        q_block, g_block = query[cols, :], d_att[cols, :]
        qs = [q_block * m for m in masks]
        ds = [g_block * m for m in masks]

        def pair(h):
            return dot(keys[...], qs[h], (1, 1)), dot(values[...], ds[h], (1, 1))

        pairs = [pair(h) for h in range(min(2, heads))]
        for h in range(heads):
            scores, d_probs = pairs[h]
            probs = jnp.exp(scores - lse[h, :, cols])
            d_scores = (probs * (d_probs - delta[h, :, cols])).astype(BF16)
            if h + 2 < heads:
                pairs.append(pair(h + 2))
            values_add = dot(probs.astype(BF16), ds[h])
            keys_add = dot(d_scores, qs[h])
            value_part = values_add if h == 0 else value_part + values_add
            key_part = keys_add if h == 0 else key_part + keys_add
            lanes = slice(h * HEAD_DIM, (h + 1) * HEAD_DIM)
            d_query_t[lanes, cols] = SCALE * dot(keys_t[lanes, :], d_scores)
        d_values[...] += value_part.astype(BF16).astype(F32)
        d_keys[...] += key_part.astype(BF16).astype(F32)
        return 0

    lax.fori_loop(0, depth, step, 0)
    for copy in later:
        copy.wait()
    d_query = jnp.transpose(d_query_t[...]).astype(BF16)
    d_key, d_value = d_keys[...].astype(BF16), d_values[...].astype(BF16)
    sender = Sender(out_sems)
    for i in range(0, depth, 2):
        rows = slice(i * block, (i + 2) * block)
        d_normed = dot(d_query[rows], wq[...], (1, 1))
        d_normed = d_normed + dot(d_key[rows], wk[...], (1, 1))
        d_normed = d_normed + dot(d_value[rows], wv[...], (1, 1))
        dns[rows, :] = d_normed.astype(BF16)
        for j in (i, i + 1):
            if j < depth - 1:
                sender.send(dns.at[pl.ds(j * block, block)], dns_h[j])
            else:
                half = block // 2
                sender.send(dns.at[pl.ds(j * block, half)], dns_h[j])
                sender.send(dns.at[pl.ds(j * block + half, half)], dns_h[j + 1])

    grad_out[...] = dot(att_t[...].astype(BF16), gs[...])
    grads = [dot(normed_t[...], d) for d in (d_query, d_key, d_value)]
    own_z, first, own_d = pos[0], pos[1] == 0, pos[2]
    for d in range(depth):
        for z in range(zs):
            sides = []
            for c in range(2):
                row, row_out = ((d * zs + z) * 2 + c) * shard, (z * 2 + c) * shard
                sides.append(
                    [g[row : row + shard] for g in grads]
                    + [grad_out[row_out : row_out + shard, d * span : (d + 1) * span]]
                )
            at = 0
            for one, two in zip(*sides):
                lanes = slice(at, at + one.shape[1])
                at += one.shape[1]
                near[z ^ own_z, d ^ own_d, :, lanes] = jnp.where(first, one, two).astype(BF16)
                far[z ^ own_z, d ^ own_d, :, lanes] = jnp.where(first, two, one).astype(BF16)
    sender.finish()


def align_kernel(dims, gain, x, upstream, *refs):
    dns, out = refs[:-1], refs[-1]
    d_normed = dns[0][...].astype(F32)
    for part in dns[1:]:
        d_normed = d_normed + part[...].astype(F32)
    unit, inverse = unit_rows(x[...])
    d_unit = d_normed * gain[...]
    out[...] = (
        upstream[...].astype(F32)
        + inverse
        * (
            d_unit
            - jnp.mean(d_unit, axis=-1, keepdims=True)
            - unit * jnp.mean(d_unit * unit, axis=-1, keepdims=True)
        )
    ).astype(BF16)


def finish_kernel(dims, *refs):
    depth, zs, shard, block, span = dims
    pos, gain, weights, acc, refs = refs[0], refs[1], refs[2:5], refs[5], refs[6:]
    parts, outs = refs[: depth - 1], refs[depth - 1 :]
    own_d = pos[2]
    blocks = [acc[0][:, : 3 * span]] + [p[...].astype(F32) for p in parts]
    for d in range(depth):
        lanes = slice(d * span, (d + 1) * span)
        total = blocks[0]
        for k in range(1, depth):
            total = jnp.where((d ^ own_d) == k, blocks[k], total)
        for i in range(3):
            outs[i][:, lanes] = total[:, i * span : (i + 1) * span]
        outs[3][:, lanes] = acc[d ^ own_d][:, 3 * span :]
    column = weights[0][...].astype(F32) * outs[0][...]
    for w, grad in zip(weights[1:], outs[1:3]):
        column = column + w[...].astype(F32) * grad[...]
    column = jnp.sum(column, axis=1, keepdims=True)
    wide = jnp.concatenate([column, jnp.zeros((128 - shard, 1), F32)], axis=0)
    row = jnp.transpose(jnp.broadcast_to(wide, (128, 128)))[0:1, :shard]
    outs[4][...] = row / gain[...]


VMEM, ANY, SMEM = pltpu.VMEM, pl.ANY, pltpu.SMEM


def call(kernel, dims, ins, outs, scratch, sems, flops, mib=56):
    args = [a for a, _ in ins]
    shapes = [jax.ShapeDtypeStruct(shape, kind) for shape, kind, _ in outs]
    size = sum(a.size * a.dtype.itemsize for a in args + shapes)
    return pl.pallas_call(
        functools.partial(kernel, dims),
        out_shape=shapes,
        in_specs=[pl.BlockSpec(memory_space=space) for _, space in ins],
        out_specs=[pl.BlockSpec(memory_space=space) for _, _, space in outs],
        scratch_shapes=[pltpu.VMEM(shape, kind) for shape, kind in scratch]
        + [pltpu.SemaphoreType.DMA((n,)) for n in sems],
        compiler_params=pltpu.CompilerParams(vmem_limit_bytes=mib * 1024 * 1024),
        cost_estimate=pl.CostEstimate(flops=flops, bytes_accessed=size, transcendentals=0),
    )(*args)


def head_body(depth, res, *args):
    x, gain, w_query, w_key, w_value, w_out, upstream = args
    homologs, _, width = x.shape
    span, zs = width // depth, res // 2
    shard = w_query.shape[0]
    total, heads = homologs * depth, span // HEAD_DIM
    dims = (depth, zs, shard, homologs, span)
    x = x.reshape(homologs, width)
    upstream = upstream.reshape(homologs, width)
    gain = gain.reshape(1, width)
    pos = jnp.stack([lax.axis_index(a) for a in ("z", "core", "depth")]).astype(jnp.int32)

    xs = [x] + [swap(x, "depth", depth, k) for k in range(1, depth - 1)]

    packed, out_cut = call(
        pack_kernel,
        dims,
        [(w, VMEM) for w in (w_query, w_key, w_value, w_out)],
        [((depth, shard, 3 * span), BF16, VMEM), ((depth, shard, span), BF16, VMEM)],
        [],
        [],
        1000,
    )
    mine = lax.all_to_all(packed, "depth", 0, 0, tiled=True)
    mine = jnp.concatenate([mine, out_cut], axis=2)
    mine, *xs = lax.optimization_barrier([mine] + xs)
    xs.append(swap(xs[0], "depth", depth, depth - 1))
    parts = [mine] + [swap(mine, "z", zs, k) for k in range(1, zs)]
    gs = [upstream] + [swap(upstream, "depth", depth, k) for k in range(1, depth)]

    rows, turned = ((total, span), BF16), ((span, total), BF16)
    half = homologs // 2
    block, halved = ((homologs, width), BF16), ((half, width), BF16)
    blocks = ((depth, homologs, width), BF16)
    norm, stats = ((total, width), BF16), ((heads, 1, total), F32)
    in_weights, out_weights = ((width, span), BF16), ((span, width), BF16)
    pass_flops = 2 * total * total * span
    normed, normed_t = call(
        norm_kernel,
        dims,
        [(gain, VMEM)] + [(a, ANY) for a in xs],
        [norm + (ANY,), ((width, total), BF16, ANY)],
        [blocks, norm, ((width, total), BF16)],
        [depth, 2 * depth],
        1000,
    )
    first_row = (lax.axis_index("depth") * res + pos[0] * 2 + pos[1]) * shard
    own_gain = lax.dynamic_slice(gain, (0, first_row), (1, shard))
    normed, pos, own_gain, *parts = lax.optimization_barrier([normed, pos, own_gain] + parts)
    w_near = jnp.stack(parts, axis=0)
    w_far = swap(w_near, "core", 2, 1)

    turned_f32 = ((span, total), F32)
    saved = [rows, rows, rows, turned, turned_f32, stats] + [in_weights] * 3 + [out_weights]
    query, keys, values, keys_t, att_t, lse, wq, wk, wv, wo, *outs = call(
        forward_kernel,
        dims,
        [(pos, SMEM), (w_near, VMEM), (w_far, VMEM), (normed, ANY)],
        [s + (ANY,) for s in saved + [block] * depth],
        [norm, rows, rows, rows, turned, turned, turned_f32, stats]
        + [in_weights] * 3
        + [out_weights, blocks],
        [1, len(saved) + depth],
        8 * pass_flops,
    )

    packed = (zs, depth, shard, 4 * span)
    near, far, *dns = call(
        backward_kernel,
        dims,
        [(pos, SMEM)]
        + [(a, ANY) for a in gs + [wo, query, keys, values, keys_t, lse, normed_t]]
        + [(a, ANY) for a in (att_t, wq, wk, wv)],
        [(packed, BF16, VMEM)] * 2 + [s + (ANY,) for s in [block] * 3 + [halved] * 2],
        [norm, out_weights, rows, rows, rows, turned, stats, ((width, total), BF16)]
        + [turned_f32, in_weights, in_weights, in_weights]
        + [rows, stats, turned_f32]
        + [((total, span), F32)] * 2
        + [((span, width), F32), norm],
        [depth + 11, depth + 1],
        24 * pass_flops,
    )

    outs = [outs[0]] + [swap(outs[k], "depth", depth, k) for k in range(1, depth)]
    near, far, dns, outs = lax.optimization_barrier((near, far, dns, outs))

    far = swap(far, "core", 2, 1)
    dn0, dn1, dn2, dn3_top, dn3_bottom = dns
    top, bottom = swap(dn3_top, "depth", depth, 1), swap(dn3_bottom, "depth", depth, 2)
    sums = [near[k].astype(F32) + far[k].astype(F32) for k in range(1, zs)]
    low = [swap(part.astype(BF16), "z", zs, k + 1) for k, part in enumerate(sums)]
    low[0], top, bottom, outs = lax.optimization_barrier((low[0], top, bottom, outs))
    dn2 = dn2.astype(F32) + jnp.concatenate([top, jnp.zeros_like(top)], axis=0).astype(F32)
    dn1 = dn1.astype(F32) + jnp.concatenate([jnp.zeros_like(bottom), bottom], axis=0).astype(F32)
    final_result = (x.astype(F32) + sum(o.astype(F32) for o in outs)).astype(BF16)
    dn1, dn2, final_result = lax.optimization_barrier(
        (dn1.astype(BF16), dn2.astype(BF16), final_result)
    )
    dn1, dn2 = swap(dn1, "depth", depth, 1), swap(dn2, "depth", depth, 2)
    acc = near[0].astype(F32) + far[0].astype(F32) + sum(p.astype(F32) for p in low)
    parts = [
        swap(acc[k, :, : 3 * span].astype(BF16), "depth", depth, k) for k in range(1, depth)
    ]
    alignment = call(
        align_kernel,
        dims,
        [(a, VMEM) for a in (gain, x, upstream, dn0, dn1, dn2)],
        [block + (VMEM,)],
        [],
        [],
        1000 * total * width,
        16,
    )[0]
    alignment, *parts = lax.optimization_barrier([alignment] + parts)
    grad_query, grad_key, grad_value, grad_out, gain_rows = call(
        finish_kernel,
        dims,
        [(pos, SMEM)]
        + [(a, VMEM) for a in [own_gain, w_query, w_key, w_value, acc] + parts],
        [((shard, width), F32, VMEM)] * 4 + [((1, shard), F32, VMEM)],
        [],
        [],
        1000,
        16,
    )
    return (
        final_result.reshape(homologs, 1, width),
        alignment.reshape(homologs, 1, width),
        grad_query,
        grad_key,
        grad_value,
        grad_out,
        gain_rows.reshape(shard),
    )


def solution(mesh):
    depth, res = mesh.shape["depth"], mesh.shape["res"]
    powers = depth & (depth - 1) == 0 and res & (res - 1) == 0 and res > 1
    if powers and depth == 4 and res >= 4 and HEADS % depth == 0:
        axes = ("depth", "z", "core")
        mesh = Mesh(mesh.devices.reshape(depth, res // 2, 2), axes)
        res_axes, run = ("z", "core"), functools.partial(head_body, depth, res)
    else:
        axes = ("depth", "res")
        res_axes, run = ("res",), general_body

    def body(*args):
        if args[0].shape[1] != 1:
            return general_body(*args, axes=axes)
        return run(*args)

    rows = P("depth", res_axes, None)
    weight = P(axes, None)
    return jax.shard_map(
        body,
        mesh=mesh,
        in_specs=(rows, P(), weight, weight, weight, weight, rows),
        out_specs=(rows, rows, weight, weight, weight, weight, P(axes)),
        check_vma=False,
    )
```

```python
import functools

import jax
import jax.numpy as jnp
from jax import lax
from jax.experimental import pallas as pl
from jax.experimental.pallas import tpu as pltpu
from jax.sharding import Mesh, PartitionSpec as P

HEADS = 12
HEAD_DIM = 64


def standardize_entries(family_activity, rescale_factor):
    payload_entries = family_activity.astype(jnp.float32)
    centered = payload_entries - jnp.mean(payload_entries, axis=-1, keepdims=True)
    reciprocal_spread = lax.rsqrt(jnp.mean(centered * centered, axis=-1, keepdims=True) + 1e-05)
    standardized_entries = centered * reciprocal_spread
    return (
        (standardized_entries * rescale_factor).astype(jnp.bfloat16),
        standardized_entries,
        reciprocal_spread,
    )


def project(rows, weight, factor):
    return (factor * jnp.dot(rows, weight, preferred_element_type=jnp.float32)).astype(jnp.bfloat16)


def to_heads(array):
    count, cols = (array.shape[0], array.shape[1])
    return jnp.transpose(array.reshape(count, cols, HEADS, HEAD_DIM), (1, 2, 0, 3)).reshape(
        cols * HEADS, count, HEAD_DIM
    )


def from_heads(array, cols):
    count = array.shape[1]
    return jnp.transpose(array.reshape(cols, HEADS, count, HEAD_DIM), (2, 0, 1, 3)).reshape(
        count, cols, HEADS * HEAD_DIM
    )


def head_pass(query, keys, payload_entries, d_att):
    scale = HEAD_DIM ** (-0.5)
    scores = jnp.dot(query, keys.T, preferred_element_type=jnp.float32)
    probs = jax.nn.softmax(scores, axis=-1)
    probs_b = probs.astype(jnp.bfloat16)
    mixed_homologs = jnp.dot(probs_b, payload_entries, preferred_element_type=jnp.float32).astype(
        jnp.bfloat16
    )
    d_probs = jnp.dot(d_att, payload_entries.T, preferred_element_type=jnp.float32)
    d_scores = probs * (d_probs - jnp.sum(probs * d_probs, axis=-1, keepdims=True))
    d_scores_b = d_scores.astype(jnp.bfloat16)
    d_query = (scale * jnp.dot(d_scores_b, keys, preferred_element_type=jnp.float32)).astype(
        jnp.bfloat16
    )
    key_part = jnp.einsum("st,sd->td", d_scores_b, query, preferred_element_type=jnp.float32)
    value_part = jnp.einsum("st,sd->td", probs_b, d_att, preferred_element_type=jnp.float32)
    return (mixed_homologs, d_query, key_part, value_part)


def general_body(
    family_activity,
    rescale_factor,
    asking_weights,
    lookup_weights,
    payload_weights,
    exit_weights,
    upstream_adjoint,
    axes=("depth", "res"),
):
    query_weight, key_weight, value_weight, output_matrix = (
        lax.all_gather(asking_weights, axes, axis=0, tiled=True),
        lax.all_gather(lookup_weights, axes, axis=0, tiled=True),
        lax.all_gather(payload_weights, axes, axis=0, tiled=True),
        lax.all_gather(exit_weights, axes, axis=0, tiled=True),
    )
    homologs_each_shard, positions_each_shard, embed_span = family_activity.shape
    standardized_source, standardized_entries, reciprocal_spread = standardize_entries(
        family_activity, rescale_factor
    )
    query = project(standardized_source, query_weight, HEAD_DIM ** (-0.5))
    keys = project(standardized_source, key_weight, 1.0)
    payload_entries = project(standardized_source, value_weight, 1.0)
    keys_all, values_all = (
        lax.all_gather(keys, "depth", axis=0, tiled=True),
        lax.all_gather(payload_entries, "depth", axis=0, tiled=True),
    )
    d_att = jnp.dot(upstream_adjoint, output_matrix.T, preferred_element_type=jnp.float32).astype(
        jnp.bfloat16
    )

    def per_head(items):
        return head_pass(items[0], items[1], items[2], items[3])

    mixed_homologs, d_query, key_part, value_part = lax.map(
        per_head, (to_heads(query), to_heads(keys_all), to_heads(values_all), to_heads(d_att))
    )
    mixed_homologs = from_heads(mixed_homologs, positions_each_shard)
    d_query = from_heads(d_query, positions_each_shard)
    key_part = from_heads(key_part, positions_each_shard)
    value_part = from_heads(value_part, positions_each_shard)
    rows = homologs_each_shard * positions_each_shard
    normed_rows = standardized_source.reshape(rows, embed_span)
    part_query = jnp.dot(
        normed_rows.T, d_query.reshape(rows, embed_span), preferred_element_type=jnp.float32
    )
    part_out = jnp.dot(
        mixed_homologs.reshape(rows, embed_span).T,
        upstream_adjoint.reshape(rows, embed_span),
        preferred_element_type=jnp.float32,
    )
    stacked = jnp.stack([key_part, value_part], axis=2).astype(jnp.bfloat16)
    summed = (
        lax.psum_scatter(stacked, "depth", scatter_dimension=0, tiled=True)
        .astype(jnp.float32)
        .astype(jnp.bfloat16)
    )
    d_keys = summed[:, :, 0, :]
    d_values = summed[:, :, 1, :]
    final_result = (
        family_activity.astype(jnp.float32)
        + jnp.dot(mixed_homologs, output_matrix, preferred_element_type=jnp.float32)
    ).astype(jnp.bfloat16)
    part_key = jnp.dot(
        normed_rows.T, d_keys.reshape(rows, embed_span), preferred_element_type=jnp.float32
    )
    part_value = jnp.dot(
        normed_rows.T, d_values.reshape(rows, embed_span), preferred_element_type=jnp.float32
    )
    d_normed = jnp.dot(d_query, query_weight.T, preferred_element_type=jnp.float32)
    d_normed = d_normed + jnp.dot(d_keys, key_weight.T, preferred_element_type=jnp.float32)
    d_normed = d_normed + jnp.dot(d_values, value_weight.T, preferred_element_type=jnp.float32)
    part_gain = jnp.sum((d_normed * standardized_entries).reshape(rows, embed_span), axis=0)
    unit_gradient = d_normed * rescale_factor
    alignment_gradient = upstream_adjoint.astype(jnp.float32) + reciprocal_spread * (
        unit_gradient
        - jnp.mean(unit_gradient, axis=-1, keepdims=True)
        - standardized_entries
        * jnp.mean(unit_gradient * standardized_entries, axis=-1, keepdims=True)
    )
    query_gradient, key_gradient, value_gradient, output_gradient, gain_gradient = (
        lax.psum_scatter(part_query, axes, scatter_dimension=0, tiled=True),
        lax.psum_scatter(part_key, axes, scatter_dimension=0, tiled=True),
        lax.psum_scatter(part_value, axes, scatter_dimension=0, tiled=True),
        lax.psum_scatter(part_out, axes, scatter_dimension=0, tiled=True),
        lax.psum_scatter(part_gain, axes, scatter_dimension=0, tiled=True),
    )
    return (
        final_result,
        alignment_gradient.astype(jnp.bfloat16),
        query_gradient,
        key_gradient,
        value_gradient,
        output_gradient,
        gain_gradient,
    )


F32, BF16 = jnp.float32, jnp.bfloat16
SCALE = HEAD_DIM ** (-0.5)


def swap(value, axis, size, bits):
    return lax.ppermute(value, axis, [(i, i ^ bits) for i in range(size)])


def dot(a, b, contract=(1, 0)):
    return lax.dot_general(
        a, b, (((contract[0],), (contract[1],)), ((), ())), preferred_element_type=F32
    )


def unit_rows(x):
    x = x.astype(F32)
    centered = x - jnp.mean(x, axis=-1, keepdims=True)
    inverse = lax.rsqrt(jnp.mean(centered * centered, axis=-1, keepdims=True) + 1e-05)
    return centered * inverse, inverse


def head_masks(span):
    lane = lax.broadcasted_iota(jnp.int32, (8, span), 1)
    return [
        ((lane >= at) & (lane < at + HEAD_DIM)).astype(F32)[0:1].astype(BF16)
        for at in range(0, span, HEAD_DIM)
    ]


def fetch(pairs, sems):
    copies = [pltpu.make_async_copy(src, dst, sems.at[i]) for i, (src, dst) in enumerate(pairs)]
    for copy in copies:
        copy.start()
    return copies


class Sender:
    def __init__(self, sems):
        self.sems, self.copies = sems, []

    def send(self, src, dst):
        copy = pltpu.make_async_copy(src, dst, self.sems.at[len(self.copies)])
        copy.start()
        self.copies.append(copy)

    def finish(self):
        for copy in self.copies:
            copy.wait()


def pack_kernel(dims, w_query, w_key, w_value, w_out, out, out_cut):
    depth, zs, shard, block, span = dims
    for d in range(depth):
        lanes = slice(d * span, (d + 1) * span)
        for i, w in enumerate((w_query, w_key, w_value)):
            out[d, :, i * span : (i + 1) * span] = w[:, lanes]
        out_cut[d] = w_out[:, lanes]


def norm_kernel(dims, *refs):
    depth, zs, shard, block, span = dims
    gain, xs_h, refs = refs[0], refs[1 : 1 + depth], refs[1 + depth :]
    normed_h, normed_t_h, xs, normed, normed_t, in_sems, out_sems = refs
    copies = fetch([(xs_h[j], xs.at[j]) for j in range(depth)], in_sems)
    sender = Sender(out_sems)
    for j in range(depth):
        copies[j].wait()
        unit, _ = unit_rows(xs[j])
        rows = pl.ds(j * block, block)
        wide = unit * gain[...]
        normed[rows, :] = wide.astype(BF16)
        sender.send(normed.at[rows], normed_h.at[rows])
        normed_t[:, rows] = jnp.transpose(wide).astype(BF16)
        sender.send(normed_t.at[:, rows], normed_t_h.at[:, rows])
    sender.finish()


def forward_kernel(dims, *refs):
    depth, zs, shard, block, span = dims
    heads = span // HEAD_DIM
    pos, w_near, w_far, normed_h = refs[:4]
    query_h, keys_h, values_h, keys_t_h, att_t_h, lse_h, wq_h, wk_h, wv_h, w_out_h = refs[4:14]
    outs_h, refs = refs[14 : 14 + depth], refs[14 + depth :]
    normed, query, keys, values, keys_t, values_t, att_t, lse = refs[:8]
    wq, wk, wv, w_out, outs, in_sems, out_sems = refs[8:]
    copies = fetch([(normed_h, normed)], in_sems)
    sender = Sender(out_sems)

    own_z, first = pos[0], pos[1] == 0
    for z in range(zs):
        for d in range(depth):
            near, far = w_near[z ^ own_z, d].astype(F32), w_far[z ^ own_z, d].astype(F32)
            both = jnp.concatenate(
                [jnp.where(first, near, far), jnp.where(first, far, near)], axis=0
            ).astype(BF16)
            rows = slice((d * zs + z) * 2 * shard, (d * zs + z + 1) * 2 * shard)
            for i, w in enumerate((wq, wk, wv)):
                w[rows, :] = both[:, i * span : (i + 1) * span]
            rows = slice(z * 2 * shard, (z + 1) * 2 * shard)
            w_out[rows, d * span : (d + 1) * span] = both[:, 3 * span :]
    for src, dst in ((wq, wq_h), (wk, wk_h), (wv, wv_h), (w_out, w_out_h)):
        sender.send(src, dst)
    copies[0].wait()

    query[...] = (SCALE * dot(normed[...], wq[...])).astype(BF16)
    key = dot(normed[...], wk[...])
    keys[...] = key.astype(BF16)
    keys_t[...] = jnp.transpose(key.astype(BF16))
    value = dot(normed[...], wv[...])
    values[...] = value.astype(BF16)
    values_t[...] = jnp.transpose(value.astype(BF16))
    for src, dst in ((query, query_h), (keys, keys_h), (values, values_h), (keys_t, keys_t_h)):
        sender.send(src, dst)

    masks = head_masks(span)

    units = [(j, h) for j in range(depth) for h in range(heads)]

    def score(j, h):
        return dot(keys[...], query[j * block : (j + 1) * block, :] * masks[h], (1, 1))

    ready = [score(*unit) for unit in units[:2]]
    for i, (j, h) in enumerate(units):
        cols, lanes = slice(j * block, (j + 1) * block), slice(h * HEAD_DIM, (h + 1) * HEAD_DIM)
        scores = ready.pop(0)
        top = jnp.max(scores, axis=0, keepdims=True)
        e = jnp.exp(scores - top)
        total = jnp.sum(e, axis=0, keepdims=True)
        if i + 2 < len(units):
            ready.append(score(*units[i + 2]))
        att_t[lanes, cols] = dot(values_t[lanes, :], e.astype(BF16)) * (1.0 / total)
        lse[h, :, cols] = top + jnp.log(total)
    sender.send(att_t, att_t_h)
    sender.send(lse, lse_h)
    att = jnp.transpose(att_t[...]).astype(BF16)
    for j in range(depth):
        outs[j] = dot(att[j * block : (j + 1) * block], w_out[...]).astype(BF16)
        sender.send(outs.at[j], outs_h[j])
    sender.finish()


def backward_kernel(dims, *refs):
    depth, zs, shard, block, span = dims
    heads = span // HEAD_DIM
    pos, refs = refs[0], refs[1:]
    gs_h, refs = refs[:depth], refs[depth:]
    (w_out_h, query_h, keys_h, values_h, keys_t_h, lse_h, normed_t_h, att_t_h) = refs[:8]
    (wq_h, wk_h, wv_h, near, far), refs = refs[8:13], refs[13:]
    dns_h, refs = refs[: depth + 1], refs[depth + 1 :]
    (gs, w_out, query, keys, values, keys_t, lse, normed_t, att_t, wq, wk, wv) = refs[:12]
    (d_att, delta, d_query_t, d_keys, d_values, grad_out, dns, in_sems, out_sems) = refs[12:]
    copies = fetch(
        [(w_out_h, w_out)]
        + [(gs_h[j], gs.at[pl.ds(j * block, block)]) for j in range(depth)]
        + [
            (att_t_h, att_t),
            (keys_h, keys),
            (query_h, query),
            (values_h, values),
            (lse_h, lse),
            (keys_t_h, keys_t),
            (normed_t_h, normed_t),
            (wq_h, wq),
            (wk_h, wk),
            (wv_h, wv),
        ],
        in_sems,
    )
    loaded, later = 7 + depth, copies[7 + depth :]

    for copy in copies[: 2 + depth]:
        copy.wait()
    part = dot(gs[...], w_out[...], (1, 1)).astype(BF16)
    d_att[...] = part
    product = jnp.transpose(part.astype(F32)) * att_t[...]
    for h in range(heads):
        delta[h] = jnp.sum(product[h * HEAD_DIM : (h + 1) * HEAD_DIM], axis=0, keepdims=True)
    for copy in copies[2 + depth : loaded]:
        copy.wait()
    masks = head_masks(span)

    units = [(j, h) for j in range(depth) for h in range(heads)]

    def pair(j, h):
        rows = slice(j * block, (j + 1) * block)
        q_head, g_head = query[rows, :] * masks[h], d_att[rows, :] * masks[h]
        scores, d_probs = dot(keys[...], q_head, (1, 1)), dot(values[...], g_head, (1, 1))
        return q_head, g_head, scores, d_probs

    def add_block(j, parts):
        probs, d_scores, qs, ds = (list(p) for p in zip(*parts))
        value_part = dot(jnp.concatenate(probs, axis=1), jnp.concatenate(ds, axis=0))
        key_part = dot(jnp.concatenate(d_scores, axis=1), jnp.concatenate(qs, axis=0))
        d_values[...] = value_part if j == 0 else d_values[...] + value_part
        d_keys[...] = key_part if j == 0 else d_keys[...] + key_part

    ready = [pair(*unit) for unit in units[:2]]
    parts, waiting = [], None
    for i, (j, h) in enumerate(units):
        cols, lanes = slice(j * block, (j + 1) * block), slice(h * HEAD_DIM, (h + 1) * HEAD_DIM)
        q_head, g_head, scores, d_probs = ready.pop(0)
        probs = jnp.exp(scores - lse[h, :, cols])
        d_scores = (probs * (d_probs - delta[h, :, cols])).astype(BF16)
        if i + 2 < len(units):
            ready.append(pair(*units[i + 2]))
        parts.append((probs.astype(BF16), d_scores, q_head, g_head))
        d_query_t[lanes, cols] = SCALE * dot(keys_t[lanes, :], d_scores)
        if waiting is not None:
            add_block(*waiting)
            waiting = None
        if h == heads - 1:
            parts, waiting = [], (j, parts)
    add_block(*waiting)
    for copy in later:
        copy.wait()
    d_query = jnp.transpose(d_query_t[...]).astype(BF16)
    d_key, d_value = d_keys[...].astype(BF16), d_values[...].astype(BF16)
    sender = Sender(out_sems)
    for i in range(0, depth, 2):
        rows = slice(i * block, (i + 2) * block)
        d_normed = dot(d_query[rows], wq[...], (1, 1))
        d_normed = d_normed + dot(d_key[rows], wk[...], (1, 1))
        d_normed = d_normed + dot(d_value[rows], wv[...], (1, 1))
        dns[rows, :] = d_normed.astype(BF16)
        for j in (i, i + 1):
            if j < depth - 1:
                sender.send(dns.at[pl.ds(j * block, block)], dns_h[j])
            else:
                half = block // 2
                sender.send(dns.at[pl.ds(j * block, half)], dns_h[j])
                sender.send(dns.at[pl.ds(j * block + half, half)], dns_h[j + 1])

    grad_out[...] = dot(att_t[...].astype(BF16), gs[...])
    grads = [dot(normed_t[...], d) for d in (d_query, d_key, d_value)]
    own_z, first, own_d = pos[0], pos[1] == 0, pos[2]
    for d in range(depth):
        for z in range(zs):
            sides = []
            for c in range(2):
                row, row_out = ((d * zs + z) * 2 + c) * shard, (z * 2 + c) * shard
                sides.append(
                    [g[row : row + shard] for g in grads]
                    + [grad_out[row_out : row_out + shard, d * span : (d + 1) * span]]
                )
            at = 0
            for one, two in zip(*sides):
                lanes = slice(at, at + one.shape[1])
                at += one.shape[1]
                near[z ^ own_z, d ^ own_d, :, lanes] = jnp.where(first, one, two).astype(BF16)
                far[z ^ own_z, d ^ own_d, :, lanes] = jnp.where(first, two, one).astype(BF16)
    sender.finish()


def align_kernel(dims, gain, x, upstream, *refs):
    dns, out = refs[:-1], refs[-1]
    d_normed = dns[0][...].astype(F32)
    for part in dns[1:]:
        d_normed = d_normed + part[...].astype(F32)
    unit, inverse = unit_rows(x[...])
    d_unit = d_normed * gain[...]
    out[...] = (
        upstream[...].astype(F32)
        + inverse
        * (
            d_unit
            - jnp.mean(d_unit, axis=-1, keepdims=True)
            - unit * jnp.mean(d_unit * unit, axis=-1, keepdims=True)
        )
    ).astype(BF16)


def finish_kernel(dims, *refs):
    depth, zs, shard, block, span = dims
    pos, gain, weights, acc, refs = refs[0], refs[1], refs[2:5], refs[5], refs[6:]
    parts, outs = refs[: depth - 1], refs[depth - 1 :]
    own_d = pos[2]
    blocks = [acc[0][:, : 3 * span]] + [p[...].astype(F32) for p in parts]
    for d in range(depth):
        lanes = slice(d * span, (d + 1) * span)
        total = blocks[0]
        for k in range(1, depth):
            total = jnp.where((d ^ own_d) == k, blocks[k], total)
        for i in range(3):
            outs[i][:, lanes] = total[:, i * span : (i + 1) * span]
        outs[3][:, lanes] = acc[d ^ own_d][:, 3 * span :]
    column = weights[0][...].astype(F32) * outs[0][...]
    for w, grad in zip(weights[1:], outs[1:3]):
        column = column + w[...].astype(F32) * grad[...]
    column = jnp.sum(column, axis=1, keepdims=True)
    wide = jnp.concatenate([column, jnp.zeros((128 - shard, 1), F32)], axis=0)
    row = jnp.transpose(jnp.broadcast_to(wide, (128, 128)))[0:1, :shard]
    outs[4][...] = row / gain[...]


VMEM, ANY, SMEM = pltpu.VMEM, pl.ANY, pltpu.SMEM


def call(kernel, dims, ins, outs, scratch, sems, flops, mib=56):
    args = [a for a, _ in ins]
    shapes = [jax.ShapeDtypeStruct(shape, kind) for shape, kind, _ in outs]
    size = sum(a.size * a.dtype.itemsize for a in args + shapes)
    return pl.pallas_call(
        functools.partial(kernel, dims),
        out_shape=shapes,
        in_specs=[pl.BlockSpec(memory_space=space) for _, space in ins],
        out_specs=[pl.BlockSpec(memory_space=space) for _, _, space in outs],
        scratch_shapes=[pltpu.VMEM(shape, kind) for shape, kind in scratch]
        + [pltpu.SemaphoreType.DMA((n,)) for n in sems],
        compiler_params=pltpu.CompilerParams(vmem_limit_bytes=mib * 1024 * 1024),
        cost_estimate=pl.CostEstimate(flops=flops, bytes_accessed=size, transcendentals=0),
    )(*args)


def head_body(depth, res, *args):
    x, gain, w_query, w_key, w_value, w_out, upstream = args
    homologs, _, width = x.shape
    span, zs = width // depth, res // 2
    shard = w_query.shape[0]
    total, heads = homologs * depth, span // HEAD_DIM
    dims = (depth, zs, shard, homologs, span)
    x = x.reshape(homologs, width)
    upstream = upstream.reshape(homologs, width)
    gain = gain.reshape(1, width)
    pos = jnp.stack([lax.axis_index(a) for a in ("z", "core", "depth")]).astype(jnp.int32)

    xs = [x] + [swap(x, "depth", depth, k) for k in range(1, depth - 1)]

    packed, out_cut = call(
        pack_kernel,
        dims,
        [(w, VMEM) for w in (w_query, w_key, w_value, w_out)],
        [((depth, shard, 3 * span), BF16, VMEM), ((depth, shard, span), BF16, VMEM)],
        [],
        [],
        1000,
    )
    mine = lax.all_to_all(packed, "depth", 0, 0, tiled=True)
    mine = jnp.concatenate([mine, out_cut], axis=2)
    mine, *xs = lax.optimization_barrier([mine] + xs)
    xs.append(swap(xs[0], "depth", depth, depth - 1))
    parts = [mine] + [swap(mine, "z", zs, k) for k in range(1, zs)]
    gs = [upstream] + [swap(upstream, "depth", depth, k) for k in range(1, depth)]

    rows, turned = ((total, span), BF16), ((span, total), BF16)
    half = homologs // 2
    block, halved = ((homologs, width), BF16), ((half, width), BF16)
    blocks = ((depth, homologs, width), BF16)
    norm, stats = ((total, width), BF16), ((heads, 1, total), F32)
    in_weights, out_weights = ((width, span), BF16), ((span, width), BF16)
    pass_flops = 2 * total * total * span
    normed, normed_t = call(
        norm_kernel,
        dims,
        [(gain, VMEM)] + [(a, ANY) for a in xs],
        [norm + (ANY,), ((width, total), BF16, ANY)],
        [blocks, norm, ((width, total), BF16)],
        [depth, 2 * depth],
        1000,
    )
    first_row = (lax.axis_index("depth") * res + pos[0] * 2 + pos[1]) * shard
    own_gain = lax.dynamic_slice(gain, (0, first_row), (1, shard))
    normed, pos, own_gain, *parts = lax.optimization_barrier([normed, pos, own_gain] + parts)
    w_near = jnp.stack(parts, axis=0)
    w_far = swap(w_near, "core", 2, 1)

    turned_f32 = ((span, total), F32)
    saved = [rows, rows, rows, turned, turned_f32, stats] + [in_weights] * 3 + [out_weights]
    query, keys, values, keys_t, att_t, lse, wq, wk, wv, wo, *outs = call(
        forward_kernel,
        dims,
        [(pos, SMEM), (w_near, VMEM), (w_far, VMEM), (normed, ANY)],
        [s + (ANY,) for s in saved + [block] * depth],
        [norm, rows, rows, rows, turned, turned, turned_f32, stats]
        + [in_weights] * 3
        + [out_weights, blocks],
        [1, len(saved) + depth],
        8 * pass_flops,
    )

    packed = (zs, depth, shard, 4 * span)
    near, far, *dns = call(
        backward_kernel,
        dims,
        [(pos, SMEM)]
        + [(a, ANY) for a in gs + [wo, query, keys, values, keys_t, lse, normed_t]]
        + [(a, ANY) for a in (att_t, wq, wk, wv)],
        [(packed, BF16, VMEM)] * 2 + [s + (ANY,) for s in [block] * 3 + [halved] * 2],
        [norm, out_weights, rows, rows, rows, turned, stats, ((width, total), BF16)]
        + [turned_f32, in_weights, in_weights, in_weights]
        + [rows, stats, turned_f32]
        + [((total, span), F32)] * 2
        + [((span, width), F32), norm],
        [depth + 11, depth + 1],
        24 * pass_flops,
    )

    outs = [outs[0]] + [swap(outs[k], "depth", depth, k) for k in range(1, depth)]
    near, far, dns, outs = lax.optimization_barrier((near, far, dns, outs))

    far = swap(far, "core", 2, 1)
    dn0, dn1, dn2, dn3_top, dn3_bottom = dns
    top, bottom = swap(dn3_top, "depth", depth, 1), swap(dn3_bottom, "depth", depth, 2)
    sums = [near[k].astype(F32) + far[k].astype(F32) for k in range(1, zs)]
    low = [swap(part.astype(BF16), "z", zs, k + 1) for k, part in enumerate(sums)]
    low[0], top, bottom, outs = lax.optimization_barrier((low[0], top, bottom, outs))
    dn2 = dn2.astype(F32) + jnp.concatenate([top, jnp.zeros_like(top)], axis=0).astype(F32)
    dn1 = dn1.astype(F32) + jnp.concatenate([jnp.zeros_like(bottom), bottom], axis=0).astype(F32)
    final_result = (x.astype(F32) + sum(o.astype(F32) for o in outs)).astype(BF16)
    dn1, dn2, final_result = lax.optimization_barrier(
        (dn1.astype(BF16), dn2.astype(BF16), final_result)
    )
    dn1, dn2 = swap(dn1, "depth", depth, 1), swap(dn2, "depth", depth, 2)
    acc = near[0].astype(F32) + far[0].astype(F32) + sum(p.astype(F32) for p in low)
    parts = [
        swap(acc[k, :, : 3 * span].astype(BF16), "depth", depth, k) for k in range(1, depth)
    ]
    alignment = call(
        align_kernel,
        dims,
        [(a, VMEM) for a in (gain, x, upstream, dn0, dn1, dn2)],
        [block + (VMEM,)],
        [],
        [],
        1000 * total * width,
        16,
    )[0]
    alignment, *parts = lax.optimization_barrier([alignment] + parts)
    grad_query, grad_key, grad_value, grad_out, gain_rows = call(
        finish_kernel,
        dims,
        [(pos, SMEM)]
        + [(a, VMEM) for a in [own_gain, w_query, w_key, w_value, acc] + parts],
        [((shard, width), F32, VMEM)] * 4 + [((1, shard), F32, VMEM)],
        [],
        [],
        1000,
        16,
    )
    return (
        final_result.reshape(homologs, 1, width),
        alignment.reshape(homologs, 1, width),
        grad_query,
        grad_key,
        grad_value,
        grad_out,
        gain_rows.reshape(shard),
    )


def solution(mesh):
    depth, res = mesh.shape["depth"], mesh.shape["res"]
    powers = depth & (depth - 1) == 0 and res & (res - 1) == 0 and res > 1
    if powers and depth == 4 and res >= 4 and HEADS % depth == 0:
        axes = ("depth", "z", "core")
        mesh = Mesh(mesh.devices.reshape(depth, res // 2, 2), axes)
        res_axes, run = ("z", "core"), functools.partial(head_body, depth, res)
    else:
        axes = ("depth", "res")
        res_axes, run = ("res",), general_body

    def body(*args):
        if args[0].shape[1] != 1:
            return general_body(*args, axes=axes)
        return run(*args)

    rows = P("depth", res_axes, None)
    weight = P(axes, None)
    return jax.shard_map(
        body,
        mesh=mesh,
        in_specs=(rows, P(), weight, weight, weight, weight, rows),
        out_specs=(rows, rows, weight, weight, weight, weight, P(axes)),
        check_vma=False,
    )
```

```python
import functools

import jax
import jax.numpy as jnp
from jax import lax
from jax.experimental import pallas as pl
from jax.experimental.pallas import tpu as pltpu
from jax.sharding import Mesh, PartitionSpec as P

HEADS = 12
HEAD_DIM = 64


def standardize_entries(family_activity, rescale_factor):
    payload_entries = family_activity.astype(jnp.float32)
    centered = payload_entries - jnp.mean(payload_entries, axis=-1, keepdims=True)
    reciprocal_spread = lax.rsqrt(jnp.mean(centered * centered, axis=-1, keepdims=True) + 1e-05)
    standardized_entries = centered * reciprocal_spread
    return (
        (standardized_entries * rescale_factor).astype(jnp.bfloat16),
        standardized_entries,
        reciprocal_spread,
    )


def project(rows, weight, factor):
    return (factor * jnp.dot(rows, weight, preferred_element_type=jnp.float32)).astype(jnp.bfloat16)


def to_heads(array):
    count, cols = (array.shape[0], array.shape[1])
    return jnp.transpose(array.reshape(count, cols, HEADS, HEAD_DIM), (1, 2, 0, 3)).reshape(
        cols * HEADS, count, HEAD_DIM
    )


def from_heads(array, cols):
    count = array.shape[1]
    return jnp.transpose(array.reshape(cols, HEADS, count, HEAD_DIM), (2, 0, 1, 3)).reshape(
        count, cols, HEADS * HEAD_DIM
    )


def head_pass(query, keys, payload_entries, d_att):
    scale = HEAD_DIM ** (-0.5)
    scores = jnp.dot(query, keys.T, preferred_element_type=jnp.float32)
    probs = jax.nn.softmax(scores, axis=-1)
    probs_b = probs.astype(jnp.bfloat16)
    mixed_homologs = jnp.dot(probs_b, payload_entries, preferred_element_type=jnp.float32).astype(
        jnp.bfloat16
    )
    d_probs = jnp.dot(d_att, payload_entries.T, preferred_element_type=jnp.float32)
    d_scores = probs * (d_probs - jnp.sum(probs * d_probs, axis=-1, keepdims=True))
    d_scores_b = d_scores.astype(jnp.bfloat16)
    d_query = (scale * jnp.dot(d_scores_b, keys, preferred_element_type=jnp.float32)).astype(
        jnp.bfloat16
    )
    key_part = jnp.einsum("st,sd->td", d_scores_b, query, preferred_element_type=jnp.float32)
    value_part = jnp.einsum("st,sd->td", probs_b, d_att, preferred_element_type=jnp.float32)
    return (mixed_homologs, d_query, key_part, value_part)


def general_body(
    family_activity,
    rescale_factor,
    asking_weights,
    lookup_weights,
    payload_weights,
    exit_weights,
    upstream_adjoint,
    axes=("depth", "res"),
):
    query_weight, key_weight, value_weight, output_matrix = (
        lax.all_gather(asking_weights, axes, axis=0, tiled=True),
        lax.all_gather(lookup_weights, axes, axis=0, tiled=True),
        lax.all_gather(payload_weights, axes, axis=0, tiled=True),
        lax.all_gather(exit_weights, axes, axis=0, tiled=True),
    )
    homologs_each_shard, positions_each_shard, embed_span = family_activity.shape
    standardized_source, standardized_entries, reciprocal_spread = standardize_entries(
        family_activity, rescale_factor
    )
    query = project(standardized_source, query_weight, HEAD_DIM ** (-0.5))
    keys = project(standardized_source, key_weight, 1.0)
    payload_entries = project(standardized_source, value_weight, 1.0)
    keys_all, values_all = (
        lax.all_gather(keys, "depth", axis=0, tiled=True),
        lax.all_gather(payload_entries, "depth", axis=0, tiled=True),
    )
    d_att = jnp.dot(upstream_adjoint, output_matrix.T, preferred_element_type=jnp.float32).astype(
        jnp.bfloat16
    )

    def per_head(items):
        return head_pass(items[0], items[1], items[2], items[3])

    mixed_homologs, d_query, key_part, value_part = lax.map(
        per_head, (to_heads(query), to_heads(keys_all), to_heads(values_all), to_heads(d_att))
    )
    mixed_homologs = from_heads(mixed_homologs, positions_each_shard)
    d_query = from_heads(d_query, positions_each_shard)
    key_part = from_heads(key_part, positions_each_shard)
    value_part = from_heads(value_part, positions_each_shard)
    rows = homologs_each_shard * positions_each_shard
    normed_rows = standardized_source.reshape(rows, embed_span)
    part_query = jnp.dot(
        normed_rows.T, d_query.reshape(rows, embed_span), preferred_element_type=jnp.float32
    )
    part_out = jnp.dot(
        mixed_homologs.reshape(rows, embed_span).T,
        upstream_adjoint.reshape(rows, embed_span),
        preferred_element_type=jnp.float32,
    )
    stacked = jnp.stack([key_part, value_part], axis=2).astype(jnp.bfloat16)
    summed = (
        lax.psum_scatter(stacked, "depth", scatter_dimension=0, tiled=True)
        .astype(jnp.float32)
        .astype(jnp.bfloat16)
    )
    d_keys = summed[:, :, 0, :]
    d_values = summed[:, :, 1, :]
    final_result = (
        family_activity.astype(jnp.float32)
        + jnp.dot(mixed_homologs, output_matrix, preferred_element_type=jnp.float32)
    ).astype(jnp.bfloat16)
    part_key = jnp.dot(
        normed_rows.T, d_keys.reshape(rows, embed_span), preferred_element_type=jnp.float32
    )
    part_value = jnp.dot(
        normed_rows.T, d_values.reshape(rows, embed_span), preferred_element_type=jnp.float32
    )
    d_normed = jnp.dot(d_query, query_weight.T, preferred_element_type=jnp.float32)
    d_normed = d_normed + jnp.dot(d_keys, key_weight.T, preferred_element_type=jnp.float32)
    d_normed = d_normed + jnp.dot(d_values, value_weight.T, preferred_element_type=jnp.float32)
    part_gain = jnp.sum((d_normed * standardized_entries).reshape(rows, embed_span), axis=0)
    unit_gradient = d_normed * rescale_factor
    alignment_gradient = upstream_adjoint.astype(jnp.float32) + reciprocal_spread * (
        unit_gradient
        - jnp.mean(unit_gradient, axis=-1, keepdims=True)
        - standardized_entries
        * jnp.mean(unit_gradient * standardized_entries, axis=-1, keepdims=True)
    )
    query_gradient, key_gradient, value_gradient, output_gradient, gain_gradient = (
        lax.psum_scatter(part_query, axes, scatter_dimension=0, tiled=True),
        lax.psum_scatter(part_key, axes, scatter_dimension=0, tiled=True),
        lax.psum_scatter(part_value, axes, scatter_dimension=0, tiled=True),
        lax.psum_scatter(part_out, axes, scatter_dimension=0, tiled=True),
        lax.psum_scatter(part_gain, axes, scatter_dimension=0, tiled=True),
    )
    return (
        final_result,
        alignment_gradient.astype(jnp.bfloat16),
        query_gradient,
        key_gradient,
        value_gradient,
        output_gradient,
        gain_gradient,
    )


F32, BF16 = jnp.float32, jnp.bfloat16
SCALE = HEAD_DIM ** (-0.5)


def swap(value, axis, size, bits):
    return lax.ppermute(value, axis, [(i, i ^ bits) for i in range(size)])


def dot(a, b, contract=(1, 0)):
    return lax.dot_general(
        a, b, (((contract[0],), (contract[1],)), ((), ())), preferred_element_type=F32
    )


def unit_rows(x):
    x = x.astype(F32)
    centered = x - jnp.mean(x, axis=-1, keepdims=True)
    inverse = lax.rsqrt(jnp.mean(centered * centered, axis=-1, keepdims=True) + 1e-05)
    return centered * inverse, inverse


def head_masks(span):
    lane = lax.broadcasted_iota(jnp.int32, (8, span), 1)
    return [
        ((lane >= at) & (lane < at + HEAD_DIM)).astype(F32)[0:1].astype(BF16)
        for at in range(0, span, HEAD_DIM)
    ]


def fetch(pairs, sems):
    copies = [pltpu.make_async_copy(src, dst, sems.at[i]) for i, (src, dst) in enumerate(pairs)]
    for copy in copies:
        copy.start()
    return copies


class Sender:
    def __init__(self, sems):
        self.sems, self.copies = sems, []

    def send(self, src, dst):
        copy = pltpu.make_async_copy(src, dst, self.sems.at[len(self.copies)])
        copy.start()
        self.copies.append(copy)

    def finish(self):
        for copy in self.copies:
            copy.wait()


def pack_kernel(dims, w_query, w_key, w_value, w_out, out, out_cut):
    depth, zs, shard, block, span = dims
    for d in range(depth):
        lanes = slice(d * span, (d + 1) * span)
        for i, w in enumerate((w_query, w_key, w_value)):
            out[d, :, i * span : (i + 1) * span] = w[:, lanes]
        out_cut[d] = w_out[:, lanes]


def norm_kernel(dims, *refs):
    depth, zs, shard, block, span = dims
    gain, xs_h, refs = refs[0], refs[1 : 1 + depth], refs[1 + depth :]
    normed_h, normed_t_h, xs, normed, normed_t, in_sems, out_sems = refs
    copies = fetch([(xs_h[j], xs.at[j]) for j in range(depth)], in_sems)
    sender = Sender(out_sems)
    for j in range(depth):
        copies[j].wait()
        unit, _ = unit_rows(xs[j])
        rows = pl.ds(j * block, block)
        wide = unit * gain[...]
        normed[rows, :] = wide.astype(BF16)
        sender.send(normed.at[rows], normed_h.at[rows])
        normed_t[:, rows] = jnp.transpose(wide).astype(BF16)
        sender.send(normed_t.at[:, rows], normed_t_h.at[:, rows])
    sender.finish()


def forward_kernel(dims, *refs):
    depth, zs, shard, block, span = dims
    heads = span // HEAD_DIM
    pos, w_near, w_far, normed_h = refs[:4]
    query_h, keys_h, values_h, keys_t_h, att_t_h, lse_h, wq_h, wk_h, wv_h, w_out_h = refs[4:14]
    outs_h, refs = refs[14 : 14 + depth], refs[14 + depth :]
    normed, query, keys, values, keys_t, values_t, att_t, lse = refs[:8]
    wq, wk, wv, w_out, outs, in_sems, out_sems = refs[8:]
    copies = fetch([(normed_h, normed)], in_sems)
    sender = Sender(out_sems)

    own_z, first = pos[0], pos[1] == 0
    for z in range(zs):
        for d in range(depth):
            near, far = w_near[z ^ own_z, d].astype(F32), w_far[z ^ own_z, d].astype(F32)
            both = jnp.concatenate(
                [jnp.where(first, near, far), jnp.where(first, far, near)], axis=0
            ).astype(BF16)
            rows = slice((d * zs + z) * 2 * shard, (d * zs + z + 1) * 2 * shard)
            for i, w in enumerate((wq, wk, wv)):
                w[rows, :] = both[:, i * span : (i + 1) * span]
            rows = slice(z * 2 * shard, (z + 1) * 2 * shard)
            w_out[rows, d * span : (d + 1) * span] = both[:, 3 * span :]
    for src, dst in ((wq, wq_h), (wk, wk_h), (wv, wv_h), (w_out, w_out_h)):
        sender.send(src, dst)
    copies[0].wait()

    query[...] = (SCALE * dot(normed[...], wq[...])).astype(BF16)
    key = dot(normed[...], wk[...])
    keys[...] = key.astype(BF16)
    keys_t[...] = jnp.transpose(key.astype(BF16))
    value = dot(normed[...], wv[...])
    values[...] = value.astype(BF16)
    values_t[...] = jnp.transpose(value.astype(BF16))
    for src, dst in ((query, query_h), (keys, keys_h), (values, values_h), (keys_t, keys_t_h)):
        sender.send(src, dst)

    masks = head_masks(span)

    units = [(j, h) for j in range(depth) for h in range(heads)]

    def score(j, h):
        return dot(keys[...], query[j * block : (j + 1) * block, :] * masks[h], (1, 1))

    ready = [score(*unit) for unit in units[:2]]
    for i, (j, h) in enumerate(units):
        cols, lanes = slice(j * block, (j + 1) * block), slice(h * HEAD_DIM, (h + 1) * HEAD_DIM)
        scores = ready.pop(0)
        top = jnp.max(scores, axis=0, keepdims=True)
        e = jnp.exp(scores - top)
        total = jnp.sum(e, axis=0, keepdims=True)
        if i + 2 < len(units):
            ready.append(score(*units[i + 2]))
        att_t[lanes, cols] = dot(values_t[lanes, :], e.astype(BF16)) * (1.0 / total)
        lse[h, :, cols] = top + jnp.log(total)
    sender.send(att_t, att_t_h)
    sender.send(lse, lse_h)
    att = jnp.transpose(att_t[...]).astype(BF16)
    for j in range(depth):
        outs[j] = dot(att[j * block : (j + 1) * block], w_out[...]).astype(BF16)
        sender.send(outs.at[j], outs_h[j])
    sender.finish()


def backward_kernel(dims, *refs):
    depth, zs, shard, block, span = dims
    heads = span // HEAD_DIM
    pos, refs = refs[0], refs[1:]
    gs_h, refs = refs[:depth], refs[depth:]
    (w_out_h, query_h, keys_h, values_h, keys_t_h, lse_h, normed_t_h, att_t_h) = refs[:8]
    (wq_h, wk_h, wv_h, near, far), refs = refs[8:13], refs[13:]
    dns_h, refs = refs[: depth + 1], refs[depth + 1 :]
    (gs, w_out, query, keys, values, keys_t, lse, normed_t, att_t, wq, wk, wv) = refs[:12]
    (d_att, delta, d_query_t, d_keys, d_values, grad_out, dns, in_sems, out_sems) = refs[12:]
    copies = fetch(
        [(w_out_h, w_out)]
        + [(gs_h[j], gs.at[pl.ds(j * block, block)]) for j in range(depth)]
        + [
            (att_t_h, att_t),
            (keys_h, keys),
            (query_h, query),
            (values_h, values),
            (lse_h, lse),
            (keys_t_h, keys_t),
            (normed_t_h, normed_t),
            (wq_h, wq),
            (wk_h, wk),
            (wv_h, wv),
        ],
        in_sems,
    )
    loaded, later = 7 + depth, copies[7 + depth :]

    for copy in copies[: 2 + depth]:
        copy.wait()
    part = dot(gs[...], w_out[...], (1, 1)).astype(BF16)
    d_att[...] = part
    product = jnp.transpose(part.astype(F32)) * att_t[...]
    for h in range(heads):
        delta[h] = jnp.sum(product[h * HEAD_DIM : (h + 1) * HEAD_DIM], axis=0, keepdims=True)
    for copy in copies[2 + depth : loaded]:
        copy.wait()
    masks = head_masks(span)

    d_keys[...] = jnp.zeros_like(d_keys)
    d_values[...] = jnp.zeros_like(d_values)

    def step(j, _):
        cols = pl.ds(pl.multiple_of(j * block, block), block)
        q_block, g_block = query[cols, :], d_att[cols, :]
        qs = [q_block * m for m in masks]
        ds = [g_block * m for m in masks]

        def pair(h):
            return dot(keys[...], qs[h], (1, 1)), dot(values[...], ds[h], (1, 1))

        pairs = [pair(h) for h in range(min(2, heads))]
        all_probs, all_scores = [], []
        for h in range(heads):
            scores, d_probs = pairs[h]
            probs = jnp.exp(scores - lse[h, :, cols])
            d_scores = (probs * (d_probs - delta[h, :, cols])).astype(BF16)
            if h + 2 < heads:
                pairs.append(pair(h + 2))
            all_probs.append(probs.astype(BF16))
            all_scores.append(d_scores)
            lanes = slice(h * HEAD_DIM, (h + 1) * HEAD_DIM)
            d_query_t[lanes, cols] = SCALE * dot(keys_t[lanes, :], d_scores)
        d_values[...] += dot(jnp.concatenate(all_probs, axis=1), jnp.concatenate(ds, axis=0))
        d_keys[...] += dot(jnp.concatenate(all_scores, axis=1), jnp.concatenate(qs, axis=0))
        return 0

    lax.fori_loop(0, depth, step, 0)
    for copy in later:
        copy.wait()
    d_query = jnp.transpose(d_query_t[...]).astype(BF16)
    d_key, d_value = d_keys[...].astype(BF16), d_values[...].astype(BF16)
    sender = Sender(out_sems)
    for i in range(0, depth, 2):
        rows = slice(i * block, (i + 2) * block)
        d_normed = dot(d_query[rows], wq[...], (1, 1))
        d_normed = d_normed + dot(d_key[rows], wk[...], (1, 1))
        d_normed = d_normed + dot(d_value[rows], wv[...], (1, 1))
        dns[rows, :] = d_normed.astype(BF16)
        for j in (i, i + 1):
            if j < depth - 1:
                sender.send(dns.at[pl.ds(j * block, block)], dns_h[j])
            else:
                half = block // 2
                sender.send(dns.at[pl.ds(j * block, half)], dns_h[j])
                sender.send(dns.at[pl.ds(j * block + half, half)], dns_h[j + 1])

    grad_out[...] = dot(att_t[...].astype(BF16), gs[...])
    grads = [dot(normed_t[...], d) for d in (d_query, d_key, d_value)]
    own_z, first, own_d = pos[0], pos[1] == 0, pos[2]
    for d in range(depth):
        for z in range(zs):
            sides = []
            for c in range(2):
                row, row_out = ((d * zs + z) * 2 + c) * shard, (z * 2 + c) * shard
                sides.append(
                    [g[row : row + shard] for g in grads]
                    + [grad_out[row_out : row_out + shard, d * span : (d + 1) * span]]
                )
            at = 0
            for one, two in zip(*sides):
                lanes = slice(at, at + one.shape[1])
                at += one.shape[1]
                near[z ^ own_z, d ^ own_d, :, lanes] = jnp.where(first, one, two).astype(BF16)
                far[z ^ own_z, d ^ own_d, :, lanes] = jnp.where(first, two, one).astype(BF16)
    sender.finish()


def align_kernel(dims, gain, x, upstream, *refs):
    dns, out = refs[:-1], refs[-1]
    d_normed = dns[0][...].astype(F32)
    for part in dns[1:]:
        d_normed = d_normed + part[...].astype(F32)
    unit, inverse = unit_rows(x[...])
    d_unit = d_normed * gain[...]
    out[...] = (
        upstream[...].astype(F32)
        + inverse
        * (
            d_unit
            - jnp.mean(d_unit, axis=-1, keepdims=True)
            - unit * jnp.mean(d_unit * unit, axis=-1, keepdims=True)
        )
    ).astype(BF16)


def finish_kernel(dims, *refs):
    depth, zs, shard, block, span = dims
    pos, gain, weights, acc, refs = refs[0], refs[1], refs[2:5], refs[5], refs[6:]
    parts, outs = refs[: depth - 1], refs[depth - 1 :]
    own_d = pos[2]
    blocks = [acc[0][:, : 3 * span]] + [p[...].astype(F32) for p in parts]
    for d in range(depth):
        lanes = slice(d * span, (d + 1) * span)
        total = blocks[0]
        for k in range(1, depth):
            total = jnp.where((d ^ own_d) == k, blocks[k], total)
        for i in range(3):
            outs[i][:, lanes] = total[:, i * span : (i + 1) * span]
        outs[3][:, lanes] = acc[d ^ own_d][:, 3 * span :]
    column = weights[0][...].astype(F32) * outs[0][...]
    for w, grad in zip(weights[1:], outs[1:3]):
        column = column + w[...].astype(F32) * grad[...]
    column = jnp.sum(column, axis=1, keepdims=True)
    wide = jnp.concatenate([column, jnp.zeros((128 - shard, 1), F32)], axis=0)
    row = jnp.transpose(jnp.broadcast_to(wide, (128, 128)))[0:1, :shard]
    outs[4][...] = row / gain[...]


VMEM, ANY, SMEM = pltpu.VMEM, pl.ANY, pltpu.SMEM


def call(kernel, dims, ins, outs, scratch, sems, flops, mib=56):
    args = [a for a, _ in ins]
    shapes = [jax.ShapeDtypeStruct(shape, kind) for shape, kind, _ in outs]
    size = sum(a.size * a.dtype.itemsize for a in args + shapes)
    return pl.pallas_call(
        functools.partial(kernel, dims),
        out_shape=shapes,
        in_specs=[pl.BlockSpec(memory_space=space) for _, space in ins],
        out_specs=[pl.BlockSpec(memory_space=space) for _, _, space in outs],
        scratch_shapes=[pltpu.VMEM(shape, kind) for shape, kind in scratch]
        + [pltpu.SemaphoreType.DMA((n,)) for n in sems],
        compiler_params=pltpu.CompilerParams(vmem_limit_bytes=mib * 1024 * 1024),
        cost_estimate=pl.CostEstimate(flops=flops, bytes_accessed=size, transcendentals=0),
    )(*args)


def head_body(depth, res, *args):
    x, gain, w_query, w_key, w_value, w_out, upstream = args
    homologs, _, width = x.shape
    span, zs = width // depth, res // 2
    shard = w_query.shape[0]
    total, heads = homologs * depth, span // HEAD_DIM
    dims = (depth, zs, shard, homologs, span)
    x = x.reshape(homologs, width)
    upstream = upstream.reshape(homologs, width)
    gain = gain.reshape(1, width)
    pos = jnp.stack([lax.axis_index(a) for a in ("z", "core", "depth")]).astype(jnp.int32)

    xs = [x] + [swap(x, "depth", depth, k) for k in range(1, depth - 1)]

    packed, out_cut = call(
        pack_kernel,
        dims,
        [(w, VMEM) for w in (w_query, w_key, w_value, w_out)],
        [((depth, shard, 3 * span), BF16, VMEM), ((depth, shard, span), BF16, VMEM)],
        [],
        [],
        1000,
    )
    mine = lax.all_to_all(packed, "depth", 0, 0, tiled=True)
    mine = jnp.concatenate([mine, out_cut], axis=2)
    mine, *xs = lax.optimization_barrier([mine] + xs)
    xs.append(swap(xs[0], "depth", depth, depth - 1))
    parts = [mine] + [swap(mine, "z", zs, k) for k in range(1, zs)]
    gs = [upstream] + [swap(upstream, "depth", depth, k) for k in range(1, depth)]

    rows, turned = ((total, span), BF16), ((span, total), BF16)
    half = homologs // 2
    block, halved = ((homologs, width), BF16), ((half, width), BF16)
    blocks = ((depth, homologs, width), BF16)
    norm, stats = ((total, width), BF16), ((heads, 1, total), F32)
    in_weights, out_weights = ((width, span), BF16), ((span, width), BF16)
    pass_flops = 2 * total * total * span
    normed, normed_t = call(
        norm_kernel,
        dims,
        [(gain, VMEM)] + [(a, ANY) for a in xs],
        [norm + (ANY,), ((width, total), BF16, ANY)],
        [blocks, norm, ((width, total), BF16)],
        [depth, 2 * depth],
        1000,
    )
    first_row = (lax.axis_index("depth") * res + pos[0] * 2 + pos[1]) * shard
    own_gain = lax.dynamic_slice(gain, (0, first_row), (1, shard))
    normed, pos, own_gain, *parts = lax.optimization_barrier([normed, pos, own_gain] + parts)
    w_near = jnp.stack(parts, axis=0)
    w_far = swap(w_near, "core", 2, 1)

    turned_f32 = ((span, total), F32)
    saved = [rows, rows, rows, turned, turned_f32, stats] + [in_weights] * 3 + [out_weights]
    query, keys, values, keys_t, att_t, lse, wq, wk, wv, wo, *outs = call(
        forward_kernel,
        dims,
        [(pos, SMEM), (w_near, VMEM), (w_far, VMEM), (normed, ANY)],
        [s + (ANY,) for s in saved + [block] * depth],
        [norm, rows, rows, rows, turned, turned, turned_f32, stats]
        + [in_weights] * 3
        + [out_weights, blocks],
        [1, len(saved) + depth],
        8 * pass_flops,
    )

    packed = (zs, depth, shard, 4 * span)
    near, far, *dns = call(
        backward_kernel,
        dims,
        [(pos, SMEM)]
        + [(a, ANY) for a in gs + [wo, query, keys, values, keys_t, lse, normed_t]]
        + [(a, ANY) for a in (att_t, wq, wk, wv)],
        [(packed, BF16, VMEM)] * 2 + [s + (ANY,) for s in [block] * 3 + [halved] * 2],
        [norm, out_weights, rows, rows, rows, turned, stats, ((width, total), BF16)]
        + [turned_f32, in_weights, in_weights, in_weights]
        + [rows, stats, turned_f32]
        + [((total, span), F32)] * 2
        + [((span, width), F32), norm],
        [depth + 11, depth + 1],
        24 * pass_flops,
    )

    outs = [outs[0]] + [swap(outs[k], "depth", depth, k) for k in range(1, depth)]
    near, far, dns, outs = lax.optimization_barrier((near, far, dns, outs))

    far = swap(far, "core", 2, 1)
    dn0, dn1, dn2, dn3_top, dn3_bottom = dns
    top, bottom = swap(dn3_top, "depth", depth, 1), swap(dn3_bottom, "depth", depth, 2)
    sums = [near[k].astype(F32) + far[k].astype(F32) for k in range(1, zs)]
    low = [swap(part.astype(BF16), "z", zs, k + 1) for k, part in enumerate(sums)]
    low[0], top, bottom, outs = lax.optimization_barrier((low[0], top, bottom, outs))
    dn2 = dn2.astype(F32) + jnp.concatenate([top, jnp.zeros_like(top)], axis=0).astype(F32)
    dn1 = dn1.astype(F32) + jnp.concatenate([jnp.zeros_like(bottom), bottom], axis=0).astype(F32)
    final_result = (x.astype(F32) + sum(o.astype(F32) for o in outs)).astype(BF16)
    dn1, dn2, final_result = lax.optimization_barrier(
        (dn1.astype(BF16), dn2.astype(BF16), final_result)
    )
    dn1, dn2 = swap(dn1, "depth", depth, 1), swap(dn2, "depth", depth, 2)
    acc = near[0].astype(F32) + far[0].astype(F32) + sum(p.astype(F32) for p in low)
    parts = [
        swap(acc[k, :, : 3 * span].astype(BF16), "depth", depth, k) for k in range(1, depth)
    ]
    alignment = call(
        align_kernel,
        dims,
        [(a, VMEM) for a in (gain, x, upstream, dn0, dn1, dn2)],
        [block + (VMEM,)],
        [],
        [],
        1000 * total * width,
        16,
    )[0]
    alignment, *parts = lax.optimization_barrier([alignment] + parts)
    grad_query, grad_key, grad_value, grad_out, gain_rows = call(
        finish_kernel,
        dims,
        [(pos, SMEM)]
        + [(a, VMEM) for a in [own_gain, w_query, w_key, w_value, acc] + parts],
        [((shard, width), F32, VMEM)] * 4 + [((1, shard), F32, VMEM)],
        [],
        [],
        1000,
        16,
    )
    return (
        final_result.reshape(homologs, 1, width),
        alignment.reshape(homologs, 1, width),
        grad_query,
        grad_key,
        grad_value,
        grad_out,
        gain_rows.reshape(shard),
    )


def solution(mesh):
    depth, res = mesh.shape["depth"], mesh.shape["res"]
    powers = depth & (depth - 1) == 0 and res & (res - 1) == 0 and res > 1
    if powers and depth == 4 and res >= 4 and HEADS % depth == 0:
        axes = ("depth", "z", "core")
        mesh = Mesh(mesh.devices.reshape(depth, res // 2, 2), axes)
        res_axes, run = ("z", "core"), functools.partial(head_body, depth, res)
    else:
        axes = ("depth", "res")
        res_axes, run = ("res",), general_body

    def body(*args):
        if args[0].shape[1] != 1:
            return general_body(*args, axes=axes)
        return run(*args)

    rows = P("depth", res_axes, None)
    weight = P(axes, None)
    return jax.shard_map(
        body,
        mesh=mesh,
        in_specs=(rows, P(), weight, weight, weight, weight, rows),
        out_specs=(rows, rows, weight, weight, weight, weight, P(axes)),
        check_vma=False,
    )
```

```python
import functools

import jax
import jax.numpy as jnp
from jax import lax
from jax.experimental import pallas as pl
from jax.experimental.pallas import tpu as pltpu
from jax.sharding import Mesh, PartitionSpec as P

HEADS = 12
HEAD_DIM = 64


def standardize_entries(family_activity, rescale_factor):
    payload_entries = family_activity.astype(jnp.float32)
    centered = payload_entries - jnp.mean(payload_entries, axis=-1, keepdims=True)
    reciprocal_spread = lax.rsqrt(jnp.mean(centered * centered, axis=-1, keepdims=True) + 1e-05)
    standardized_entries = centered * reciprocal_spread
    return (
        (standardized_entries * rescale_factor).astype(jnp.bfloat16),
        standardized_entries,
        reciprocal_spread,
    )


def project(rows, weight, factor):
    return (factor * jnp.dot(rows, weight, preferred_element_type=jnp.float32)).astype(jnp.bfloat16)


def to_heads(array):
    count, cols = (array.shape[0], array.shape[1])
    return jnp.transpose(array.reshape(count, cols, HEADS, HEAD_DIM), (1, 2, 0, 3)).reshape(
        cols * HEADS, count, HEAD_DIM
    )


def from_heads(array, cols):
    count = array.shape[1]
    return jnp.transpose(array.reshape(cols, HEADS, count, HEAD_DIM), (2, 0, 1, 3)).reshape(
        count, cols, HEADS * HEAD_DIM
    )


def head_pass(query, keys, payload_entries, d_att):
    scale = HEAD_DIM ** (-0.5)
    scores = jnp.dot(query, keys.T, preferred_element_type=jnp.float32)
    probs = jax.nn.softmax(scores, axis=-1)
    probs_b = probs.astype(jnp.bfloat16)
    mixed_homologs = jnp.dot(probs_b, payload_entries, preferred_element_type=jnp.float32).astype(
        jnp.bfloat16
    )
    d_probs = jnp.dot(d_att, payload_entries.T, preferred_element_type=jnp.float32)
    d_scores = probs * (d_probs - jnp.sum(probs * d_probs, axis=-1, keepdims=True))
    d_scores_b = d_scores.astype(jnp.bfloat16)
    d_query = (scale * jnp.dot(d_scores_b, keys, preferred_element_type=jnp.float32)).astype(
        jnp.bfloat16
    )
    key_part = jnp.einsum("st,sd->td", d_scores_b, query, preferred_element_type=jnp.float32)
    value_part = jnp.einsum("st,sd->td", probs_b, d_att, preferred_element_type=jnp.float32)
    return (mixed_homologs, d_query, key_part, value_part)


def general_body(
    family_activity,
    rescale_factor,
    asking_weights,
    lookup_weights,
    payload_weights,
    exit_weights,
    upstream_adjoint,
    axes=("depth", "res"),
):
    query_weight, key_weight, value_weight, output_matrix = (
        lax.all_gather(asking_weights, axes, axis=0, tiled=True),
        lax.all_gather(lookup_weights, axes, axis=0, tiled=True),
        lax.all_gather(payload_weights, axes, axis=0, tiled=True),
        lax.all_gather(exit_weights, axes, axis=0, tiled=True),
    )
    homologs_each_shard, positions_each_shard, embed_span = family_activity.shape
    standardized_source, standardized_entries, reciprocal_spread = standardize_entries(
        family_activity, rescale_factor
    )
    query = project(standardized_source, query_weight, HEAD_DIM ** (-0.5))
    keys = project(standardized_source, key_weight, 1.0)
    payload_entries = project(standardized_source, value_weight, 1.0)
    keys_all, values_all = (
        lax.all_gather(keys, "depth", axis=0, tiled=True),
        lax.all_gather(payload_entries, "depth", axis=0, tiled=True),
    )
    d_att = jnp.dot(upstream_adjoint, output_matrix.T, preferred_element_type=jnp.float32).astype(
        jnp.bfloat16
    )

    def per_head(items):
        return head_pass(items[0], items[1], items[2], items[3])

    mixed_homologs, d_query, key_part, value_part = lax.map(
        per_head, (to_heads(query), to_heads(keys_all), to_heads(values_all), to_heads(d_att))
    )
    mixed_homologs = from_heads(mixed_homologs, positions_each_shard)
    d_query = from_heads(d_query, positions_each_shard)
    key_part = from_heads(key_part, positions_each_shard)
    value_part = from_heads(value_part, positions_each_shard)
    rows = homologs_each_shard * positions_each_shard
    normed_rows = standardized_source.reshape(rows, embed_span)
    part_query = jnp.dot(
        normed_rows.T, d_query.reshape(rows, embed_span), preferred_element_type=jnp.float32
    )
    part_out = jnp.dot(
        mixed_homologs.reshape(rows, embed_span).T,
        upstream_adjoint.reshape(rows, embed_span),
        preferred_element_type=jnp.float32,
    )
    stacked = jnp.stack([key_part, value_part], axis=2).astype(jnp.bfloat16)
    summed = (
        lax.psum_scatter(stacked, "depth", scatter_dimension=0, tiled=True)
        .astype(jnp.float32)
        .astype(jnp.bfloat16)
    )
    d_keys = summed[:, :, 0, :]
    d_values = summed[:, :, 1, :]
    final_result = (
        family_activity.astype(jnp.float32)
        + jnp.dot(mixed_homologs, output_matrix, preferred_element_type=jnp.float32)
    ).astype(jnp.bfloat16)
    part_key = jnp.dot(
        normed_rows.T, d_keys.reshape(rows, embed_span), preferred_element_type=jnp.float32
    )
    part_value = jnp.dot(
        normed_rows.T, d_values.reshape(rows, embed_span), preferred_element_type=jnp.float32
    )
    d_normed = jnp.dot(d_query, query_weight.T, preferred_element_type=jnp.float32)
    d_normed = d_normed + jnp.dot(d_keys, key_weight.T, preferred_element_type=jnp.float32)
    d_normed = d_normed + jnp.dot(d_values, value_weight.T, preferred_element_type=jnp.float32)
    part_gain = jnp.sum((d_normed * standardized_entries).reshape(rows, embed_span), axis=0)
    unit_gradient = d_normed * rescale_factor
    alignment_gradient = upstream_adjoint.astype(jnp.float32) + reciprocal_spread * (
        unit_gradient
        - jnp.mean(unit_gradient, axis=-1, keepdims=True)
        - standardized_entries
        * jnp.mean(unit_gradient * standardized_entries, axis=-1, keepdims=True)
    )
    query_gradient, key_gradient, value_gradient, output_gradient, gain_gradient = (
        lax.psum_scatter(part_query, axes, scatter_dimension=0, tiled=True),
        lax.psum_scatter(part_key, axes, scatter_dimension=0, tiled=True),
        lax.psum_scatter(part_value, axes, scatter_dimension=0, tiled=True),
        lax.psum_scatter(part_out, axes, scatter_dimension=0, tiled=True),
        lax.psum_scatter(part_gain, axes, scatter_dimension=0, tiled=True),
    )
    return (
        final_result,
        alignment_gradient.astype(jnp.bfloat16),
        query_gradient,
        key_gradient,
        value_gradient,
        output_gradient,
        gain_gradient,
    )


F32, BF16 = jnp.float32, jnp.bfloat16
SCALE = HEAD_DIM ** (-0.5)


def swap(value, axis, size, bits):
    return lax.ppermute(value, axis, [(i, i ^ bits) for i in range(size)])


def dot(a, b, contract=(1, 0)):
    return lax.dot_general(
        a, b, (((contract[0],), (contract[1],)), ((), ())), preferred_element_type=F32
    )


def unit_rows(x):
    x = x.astype(F32)
    centered = x - jnp.mean(x, axis=-1, keepdims=True)
    inverse = lax.rsqrt(jnp.mean(centered * centered, axis=-1, keepdims=True) + 1e-05)
    return centered * inverse, inverse


def head_masks(span):
    lane = lax.broadcasted_iota(jnp.int32, (8, span), 1)
    return [
        ((lane >= at) & (lane < at + HEAD_DIM)).astype(F32)[0:1].astype(BF16)
        for at in range(0, span, HEAD_DIM)
    ]


def only_head(turned, h):
    low, high = h * HEAD_DIM, (h + 1) * HEAD_DIM
    parts = [jnp.zeros((low, turned.shape[1]), turned.dtype)] if low else []
    parts.append(turned[low:high])
    if high < turned.shape[0]:
        parts.append(jnp.zeros((turned.shape[0] - high, turned.shape[1]), turned.dtype))
    return jnp.concatenate(parts, axis=0)


def fetch(pairs, sems):
    copies = [pltpu.make_async_copy(src, dst, sems.at[i]) for i, (src, dst) in enumerate(pairs)]
    for copy in copies:
        copy.start()
    return copies


class Sender:
    def __init__(self, sems):
        self.sems, self.copies = sems, []

    def send(self, src, dst):
        copy = pltpu.make_async_copy(src, dst, self.sems.at[len(self.copies)])
        copy.start()
        self.copies.append(copy)

    def finish(self):
        for copy in self.copies:
            copy.wait()


def pack_kernel(dims, w_query, w_key, w_value, w_out, out, out_cut):
    depth, zs, shard, block, span = dims
    for d in range(depth):
        lanes = slice(d * span, (d + 1) * span)
        for i, w in enumerate((w_query, w_key, w_value)):
            out[d, :, i * span : (i + 1) * span] = w[:, lanes]
        out_cut[d] = w_out[:, lanes]


def norm_kernel(dims, *refs):
    depth, zs, shard, block, span = dims
    gain, xs_h, refs = refs[0], refs[1 : 1 + depth], refs[1 + depth :]
    normed_h, normed_t_h, xs, normed, normed_t, in_sems, out_sems = refs
    copies = fetch([(xs_h[j], xs.at[j]) for j in range(depth)], in_sems)
    sender = Sender(out_sems)
    for j in range(depth):
        copies[j].wait()
        unit, _ = unit_rows(xs[j])
        rows = pl.ds(j * block, block)
        wide = unit * gain[...]
        normed[rows, :] = wide.astype(BF16)
        sender.send(normed.at[rows], normed_h.at[rows])
        normed_t[:, rows] = jnp.transpose(wide).astype(BF16)
        sender.send(normed_t.at[:, rows], normed_t_h.at[:, rows])
    sender.finish()


def forward_kernel(dims, *refs):
    depth, zs, shard, block, span = dims
    heads = span // HEAD_DIM
    pos, w_near, w_far, normed_h = refs[:4]
    (query_h, query_t_h, keys_h, values_h, keys_t_h, att_t_h, lse_h) = refs[4:11]
    (wq_t_h, wk_t_h, wv_t_h, w_out_t_h), outs_h = refs[11:15], refs[15 : 15 + depth]
    refs = refs[15 + depth :]
    normed, query, query_t, keys, values, keys_t, values_t, att_t, lse = refs[:9]
    wq, wk, wv, w_out, wq_t, wk_t, wv_t, w_out_t, outs, in_sems, out_sems = refs[9:]
    copies = fetch([(normed_h, normed)], in_sems)
    sender = Sender(out_sems)

    own_z, first = pos[0], pos[1] == 0
    for z in range(zs):
        for d in range(depth):
            near, far = w_near[z ^ own_z, d].astype(F32), w_far[z ^ own_z, d].astype(F32)
            both = jnp.concatenate(
                [jnp.where(first, near, far), jnp.where(first, far, near)], axis=0
            ).astype(BF16)
            rows = slice((d * zs + z) * 2 * shard, (d * zs + z + 1) * 2 * shard)
            for i, w in enumerate((wq, wk, wv)):
                w[rows, :] = both[:, i * span : (i + 1) * span]
            rows = slice(z * 2 * shard, (z + 1) * 2 * shard)
            w_out[rows, d * span : (d + 1) * span] = both[:, 3 * span :]
    copies[0].wait()

    for scale, w, full, turned, full_h, turned_h in (
        (SCALE, wq, query, query_t, query_h, query_t_h),
        (1.0, wk, keys, keys_t, keys_h, keys_t_h),
        (1.0, wv, values, values_t, values_h, None),
    ):
        rows = (scale * dot(normed[...], w[...])).astype(BF16)
        full[...] = rows
        turned[...] = jnp.transpose(rows)
        sender.send(full, full_h)
        if turned_h is not None:
            sender.send(turned, turned_h)
    for w, turned, turned_h in (
        (wq, wq_t, wq_t_h),
        (wk, wk_t, wk_t_h),
        (wv, wv_t, wv_t_h),
        (w_out, w_out_t, w_out_t_h),
    ):
        turned[...] = jnp.transpose(w[...])
        sender.send(turned, turned_h)


    units = [(j, h) for j in range(depth) for h in range(heads)]

    def score(j, h):
        return dot(keys[...], only_head(query_t[:, j * block : (j + 1) * block], h))

    ready = [score(*unit) for unit in units[:2]]
    for i, (j, h) in enumerate(units):
        cols, lanes = slice(j * block, (j + 1) * block), slice(h * HEAD_DIM, (h + 1) * HEAD_DIM)
        scores = ready.pop(0)
        top = jnp.max(scores, axis=0, keepdims=True)
        e = jnp.exp(scores - top)
        total = jnp.sum(e, axis=0, keepdims=True)
        if i + 2 < len(units):
            ready.append(score(*units[i + 2]))
        att_t[lanes, cols] = dot(values_t[lanes, :], e.astype(BF16)) * (1.0 / total)
        lse[h, :, cols] = top + jnp.log(total)
    sender.send(att_t, att_t_h)
    sender.send(lse, lse_h)
    att = jnp.transpose(att_t[...]).astype(BF16)
    for j in range(depth):
        outs[j] = dot(att[j * block : (j + 1) * block], w_out[...]).astype(BF16)
        sender.send(outs.at[j], outs_h[j])
    sender.finish()


def backward_kernel(dims, *refs):
    depth, zs, shard, block, span = dims
    heads = span // HEAD_DIM
    pos, refs = refs[0], refs[1:]
    gs_h, refs = refs[:depth], refs[depth:]
    (w_out_t_h, query_h, query_t_h, keys_h, values_h, keys_t_h, lse_h, normed_t_h) = refs[:8]
    (att_t_h, wq_t_h, wk_t_h, wv_t_h, near, far), refs = refs[8:14], refs[14:]
    dns_h, refs = refs[: depth + 1], refs[depth + 1 :]
    (gs, w_out_t, query, query_t, keys, values, keys_t, lse, normed_t, att_t) = refs[:10]
    (wq_t, wk_t, wv_t, d_att, d_att_t, delta, d_query_t, d_keys, d_values) = refs[10:19]
    grad_out, dns, in_sems, out_sems = refs[19:]
    copies = fetch(
        [(w_out_t_h, w_out_t)]
        + [(gs_h[j], gs.at[pl.ds(j * block, block)]) for j in range(depth)]
        + [
            (att_t_h, att_t),
            (keys_h, keys),
            (query_h, query),
            (query_t_h, query_t),
            (values_h, values),
            (lse_h, lse),
            (keys_t_h, keys_t),
            (normed_t_h, normed_t),
            (wq_t_h, wq_t),
            (wk_t_h, wk_t),
            (wv_t_h, wv_t),
        ],
        in_sems,
    )
    loaded, later = 8 + depth, copies[8 + depth :]

    d_keys[...] = jnp.zeros_like(d_keys)
    d_values[...] = jnp.zeros_like(d_values)
    for copy in copies[: 2 + depth]:
        copy.wait()
    part = dot(gs[...], w_out_t[...]).astype(BF16)
    d_att[...] = part
    part = jnp.transpose(part)
    d_att_t[...] = part
    product = part.astype(F32) * att_t[...]
    for h in range(heads):
        delta[h] = jnp.sum(product[h * HEAD_DIM : (h + 1) * HEAD_DIM], axis=0, keepdims=True)
    for copy in copies[2 + depth : loaded]:
        copy.wait()
    masks = head_masks(span)

    def step(j, _):
        cols = pl.ds(pl.multiple_of(j * block, block), block)
        q_block, g_block = query[cols, :], d_att[cols, :]
        qs = [q_block * m for m in masks]
        ds = [g_block * m for m in masks]

        def pair(h):
            q_turned = only_head(query_t[:, cols], h)
            d_turned = only_head(d_att_t[:, cols], h)
            return dot(keys[...], q_turned), dot(values[...], d_turned)

        pairs = [pair(h) for h in range(min(2, heads))]
        for h in range(heads):
            scores, d_probs = pairs[h]
            probs = jnp.exp(scores - lse[h, :, cols])
            d_scores = (probs * (d_probs - delta[h, :, cols])).astype(BF16)
            if h + 2 < heads:
                pairs.append(pair(h + 2))
            values_add = dot(probs.astype(BF16), ds[h])
            keys_add = dot(d_scores, qs[h])
            value_part = values_add if h == 0 else value_part + values_add
            key_part = keys_add if h == 0 else key_part + keys_add
            lanes = slice(h * HEAD_DIM, (h + 1) * HEAD_DIM)
            d_query_t[lanes, cols] = SCALE * dot(keys_t[lanes, :], d_scores)
        d_values[...] += value_part.astype(BF16).astype(F32)
        d_keys[...] += key_part.astype(BF16).astype(F32)
        return 0

    lax.fori_loop(0, depth, step, 0)
    for copy in later:
        copy.wait()
    d_query = jnp.transpose(d_query_t[...].astype(BF16))
    d_key, d_value = d_keys[...].astype(BF16), d_values[...].astype(BF16)
    sender = Sender(out_sems)
    for i in range(0, depth, 2):
        rows = slice(i * block, (i + 2) * block)
        d_normed = dot(d_query[rows], wq_t[...])
        d_normed = d_normed + dot(d_key[rows], wk_t[...])
        d_normed = d_normed + dot(d_value[rows], wv_t[...])
        dns[rows, :] = d_normed.astype(BF16)
        for j in (i, i + 1):
            if j < depth - 1:
                sender.send(dns.at[pl.ds(j * block, block)], dns_h[j])
            else:
                half = block // 2
                sender.send(dns.at[pl.ds(j * block, half)], dns_h[j])
                sender.send(dns.at[pl.ds(j * block + half, half)], dns_h[j + 1])

    grad_out[...] = dot(att_t[...].astype(BF16), gs[...])
    grads = [dot(normed_t[...], d) for d in (d_query, d_key, d_value)]
    own_z, first, own_d = pos[0], pos[1] == 0, pos[2]
    for d in range(depth):
        for z in range(zs):
            sides = []
            for c in range(2):
                row, row_out = ((d * zs + z) * 2 + c) * shard, (z * 2 + c) * shard
                sides.append(
                    [g[row : row + shard] for g in grads]
                    + [grad_out[row_out : row_out + shard, d * span : (d + 1) * span]]
                )
            at = 0
            for one, two in zip(*sides):
                lanes = slice(at, at + one.shape[1])
                at += one.shape[1]
                near[z ^ own_z, d ^ own_d, :, lanes] = jnp.where(first, one, two).astype(BF16)
                far[z ^ own_z, d ^ own_d, :, lanes] = jnp.where(first, two, one).astype(BF16)
    sender.finish()


def align_kernel(dims, gain, x, upstream, *refs):
    dns, out = refs[:-1], refs[-1]
    d_normed = dns[0][...].astype(F32)
    for part in dns[1:]:
        d_normed = d_normed + part[...].astype(F32)
    unit, inverse = unit_rows(x[...])
    d_unit = d_normed * gain[...]
    out[...] = (
        upstream[...].astype(F32)
        + inverse
        * (
            d_unit
            - jnp.mean(d_unit, axis=-1, keepdims=True)
            - unit * jnp.mean(d_unit * unit, axis=-1, keepdims=True)
        )
    ).astype(BF16)


def finish_kernel(dims, *refs):
    depth, zs, shard, block, span = dims
    pos, gain, weights, acc, refs = refs[0], refs[1], refs[2:5], refs[5], refs[6:]
    parts, outs = refs[: depth - 1], refs[depth - 1 :]
    own_d = pos[2]
    blocks = [acc[0][:, : 3 * span]] + [p[...].astype(F32) for p in parts]
    for d in range(depth):
        lanes = slice(d * span, (d + 1) * span)
        total = blocks[0]
        for k in range(1, depth):
            total = jnp.where((d ^ own_d) == k, blocks[k], total)
        for i in range(3):
            outs[i][:, lanes] = total[:, i * span : (i + 1) * span]
        outs[3][:, lanes] = acc[d ^ own_d][:, 3 * span :]
    column = weights[0][...].astype(F32) * outs[0][...]
    for w, grad in zip(weights[1:], outs[1:3]):
        column = column + w[...].astype(F32) * grad[...]
    column = jnp.sum(column, axis=1, keepdims=True)
    wide = jnp.concatenate([column, jnp.zeros((128 - shard, 1), F32)], axis=0)
    row = jnp.transpose(jnp.broadcast_to(wide, (128, 128)))[0:1, :shard]
    outs[4][...] = row / gain[...]


VMEM, ANY, SMEM = pltpu.VMEM, pl.ANY, pltpu.SMEM


def call(kernel, dims, ins, outs, scratch, sems, flops, mib=56):
    args = [a for a, _ in ins]
    shapes = [jax.ShapeDtypeStruct(shape, kind) for shape, kind, _ in outs]
    size = sum(a.size * a.dtype.itemsize for a in args + shapes)
    return pl.pallas_call(
        functools.partial(kernel, dims),
        out_shape=shapes,
        in_specs=[pl.BlockSpec(memory_space=space) for _, space in ins],
        out_specs=[pl.BlockSpec(memory_space=space) for _, _, space in outs],
        scratch_shapes=[pltpu.VMEM(shape, kind) for shape, kind in scratch]
        + [pltpu.SemaphoreType.DMA((n,)) for n in sems],
        compiler_params=pltpu.CompilerParams(vmem_limit_bytes=mib * 1024 * 1024),
        cost_estimate=pl.CostEstimate(flops=flops, bytes_accessed=size, transcendentals=0),
    )(*args)


def head_body(depth, res, *args):
    x, gain, w_query, w_key, w_value, w_out, upstream = args
    homologs, _, width = x.shape
    span, zs = width // depth, res // 2
    shard = w_query.shape[0]
    total, heads = homologs * depth, span // HEAD_DIM
    dims = (depth, zs, shard, homologs, span)
    x = x.reshape(homologs, width)
    upstream = upstream.reshape(homologs, width)
    gain = gain.reshape(1, width)
    pos = jnp.stack([lax.axis_index(a) for a in ("z", "core", "depth")]).astype(jnp.int32)

    xs = [x] + [swap(x, "depth", depth, k) for k in range(1, depth - 1)]

    packed, out_cut = call(
        pack_kernel,
        dims,
        [(w, VMEM) for w in (w_query, w_key, w_value, w_out)],
        [((depth, shard, 3 * span), BF16, VMEM), ((depth, shard, span), BF16, VMEM)],
        [],
        [],
        1000,
    )
    mine = lax.all_to_all(packed, "depth", 0, 0, tiled=True)
    mine = jnp.concatenate([mine, out_cut], axis=2)
    mine, *xs = lax.optimization_barrier([mine] + xs)
    xs.append(swap(xs[0], "depth", depth, depth - 1))
    parts = [mine] + [swap(mine, "z", zs, k) for k in range(1, zs)]
    gs = [upstream] + [swap(upstream, "depth", depth, k) for k in range(1, depth)]

    rows, turned = ((total, span), BF16), ((span, total), BF16)
    half = homologs // 2
    block, halved = ((homologs, width), BF16), ((half, width), BF16)
    blocks = ((depth, homologs, width), BF16)
    norm, stats = ((total, width), BF16), ((heads, 1, total), F32)
    in_weights, out_weights = ((width, span), BF16), ((span, width), BF16)
    pass_flops = 2 * total * total * span
    normed, normed_t = call(
        norm_kernel,
        dims,
        [(gain, VMEM)] + [(a, ANY) for a in xs],
        [norm + (ANY,), ((width, total), BF16, ANY)],
        [blocks, norm, ((width, total), BF16)],
        [depth, 2 * depth],
        1000,
    )
    first_row = (lax.axis_index("depth") * res + pos[0] * 2 + pos[1]) * shard
    own_gain = lax.dynamic_slice(gain, (0, first_row), (1, shard))
    normed, pos, own_gain, *parts = lax.optimization_barrier([normed, pos, own_gain] + parts)
    w_near = jnp.stack(parts, axis=0)
    w_far = swap(w_near, "core", 2, 1)

    turned_f32 = ((span, total), F32)
    saved = [rows, turned, rows, rows, turned, turned_f32, stats]
    saved = saved + [out_weights] * 3 + [in_weights]
    query, query_t, keys, values, keys_t, att_t, lse, wq_t, wk_t, wv_t, wo_t, *outs = call(
        forward_kernel,
        dims,
        [(pos, SMEM), (w_near, VMEM), (w_far, VMEM), (normed, ANY)],
        [s + (ANY,) for s in saved + [block] * depth],
        [norm, rows, turned, rows, rows, turned, turned, turned_f32, stats]
        + [in_weights] * 3
        + [out_weights] * 4
        + [in_weights, blocks],
        [1, len(saved) + depth],
        8 * pass_flops,
    )

    packed = (zs, depth, shard, 4 * span)
    near, far, *dns = call(
        backward_kernel,
        dims,
        [(pos, SMEM)]
        + [(a, ANY) for a in gs + [wo_t, query, query_t, keys, values, keys_t, lse, normed_t]]
        + [(a, ANY) for a in (att_t, wq_t, wk_t, wv_t)],
        [(packed, BF16, VMEM)] * 2 + [s + (ANY,) for s in [block] * 3 + [halved] * 2],
        [norm, in_weights, rows, turned, rows, rows, turned, stats, ((width, total), BF16)]
        + [turned_f32, out_weights, out_weights, out_weights]
        + [rows, turned, stats, turned_f32]
        + [((total, span), F32)] * 2
        + [((span, width), F32), norm],
        [depth + 12, depth + 1],
        24 * pass_flops,
    )

    outs = [outs[0]] + [swap(outs[k], "depth", depth, k) for k in range(1, depth)]
    near, far, dns, outs = lax.optimization_barrier((near, far, dns, outs))

    far = swap(far, "core", 2, 1)
    dn0, dn1, dn2, dn3_top, dn3_bottom = dns
    top, bottom = swap(dn3_top, "depth", depth, 1), swap(dn3_bottom, "depth", depth, 2)
    sums = [near[k].astype(F32) + far[k].astype(F32) for k in range(1, zs)]
    low = [swap(part.astype(BF16), "z", zs, k + 1) for k, part in enumerate(sums)]
    low[0], top, bottom, outs = lax.optimization_barrier((low[0], top, bottom, outs))
    dn2 = dn2.astype(F32) + jnp.concatenate([top, jnp.zeros_like(top)], axis=0).astype(F32)
    dn1 = dn1.astype(F32) + jnp.concatenate([jnp.zeros_like(bottom), bottom], axis=0).astype(F32)
    final_result = (x.astype(F32) + sum(o.astype(F32) for o in outs)).astype(BF16)
    own = near[0].astype(F32) + far[0].astype(F32)
    dn1, dn2, final_result, own = lax.optimization_barrier(
        (dn1.astype(BF16), dn2.astype(BF16), final_result, own)
    )
    dn1, dn2 = swap(dn1, "depth", depth, 1), swap(dn2, "depth", depth, 2)
    acc = own + sum(p.astype(F32) for p in low)
    parts = [
        swap(acc[k, :, : 3 * span].astype(BF16), "depth", depth, k) for k in range(1, depth)
    ]
    alignment = call(
        align_kernel,
        dims,
        [(a, VMEM) for a in (gain, x, upstream, dn0, dn1, dn2)],
        [block + (VMEM,)],
        [],
        [],
        1000 * total * width,
        16,
    )[0]
    alignment, *parts = lax.optimization_barrier([alignment] + parts)
    grad_query, grad_key, grad_value, grad_out, gain_rows = call(
        finish_kernel,
        dims,
        [(pos, SMEM)]
        + [(a, VMEM) for a in [own_gain, w_query, w_key, w_value, acc] + parts],
        [((shard, width), F32, VMEM)] * 4 + [((1, shard), F32, VMEM)],
        [],
        [],
        1000,
        16,
    )
    return (
        final_result.reshape(homologs, 1, width),
        alignment.reshape(homologs, 1, width),
        grad_query,
        grad_key,
        grad_value,
        grad_out,
        gain_rows.reshape(shard),
    )


def solution(mesh):
    depth, res = mesh.shape["depth"], mesh.shape["res"]
    powers = depth & (depth - 1) == 0 and res & (res - 1) == 0 and res > 1
    if powers and depth == 4 and res >= 4 and HEADS % depth == 0:
        axes = ("depth", "z", "core")
        mesh = Mesh(mesh.devices.reshape(depth, res // 2, 2), axes)
        res_axes, run = ("z", "core"), functools.partial(head_body, depth, res)
    else:
        axes = ("depth", "res")
        res_axes, run = ("res",), general_body

    def body(*args):
        if args[0].shape[1] != 1:
            return general_body(*args, axes=axes)
        return run(*args)

    rows = P("depth", res_axes, None)
    weight = P(axes, None)
    return jax.shard_map(
        body,
        mesh=mesh,
        in_specs=(rows, P(), weight, weight, weight, weight, rows),
        out_specs=(rows, rows, weight, weight, weight, weight, P(axes)),
        check_vma=False,
    )
```

```python
import functools

import jax
import jax.numpy as jnp
from jax import lax
from jax.experimental import pallas as pl
from jax.experimental.pallas import tpu as pltpu
from jax.sharding import Mesh, PartitionSpec as P

HEADS = 12
HEAD_DIM = 64


def standardize_entries(family_activity, rescale_factor):
    payload_entries = family_activity.astype(jnp.float32)
    centered = payload_entries - jnp.mean(payload_entries, axis=-1, keepdims=True)
    reciprocal_spread = lax.rsqrt(jnp.mean(centered * centered, axis=-1, keepdims=True) + 1e-05)
    standardized_entries = centered * reciprocal_spread
    return (
        (standardized_entries * rescale_factor).astype(jnp.bfloat16),
        standardized_entries,
        reciprocal_spread,
    )


def project(rows, weight, factor):
    return (factor * jnp.dot(rows, weight, preferred_element_type=jnp.float32)).astype(jnp.bfloat16)


def to_heads(array):
    count, cols = (array.shape[0], array.shape[1])
    return jnp.transpose(array.reshape(count, cols, HEADS, HEAD_DIM), (1, 2, 0, 3)).reshape(
        cols * HEADS, count, HEAD_DIM
    )


def from_heads(array, cols):
    count = array.shape[1]
    return jnp.transpose(array.reshape(cols, HEADS, count, HEAD_DIM), (2, 0, 1, 3)).reshape(
        count, cols, HEADS * HEAD_DIM
    )


def head_pass(query, keys, payload_entries, d_att):
    scale = HEAD_DIM ** (-0.5)
    scores = jnp.dot(query, keys.T, preferred_element_type=jnp.float32)
    probs = jax.nn.softmax(scores, axis=-1)
    probs_b = probs.astype(jnp.bfloat16)
    mixed_homologs = jnp.dot(probs_b, payload_entries, preferred_element_type=jnp.float32).astype(
        jnp.bfloat16
    )
    d_probs = jnp.dot(d_att, payload_entries.T, preferred_element_type=jnp.float32)
    d_scores = probs * (d_probs - jnp.sum(probs * d_probs, axis=-1, keepdims=True))
    d_scores_b = d_scores.astype(jnp.bfloat16)
    d_query = (scale * jnp.dot(d_scores_b, keys, preferred_element_type=jnp.float32)).astype(
        jnp.bfloat16
    )
    key_part = jnp.einsum("st,sd->td", d_scores_b, query, preferred_element_type=jnp.float32)
    value_part = jnp.einsum("st,sd->td", probs_b, d_att, preferred_element_type=jnp.float32)
    return (mixed_homologs, d_query, key_part, value_part)


def general_body(
    family_activity,
    rescale_factor,
    asking_weights,
    lookup_weights,
    payload_weights,
    exit_weights,
    upstream_adjoint,
    axes=("depth", "res"),
):
    query_weight, key_weight, value_weight, output_matrix = (
        lax.all_gather(asking_weights, axes, axis=0, tiled=True),
        lax.all_gather(lookup_weights, axes, axis=0, tiled=True),
        lax.all_gather(payload_weights, axes, axis=0, tiled=True),
        lax.all_gather(exit_weights, axes, axis=0, tiled=True),
    )
    homologs_each_shard, positions_each_shard, embed_span = family_activity.shape
    standardized_source, standardized_entries, reciprocal_spread = standardize_entries(
        family_activity, rescale_factor
    )
    query = project(standardized_source, query_weight, HEAD_DIM ** (-0.5))
    keys = project(standardized_source, key_weight, 1.0)
    payload_entries = project(standardized_source, value_weight, 1.0)
    keys_all, values_all = (
        lax.all_gather(keys, "depth", axis=0, tiled=True),
        lax.all_gather(payload_entries, "depth", axis=0, tiled=True),
    )
    d_att = jnp.dot(upstream_adjoint, output_matrix.T, preferred_element_type=jnp.float32).astype(
        jnp.bfloat16
    )

    def per_head(items):
        return head_pass(items[0], items[1], items[2], items[3])

    mixed_homologs, d_query, key_part, value_part = lax.map(
        per_head, (to_heads(query), to_heads(keys_all), to_heads(values_all), to_heads(d_att))
    )
    mixed_homologs = from_heads(mixed_homologs, positions_each_shard)
    d_query = from_heads(d_query, positions_each_shard)
    key_part = from_heads(key_part, positions_each_shard)
    value_part = from_heads(value_part, positions_each_shard)
    rows = homologs_each_shard * positions_each_shard
    normed_rows = standardized_source.reshape(rows, embed_span)
    part_query = jnp.dot(
        normed_rows.T, d_query.reshape(rows, embed_span), preferred_element_type=jnp.float32
    )
    part_out = jnp.dot(
        mixed_homologs.reshape(rows, embed_span).T,
        upstream_adjoint.reshape(rows, embed_span),
        preferred_element_type=jnp.float32,
    )
    stacked = jnp.stack([key_part, value_part], axis=2).astype(jnp.bfloat16)
    summed = (
        lax.psum_scatter(stacked, "depth", scatter_dimension=0, tiled=True)
        .astype(jnp.float32)
        .astype(jnp.bfloat16)
    )
    d_keys = summed[:, :, 0, :]
    d_values = summed[:, :, 1, :]
    final_result = (
        family_activity.astype(jnp.float32)
        + jnp.dot(mixed_homologs, output_matrix, preferred_element_type=jnp.float32)
    ).astype(jnp.bfloat16)
    part_key = jnp.dot(
        normed_rows.T, d_keys.reshape(rows, embed_span), preferred_element_type=jnp.float32
    )
    part_value = jnp.dot(
        normed_rows.T, d_values.reshape(rows, embed_span), preferred_element_type=jnp.float32
    )
    d_normed = jnp.dot(d_query, query_weight.T, preferred_element_type=jnp.float32)
    d_normed = d_normed + jnp.dot(d_keys, key_weight.T, preferred_element_type=jnp.float32)
    d_normed = d_normed + jnp.dot(d_values, value_weight.T, preferred_element_type=jnp.float32)
    part_gain = jnp.sum((d_normed * standardized_entries).reshape(rows, embed_span), axis=0)
    unit_gradient = d_normed * rescale_factor
    alignment_gradient = upstream_adjoint.astype(jnp.float32) + reciprocal_spread * (
        unit_gradient
        - jnp.mean(unit_gradient, axis=-1, keepdims=True)
        - standardized_entries
        * jnp.mean(unit_gradient * standardized_entries, axis=-1, keepdims=True)
    )
    query_gradient, key_gradient, value_gradient, output_gradient, gain_gradient = (
        lax.psum_scatter(part_query, axes, scatter_dimension=0, tiled=True),
        lax.psum_scatter(part_key, axes, scatter_dimension=0, tiled=True),
        lax.psum_scatter(part_value, axes, scatter_dimension=0, tiled=True),
        lax.psum_scatter(part_out, axes, scatter_dimension=0, tiled=True),
        lax.psum_scatter(part_gain, axes, scatter_dimension=0, tiled=True),
    )
    return (
        final_result,
        alignment_gradient.astype(jnp.bfloat16),
        query_gradient,
        key_gradient,
        value_gradient,
        output_gradient,
        gain_gradient,
    )


F32, BF16 = jnp.float32, jnp.bfloat16
SCALE = HEAD_DIM ** (-0.5)


def swap(value, axis, size, bits):
    return lax.ppermute(value, axis, [(i, i ^ bits) for i in range(size)])


def dot(a, b, contract=(1, 0)):
    return lax.dot_general(
        a, b, (((contract[0],), (contract[1],)), ((), ())), preferred_element_type=F32
    )


def unit_rows(x):
    x = x.astype(F32)
    centered = x - jnp.mean(x, axis=-1, keepdims=True)
    inverse = lax.rsqrt(jnp.mean(centered * centered, axis=-1, keepdims=True) + 1e-05)
    return centered * inverse, inverse


def head_masks(span):
    lane = lax.broadcasted_iota(jnp.int32, (8, span), 1)
    return [
        ((lane >= at) & (lane < at + HEAD_DIM)).astype(F32)[0:1].astype(BF16)
        for at in range(0, span, HEAD_DIM)
    ]


def only_head(turned, h):
    low, high = h * HEAD_DIM, (h + 1) * HEAD_DIM
    parts = [jnp.zeros((low, turned.shape[1]), turned.dtype)] if low else []
    parts.append(turned[low:high])
    if high < turned.shape[0]:
        parts.append(jnp.zeros((turned.shape[0] - high, turned.shape[1]), turned.dtype))
    return jnp.concatenate(parts, axis=0)


def fetch(pairs, sems):
    copies = [pltpu.make_async_copy(src, dst, sems.at[i]) for i, (src, dst) in enumerate(pairs)]
    for copy in copies:
        copy.start()
    return copies


class Sender:
    def __init__(self, sems):
        self.sems, self.copies = sems, []

    def send(self, src, dst):
        copy = pltpu.make_async_copy(src, dst, self.sems.at[len(self.copies)])
        copy.start()
        self.copies.append(copy)

    def finish(self):
        for copy in self.copies:
            copy.wait()


def pack_kernel(dims, w_query, w_key, w_value, w_out, out, out_cut):
    depth, zs, shard, block, span = dims
    for d in range(depth):
        lanes = slice(d * span, (d + 1) * span)
        for i, w in enumerate((w_query, w_key, w_value)):
            out[d, :, i * span : (i + 1) * span] = w[:, lanes]
        out_cut[d] = w_out[:, lanes]


def norm_kernel(dims, *refs):
    depth, zs, shard, block, span = dims
    gain, xs_h, refs = refs[0], refs[1 : 1 + depth], refs[1 + depth :]
    normed_h, normed_t_h, xs, normed, normed_t, in_sems, out_sems = refs
    copies = fetch([(xs_h[j], xs.at[j]) for j in range(depth)], in_sems)
    sender = Sender(out_sems)
    for j in range(depth):
        copies[j].wait()
        unit, _ = unit_rows(xs[j])
        rows = pl.ds(j * block, block)
        wide = unit * gain[...]
        normed[rows, :] = wide.astype(BF16)
        sender.send(normed.at[rows], normed_h.at[rows])
        normed_t[:, rows] = jnp.transpose(wide).astype(BF16)
        sender.send(normed_t.at[:, rows], normed_t_h.at[:, rows])
    sender.finish()


def forward_kernel(dims, *refs):
    depth, zs, shard, block, span = dims
    heads = span // HEAD_DIM
    pos, w_near, w_far, normed_h = refs[:4]
    (query_h, query_t_h, keys_h, values_h, keys_t_h, att_t_h, lse_h) = refs[4:11]
    (weights_t_h, w_out_t_h), outs_h = refs[11:13], refs[13 : 13 + depth]
    refs = refs[13 + depth :]
    normed, query, query_t, keys, values, keys_t, values_t, att_t, lse = refs[:9]
    wq, wk, wv, w_out, weights_t, w_out_t, outs, in_sems, out_sems = refs[9:]
    copies = fetch([(normed_h, normed)], in_sems)
    sender = Sender(out_sems)

    own_z, first = pos[0], pos[1] == 0
    for z in range(zs):
        for d in range(depth):
            near, far = w_near[z ^ own_z, d].astype(F32), w_far[z ^ own_z, d].astype(F32)
            both = jnp.concatenate(
                [jnp.where(first, near, far), jnp.where(first, far, near)], axis=0
            ).astype(BF16)
            rows = slice((d * zs + z) * 2 * shard, (d * zs + z + 1) * 2 * shard)
            for i, w in enumerate((wq, wk, wv)):
                w[rows, :] = both[:, i * span : (i + 1) * span]
            rows = slice(z * 2 * shard, (z + 1) * 2 * shard)
            w_out[rows, d * span : (d + 1) * span] = both[:, 3 * span :]
    copies[0].wait()

    for scale, w, full, turned, full_h, turned_h in (
        (SCALE, wq, query, query_t, query_h, query_t_h),
        (1.0, wk, keys, keys_t, keys_h, keys_t_h),
        (1.0, wv, values, values_t, values_h, None),
    ):
        rows = (scale * dot(normed[...], w[...])).astype(BF16)
        full[...] = rows
        turned[...] = jnp.transpose(rows)
        sender.send(full, full_h)
        if turned_h is not None:
            sender.send(turned, turned_h)
    for i, w in enumerate((wq, wk, wv)):
        weights_t[i * span : (i + 1) * span, :] = jnp.transpose(w[...])
    sender.send(weights_t, weights_t_h)
    w_out_t[...] = jnp.transpose(w_out[...])
    sender.send(w_out_t, w_out_t_h)


    units = [(j, h) for j in range(depth) for h in range(heads)]

    def score(j, h):
        return dot(keys[...], only_head(query_t[:, j * block : (j + 1) * block], h))

    ready = [score(*unit) for unit in units[:2]]
    for i, (j, h) in enumerate(units):
        cols, lanes = slice(j * block, (j + 1) * block), slice(h * HEAD_DIM, (h + 1) * HEAD_DIM)
        scores = ready.pop(0)
        top = jnp.max(scores, axis=0, keepdims=True)
        e = jnp.exp(scores - top)
        total = jnp.sum(e, axis=0, keepdims=True)
        if i + 2 < len(units):
            ready.append(score(*units[i + 2]))
        att_t[lanes, cols] = dot(values_t[lanes, :], e.astype(BF16)) * (1.0 / total)
        lse[h, :, cols] = top + jnp.log(total)
    sender.send(att_t, att_t_h)
    sender.send(lse, lse_h)
    att = jnp.transpose(att_t[...]).astype(BF16)
    for j in range(depth):
        outs[j] = dot(att[j * block : (j + 1) * block], w_out[...]).astype(BF16)
        sender.send(outs.at[j], outs_h[j])
    sender.finish()


def backward_kernel(dims, *refs):
    depth, zs, shard, block, span = dims
    heads = span // HEAD_DIM
    pos, refs = refs[0], refs[1:]
    gs_h, refs = refs[:depth], refs[depth:]
    (w_out_t_h, query_h, query_t_h, keys_h, values_h, keys_t_h, lse_h, normed_t_h) = refs[:8]
    (att_t_h, weights_t_h, near, far), refs = refs[8:12], refs[12:]
    dns_h, refs = refs[: depth + 1], refs[depth + 1 :]
    (gs, w_out_t, query, query_t, keys, values, keys_t, lse, normed_t, att_t) = refs[:10]
    (weights_t, d_att, d_att_t, delta, d_query_t, d_keys, d_values, d_qkv) = refs[10:18]
    grad_out, dns, in_sems, out_sems = refs[18:]
    first = fetch(
        [(w_out_t_h, w_out_t)]
        + [(gs_h[j], gs.at[pl.ds(j * block, block)]) for j in range(depth)]
        + [(att_t_h, att_t)],
        in_sems.at[pl.ds(0, 2 + depth)],
    )
    second = [
        (keys_h, keys),
        (query_t_h, query_t),
        (values_h, values),
        (lse_h, lse),
        (query_h, query),
        (keys_t_h, keys_t),
    ]
    third = [(normed_t_h, normed_t), (weights_t_h, weights_t)]

    d_keys[...] = jnp.zeros_like(d_keys)
    d_values[...] = jnp.zeros_like(d_values)
    for copy in first:
        copy.wait()
    second = fetch(second, in_sems.at[pl.ds(2 + depth, 6)])
    part = dot(gs[...], w_out_t[...]).astype(BF16)
    d_att[...] = part
    part = jnp.transpose(part)
    d_att_t[...] = part
    product = part.astype(F32) * att_t[...]
    for h in range(heads):
        delta[h] = jnp.sum(product[h * HEAD_DIM : (h + 1) * HEAD_DIM], axis=0, keepdims=True)
    for copy in second:
        copy.wait()
    third = fetch(third, in_sems.at[pl.ds(8 + depth, 2)])
    masks = head_masks(span)

    def step(j, _):
        cols = pl.ds(pl.multiple_of(j * block, block), block)
        q_block, g_block = query[cols, :], d_att[cols, :]
        qs = [q_block * m for m in masks]
        ds = [g_block * m for m in masks]

        def pair(h):
            q_turned = only_head(query_t[:, cols], h)
            d_turned = only_head(d_att_t[:, cols], h)
            return dot(keys[...], q_turned), dot(values[...], d_turned)

        pairs = [pair(h) for h in range(min(2, heads))]
        for h in range(heads):
            scores, d_probs = pairs[h]
            probs = jnp.exp(scores - lse[h, :, cols])
            d_scores = (probs * (d_probs - delta[h, :, cols])).astype(BF16)
            if h + 2 < heads:
                pairs.append(pair(h + 2))
            values_add = dot(probs.astype(BF16), ds[h])
            keys_add = dot(d_scores, qs[h])
            value_part = values_add if h == 0 else value_part + values_add
            key_part = keys_add if h == 0 else key_part + keys_add
            lanes = slice(h * HEAD_DIM, (h + 1) * HEAD_DIM)
            d_query_t[lanes, cols] = SCALE * dot(keys_t[lanes, :], d_scores)
        d_values[...] += value_part.astype(BF16).astype(F32)
        d_keys[...] += key_part.astype(BF16).astype(F32)
        return 0

    lax.fori_loop(0, depth, step, 0)
    d_qkv[:, :span] = jnp.transpose(d_query_t[...].astype(BF16))
    d_qkv[:, span : 2 * span] = d_keys[...].astype(BF16)
    d_qkv[:, 2 * span :] = d_values[...].astype(BF16)
    for copy in third:
        copy.wait()
    sender = Sender(out_sems)
    for i in range(0, depth, 2):
        rows = slice(i * block, (i + 2) * block)
        dns[rows, :] = dot(d_qkv[rows, :], weights_t[...]).astype(BF16)
        for j in (i, i + 1):
            if j < depth - 1:
                sender.send(dns.at[pl.ds(j * block, block)], dns_h[j])
            else:
                half = block // 2
                sender.send(dns.at[pl.ds(j * block, half)], dns_h[j])
                sender.send(dns.at[pl.ds(j * block + half, half)], dns_h[j + 1])

    grad_out[...] = dot(att_t[...].astype(BF16), gs[...])
    grads = dot(normed_t[...], d_qkv[...])
    own_z, first, own_d = pos[0], pos[1] == 0, pos[2]
    for d in range(depth):
        for z in range(zs):
            sides = []
            for c in range(2):
                row, row_out = ((d * zs + z) * 2 + c) * shard, (z * 2 + c) * shard
                sides.append(
                    (
                        grads[row : row + shard],
                        grad_out[row_out : row_out + shard, d * span : (d + 1) * span],
                    )
                )
            at = 0
            for one, two in zip(*sides):
                lanes = slice(at, at + one.shape[1])
                at += one.shape[1]
                near[z ^ own_z, d ^ own_d, :, lanes] = jnp.where(first, one, two).astype(BF16)
                far[z ^ own_z, d ^ own_d, :, lanes] = jnp.where(first, two, one).astype(BF16)
    sender.finish()


def align_kernel(dims, gain, x, upstream, *refs):
    dns, out = refs[:-1], refs[-1]
    d_normed = dns[0][...].astype(F32)
    for part in dns[1:]:
        d_normed = d_normed + part[...].astype(F32)
    unit, inverse = unit_rows(x[...])
    d_unit = d_normed * gain[...]
    out[...] = (
        upstream[...].astype(F32)
        + inverse
        * (
            d_unit
            - jnp.mean(d_unit, axis=-1, keepdims=True)
            - unit * jnp.mean(d_unit * unit, axis=-1, keepdims=True)
        )
    ).astype(BF16)


def finish_kernel(dims, *refs):
    depth, zs, shard, block, span = dims
    pos, gain, weights, acc, refs = refs[0], refs[1], refs[2:5], refs[5], refs[6:]
    parts, outs = refs[: depth - 1], refs[depth - 1 :]
    own_d = pos[2]
    blocks = [acc[0][:, : 3 * span]] + [p[...].astype(F32) for p in parts]
    for d in range(depth):
        lanes = slice(d * span, (d + 1) * span)
        total = blocks[0]
        for k in range(1, depth):
            total = jnp.where((d ^ own_d) == k, blocks[k], total)
        for i in range(3):
            outs[i][:, lanes] = total[:, i * span : (i + 1) * span]
        outs[3][:, lanes] = acc[d ^ own_d][:, 3 * span :]
    column = weights[0][...].astype(F32) * outs[0][...]
    for w, grad in zip(weights[1:], outs[1:3]):
        column = column + w[...].astype(F32) * grad[...]
    column = jnp.sum(column, axis=1, keepdims=True)
    wide = jnp.concatenate([column, jnp.zeros((128 - shard, 1), F32)], axis=0)
    row = jnp.transpose(jnp.broadcast_to(wide, (128, 128)))[0:1, :shard]
    outs[4][...] = row / gain[...]


VMEM, ANY, SMEM = pltpu.VMEM, pl.ANY, pltpu.SMEM


def call(kernel, dims, ins, outs, scratch, sems, flops, mib=56):
    args = [a for a, _ in ins]
    shapes = [jax.ShapeDtypeStruct(shape, kind) for shape, kind, _ in outs]
    size = sum(a.size * a.dtype.itemsize for a in args + shapes)
    return pl.pallas_call(
        functools.partial(kernel, dims),
        out_shape=shapes,
        in_specs=[pl.BlockSpec(memory_space=space) for _, space in ins],
        out_specs=[pl.BlockSpec(memory_space=space) for _, _, space in outs],
        scratch_shapes=[pltpu.VMEM(shape, kind) for shape, kind in scratch]
        + [pltpu.SemaphoreType.DMA((n,)) for n in sems],
        compiler_params=pltpu.CompilerParams(vmem_limit_bytes=mib * 1024 * 1024),
        cost_estimate=pl.CostEstimate(flops=flops, bytes_accessed=size, transcendentals=0),
    )(*args)


def head_body(depth, res, *args):
    x, gain, w_query, w_key, w_value, w_out, upstream = args
    homologs, _, width = x.shape
    span, zs = width // depth, res // 2
    shard = w_query.shape[0]
    total, heads = homologs * depth, span // HEAD_DIM
    dims = (depth, zs, shard, homologs, span)
    x = x.reshape(homologs, width)
    upstream = upstream.reshape(homologs, width)
    gain = gain.reshape(1, width)
    pos = jnp.stack([lax.axis_index(a) for a in ("z", "core", "depth")]).astype(jnp.int32)

    xs = [x] + [swap(x, "depth", depth, k) for k in range(1, depth - 1)]

    packed, out_cut = call(
        pack_kernel,
        dims,
        [(w, VMEM) for w in (w_query, w_key, w_value, w_out)],
        [((depth, shard, 3 * span), BF16, VMEM), ((depth, shard, span), BF16, VMEM)],
        [],
        [],
        1000,
    )
    mine = lax.all_to_all(packed, "depth", 0, 0, tiled=True)
    mine = jnp.concatenate([mine, out_cut], axis=2)
    mine, *xs = lax.optimization_barrier([mine] + xs)
    xs.append(swap(xs[0], "depth", depth, depth - 1))
    parts = [mine] + [swap(mine, "z", zs, k) for k in range(1, zs)]
    gs = [upstream] + [swap(upstream, "depth", depth, k) for k in range(1, depth)]

    rows, turned = ((total, span), BF16), ((span, total), BF16)
    half = homologs // 2
    block, halved = ((homologs, width), BF16), ((half, width), BF16)
    blocks = ((depth, homologs, width), BF16)
    norm, stats = ((total, width), BF16), ((heads, 1, total), F32)
    in_weights, out_weights = ((width, span), BF16), ((span, width), BF16)
    pass_flops = 2 * total * total * span
    normed, normed_t = call(
        norm_kernel,
        dims,
        [(gain, VMEM)] + [(a, ANY) for a in xs],
        [norm + (ANY,), ((width, total), BF16, ANY)],
        [blocks, norm, ((width, total), BF16)],
        [depth, 2 * depth],
        1000,
    )
    first_row = (lax.axis_index("depth") * res + pos[0] * 2 + pos[1]) * shard
    own_gain = lax.dynamic_slice(gain, (0, first_row), (1, shard))
    normed, pos, own_gain, *parts = lax.optimization_barrier([normed, pos, own_gain] + parts)
    w_near = jnp.stack(parts, axis=0)
    w_far = swap(w_near, "core", 2, 1)

    turned_f32 = ((span, total), F32)
    saved = [rows, turned, rows, rows, turned, turned_f32, stats]
    weights_shape = ((3 * span, width), BF16)
    saved = saved + [weights_shape, in_weights]
    query, query_t, keys, values, keys_t, att_t, lse, weights_t, wo_t, *outs = call(
        forward_kernel,
        dims,
        [(pos, SMEM), (w_near, VMEM), (w_far, VMEM), (normed, ANY)],
        [s + (ANY,) for s in saved + [block] * depth],
        [norm, rows, turned, rows, rows, turned, turned, turned_f32, stats]
        + [in_weights] * 3
        + [out_weights, weights_shape, in_weights, blocks],
        [1, len(saved) + depth],
        8 * pass_flops,
    )

    packed = (zs, depth, shard, 4 * span)
    near, far, *dns = call(
        backward_kernel,
        dims,
        [(pos, SMEM)]
        + [(a, ANY) for a in gs + [wo_t, query, query_t, keys, values, keys_t, lse, normed_t]]
        + [(a, ANY) for a in (att_t, weights_t)],
        [(packed, BF16, VMEM)] * 2 + [s + (ANY,) for s in [block] * 3 + [halved] * 2],
        [norm, in_weights, rows, turned, rows, rows, turned, stats, ((width, total), BF16)]
        + [turned_f32, weights_shape, rows, turned, stats, turned_f32]
        + [((total, span), F32)] * 2
        + [((total, 3 * span), BF16), ((span, width), F32), norm],
        [depth + 10, depth + 1],
        24 * pass_flops,
    )

    outs = [outs[0]] + [swap(outs[k], "depth", depth, k) for k in range(1, depth)]
    near, far, dns, outs = lax.optimization_barrier((near, far, dns, outs))

    far = swap(far, "core", 2, 1)
    dn0, dn1, dn2, dn3_top, dn3_bottom = dns
    top, bottom = swap(dn3_top, "depth", depth, 1), swap(dn3_bottom, "depth", depth, 2)
    sums = [near[k].astype(F32) + far[k].astype(F32) for k in range(1, zs)]
    low = [swap(part.astype(BF16), "z", zs, k + 1) for k, part in enumerate(sums)]
    low[0], top, bottom, outs = lax.optimization_barrier((low[0], top, bottom, outs))
    dn2 = dn2.astype(F32) + jnp.concatenate([top, jnp.zeros_like(top)], axis=0).astype(F32)
    dn1 = dn1.astype(F32) + jnp.concatenate([jnp.zeros_like(bottom), bottom], axis=0).astype(F32)
    final_result = (x.astype(F32) + sum(o.astype(F32) for o in outs)).astype(BF16)
    own = near[0].astype(F32) + far[0].astype(F32)
    dn1, dn2, final_result, own = lax.optimization_barrier(
        (dn1.astype(BF16), dn2.astype(BF16), final_result, own)
    )
    dn1, dn2 = swap(dn1, "depth", depth, 1), swap(dn2, "depth", depth, 2)
    acc = own + sum(p.astype(F32) for p in low)
    parts = [
        swap(acc[k, :, : 3 * span].astype(BF16), "depth", depth, k) for k in range(1, depth)
    ]
    alignment = call(
        align_kernel,
        dims,
        [(a, VMEM) for a in (gain, x, upstream, dn0, dn1, dn2)],
        [block + (VMEM,)],
        [],
        [],
        1000 * total * width,
        16,
    )[0]
    alignment, *parts = lax.optimization_barrier([alignment] + parts)
    grad_query, grad_key, grad_value, grad_out, gain_rows = call(
        finish_kernel,
        dims,
        [(pos, SMEM)]
        + [(a, VMEM) for a in [own_gain, w_query, w_key, w_value, acc] + parts],
        [((shard, width), F32, VMEM)] * 4 + [((1, shard), F32, VMEM)],
        [],
        [],
        1000,
        16,
    )
    return (
        final_result.reshape(homologs, 1, width),
        alignment.reshape(homologs, 1, width),
        grad_query,
        grad_key,
        grad_value,
        grad_out,
        gain_rows.reshape(shard),
    )


def solution(mesh):
    depth, res = mesh.shape["depth"], mesh.shape["res"]
    powers = depth & (depth - 1) == 0 and res & (res - 1) == 0 and res > 1
    if powers and depth == 4 and res >= 4 and HEADS % depth == 0:
        axes = ("depth", "z", "core")
        mesh = Mesh(mesh.devices.reshape(depth, res // 2, 2), axes)
        res_axes, run = ("z", "core"), functools.partial(head_body, depth, res)
    else:
        axes = ("depth", "res")
        res_axes, run = ("res",), general_body

    def body(*args):
        if args[0].shape[1] != 1:
            return general_body(*args, axes=axes)
        return run(*args)

    rows = P("depth", res_axes, None)
    weight = P(axes, None)
    return jax.shard_map(
        body,
        mesh=mesh,
        in_specs=(rows, P(), weight, weight, weight, weight, rows),
        out_specs=(rows, rows, weight, weight, weight, weight, P(axes)),
        check_vma=False,
    )
```

```python
import functools

import jax
import jax.numpy as jnp
from jax import lax
from jax.experimental import pallas as pl
from jax.experimental.pallas import tpu as pltpu
from jax.sharding import Mesh, PartitionSpec as P

HEADS = 12
HEAD_DIM = 64


def standardize_entries(family_activity, rescale_factor):
    payload_entries = family_activity.astype(jnp.float32)
    centered = payload_entries - jnp.mean(payload_entries, axis=-1, keepdims=True)
    reciprocal_spread = lax.rsqrt(jnp.mean(centered * centered, axis=-1, keepdims=True) + 1e-05)
    standardized_entries = centered * reciprocal_spread
    return (
        (standardized_entries * rescale_factor).astype(jnp.bfloat16),
        standardized_entries,
        reciprocal_spread,
    )


def project(rows, weight, factor):
    return (factor * jnp.dot(rows, weight, preferred_element_type=jnp.float32)).astype(jnp.bfloat16)


def to_heads(array):
    count, cols = (array.shape[0], array.shape[1])
    return jnp.transpose(array.reshape(count, cols, HEADS, HEAD_DIM), (1, 2, 0, 3)).reshape(
        cols * HEADS, count, HEAD_DIM
    )


def from_heads(array, cols):
    count = array.shape[1]
    return jnp.transpose(array.reshape(cols, HEADS, count, HEAD_DIM), (2, 0, 1, 3)).reshape(
        count, cols, HEADS * HEAD_DIM
    )


def head_pass(query, keys, payload_entries, d_att):
    scale = HEAD_DIM ** (-0.5)
    scores = jnp.dot(query, keys.T, preferred_element_type=jnp.float32)
    probs = jax.nn.softmax(scores, axis=-1)
    probs_b = probs.astype(jnp.bfloat16)
    mixed_homologs = jnp.dot(probs_b, payload_entries, preferred_element_type=jnp.float32).astype(
        jnp.bfloat16
    )
    d_probs = jnp.dot(d_att, payload_entries.T, preferred_element_type=jnp.float32)
    d_scores = probs * (d_probs - jnp.sum(probs * d_probs, axis=-1, keepdims=True))
    d_scores_b = d_scores.astype(jnp.bfloat16)
    d_query = (scale * jnp.dot(d_scores_b, keys, preferred_element_type=jnp.float32)).astype(
        jnp.bfloat16
    )
    key_part = jnp.einsum("st,sd->td", d_scores_b, query, preferred_element_type=jnp.float32)
    value_part = jnp.einsum("st,sd->td", probs_b, d_att, preferred_element_type=jnp.float32)
    return (mixed_homologs, d_query, key_part, value_part)


def general_body(
    family_activity,
    rescale_factor,
    asking_weights,
    lookup_weights,
    payload_weights,
    exit_weights,
    upstream_adjoint,
    axes=("depth", "res"),
):
    query_weight, key_weight, value_weight, output_matrix = (
        lax.all_gather(asking_weights, axes, axis=0, tiled=True),
        lax.all_gather(lookup_weights, axes, axis=0, tiled=True),
        lax.all_gather(payload_weights, axes, axis=0, tiled=True),
        lax.all_gather(exit_weights, axes, axis=0, tiled=True),
    )
    homologs_each_shard, positions_each_shard, embed_span = family_activity.shape
    standardized_source, standardized_entries, reciprocal_spread = standardize_entries(
        family_activity, rescale_factor
    )
    query = project(standardized_source, query_weight, HEAD_DIM ** (-0.5))
    keys = project(standardized_source, key_weight, 1.0)
    payload_entries = project(standardized_source, value_weight, 1.0)
    keys_all, values_all = (
        lax.all_gather(keys, "depth", axis=0, tiled=True),
        lax.all_gather(payload_entries, "depth", axis=0, tiled=True),
    )
    d_att = jnp.dot(upstream_adjoint, output_matrix.T, preferred_element_type=jnp.float32).astype(
        jnp.bfloat16
    )

    def per_head(items):
        return head_pass(items[0], items[1], items[2], items[3])

    mixed_homologs, d_query, key_part, value_part = lax.map(
        per_head, (to_heads(query), to_heads(keys_all), to_heads(values_all), to_heads(d_att))
    )
    mixed_homologs = from_heads(mixed_homologs, positions_each_shard)
    d_query = from_heads(d_query, positions_each_shard)
    key_part = from_heads(key_part, positions_each_shard)
    value_part = from_heads(value_part, positions_each_shard)
    rows = homologs_each_shard * positions_each_shard
    normed_rows = standardized_source.reshape(rows, embed_span)
    part_query = jnp.dot(
        normed_rows.T, d_query.reshape(rows, embed_span), preferred_element_type=jnp.float32
    )
    part_out = jnp.dot(
        mixed_homologs.reshape(rows, embed_span).T,
        upstream_adjoint.reshape(rows, embed_span),
        preferred_element_type=jnp.float32,
    )
    stacked = jnp.stack([key_part, value_part], axis=2).astype(jnp.bfloat16)
    summed = (
        lax.psum_scatter(stacked, "depth", scatter_dimension=0, tiled=True)
        .astype(jnp.float32)
        .astype(jnp.bfloat16)
    )
    d_keys = summed[:, :, 0, :]
    d_values = summed[:, :, 1, :]
    final_result = (
        family_activity.astype(jnp.float32)
        + jnp.dot(mixed_homologs, output_matrix, preferred_element_type=jnp.float32)
    ).astype(jnp.bfloat16)
    part_key = jnp.dot(
        normed_rows.T, d_keys.reshape(rows, embed_span), preferred_element_type=jnp.float32
    )
    part_value = jnp.dot(
        normed_rows.T, d_values.reshape(rows, embed_span), preferred_element_type=jnp.float32
    )
    d_normed = jnp.dot(d_query, query_weight.T, preferred_element_type=jnp.float32)
    d_normed = d_normed + jnp.dot(d_keys, key_weight.T, preferred_element_type=jnp.float32)
    d_normed = d_normed + jnp.dot(d_values, value_weight.T, preferred_element_type=jnp.float32)
    part_gain = jnp.sum((d_normed * standardized_entries).reshape(rows, embed_span), axis=0)
    unit_gradient = d_normed * rescale_factor
    alignment_gradient = upstream_adjoint.astype(jnp.float32) + reciprocal_spread * (
        unit_gradient
        - jnp.mean(unit_gradient, axis=-1, keepdims=True)
        - standardized_entries
        * jnp.mean(unit_gradient * standardized_entries, axis=-1, keepdims=True)
    )
    query_gradient, key_gradient, value_gradient, output_gradient, gain_gradient = (
        lax.psum_scatter(part_query, axes, scatter_dimension=0, tiled=True),
        lax.psum_scatter(part_key, axes, scatter_dimension=0, tiled=True),
        lax.psum_scatter(part_value, axes, scatter_dimension=0, tiled=True),
        lax.psum_scatter(part_out, axes, scatter_dimension=0, tiled=True),
        lax.psum_scatter(part_gain, axes, scatter_dimension=0, tiled=True),
    )
    return (
        final_result,
        alignment_gradient.astype(jnp.bfloat16),
        query_gradient,
        key_gradient,
        value_gradient,
        output_gradient,
        gain_gradient,
    )


F32, BF16 = jnp.float32, jnp.bfloat16
SCALE = HEAD_DIM ** (-0.5)


def swap(value, axis, size, bits):
    return lax.ppermute(value, axis, [(i, i ^ bits) for i in range(size)])


def dot(a, b, contract=(1, 0)):
    return lax.dot_general(
        a, b, (((contract[0],), (contract[1],)), ((), ())), preferred_element_type=F32
    )


def unit_rows(x):
    x = x.astype(F32)
    centered = x - jnp.mean(x, axis=-1, keepdims=True)
    inverse = lax.rsqrt(jnp.mean(centered * centered, axis=-1, keepdims=True) + 1e-05)
    return centered * inverse, inverse


def head_masks(span):
    lane = lax.broadcasted_iota(jnp.int32, (8, span), 1)
    return [
        ((lane >= at) & (lane < at + HEAD_DIM)).astype(F32)[0:1].astype(BF16)
        for at in range(0, span, HEAD_DIM)
    ]


def only_head(turned, h):
    low, high = h * HEAD_DIM, (h + 1) * HEAD_DIM
    parts = [jnp.zeros((low, turned.shape[1]), turned.dtype)] if low else []
    parts.append(turned[low:high])
    if high < turned.shape[0]:
        parts.append(jnp.zeros((turned.shape[0] - high, turned.shape[1]), turned.dtype))
    return jnp.concatenate(parts, axis=0)


def fetch(pairs, sems):
    copies = [pltpu.make_async_copy(src, dst, sems.at[i]) for i, (src, dst) in enumerate(pairs)]
    for copy in copies:
        copy.start()
    return copies


class Sender:
    def __init__(self, sems):
        self.sems, self.copies = sems, []

    def send(self, src, dst):
        copy = pltpu.make_async_copy(src, dst, self.sems.at[len(self.copies)])
        copy.start()
        self.copies.append(copy)

    def finish(self):
        for copy in self.copies:
            copy.wait()


def pack_kernel(dims, w_query, w_key, w_value, w_out, out, out_cut):
    depth, zs, shard, block, span = dims
    for d in range(depth):
        lanes = slice(d * span, (d + 1) * span)
        for i, w in enumerate((w_query, w_key, w_value)):
            out[d, :, i * span : (i + 1) * span] = w[:, lanes]
        out_cut[d] = w_out[:, lanes]


def norm_kernel(dims, *refs):
    depth, zs, shard, block, span = dims
    gain, xs_h, refs = refs[0], refs[1 : 1 + depth], refs[1 + depth :]
    normed_h, normed_t_h, xs, normed, normed_t, in_sems, out_sems = refs
    copies = fetch([(xs_h[j], xs.at[j]) for j in range(depth)], in_sems)
    sender = Sender(out_sems)
    for j in range(depth):
        copies[j].wait()
        unit, _ = unit_rows(xs[j])
        rows = pl.ds(j * block, block)
        wide = unit * gain[...]
        normed[rows, :] = wide.astype(BF16)
        sender.send(normed.at[rows], normed_h.at[rows])
        normed_t[:, rows] = jnp.transpose(wide).astype(BF16)
        sender.send(normed_t.at[:, rows], normed_t_h.at[:, rows])
    sender.finish()


def forward_kernel(dims, *refs):
    depth, zs, shard, block, span = dims
    heads = span // HEAD_DIM
    pos, w_near, w_far, normed_h = refs[:4]
    (query_h, query_t_h, keys_h, values_h, keys_t_h, att_t_h, lse_h) = refs[4:11]
    (weights_t_h, w_out_t_h), outs_h = refs[11:13], refs[13 : 13 + depth]
    refs = refs[13 + depth :]
    normed, query, query_t, keys, values, keys_t, values_t, att_t, lse = refs[:9]
    wq, wk, wv, w_out, weights_t, w_out_t, outs, in_sems, out_sems = refs[9:]
    copies = fetch([(normed_h, normed)], in_sems)
    sender = Sender(out_sems)

    own_z, first = pos[0], pos[1] == 0
    for z in range(zs):
        for d in range(depth):
            near, far = w_near[z ^ own_z, d].astype(F32), w_far[z ^ own_z, d].astype(F32)
            both = jnp.concatenate(
                [jnp.where(first, near, far), jnp.where(first, far, near)], axis=0
            ).astype(BF16)
            rows = slice((d * zs + z) * 2 * shard, (d * zs + z + 1) * 2 * shard)
            for i, w in enumerate((wq, wk, wv)):
                w[rows, :] = both[:, i * span : (i + 1) * span]
            rows = slice(z * 2 * shard, (z + 1) * 2 * shard)
            w_out[rows, d * span : (d + 1) * span] = both[:, 3 * span :]
    copies[0].wait()

    for scale, w, full, turned, full_h, turned_h in (
        (SCALE, wq, query, query_t, query_h, query_t_h),
        (1.0, wk, keys, keys_t, keys_h, keys_t_h),
        (1.0, wv, values, values_t, values_h, None),
    ):
        rows = (scale * dot(normed[...], w[...])).astype(BF16)
        full[...] = rows
        turned[...] = jnp.transpose(rows)
        sender.send(full, full_h)
        if turned_h is not None:
            sender.send(turned, turned_h)
    for i, w in enumerate((wq, wk, wv)):
        weights_t[i * span : (i + 1) * span, :] = jnp.transpose(w[...])
    sender.send(weights_t, weights_t_h)
    w_out_t[...] = jnp.transpose(w_out[...])
    sender.send(w_out_t, w_out_t_h)


    units = [(j, h) for j in range(depth) for h in range(heads)]

    def score(j, h):
        return dot(keys[...], only_head(query_t[:, j * block : (j + 1) * block], h))

    ready = [score(*unit) for unit in units[:2]]
    for i, (j, h) in enumerate(units):
        cols, lanes = slice(j * block, (j + 1) * block), slice(h * HEAD_DIM, (h + 1) * HEAD_DIM)
        scores = ready.pop(0)
        top = jnp.max(scores, axis=0, keepdims=True)
        e = jnp.exp(scores - top)
        total = jnp.sum(e, axis=0, keepdims=True)
        if i + 2 < len(units):
            ready.append(score(*units[i + 2]))
        att_t[lanes, cols] = dot(values_t[lanes, :], e.astype(BF16)) * (1.0 / total)
        lse[h, :, cols] = top + jnp.log(total)
    sender.send(att_t, att_t_h)
    sender.send(lse, lse_h)
    att = jnp.transpose(att_t[...]).astype(BF16)
    for j in range(depth):
        outs[j] = dot(att[j * block : (j + 1) * block], w_out[...]).astype(BF16)
        sender.send(outs.at[j], outs_h[j])
    sender.finish()


def backward_kernel(dims, *refs):
    depth, zs, shard, block, span = dims
    heads = span // HEAD_DIM
    pos, refs = refs[0], refs[1:]
    gs_h, refs = refs[:depth], refs[depth:]
    (w_out_t_h, query_h, query_t_h, keys_h, values_h, keys_t_h, lse_h, normed_t_h) = refs[:8]
    (att_t_h, weights_t_h, near, far), refs = refs[8:12], refs[12:]
    dns_h, refs = refs[: depth + 1], refs[depth + 1 :]
    (gs, w_out_t, query, query_t, keys, values, keys_t, lse, normed_t, att_t) = refs[:10]
    (weights_t, d_att, d_att_t, delta, d_query_t, d_keys, d_values, d_qkv) = refs[10:18]
    grad_out, dns, in_sems, out_sems = refs[18:]
    copies = fetch(
        [(w_out_t_h, w_out_t)]
        + [(gs_h[j], gs.at[pl.ds(j * block, block)]) for j in range(depth)]
        + [
            (att_t_h, att_t),
            (keys_h, keys),
            (query_t_h, query_t),
            (values_h, values),
            (lse_h, lse),
            (query_h, query),
            (keys_t_h, keys_t),
            (normed_t_h, normed_t),
            (weights_t_h, weights_t),
        ],
        in_sems,
    )
    first, second, third = copies[: 2 + depth], copies[2 + depth : 8 + depth], copies[8 + depth :]

    d_keys[...] = jnp.zeros_like(d_keys)
    d_values[...] = jnp.zeros_like(d_values)
    for copy in first:
        copy.wait()
    part = dot(gs[...], w_out_t[...]).astype(BF16)
    d_att[...] = part
    part = jnp.transpose(part)
    d_att_t[...] = part
    product = part.astype(F32) * att_t[...]
    for h in range(heads):
        delta[h] = jnp.sum(product[h * HEAD_DIM : (h + 1) * HEAD_DIM], axis=0, keepdims=True)
    for copy in second:
        copy.wait()
    masks = head_masks(span)

    def step(j, _):
        cols = pl.ds(pl.multiple_of(j * block, block), block)
        q_block, g_block = query[cols, :], d_att[cols, :]
        qs = [q_block * m for m in masks]
        ds = [g_block * m for m in masks]

        def pair(h):
            q_turned = only_head(query_t[:, cols], h)
            d_turned = only_head(d_att_t[:, cols], h)
            return dot(keys[...], q_turned), dot(values[...], d_turned)

        pairs = [pair(h) for h in range(min(2, heads))]
        for h in range(heads):
            scores, d_probs = pairs[h]
            probs = jnp.exp(scores - lse[h, :, cols])
            d_scores = (probs * (d_probs - delta[h, :, cols])).astype(BF16)
            if h + 2 < heads:
                pairs.append(pair(h + 2))
            values_add = dot(probs.astype(BF16), ds[h])
            keys_add = dot(d_scores, qs[h])
            value_part = values_add if h == 0 else value_part + values_add
            key_part = keys_add if h == 0 else key_part + keys_add
            lanes = slice(h * HEAD_DIM, (h + 1) * HEAD_DIM)
            d_query_t[lanes, cols] = SCALE * dot(keys_t[lanes, :], d_scores)
        d_values[...] += value_part.astype(BF16).astype(F32)
        d_keys[...] += key_part.astype(BF16).astype(F32)
        return 0

    lax.fori_loop(0, depth, step, 0)
    d_qkv[:, :span] = jnp.transpose(d_query_t[...].astype(BF16))
    d_qkv[:, span : 2 * span] = d_keys[...].astype(BF16)
    d_qkv[:, 2 * span :] = d_values[...].astype(BF16)
    for copy in third:
        copy.wait()
    sender = Sender(out_sems)
    for i in range(0, depth, 2):
        rows = slice(i * block, (i + 2) * block)
        dns[rows, :] = dot(d_qkv[rows, :], weights_t[...]).astype(BF16)
        for j in (i, i + 1):
            if j < depth - 1:
                sender.send(dns.at[pl.ds(j * block, block)], dns_h[j])
            else:
                half = block // 2
                sender.send(dns.at[pl.ds(j * block, half)], dns_h[j])
                sender.send(dns.at[pl.ds(j * block + half, half)], dns_h[j + 1])

    grad_out[...] = dot(att_t[...].astype(BF16), gs[...])
    grads = dot(normed_t[...], d_qkv[...])
    own_z, first, own_d = pos[0], pos[1] == 0, pos[2]
    for d in range(depth):
        for z in range(zs):
            sides = []
            for c in range(2):
                row, row_out = ((d * zs + z) * 2 + c) * shard, (z * 2 + c) * shard
                sides.append(
                    (
                        grads[row : row + shard],
                        grad_out[row_out : row_out + shard, d * span : (d + 1) * span],
                    )
                )
            at = 0
            for one, two in zip(*sides):
                lanes = slice(at, at + one.shape[1])
                at += one.shape[1]
                near[z ^ own_z, d ^ own_d, :, lanes] = jnp.where(first, one, two).astype(BF16)
                far[z ^ own_z, d ^ own_d, :, lanes] = jnp.where(first, two, one).astype(BF16)
    sender.finish()


def finish_kernel(dims, *refs):
    depth, zs, shard, block, span = dims
    pos, gain, gain_row, x, upstream, refs = *refs[:5], refs[5:]
    dns, weights, acc, refs = refs[:3], refs[3:6], refs[6], refs[7:]
    parts, outs = refs[: depth - 1], refs[depth - 1 :]
    own_d = pos[2]

    d_unit = dns[0][...].astype(F32) + dns[1][...].astype(F32) + dns[2][...].astype(F32)
    unit, inverse = unit_rows(x[...])
    d_unit = d_unit * gain_row[...]
    outs[5][...] = (
        upstream[...].astype(F32)
        + inverse
        * (
            d_unit
            - jnp.mean(d_unit, axis=-1, keepdims=True)
            - unit * jnp.mean(d_unit * unit, axis=-1, keepdims=True)
        )
    ).astype(BF16)

    blocks = [acc[0][:, : 3 * span]] + [p[...].astype(F32) for p in parts]
    for d in range(depth):
        lanes = slice(d * span, (d + 1) * span)
        total = blocks[0]
        for k in range(1, depth):
            total = jnp.where((d ^ own_d) == k, blocks[k], total)
        for i in range(3):
            outs[i][:, lanes] = total[:, i * span : (i + 1) * span]
        outs[3][:, lanes] = acc[d ^ own_d][:, 3 * span :]
    column = weights[0][...].astype(F32) * outs[0][...]
    for w, grad in zip(weights[1:], outs[1:3]):
        column = column + w[...].astype(F32) * grad[...]
    column = jnp.sum(column, axis=1, keepdims=True)
    wide = jnp.concatenate([column, jnp.zeros((128 - shard, 1), F32)], axis=0)
    row = jnp.transpose(jnp.broadcast_to(wide, (128, 128)))[0:1, :shard]
    outs[4][...] = row / gain[...]


VMEM, ANY, SMEM = pltpu.VMEM, pl.ANY, pltpu.SMEM


def call(kernel, dims, ins, outs, scratch, sems, flops, mib=56):
    args = [a for a, _ in ins]
    shapes = [jax.ShapeDtypeStruct(shape, kind) for shape, kind, _ in outs]
    size = sum(a.size * a.dtype.itemsize for a in args + shapes)
    return pl.pallas_call(
        functools.partial(kernel, dims),
        out_shape=shapes,
        in_specs=[pl.BlockSpec(memory_space=space) for _, space in ins],
        out_specs=[pl.BlockSpec(memory_space=space) for _, _, space in outs],
        scratch_shapes=[pltpu.VMEM(shape, kind) for shape, kind in scratch]
        + [pltpu.SemaphoreType.DMA((n,)) for n in sems],
        compiler_params=pltpu.CompilerParams(vmem_limit_bytes=mib * 1024 * 1024),
        cost_estimate=pl.CostEstimate(flops=flops, bytes_accessed=size, transcendentals=0),
    )(*args)


def head_body(depth, res, *args):
    x, gain, w_query, w_key, w_value, w_out, upstream = args
    homologs, _, width = x.shape
    span, zs = width // depth, res // 2
    shard = w_query.shape[0]
    total, heads = homologs * depth, span // HEAD_DIM
    dims = (depth, zs, shard, homologs, span)
    x = x.reshape(homologs, width)
    upstream = upstream.reshape(homologs, width)
    gain = gain.reshape(1, width)
    pos = jnp.stack([lax.axis_index(a) for a in ("z", "core", "depth")]).astype(jnp.int32)

    xs = [x] + [swap(x, "depth", depth, k) for k in range(1, depth - 1)]

    packed, out_cut = call(
        pack_kernel,
        dims,
        [(w, VMEM) for w in (w_query, w_key, w_value, w_out)],
        [((depth, shard, 3 * span), BF16, VMEM), ((depth, shard, span), BF16, VMEM)],
        [],
        [],
        1000,
    )
    mine = lax.all_to_all(packed, "depth", 0, 0, tiled=True)
    mine = jnp.concatenate([mine, out_cut], axis=2)
    mine, *xs = lax.optimization_barrier([mine] + xs)
    xs.append(swap(xs[0], "depth", depth, depth - 1))
    parts = [mine] + [swap(mine, "z", zs, k) for k in range(1, zs)]
    gs = [upstream] + [swap(upstream, "depth", depth, k) for k in range(1, depth)]

    rows, turned = ((total, span), BF16), ((span, total), BF16)
    half = homologs // 2
    block, halved = ((homologs, width), BF16), ((half, width), BF16)
    blocks = ((depth, homologs, width), BF16)
    norm, stats = ((total, width), BF16), ((heads, 1, total), F32)
    in_weights, out_weights = ((width, span), BF16), ((span, width), BF16)
    pass_flops = 2 * total * total * span
    normed, normed_t = call(
        norm_kernel,
        dims,
        [(gain, VMEM)] + [(a, ANY) for a in xs],
        [norm + (ANY,), ((width, total), BF16, ANY)],
        [blocks, norm, ((width, total), BF16)],
        [depth, 2 * depth],
        1000,
    )
    first_row = (lax.axis_index("depth") * res + pos[0] * 2 + pos[1]) * shard
    own_gain = lax.dynamic_slice(gain, (0, first_row), (1, shard))
    normed, pos, own_gain, *parts = lax.optimization_barrier([normed, pos, own_gain] + parts)
    w_near = jnp.stack(parts, axis=0)
    w_far = swap(w_near, "core", 2, 1)

    turned_f32 = ((span, total), F32)
    saved = [rows, turned, rows, rows, turned, turned_f32, stats]
    weights_shape = ((3 * span, width), BF16)
    saved = saved + [weights_shape, in_weights]
    query, query_t, keys, values, keys_t, att_t, lse, weights_t, wo_t, *outs = call(
        forward_kernel,
        dims,
        [(pos, SMEM), (w_near, VMEM), (w_far, VMEM), (normed, ANY)],
        [s + (ANY,) for s in saved + [block] * depth],
        [norm, rows, turned, rows, rows, turned, turned, turned_f32, stats]
        + [in_weights] * 3
        + [out_weights, weights_shape, in_weights, blocks],
        [1, len(saved) + depth],
        8 * pass_flops,
    )

    packed = (zs, depth, shard, 4 * span)
    near, far, *dns = call(
        backward_kernel,
        dims,
        [(pos, SMEM)]
        + [(a, ANY) for a in gs + [wo_t, query, query_t, keys, values, keys_t, lse, normed_t]]
        + [(a, ANY) for a in (att_t, weights_t)],
        [(packed, BF16, VMEM)] * 2 + [s + (ANY,) for s in [block] * 3 + [halved] * 2],
        [norm, in_weights, rows, turned, rows, rows, turned, stats, ((width, total), BF16)]
        + [turned_f32, weights_shape, rows, turned, stats, turned_f32]
        + [((total, span), F32)] * 2
        + [((total, 3 * span), BF16), ((span, width), F32), norm],
        [depth + 10, depth + 1],
        24 * pass_flops,
    )

    outs = [outs[0]] + [swap(outs[k], "depth", depth, k) for k in range(1, depth)]
    near, far, dns, outs = lax.optimization_barrier((near, far, dns, outs))

    far = swap(far, "core", 2, 1)
    dn0, dn1, dn2, dn3_top, dn3_bottom = dns
    top, bottom = swap(dn3_top, "depth", depth, 1), swap(dn3_bottom, "depth", depth, 2)
    sums = [near[k].astype(F32) + far[k].astype(F32) for k in range(1, zs)]
    low = [swap(part.astype(BF16), "z", zs, k + 1) for k, part in enumerate(sums)]
    low[0], top, bottom, outs = lax.optimization_barrier((low[0], top, bottom, outs))
    dn2 = dn2.astype(F32) + jnp.concatenate([top, jnp.zeros_like(top)], axis=0).astype(F32)
    dn1 = dn1.astype(F32) + jnp.concatenate([jnp.zeros_like(bottom), bottom], axis=0).astype(F32)
    final_result = (x.astype(F32) + sum(o.astype(F32) for o in outs)).astype(BF16)
    own = near[0].astype(F32) + far[0].astype(F32)
    dn1, dn2, final_result, own = lax.optimization_barrier(
        (dn1.astype(BF16), dn2.astype(BF16), final_result, own)
    )
    dn1, dn2 = swap(dn1, "depth", depth, 1), swap(dn2, "depth", depth, 2)
    acc = own + sum(p.astype(F32) for p in low)
    parts = [
        swap(acc[k, :, : 3 * span].astype(BF16), "depth", depth, k) for k in range(1, depth)
    ]
    grad_query, grad_key, grad_value, grad_out, gain_rows, alignment = call(
        finish_kernel,
        dims,
        [(pos, SMEM)]
        + [(a, VMEM) for a in (own_gain, gain, x, upstream, dn0, dn1, dn2)]
        + [(a, VMEM) for a in [w_query, w_key, w_value, acc] + parts],
        [((shard, width), F32, VMEM)] * 4 + [((1, shard), F32, VMEM), block + (VMEM,)],
        [],
        [],
        1000 * total * width,
        16,
    )
    return (
        final_result.reshape(homologs, 1, width),
        alignment.reshape(homologs, 1, width),
        grad_query,
        grad_key,
        grad_value,
        grad_out,
        gain_rows.reshape(shard),
    )


def solution(mesh):
    depth, res = mesh.shape["depth"], mesh.shape["res"]
    powers = depth & (depth - 1) == 0 and res & (res - 1) == 0 and res > 1
    if powers and depth == 4 and res >= 4 and HEADS % depth == 0:
        axes = ("depth", "z", "core")
        mesh = Mesh(mesh.devices.reshape(depth, res // 2, 2), axes)
        res_axes, run = ("z", "core"), functools.partial(head_body, depth, res)
    else:
        axes = ("depth", "res")
        res_axes, run = ("res",), general_body

    def body(*args):
        if args[0].shape[1] != 1:
            return general_body(*args, axes=axes)
        return run(*args)

    rows = P("depth", res_axes, None)
    weight = P(axes, None)
    return jax.shard_map(
        body,
        mesh=mesh,
        in_specs=(rows, P(), weight, weight, weight, weight, rows),
        out_specs=(rows, rows, weight, weight, weight, weight, P(axes)),
        check_vma=False,
    )
```

```python
import functools

import jax
import jax.numpy as jnp
from jax import lax
from jax.experimental import pallas as pl
from jax.experimental.pallas import tpu as pltpu
from jax.sharding import Mesh, PartitionSpec as P

HEADS = 12
HEAD_DIM = 64


def standardize_entries(family_activity, rescale_factor):
    payload_entries = family_activity.astype(jnp.float32)
    centered = payload_entries - jnp.mean(payload_entries, axis=-1, keepdims=True)
    reciprocal_spread = lax.rsqrt(jnp.mean(centered * centered, axis=-1, keepdims=True) + 1e-05)
    standardized_entries = centered * reciprocal_spread
    return (
        (standardized_entries * rescale_factor).astype(jnp.bfloat16),
        standardized_entries,
        reciprocal_spread,
    )


def project(rows, weight, factor):
    return (factor * jnp.dot(rows, weight, preferred_element_type=jnp.float32)).astype(jnp.bfloat16)


def to_heads(array):
    count, cols = (array.shape[0], array.shape[1])
    return jnp.transpose(array.reshape(count, cols, HEADS, HEAD_DIM), (1, 2, 0, 3)).reshape(
        cols * HEADS, count, HEAD_DIM
    )


def from_heads(array, cols):
    count = array.shape[1]
    return jnp.transpose(array.reshape(cols, HEADS, count, HEAD_DIM), (2, 0, 1, 3)).reshape(
        count, cols, HEADS * HEAD_DIM
    )


def head_pass(query, keys, payload_entries, d_att):
    scale = HEAD_DIM ** (-0.5)
    scores = jnp.dot(query, keys.T, preferred_element_type=jnp.float32)
    probs = jax.nn.softmax(scores, axis=-1)
    probs_b = probs.astype(jnp.bfloat16)
    mixed_homologs = jnp.dot(probs_b, payload_entries, preferred_element_type=jnp.float32).astype(
        jnp.bfloat16
    )
    d_probs = jnp.dot(d_att, payload_entries.T, preferred_element_type=jnp.float32)
    d_scores = probs * (d_probs - jnp.sum(probs * d_probs, axis=-1, keepdims=True))
    d_scores_b = d_scores.astype(jnp.bfloat16)
    d_query = (scale * jnp.dot(d_scores_b, keys, preferred_element_type=jnp.float32)).astype(
        jnp.bfloat16
    )
    key_part = jnp.einsum("st,sd->td", d_scores_b, query, preferred_element_type=jnp.float32)
    value_part = jnp.einsum("st,sd->td", probs_b, d_att, preferred_element_type=jnp.float32)
    return (mixed_homologs, d_query, key_part, value_part)


def general_body(
    family_activity,
    rescale_factor,
    asking_weights,
    lookup_weights,
    payload_weights,
    exit_weights,
    upstream_adjoint,
    axes=("depth", "res"),
):
    query_weight, key_weight, value_weight, output_matrix = (
        lax.all_gather(asking_weights, axes, axis=0, tiled=True),
        lax.all_gather(lookup_weights, axes, axis=0, tiled=True),
        lax.all_gather(payload_weights, axes, axis=0, tiled=True),
        lax.all_gather(exit_weights, axes, axis=0, tiled=True),
    )
    homologs_each_shard, positions_each_shard, embed_span = family_activity.shape
    standardized_source, standardized_entries, reciprocal_spread = standardize_entries(
        family_activity, rescale_factor
    )
    query = project(standardized_source, query_weight, HEAD_DIM ** (-0.5))
    keys = project(standardized_source, key_weight, 1.0)
    payload_entries = project(standardized_source, value_weight, 1.0)
    keys_all, values_all = (
        lax.all_gather(keys, "depth", axis=0, tiled=True),
        lax.all_gather(payload_entries, "depth", axis=0, tiled=True),
    )
    d_att = jnp.dot(upstream_adjoint, output_matrix.T, preferred_element_type=jnp.float32).astype(
        jnp.bfloat16
    )

    def per_head(items):
        return head_pass(items[0], items[1], items[2], items[3])

    mixed_homologs, d_query, key_part, value_part = lax.map(
        per_head, (to_heads(query), to_heads(keys_all), to_heads(values_all), to_heads(d_att))
    )
    mixed_homologs = from_heads(mixed_homologs, positions_each_shard)
    d_query = from_heads(d_query, positions_each_shard)
    key_part = from_heads(key_part, positions_each_shard)
    value_part = from_heads(value_part, positions_each_shard)
    rows = homologs_each_shard * positions_each_shard
    normed_rows = standardized_source.reshape(rows, embed_span)
    part_query = jnp.dot(
        normed_rows.T, d_query.reshape(rows, embed_span), preferred_element_type=jnp.float32
    )
    part_out = jnp.dot(
        mixed_homologs.reshape(rows, embed_span).T,
        upstream_adjoint.reshape(rows, embed_span),
        preferred_element_type=jnp.float32,
    )
    stacked = jnp.stack([key_part, value_part], axis=2).astype(jnp.bfloat16)
    summed = (
        lax.psum_scatter(stacked, "depth", scatter_dimension=0, tiled=True)
        .astype(jnp.float32)
        .astype(jnp.bfloat16)
    )
    d_keys = summed[:, :, 0, :]
    d_values = summed[:, :, 1, :]
    final_result = (
        family_activity.astype(jnp.float32)
        + jnp.dot(mixed_homologs, output_matrix, preferred_element_type=jnp.float32)
    ).astype(jnp.bfloat16)
    part_key = jnp.dot(
        normed_rows.T, d_keys.reshape(rows, embed_span), preferred_element_type=jnp.float32
    )
    part_value = jnp.dot(
        normed_rows.T, d_values.reshape(rows, embed_span), preferred_element_type=jnp.float32
    )
    d_normed = jnp.dot(d_query, query_weight.T, preferred_element_type=jnp.float32)
    d_normed = d_normed + jnp.dot(d_keys, key_weight.T, preferred_element_type=jnp.float32)
    d_normed = d_normed + jnp.dot(d_values, value_weight.T, preferred_element_type=jnp.float32)
    part_gain = jnp.sum((d_normed * standardized_entries).reshape(rows, embed_span), axis=0)
    unit_gradient = d_normed * rescale_factor
    alignment_gradient = upstream_adjoint.astype(jnp.float32) + reciprocal_spread * (
        unit_gradient
        - jnp.mean(unit_gradient, axis=-1, keepdims=True)
        - standardized_entries
        * jnp.mean(unit_gradient * standardized_entries, axis=-1, keepdims=True)
    )
    query_gradient, key_gradient, value_gradient, output_gradient, gain_gradient = (
        lax.psum_scatter(part_query, axes, scatter_dimension=0, tiled=True),
        lax.psum_scatter(part_key, axes, scatter_dimension=0, tiled=True),
        lax.psum_scatter(part_value, axes, scatter_dimension=0, tiled=True),
        lax.psum_scatter(part_out, axes, scatter_dimension=0, tiled=True),
        lax.psum_scatter(part_gain, axes, scatter_dimension=0, tiled=True),
    )
    return (
        final_result,
        alignment_gradient.astype(jnp.bfloat16),
        query_gradient,
        key_gradient,
        value_gradient,
        output_gradient,
        gain_gradient,
    )


F32, BF16 = jnp.float32, jnp.bfloat16
SCALE = HEAD_DIM ** (-0.5)


def swap(value, axis, size, bits):
    return lax.ppermute(value, axis, [(i, i ^ bits) for i in range(size)])


def dot(a, b, contract=(1, 0)):
    return lax.dot_general(
        a, b, (((contract[0],), (contract[1],)), ((), ())), preferred_element_type=F32
    )


def unit_rows(x):
    x = x.astype(F32)
    centered = x - jnp.mean(x, axis=-1, keepdims=True)
    inverse = lax.rsqrt(jnp.mean(centered * centered, axis=-1, keepdims=True) + 1e-05)
    return centered * inverse, inverse


def head_masks(span):
    lane = lax.broadcasted_iota(jnp.int32, (8, span), 1)
    return [
        ((lane >= at) & (lane < at + HEAD_DIM)).astype(F32)[0:1].astype(BF16)
        for at in range(0, span, HEAD_DIM)
    ]


def only_head(turned, h):
    low, high = h * HEAD_DIM, (h + 1) * HEAD_DIM
    parts = [jnp.zeros((low, turned.shape[1]), turned.dtype)] if low else []
    parts.append(turned[low:high])
    if high < turned.shape[0]:
        parts.append(jnp.zeros((turned.shape[0] - high, turned.shape[1]), turned.dtype))
    return jnp.concatenate(parts, axis=0)


def fetch(pairs, sems):
    copies = [pltpu.make_async_copy(src, dst, sems.at[i]) for i, (src, dst) in enumerate(pairs)]
    for copy in copies:
        copy.start()
    return copies


class Sender:
    def __init__(self, sems):
        self.sems, self.copies = sems, []

    def send(self, src, dst):
        copy = pltpu.make_async_copy(src, dst, self.sems.at[len(self.copies)])
        copy.start()
        self.copies.append(copy)

    def finish(self):
        for copy in self.copies:
            copy.wait()


def pack_kernel(dims, w_query, w_key, w_value, w_out, out, out_cut):
    depth, zs, shard, block, span = dims
    for d in range(depth):
        lanes = slice(d * span, (d + 1) * span)
        for i, w in enumerate((w_query, w_key, w_value)):
            out[d, :, i * span : (i + 1) * span] = w[:, lanes]
        out[d, :, 3 * span :] = w_out[:, lanes]
        out_cut[d] = w_out[:, lanes]


def norm_kernel(dims, *refs):
    depth, zs, shard, block, span = dims
    gain, xs_h, refs = refs[0], refs[1 : 1 + depth], refs[1 + depth :]
    normed_h, normed_t_h, xs, normed, normed_t, in_sems, out_sems = refs
    copies = fetch([(xs_h[j], xs.at[j]) for j in range(depth)], in_sems)
    sender = Sender(out_sems)
    for j in range(depth):
        copies[j].wait()
        unit, _ = unit_rows(xs[j])
        rows = pl.ds(j * block, block)
        wide = unit * gain[...]
        normed[rows, :] = wide.astype(BF16)
        sender.send(normed.at[rows], normed_h.at[rows])
        normed_t[:, rows] = jnp.transpose(wide).astype(BF16)
        sender.send(normed_t.at[:, rows], normed_t_h.at[:, rows])
    sender.finish()


def forward_kernel(dims, *refs):
    depth, zs, shard, block, span = dims
    heads = span // HEAD_DIM
    pos, w_near, w_far, normed_h = refs[:4]
    (query_h, query_t_h, keys_h, values_h, keys_t_h, att_t_h, lse_h) = refs[4:11]
    (wq_t_h, wk_t_h, wv_t_h, w_out_t_h), outs_h = refs[11:15], refs[15 : 15 + depth]
    refs = refs[15 + depth :]
    normed, query, query_t, keys, values, keys_t, values_t, att_t, lse = refs[:9]
    wq, wk, wv, w_out, wq_t, wk_t, wv_t, w_out_t, outs, in_sems, out_sems = refs[9:]
    copies = fetch([(normed_h, normed)], in_sems)
    sender = Sender(out_sems)

    own_z, first = pos[0], pos[1] == 0
    for z in range(zs):
        for d in range(depth):
            near, far = w_near[z ^ own_z, d].astype(F32), w_far[z ^ own_z, d].astype(F32)
            both = jnp.concatenate(
                [jnp.where(first, near, far), jnp.where(first, far, near)], axis=0
            ).astype(BF16)
            rows = slice((d * zs + z) * 2 * shard, (d * zs + z + 1) * 2 * shard)
            for i, w in enumerate((wq, wk, wv)):
                w[rows, :] = both[:, i * span : (i + 1) * span]
            rows = slice(z * 2 * shard, (z + 1) * 2 * shard)
            w_out[rows, d * span : (d + 1) * span] = both[:, 3 * span :]
    copies[0].wait()

    for scale, w, full, turned, full_h, turned_h in (
        (SCALE, wq, query, query_t, query_h, query_t_h),
        (1.0, wk, keys, keys_t, keys_h, keys_t_h),
        (1.0, wv, values, values_t, values_h, None),
    ):
        rows = (scale * dot(normed[...], w[...])).astype(BF16)
        full[...] = rows
        turned[...] = jnp.transpose(rows)
        sender.send(full, full_h)
        if turned_h is not None:
            sender.send(turned, turned_h)
    for w, turned, turned_h in (
        (wq, wq_t, wq_t_h),
        (wk, wk_t, wk_t_h),
        (wv, wv_t, wv_t_h),
        (w_out, w_out_t, w_out_t_h),
    ):
        turned[...] = jnp.transpose(w[...])
        sender.send(turned, turned_h)


    units = [(j, h) for j in range(depth) for h in range(heads)]

    def score(j, h):
        return dot(keys[...], only_head(query_t[:, j * block : (j + 1) * block], h))

    ready = [score(*unit) for unit in units[:2]]
    for i, (j, h) in enumerate(units):
        cols, lanes = slice(j * block, (j + 1) * block), slice(h * HEAD_DIM, (h + 1) * HEAD_DIM)
        scores = ready.pop(0)
        top = jnp.max(scores, axis=0, keepdims=True)
        e = jnp.exp(scores - top)
        total = jnp.sum(e, axis=0, keepdims=True)
        if i + 2 < len(units):
            ready.append(score(*units[i + 2]))
        att_t[lanes, cols] = dot(values_t[lanes, :], e.astype(BF16)) * (1.0 / total)
        lse[h, :, cols] = top + jnp.log(total)
    sender.send(att_t, att_t_h)
    sender.send(lse, lse_h)
    att = jnp.transpose(att_t[...]).astype(BF16)
    for j in range(depth):
        outs[j] = dot(att[j * block : (j + 1) * block], w_out[...]).astype(BF16)
        sender.send(outs.at[j], outs_h[j])
    sender.finish()


def backward_kernel(dims, *refs):
    depth, zs, shard, block, span = dims
    heads = span // HEAD_DIM
    pos, refs = refs[0], refs[1:]
    gs_h, refs = refs[:depth], refs[depth:]
    (w_out_t_h, query_h, query_t_h, keys_h, values_h, keys_t_h, lse_h, normed_t_h) = refs[:8]
    (att_t_h, wq_t_h, wk_t_h, wv_t_h, near, far), refs = refs[8:14], refs[14:]
    dns_h, refs = refs[: depth + 1], refs[depth + 1 :]
    (gs, w_out_t, query, query_t, keys, values, keys_t, lse, normed_t, att_t) = refs[:10]
    (wq_t, wk_t, wv_t, d_att, d_att_t, delta, d_query_t, d_keys, d_values) = refs[10:19]
    grad_out, dns, in_sems, out_sems = refs[19:]
    copies = fetch(
        [(w_out_t_h, w_out_t)]
        + [(gs_h[j], gs.at[pl.ds(j * block, block)]) for j in range(depth)]
        + [
            (att_t_h, att_t),
            (keys_h, keys),
            (query_h, query),
            (query_t_h, query_t),
            (values_h, values),
            (lse_h, lse),
            (keys_t_h, keys_t),
            (normed_t_h, normed_t),
            (wq_t_h, wq_t),
            (wk_t_h, wk_t),
            (wv_t_h, wv_t),
        ],
        in_sems,
    )
    loaded, later = 8 + depth, copies[8 + depth :]

    d_keys[...] = jnp.zeros_like(d_keys)
    d_values[...] = jnp.zeros_like(d_values)
    for copy in copies[: 2 + depth]:
        copy.wait()
    part = dot(gs[...], w_out_t[...]).astype(BF16)
    d_att[...] = part
    part = jnp.transpose(part)
    d_att_t[...] = part
    product = part.astype(F32) * att_t[...]
    for h in range(heads):
        delta[h] = jnp.sum(product[h * HEAD_DIM : (h + 1) * HEAD_DIM], axis=0, keepdims=True)
    for copy in copies[2 + depth : loaded]:
        copy.wait()
    masks = head_masks(span)

    def step(j, _):
        cols = pl.ds(pl.multiple_of(j * block, block), block)
        q_block, g_block = query[cols, :], d_att[cols, :]
        qs = [q_block * m for m in masks]
        ds = [g_block * m for m in masks]

        def pair(h):
            q_turned = only_head(query_t[:, cols], h)
            d_turned = only_head(d_att_t[:, cols], h)
            return dot(keys[...], q_turned), dot(values[...], d_turned)

        pairs = [pair(h) for h in range(min(2, heads))]
        for h in range(heads):
            scores, d_probs = pairs[h]
            probs = jnp.exp(scores - lse[h, :, cols])
            d_scores = (probs * (d_probs - delta[h, :, cols])).astype(BF16)
            if h + 2 < heads:
                pairs.append(pair(h + 2))
            values_add = dot(probs.astype(BF16), ds[h])
            keys_add = dot(d_scores, qs[h])
            value_part = values_add if h == 0 else value_part + values_add
            key_part = keys_add if h == 0 else key_part + keys_add
            lanes = slice(h * HEAD_DIM, (h + 1) * HEAD_DIM)
            d_query_t[lanes, cols] = SCALE * dot(keys_t[lanes, :], d_scores)
        d_values[...] += value_part.astype(BF16).astype(F32)
        d_keys[...] += key_part.astype(BF16).astype(F32)
        return 0

    lax.fori_loop(0, depth, step, 0)
    for copy in later:
        copy.wait()
    d_query = jnp.transpose(d_query_t[...].astype(BF16))
    d_key, d_value = d_keys[...].astype(BF16), d_values[...].astype(BF16)
    sender = Sender(out_sems)
    for i in range(0, depth, 2):
        rows = slice(i * block, (i + 2) * block)
        d_normed = dot(d_query[rows], wq_t[...])
        d_normed = d_normed + dot(d_key[rows], wk_t[...])
        d_normed = d_normed + dot(d_value[rows], wv_t[...])
        dns[rows, :] = d_normed.astype(BF16)
        for j in (i, i + 1):
            if j < depth - 1:
                sender.send(dns.at[pl.ds(j * block, block)], dns_h[j])
            else:
                half = block // 2
                sender.send(dns.at[pl.ds(j * block, half)], dns_h[j])
                sender.send(dns.at[pl.ds(j * block + half, half)], dns_h[j + 1])

    grad_out[...] = dot(att_t[...].astype(BF16), gs[...])
    grads = [dot(normed_t[...], d) for d in (d_query, d_key, d_value)]
    own_z, first, own_d = pos[0], pos[1] == 0, pos[2]
    for d in range(depth):
        for z in range(zs):
            sides = []
            for c in range(2):
                row, row_out = ((d * zs + z) * 2 + c) * shard, (z * 2 + c) * shard
                sides.append(
                    [g[row : row + shard] for g in grads]
                    + [grad_out[row_out : row_out + shard, d * span : (d + 1) * span]]
                )
            at = 0
            for one, two in zip(*sides):
                lanes = slice(at, at + one.shape[1])
                at += one.shape[1]
                near[z ^ own_z, d ^ own_d, :, lanes] = jnp.where(first, one, two).astype(BF16)
                far[z ^ own_z, d ^ own_d, :, lanes] = jnp.where(first, two, one).astype(BF16)
    sender.finish()


def align_kernel(dims, gain, x, upstream, *refs):
    dns, out = refs[:-1], refs[-1]
    d_normed = dns[0][...].astype(F32)
    for part in dns[1:]:
        d_normed = d_normed + part[...].astype(F32)
    unit, inverse = unit_rows(x[...])
    d_unit = d_normed * gain[...]
    out[...] = (
        upstream[...].astype(F32)
        + inverse
        * (
            d_unit
            - jnp.mean(d_unit, axis=-1, keepdims=True)
            - unit * jnp.mean(d_unit * unit, axis=-1, keepdims=True)
        )
    ).astype(BF16)


def finish_kernel(dims, *refs):
    depth, zs, shard, block, span = dims
    pos, gain, weights, acc, refs = refs[0], refs[1], refs[2:5], refs[5], refs[6:]
    parts, outs = refs[: depth - 1], refs[depth - 1 :]
    own_d = pos[2]
    blocks = [acc[0][:, : 3 * span]] + [p[...].astype(F32) for p in parts]
    for d in range(depth):
        lanes = slice(d * span, (d + 1) * span)
        total = blocks[0]
        for k in range(1, depth):
            total = jnp.where((d ^ own_d) == k, blocks[k], total)
        for i in range(3):
            outs[i][:, lanes] = total[:, i * span : (i + 1) * span]
        outs[3][:, lanes] = acc[d ^ own_d][:, 3 * span :]
    column = weights[0][...].astype(F32) * outs[0][...]
    for w, grad in zip(weights[1:], outs[1:3]):
        column = column + w[...].astype(F32) * grad[...]
    column = jnp.sum(column, axis=1, keepdims=True)
    wide = jnp.concatenate([column, jnp.zeros((128 - shard, 1), F32)], axis=0)
    row = jnp.transpose(jnp.broadcast_to(wide, (128, 128)))[0:1, :shard]
    outs[4][...] = row / gain[...]


VMEM, ANY, SMEM = pltpu.VMEM, pl.ANY, pltpu.SMEM


def call(kernel, dims, ins, outs, scratch, sems, flops, mib=56):
    args = [a for a, _ in ins]
    shapes = [jax.ShapeDtypeStruct(shape, kind) for shape, kind, _ in outs]
    size = sum(a.size * a.dtype.itemsize for a in args + shapes)
    return pl.pallas_call(
        functools.partial(kernel, dims),
        out_shape=shapes,
        in_specs=[pl.BlockSpec(memory_space=space) for _, space in ins],
        out_specs=[pl.BlockSpec(memory_space=space) for _, _, space in outs],
        scratch_shapes=[pltpu.VMEM(shape, kind) for shape, kind in scratch]
        + [pltpu.SemaphoreType.DMA((n,)) for n in sems],
        compiler_params=pltpu.CompilerParams(vmem_limit_bytes=mib * 1024 * 1024),
        cost_estimate=pl.CostEstimate(flops=flops, bytes_accessed=size, transcendentals=0),
    )(*args)


def head_body(depth, res, *args):
    x, gain, w_query, w_key, w_value, w_out, upstream = args
    homologs, _, width = x.shape
    span, zs = width // depth, res // 2
    shard = w_query.shape[0]
    total, heads = homologs * depth, span // HEAD_DIM
    dims = (depth, zs, shard, homologs, span)
    x = x.reshape(homologs, width)
    upstream = upstream.reshape(homologs, width)
    gain = gain.reshape(1, width)
    pos = jnp.stack([lax.axis_index(a) for a in ("z", "core", "depth")]).astype(jnp.int32)

    xs = [x] + [swap(x, "depth", depth, k) for k in range(1, depth - 1)]

    packed, out_cut = call(
        pack_kernel,
        dims,
        [(w, VMEM) for w in (w_query, w_key, w_value, w_out)],
        [((depth, shard, 4 * span), BF16, VMEM), ((depth, shard, span), BF16, VMEM)],
        [],
        [],
        1000,
    )
    mine = lax.all_to_all(packed, "depth", 0, 0, tiled=True)
    mine = lax.dynamic_update_slice(mine, out_cut, (0, 0, 3 * span))
    mine, *xs = lax.optimization_barrier([mine] + xs)
    xs.append(swap(xs[0], "depth", depth, depth - 1))
    parts = [mine] + [swap(mine, "z", zs, k) for k in range(1, zs)]
    gs = [upstream] + [swap(upstream, "depth", depth, k) for k in range(1, depth)]

    rows, turned = ((total, span), BF16), ((span, total), BF16)
    half = homologs // 2
    block, halved = ((homologs, width), BF16), ((half, width), BF16)
    blocks = ((depth, homologs, width), BF16)
    norm, stats = ((total, width), BF16), ((heads, 1, total), F32)
    in_weights, out_weights = ((width, span), BF16), ((span, width), BF16)
    pass_flops = 2 * total * total * span
    normed, normed_t = call(
        norm_kernel,
        dims,
        [(gain, VMEM)] + [(a, ANY) for a in xs],
        [norm + (ANY,), ((width, total), BF16, ANY)],
        [blocks, norm, ((width, total), BF16)],
        [depth, 2 * depth],
        1000,
    )
    first_row = (lax.axis_index("depth") * res + pos[0] * 2 + pos[1]) * shard
    own_gain = lax.dynamic_slice(gain, (0, first_row), (1, shard))
    normed, pos, own_gain, *parts = lax.optimization_barrier([normed, pos, own_gain] + parts)
    w_near = jnp.stack(parts, axis=0)
    w_far = swap(w_near, "core", 2, 1)

    turned_f32 = ((span, total), F32)
    saved = [rows, turned, rows, rows, turned, turned_f32, stats]
    saved = saved + [out_weights] * 3 + [in_weights]
    query, query_t, keys, values, keys_t, att_t, lse, wq_t, wk_t, wv_t, wo_t, *outs = call(
        forward_kernel,
        dims,
        [(pos, SMEM), (w_near, VMEM), (w_far, VMEM), (normed, ANY)],
        [s + (ANY,) for s in saved + [block] * depth],
        [norm, rows, turned, rows, rows, turned, turned, turned_f32, stats]
        + [in_weights] * 3
        + [out_weights] * 4
        + [in_weights, blocks],
        [1, len(saved) + depth],
        8 * pass_flops,
    )

    packed = (zs, depth, shard, 4 * span)
    near, far, *dns = call(
        backward_kernel,
        dims,
        [(pos, SMEM)]
        + [(a, ANY) for a in gs + [wo_t, query, query_t, keys, values, keys_t, lse, normed_t]]
        + [(a, ANY) for a in (att_t, wq_t, wk_t, wv_t)],
        [(packed, BF16, VMEM)] * 2 + [s + (ANY,) for s in [block] * 3 + [halved] * 2],
        [norm, in_weights, rows, turned, rows, rows, turned, stats, ((width, total), BF16)]
        + [turned_f32, out_weights, out_weights, out_weights]
        + [rows, turned, stats, turned_f32]
        + [((total, span), F32)] * 2
        + [((span, width), F32), norm],
        [depth + 12, depth + 1],
        24 * pass_flops,
        50,
    )

    outs = [outs[0]] + [swap(outs[k], "depth", depth, k) for k in range(1, depth)]
    near, far, dns, outs = lax.optimization_barrier((near, far, dns, outs))

    far = swap(far, "core", 2, 1)
    dn0, dn1, dn2, dn3_top, dn3_bottom = dns
    top, bottom = swap(dn3_top, "depth", depth, 1), swap(dn3_bottom, "depth", depth, 2)
    sums = [near[k].astype(F32) + far[k].astype(F32) for k in range(1, zs)]
    low = [swap(part.astype(BF16), "z", zs, k + 1) for k, part in enumerate(sums)]
    low[0], top, bottom, outs = lax.optimization_barrier((low[0], top, bottom, outs))
    dn2 = dn2.astype(F32) + jnp.concatenate([top, jnp.zeros_like(top)], axis=0).astype(F32)
    dn1 = dn1.astype(F32) + jnp.concatenate([jnp.zeros_like(bottom), bottom], axis=0).astype(F32)
    final_result = (x.astype(F32) + sum(o.astype(F32) for o in outs)).astype(BF16)
    own = near[0].astype(F32) + far[0].astype(F32)
    dn1, dn2, final_result, own = lax.optimization_barrier(
        (dn1.astype(BF16), dn2.astype(BF16), final_result, own)
    )
    dn1, dn2 = swap(dn1, "depth", depth, 1), swap(dn2, "depth", depth, 2)
    acc = own + sum(p.astype(F32) for p in low)
    parts = [
        swap(acc[k, :, : 3 * span].astype(BF16), "depth", depth, k) for k in range(1, depth)
    ]
    alignment = call(
        align_kernel,
        dims,
        [(a, VMEM) for a in (gain, x, upstream, dn0, dn1, dn2)],
        [block + (VMEM,)],
        [],
        [],
        1000 * total * width,
        16,
    )[0]
    alignment, *parts = lax.optimization_barrier([alignment] + parts)
    grad_query, grad_key, grad_value, grad_out, gain_rows = call(
        finish_kernel,
        dims,
        [(pos, SMEM)]
        + [(a, VMEM) for a in [own_gain, w_query, w_key, w_value, acc] + parts],
        [((shard, width), F32, VMEM)] * 4 + [((1, shard), F32, VMEM)],
        [],
        [],
        1000,
        16,
    )
    return (
        final_result.reshape(homologs, 1, width),
        alignment.reshape(homologs, 1, width),
        grad_query,
        grad_key,
        grad_value,
        grad_out,
        gain_rows.reshape(shard),
    )


def solution(mesh):
    depth, res = mesh.shape["depth"], mesh.shape["res"]
    powers = depth & (depth - 1) == 0 and res & (res - 1) == 0 and res > 1
    if powers and depth == 4 and res >= 4 and HEADS % depth == 0:
        axes = ("depth", "z", "core")
        mesh = Mesh(mesh.devices.reshape(depth, res // 2, 2), axes)
        res_axes, run = ("z", "core"), functools.partial(head_body, depth, res)
    else:
        axes = ("depth", "res")
        res_axes, run = ("res",), general_body

    def body(*args):
        if args[0].shape[1] != 1:
            return general_body(*args, axes=axes)
        return run(*args)

    rows = P("depth", res_axes, None)
    weight = P(axes, None)
    return jax.shard_map(
        body,
        mesh=mesh,
        in_specs=(rows, P(), weight, weight, weight, weight, rows),
        out_specs=(rows, rows, weight, weight, weight, weight, P(axes)),
        check_vma=False,
    )
```

```python
import functools

import jax
import jax.numpy as jnp
from jax import lax
from jax.experimental import pallas as pl
from jax.experimental.pallas import tpu as pltpu
from jax.sharding import Mesh, PartitionSpec as P

HEADS = 12
HEAD_DIM = 64


def standardize_entries(family_activity, rescale_factor):
    payload_entries = family_activity.astype(jnp.float32)
    centered = payload_entries - jnp.mean(payload_entries, axis=-1, keepdims=True)
    reciprocal_spread = lax.rsqrt(jnp.mean(centered * centered, axis=-1, keepdims=True) + 1e-05)
    standardized_entries = centered * reciprocal_spread
    return (
        (standardized_entries * rescale_factor).astype(jnp.bfloat16),
        standardized_entries,
        reciprocal_spread,
    )


def project(rows, weight, factor):
    return (factor * jnp.dot(rows, weight, preferred_element_type=jnp.float32)).astype(jnp.bfloat16)


def to_heads(array):
    count, cols = (array.shape[0], array.shape[1])
    return jnp.transpose(array.reshape(count, cols, HEADS, HEAD_DIM), (1, 2, 0, 3)).reshape(
        cols * HEADS, count, HEAD_DIM
    )


def from_heads(array, cols):
    count = array.shape[1]
    return jnp.transpose(array.reshape(cols, HEADS, count, HEAD_DIM), (2, 0, 1, 3)).reshape(
        count, cols, HEADS * HEAD_DIM
    )


def head_pass(query, keys, payload_entries, d_att):
    scale = HEAD_DIM ** (-0.5)
    scores = jnp.dot(query, keys.T, preferred_element_type=jnp.float32)
    probs = jax.nn.softmax(scores, axis=-1)
    probs_b = probs.astype(jnp.bfloat16)
    mixed_homologs = jnp.dot(probs_b, payload_entries, preferred_element_type=jnp.float32).astype(
        jnp.bfloat16
    )
    d_probs = jnp.dot(d_att, payload_entries.T, preferred_element_type=jnp.float32)
    d_scores = probs * (d_probs - jnp.sum(probs * d_probs, axis=-1, keepdims=True))
    d_scores_b = d_scores.astype(jnp.bfloat16)
    d_query = (scale * jnp.dot(d_scores_b, keys, preferred_element_type=jnp.float32)).astype(
        jnp.bfloat16
    )
    key_part = jnp.einsum("st,sd->td", d_scores_b, query, preferred_element_type=jnp.float32)
    value_part = jnp.einsum("st,sd->td", probs_b, d_att, preferred_element_type=jnp.float32)
    return (mixed_homologs, d_query, key_part, value_part)


def general_body(
    family_activity,
    rescale_factor,
    asking_weights,
    lookup_weights,
    payload_weights,
    exit_weights,
    upstream_adjoint,
    axes=("depth", "res"),
):
    query_weight, key_weight, value_weight, output_matrix = (
        lax.all_gather(asking_weights, axes, axis=0, tiled=True),
        lax.all_gather(lookup_weights, axes, axis=0, tiled=True),
        lax.all_gather(payload_weights, axes, axis=0, tiled=True),
        lax.all_gather(exit_weights, axes, axis=0, tiled=True),
    )
    homologs_each_shard, positions_each_shard, embed_span = family_activity.shape
    standardized_source, standardized_entries, reciprocal_spread = standardize_entries(
        family_activity, rescale_factor
    )
    query = project(standardized_source, query_weight, HEAD_DIM ** (-0.5))
    keys = project(standardized_source, key_weight, 1.0)
    payload_entries = project(standardized_source, value_weight, 1.0)
    keys_all, values_all = (
        lax.all_gather(keys, "depth", axis=0, tiled=True),
        lax.all_gather(payload_entries, "depth", axis=0, tiled=True),
    )
    d_att = jnp.dot(upstream_adjoint, output_matrix.T, preferred_element_type=jnp.float32).astype(
        jnp.bfloat16
    )

    def per_head(items):
        return head_pass(items[0], items[1], items[2], items[3])

    mixed_homologs, d_query, key_part, value_part = lax.map(
        per_head, (to_heads(query), to_heads(keys_all), to_heads(values_all), to_heads(d_att))
    )
    mixed_homologs = from_heads(mixed_homologs, positions_each_shard)
    d_query = from_heads(d_query, positions_each_shard)
    key_part = from_heads(key_part, positions_each_shard)
    value_part = from_heads(value_part, positions_each_shard)
    rows = homologs_each_shard * positions_each_shard
    normed_rows = standardized_source.reshape(rows, embed_span)
    part_query = jnp.dot(
        normed_rows.T, d_query.reshape(rows, embed_span), preferred_element_type=jnp.float32
    )
    part_out = jnp.dot(
        mixed_homologs.reshape(rows, embed_span).T,
        upstream_adjoint.reshape(rows, embed_span),
        preferred_element_type=jnp.float32,
    )
    stacked = jnp.stack([key_part, value_part], axis=2).astype(jnp.bfloat16)
    summed = (
        lax.psum_scatter(stacked, "depth", scatter_dimension=0, tiled=True)
        .astype(jnp.float32)
        .astype(jnp.bfloat16)
    )
    d_keys = summed[:, :, 0, :]
    d_values = summed[:, :, 1, :]
    final_result = (
        family_activity.astype(jnp.float32)
        + jnp.dot(mixed_homologs, output_matrix, preferred_element_type=jnp.float32)
    ).astype(jnp.bfloat16)
    part_key = jnp.dot(
        normed_rows.T, d_keys.reshape(rows, embed_span), preferred_element_type=jnp.float32
    )
    part_value = jnp.dot(
        normed_rows.T, d_values.reshape(rows, embed_span), preferred_element_type=jnp.float32
    )
    d_normed = jnp.dot(d_query, query_weight.T, preferred_element_type=jnp.float32)
    d_normed = d_normed + jnp.dot(d_keys, key_weight.T, preferred_element_type=jnp.float32)
    d_normed = d_normed + jnp.dot(d_values, value_weight.T, preferred_element_type=jnp.float32)
    part_gain = jnp.sum((d_normed * standardized_entries).reshape(rows, embed_span), axis=0)
    unit_gradient = d_normed * rescale_factor
    alignment_gradient = upstream_adjoint.astype(jnp.float32) + reciprocal_spread * (
        unit_gradient
        - jnp.mean(unit_gradient, axis=-1, keepdims=True)
        - standardized_entries
        * jnp.mean(unit_gradient * standardized_entries, axis=-1, keepdims=True)
    )
    query_gradient, key_gradient, value_gradient, output_gradient, gain_gradient = (
        lax.psum_scatter(part_query, axes, scatter_dimension=0, tiled=True),
        lax.psum_scatter(part_key, axes, scatter_dimension=0, tiled=True),
        lax.psum_scatter(part_value, axes, scatter_dimension=0, tiled=True),
        lax.psum_scatter(part_out, axes, scatter_dimension=0, tiled=True),
        lax.psum_scatter(part_gain, axes, scatter_dimension=0, tiled=True),
    )
    return (
        final_result,
        alignment_gradient.astype(jnp.bfloat16),
        query_gradient,
        key_gradient,
        value_gradient,
        output_gradient,
        gain_gradient,
    )


F32, BF16 = jnp.float32, jnp.bfloat16
SCALE = HEAD_DIM ** (-0.5)


def swap(value, axis, size, bits):
    return lax.ppermute(value, axis, [(i, i ^ bits) for i in range(size)])


def dot(a, b, contract=(1, 0)):
    return lax.dot_general(
        a, b, (((contract[0],), (contract[1],)), ((), ())), preferred_element_type=F32
    )


def unit_rows(x):
    x = x.astype(F32)
    centered = x - jnp.mean(x, axis=-1, keepdims=True)
    inverse = lax.rsqrt(jnp.mean(centered * centered, axis=-1, keepdims=True) + 1e-05)
    return centered * inverse, inverse


def head_masks(span):
    lane = lax.broadcasted_iota(jnp.int32, (8, span), 1)
    return [
        ((lane >= at) & (lane < at + HEAD_DIM)).astype(F32)[0:1].astype(BF16)
        for at in range(0, span, HEAD_DIM)
    ]


def only_head(turned, h):
    low, high = h * HEAD_DIM, (h + 1) * HEAD_DIM
    parts = [jnp.zeros((low, turned.shape[1]), turned.dtype)] if low else []
    parts.append(turned[low:high])
    if high < turned.shape[0]:
        parts.append(jnp.zeros((turned.shape[0] - high, turned.shape[1]), turned.dtype))
    return jnp.concatenate(parts, axis=0)


def fetch(pairs, sems):
    copies = [pltpu.make_async_copy(src, dst, sems.at[i]) for i, (src, dst) in enumerate(pairs)]
    for copy in copies:
        copy.start()
    return copies


class Sender:
    def __init__(self, sems):
        self.sems, self.copies = sems, []

    def send(self, src, dst):
        copy = pltpu.make_async_copy(src, dst, self.sems.at[len(self.copies)])
        copy.start()
        self.copies.append(copy)

    def finish(self):
        for copy in self.copies:
            copy.wait()


def pack_kernel(dims, w_query, w_key, w_value, w_out, out, out_cut):
    depth, zs, shard, block, span = dims
    for d in range(depth):
        lanes = slice(d * span, (d + 1) * span)
        for i, w in enumerate((w_query, w_key, w_value)):
            out[d, :, i * span : (i + 1) * span] = w[:, lanes]
        out_cut[d] = w_out[:, lanes]


def norm_kernel(dims, *refs):
    depth, zs, shard, block, span = dims
    gain, xs_h, refs = refs[0], refs[1 : 1 + depth], refs[1 + depth :]
    normed_h, normed_t_h, xs, normed, normed_t, in_sems, out_sems = refs
    copies = fetch([(xs_h[j], xs.at[j]) for j in range(depth)], in_sems)
    sender = Sender(out_sems)
    for j in range(depth):
        copies[j].wait()
        unit, _ = unit_rows(xs[j])
        rows = pl.ds(j * block, block)
        wide = unit * gain[...]
        normed[rows, :] = wide.astype(BF16)
        sender.send(normed.at[rows], normed_h.at[rows])
        normed_t[:, rows] = jnp.transpose(wide).astype(BF16)
        sender.send(normed_t.at[:, rows], normed_t_h.at[:, rows])
    sender.finish()


def forward_kernel(dims, *refs):
    depth, zs, shard, block, span = dims
    heads = span // HEAD_DIM
    pos, w_near, w_far, normed_h = refs[:4]
    (query_h, query_t_h, keys_h, values_h, keys_t_h, att_t_h, lse_h) = refs[4:11]
    (wq_t_h, wk_t_h, wv_t_h, w_out_t_h), outs_h = refs[11:15], refs[15 : 15 + depth]
    refs = refs[15 + depth :]
    normed, query, query_t, keys, values, keys_t, values_t, att_t, lse = refs[:9]
    wq, wk, wv, w_out, wq_t, wk_t, wv_t, w_out_t, outs, in_sems, out_sems = refs[9:]
    copies = fetch([(normed_h, normed)], in_sems)
    sender = Sender(out_sems)

    own_z, first = pos[0], pos[1] == 0
    for z in range(zs):
        for d in range(depth):
            near, far = w_near[z ^ own_z, d].astype(F32), w_far[z ^ own_z, d].astype(F32)
            both = jnp.concatenate(
                [jnp.where(first, near, far), jnp.where(first, far, near)], axis=0
            ).astype(BF16)
            rows = slice((d * zs + z) * 2 * shard, (d * zs + z + 1) * 2 * shard)
            for i, w in enumerate((wq, wk, wv)):
                w[rows, :] = both[:, i * span : (i + 1) * span]
            rows = slice(z * 2 * shard, (z + 1) * 2 * shard)
            w_out[rows, d * span : (d + 1) * span] = both[:, 3 * span :]
    copies[0].wait()

    for scale, w, full, turned, full_h, turned_h in (
        (SCALE, wq, query, query_t, query_h, query_t_h),
        (1.0, wk, keys, keys_t, keys_h, keys_t_h),
        (1.0, wv, values, values_t, values_h, None),
    ):
        rows = (scale * dot(normed[...], w[...])).astype(BF16)
        full[...] = rows
        turned[...] = jnp.transpose(rows)
        sender.send(full, full_h)
        if turned_h is not None:
            sender.send(turned, turned_h)
    for w, turned, turned_h in (
        (wq, wq_t, wq_t_h),
        (wk, wk_t, wk_t_h),
        (wv, wv_t, wv_t_h),
        (w_out, w_out_t, w_out_t_h),
    ):
        turned[...] = jnp.transpose(w[...])
        sender.send(turned, turned_h)


    units = [(j, h) for j in range(depth) for h in range(heads)]

    def score(j, h):
        return dot(keys[...], only_head(query_t[:, j * block : (j + 1) * block], h))

    ready = [score(*unit) for unit in units[:2]]
    for i, (j, h) in enumerate(units):
        cols, lanes = slice(j * block, (j + 1) * block), slice(h * HEAD_DIM, (h + 1) * HEAD_DIM)
        scores = ready.pop(0)
        top = jnp.max(scores, axis=0, keepdims=True)
        e = jnp.exp(scores - top)
        total = jnp.sum(e, axis=0, keepdims=True)
        if i + 2 < len(units):
            ready.append(score(*units[i + 2]))
        att_t[lanes, cols] = dot(values_t[lanes, :], e.astype(BF16)) * (1.0 / total)
        lse[h, :, cols] = top + jnp.log(total)
    sender.send(att_t, att_t_h)
    sender.send(lse, lse_h)
    att = jnp.transpose(att_t[...]).astype(BF16)
    for j in range(depth):
        outs[j] = dot(att[j * block : (j + 1) * block], w_out[...]).astype(BF16)
        sender.send(outs.at[j], outs_h[j])
    sender.finish()


def backward_kernel(dims, *refs):
    depth, zs, shard, block, span = dims
    heads = span // HEAD_DIM
    pos, refs = refs[0], refs[1:]
    gs_h, refs = refs[:depth], refs[depth:]
    (w_out_t_h, query_h, query_t_h, keys_h, values_h, keys_t_h, lse_h, normed_t_h) = refs[:8]
    (att_t_h, wq_t_h, wk_t_h, wv_t_h, near, far), refs = refs[8:14], refs[14:]
    dns_h, refs = refs[: depth + 1], refs[depth + 1 :]
    (gs, w_out_t, query, query_t, keys, values, keys_t, lse, normed_t, att_t) = refs[:10]
    (wq_t, wk_t, wv_t, d_att, d_att_t, delta, d_query_t, d_keys, d_values) = refs[10:19]
    grad_out, dns, in_sems, out_sems = refs[19:]
    copies = fetch(
        [(w_out_t_h, w_out_t)]
        + [(gs_h[j], gs.at[pl.ds(j * block, block)]) for j in range(depth)]
        + [
            (att_t_h, att_t),
            (keys_h, keys),
            (query_h, query),
            (query_t_h, query_t),
            (values_h, values),
            (lse_h, lse),
            (keys_t_h, keys_t),
            (normed_t_h, normed_t),
            (wq_t_h, wq_t),
            (wk_t_h, wk_t),
            (wv_t_h, wv_t),
        ],
        in_sems,
    )
    loaded, later = 8 + depth, copies[8 + depth :]

    d_keys[...] = jnp.zeros_like(d_keys)
    d_values[...] = jnp.zeros_like(d_values)
    for copy in copies[: 2 + depth]:
        copy.wait()
    part = dot(gs[...], w_out_t[...]).astype(BF16)
    d_att[...] = part
    part = jnp.transpose(part)
    d_att_t[...] = part
    product = part.astype(F32) * att_t[...]
    for h in range(heads):
        delta[h] = jnp.sum(product[h * HEAD_DIM : (h + 1) * HEAD_DIM], axis=0, keepdims=True)
    for copy in copies[2 + depth : loaded]:
        copy.wait()
    masks = head_masks(span)

    def step(j, _):
        cols = pl.ds(pl.multiple_of(j * block, block), block)
        q_block, g_block = query[cols, :], d_att[cols, :]
        qs = [q_block * m for m in masks]
        ds = [g_block * m for m in masks]

        def pair(h):
            q_turned = only_head(query_t[:, cols], h)
            d_turned = only_head(d_att_t[:, cols], h)
            return dot(keys[...], q_turned), dot(values[...], d_turned)

        pairs = [pair(h) for h in range(min(2, heads))]
        for h in range(heads):
            scores, d_probs = pairs[h]
            probs = jnp.exp(scores - lse[h, :, cols])
            d_scores = (probs * (d_probs - delta[h, :, cols])).astype(BF16)
            if h + 2 < heads:
                pairs.append(pair(h + 2))
            values_add = dot(probs.astype(BF16), ds[h])
            keys_add = dot(d_scores, qs[h])
            value_part = values_add if h == 0 else value_part + values_add
            key_part = keys_add if h == 0 else key_part + keys_add
            lanes = slice(h * HEAD_DIM, (h + 1) * HEAD_DIM)
            d_query_t[lanes, cols] = SCALE * dot(keys_t[lanes, :], d_scores)
        d_values[...] += value_part.astype(BF16).astype(F32)
        d_keys[...] += key_part.astype(BF16).astype(F32)
        return 0

    lax.fori_loop(0, depth, step, 0)
    for copy in later:
        copy.wait()
    d_query = jnp.transpose(d_query_t[...].astype(BF16))
    d_key, d_value = d_keys[...].astype(BF16), d_values[...].astype(BF16)
    sender = Sender(out_sems)
    for i in range(0, depth, 2):
        rows = slice(i * block, (i + 2) * block)
        d_normed = dot(d_query[rows], wq_t[...])
        d_normed = d_normed + dot(d_key[rows], wk_t[...])
        d_normed = d_normed + dot(d_value[rows], wv_t[...])
        dns[rows, :] = d_normed.astype(BF16)
        for j in (i, i + 1):
            if j < depth - 1:
                sender.send(dns.at[pl.ds(j * block, block)], dns_h[j])
            else:
                half = block // 2
                sender.send(dns.at[pl.ds(j * block, half)], dns_h[j])
                sender.send(dns.at[pl.ds(j * block + half, half)], dns_h[j + 1])

    grad_out[...] = dot(att_t[...].astype(BF16), gs[...])
    grads = [dot(normed_t[...], d) for d in (d_query, d_key, d_value)]
    own_z, first, own_d = pos[0], pos[1] == 0, pos[2]
    for d in range(depth):
        for z in range(zs):
            sides = []
            for c in range(2):
                row, row_out = ((d * zs + z) * 2 + c) * shard, (z * 2 + c) * shard
                sides.append(
                    [g[row : row + shard] for g in grads]
                    + [grad_out[row_out : row_out + shard, d * span : (d + 1) * span]]
                )
            at = 0
            for one, two in zip(*sides):
                lanes = slice(at, at + one.shape[1])
                at += one.shape[1]
                near[z ^ own_z, d ^ own_d, :, lanes] = jnp.where(first, one, two).astype(BF16)
                far[z ^ own_z, d ^ own_d, :, lanes] = jnp.where(first, two, one).astype(BF16)
    sender.finish()


def align_kernel(dims, gain, x, upstream, *refs):
    dns, out = refs[:-1], refs[-1]
    d_normed = dns[0][...].astype(F32)
    for part in dns[1:]:
        d_normed = d_normed + part[...].astype(F32)
    unit, inverse = unit_rows(x[...])
    d_unit = d_normed * gain[...]
    out[...] = (
        upstream[...].astype(F32)
        + inverse
        * (
            d_unit
            - jnp.mean(d_unit, axis=-1, keepdims=True)
            - unit * jnp.mean(d_unit * unit, axis=-1, keepdims=True)
        )
    ).astype(BF16)


def finish_kernel(dims, *refs):
    depth, zs, shard, block, span = dims
    pos, gain, weights, acc, refs = refs[0], refs[1], refs[2:5], refs[5], refs[6:]
    parts, outs = refs[: depth - 1], refs[depth - 1 :]
    own_d = pos[2]
    blocks = [acc[0][:, : 3 * span]] + [p[...].astype(F32) for p in parts]
    for d in range(depth):
        lanes = slice(d * span, (d + 1) * span)
        total = blocks[0]
        for k in range(1, depth):
            total = jnp.where((d ^ own_d) == k, blocks[k], total)
        for i in range(3):
            outs[i][:, lanes] = total[:, i * span : (i + 1) * span]
        outs[3][:, lanes] = acc[d ^ own_d][:, 3 * span :]
    column = weights[0][...].astype(F32) * outs[0][...]
    for w, grad in zip(weights[1:], outs[1:3]):
        column = column + w[...].astype(F32) * grad[...]
    column = jnp.sum(column, axis=1, keepdims=True)
    wide = jnp.concatenate([column, jnp.zeros((128 - shard, 1), F32)], axis=0)
    row = jnp.transpose(jnp.broadcast_to(wide, (128, 128)))[0:1, :shard]
    outs[4][...] = row / gain[...]


VMEM, ANY, SMEM = pltpu.VMEM, pl.ANY, pltpu.SMEM


def call(kernel, dims, ins, outs, scratch, sems, flops, mib=62):
    args = [a for a, _ in ins]
    shapes = [jax.ShapeDtypeStruct(shape, kind) for shape, kind, _ in outs]
    size = sum(a.size * a.dtype.itemsize for a in args + shapes)
    return pl.pallas_call(
        functools.partial(kernel, dims),
        out_shape=shapes,
        in_specs=[pl.BlockSpec(memory_space=space) for _, space in ins],
        out_specs=[pl.BlockSpec(memory_space=space) for _, _, space in outs],
        scratch_shapes=[pltpu.VMEM(shape, kind) for shape, kind in scratch]
        + [pltpu.SemaphoreType.DMA((n,)) for n in sems],
        compiler_params=pltpu.CompilerParams(vmem_limit_bytes=mib * 1024 * 1024),
        cost_estimate=pl.CostEstimate(flops=flops, bytes_accessed=size, transcendentals=0),
    )(*args)


def head_body(depth, res, *args):
    x, gain, w_query, w_key, w_value, w_out, upstream = args
    homologs, _, width = x.shape
    span, zs = width // depth, res // 2
    shard = w_query.shape[0]
    total, heads = homologs * depth, span // HEAD_DIM
    dims = (depth, zs, shard, homologs, span)
    x = x.reshape(homologs, width)
    upstream = upstream.reshape(homologs, width)
    gain = gain.reshape(1, width)
    pos = jnp.stack([lax.axis_index(a) for a in ("z", "core", "depth")]).astype(jnp.int32)

    xs = [x] + [swap(x, "depth", depth, k) for k in range(1, depth - 1)]

    packed, out_cut = call(
        pack_kernel,
        dims,
        [(w, VMEM) for w in (w_query, w_key, w_value, w_out)],
        [((depth, shard, 3 * span), BF16, VMEM), ((depth, shard, span), BF16, VMEM)],
        [],
        [],
        1000,
    )
    mine = lax.all_to_all(packed, "depth", 0, 0, tiled=True)
    mine = jnp.concatenate([mine, out_cut], axis=2)
    mine, *xs = lax.optimization_barrier([mine] + xs)
    xs.append(swap(xs[0], "depth", depth, depth - 1))
    parts = [mine] + [swap(mine, "z", zs, k) for k in range(1, zs)]
    gs = [upstream] + [swap(upstream, "depth", depth, k) for k in range(1, depth)]

    rows, turned = ((total, span), BF16), ((span, total), BF16)
    half = homologs // 2
    block, halved = ((homologs, width), BF16), ((half, width), BF16)
    blocks = ((depth, homologs, width), BF16)
    norm, stats = ((total, width), BF16), ((heads, 1, total), F32)
    in_weights, out_weights = ((width, span), BF16), ((span, width), BF16)
    pass_flops = 2 * total * total * span
    normed, normed_t = call(
        norm_kernel,
        dims,
        [(gain, VMEM)] + [(a, ANY) for a in xs],
        [norm + (ANY,), ((width, total), BF16, ANY)],
        [blocks, norm, ((width, total), BF16)],
        [depth, 2 * depth],
        1000,
    )
    first_row = (lax.axis_index("depth") * res + pos[0] * 2 + pos[1]) * shard
    own_gain = lax.dynamic_slice(gain, (0, first_row), (1, shard))
    normed, pos, own_gain, *parts = lax.optimization_barrier([normed, pos, own_gain] + parts)
    w_near = jnp.stack(parts, axis=0)
    w_far = swap(w_near, "core", 2, 1)

    turned_f32 = ((span, total), F32)
    saved = [rows, turned, rows, rows, turned, turned_f32, stats]
    saved = saved + [out_weights] * 3 + [in_weights]
    query, query_t, keys, values, keys_t, att_t, lse, wq_t, wk_t, wv_t, wo_t, *outs = call(
        forward_kernel,
        dims,
        [(pos, SMEM), (w_near, VMEM), (w_far, VMEM), (normed, ANY)],
        [s + (ANY,) for s in saved + [block] * depth],
        [norm, rows, turned, rows, rows, turned, turned, turned_f32, stats]
        + [in_weights] * 3
        + [out_weights] * 4
        + [in_weights, blocks],
        [1, len(saved) + depth],
        8 * pass_flops,
    )

    packed = (zs, depth, shard, 4 * span)
    near, far, *dns = call(
        backward_kernel,
        dims,
        [(pos, SMEM)]
        + [(a, ANY) for a in gs + [wo_t, query, query_t, keys, values, keys_t, lse, normed_t]]
        + [(a, ANY) for a in (att_t, wq_t, wk_t, wv_t)],
        [(packed, BF16, VMEM)] * 2 + [s + (ANY,) for s in [block] * 3 + [halved] * 2],
        [norm, in_weights, rows, turned, rows, rows, turned, stats, ((width, total), BF16)]
        + [turned_f32, out_weights, out_weights, out_weights]
        + [rows, turned, stats, turned_f32]
        + [((total, span), F32)] * 2
        + [((span, width), F32), norm],
        [depth + 12, depth + 1],
        24 * pass_flops,
    )

    outs = [outs[0]] + [swap(outs[k], "depth", depth, k) for k in range(1, depth)]
    near, far, dns, outs = lax.optimization_barrier((near, far, dns, outs))

    far = swap(far, "core", 2, 1)
    dn0, dn1, dn2, dn3_top, dn3_bottom = dns
    top, bottom = swap(dn3_top, "depth", depth, 1), swap(dn3_bottom, "depth", depth, 2)
    sums = [near[k].astype(F32) + far[k].astype(F32) for k in range(1, zs)]
    low = [swap(part.astype(BF16), "z", zs, k + 1) for k, part in enumerate(sums)]
    low[0], top, bottom, outs = lax.optimization_barrier((low[0], top, bottom, outs))
    dn2 = dn2.astype(F32) + jnp.concatenate([top, jnp.zeros_like(top)], axis=0).astype(F32)
    dn1 = dn1.astype(F32) + jnp.concatenate([jnp.zeros_like(bottom), bottom], axis=0).astype(F32)
    final_result = (x.astype(F32) + sum(o.astype(F32) for o in outs)).astype(BF16)
    own = near[0].astype(F32) + far[0].astype(F32)
    dn1, dn2, final_result, own = lax.optimization_barrier(
        (dn1.astype(BF16), dn2.astype(BF16), final_result, own)
    )
    dn1, dn2 = swap(dn1, "depth", depth, 1), swap(dn2, "depth", depth, 2)
    acc = own + sum(p.astype(F32) for p in low)
    parts = [
        swap(acc[k, :, : 3 * span].astype(BF16), "depth", depth, k) for k in range(1, depth)
    ]
    alignment = call(
        align_kernel,
        dims,
        [(a, VMEM) for a in (gain, x, upstream, dn0, dn1, dn2)],
        [block + (VMEM,)],
        [],
        [],
        1000 * total * width,
        16,
    )[0]
    alignment, *parts = lax.optimization_barrier([alignment] + parts)
    grad_query, grad_key, grad_value, grad_out, gain_rows = call(
        finish_kernel,
        dims,
        [(pos, SMEM)]
        + [(a, VMEM) for a in [own_gain, w_query, w_key, w_value, acc] + parts],
        [((shard, width), F32, VMEM)] * 4 + [((1, shard), F32, VMEM)],
        [],
        [],
        1000,
        16,
    )
    return (
        final_result.reshape(homologs, 1, width),
        alignment.reshape(homologs, 1, width),
        grad_query,
        grad_key,
        grad_value,
        grad_out,
        gain_rows.reshape(shard),
    )


def solution(mesh):
    depth, res = mesh.shape["depth"], mesh.shape["res"]
    powers = depth & (depth - 1) == 0 and res & (res - 1) == 0 and res > 1
    if powers and depth == 4 and res >= 4 and HEADS % depth == 0:
        axes = ("depth", "z", "core")
        mesh = Mesh(mesh.devices.reshape(depth, res // 2, 2), axes)
        res_axes, run = ("z", "core"), functools.partial(head_body, depth, res)
    else:
        axes = ("depth", "res")
        res_axes, run = ("res",), general_body

    def body(*args):
        if args[0].shape[1] != 1:
            return general_body(*args, axes=axes)
        return run(*args)

    rows = P("depth", res_axes, None)
    weight = P(axes, None)
    return jax.shard_map(
        body,
        mesh=mesh,
        in_specs=(rows, P(), weight, weight, weight, weight, rows),
        out_specs=(rows, rows, weight, weight, weight, weight, P(axes)),
        check_vma=False,
    )
```
